128 devices in a mesh: dp: 4 (over y), seq: 32 (over z, x, core).
Axes of the slice: x: 4, y: 4, z: 4, core: 2. Of those that a mesh axis runs over, the one named last changes fastest.
Arguments:
- first_in: bfloat16 [16384, 1024], P(('dp', 'seq')), may hold values from -6 to 6
- second_in: bfloat16 [16384, 1024], P(('dp', 'seq')), may hold values from -6 to 6
- attn_gain: bfloat16 [1024], P(('dp', 'seq')), may hold values from 0.5 to 1.5
- attn_shift: bfloat16 [1024], P(('dp', 'seq')), may hold values from -3 to 3
- w_joint: bfloat16 [1024, 1024], P(('dp', 'seq')), may hold values from -0.375 to 0.375
- w_value: bfloat16 [1024, 1024], P(('dp', 'seq')), may hold values from -0.1875 to 0.1875
- w_output: bfloat16 [1024, 1024], P(('dp', 'seq')), may hold values from -0.75 to 0.75
- ffn_gain: bfloat16 [1024], P(('dp', 'seq')), may hold values from 0.5 to 1.5
- ffn_shift: bfloat16 [1024], P(('dp', 'seq')), may hold values from -3 to 3
- w_inner: bfloat16 [1024, 4096], P(('dp', 'seq')), may hold values from -0.1875 to 0.1875
- b_inner: bfloat16 [4096], P(('dp', 'seq')), may hold values from -3 to 3
- w_outer: bfloat16 [4096, 1024], P(('dp', 'seq')), may hold values from -0.09375 to 0.09375
- b_outer: bfloat16 [1024], P(('dp', 'seq')), may hold values from -3 to 3
- buckets: int32 [4, 16384, 1], P(None, ('dp', 'seq')), may hold values from 0 to 31; in each aligned block of 128 rows (0 to 127, 128 to 255, ..., all dimensions but the last counted through in order) at most 8 rows name the same one
- cot_first: bfloat16 [16384, 1024], P(('dp', 'seq')), may hold values from -6 to 6
- cot_second: bfloat16 [16384, 1024], P(('dp', 'seq')), may hold values from -6 to 6
Outputs:
- first_out: bfloat16 [16384, 1024], P(('dp', 'seq'))
- second_out: bfloat16 [16384, 1024], P(('dp', 'seq'))
- grad_first: bfloat16 [16384, 1024], P(('dp', 'seq'))
- grad_second: bfloat16 [16384, 1024], P(('dp', 'seq'))
- grad_attn_gain: float32 [1024], P(('dp', 'seq'))
- grad_attn_shift: float32 [1024], P(('dp', 'seq'))
- grad_joint: float32 [1024, 1024], P(('dp', 'seq'))
- grad_value: float32 [1024, 1024], P(('dp', 'seq'))
- grad_output: float32 [1024, 1024], P(('dp', 'seq'))
- grad_ffn_gain: float32 [1024], P(('dp', 'seq'))
- grad_ffn_shift: float32 [1024], P(('dp', 'seq'))
- grad_inner: float32 [1024, 4096], P(('dp', 'seq'))
- grad_b_inner: float32 [4096], P(('dp', 'seq'))
- grad_outer: float32 [4096, 1024], P(('dp', 'seq'))
- grad_b_outer: float32 [1024], P(('dp', 'seq'))
The draws below stay inside these ranges and needn't reach their ends.
Inputs may be any that keep to these rules, and one draw needn't show every extreme that they name: `buckets`: in each round, among the 128 tokens of one device (aligned blocks of rows), no bucket id appears more than 8 times, and in every draw some bucket appears exactly 8 times in some block.
All inputs are finite; a program needn't handle non-finite values.
Results may differ from the reference program's by a relative error of at most 0.015.
The reference program's roundings to bfloat16 on the way count: a program that leaves them out, or rounds other values in their place, can miss the bound.
Values may be sent and summed in bfloat16 or wider, within the bound.
No kernel may reach another device: no remote copies, remote signals or barrier semaphores. Data moves between devices by JAX's collectives and lax.ppermute only.
A program may use at most 192 MiB of HBM per device.

```python
import math
import jax
import jax.numpy as jnp
import numpy as np
from jax import lax

D = 1024
FF = 4096
HEADS = 8
HEAD_DIM = 128
ROUNDS = 4
TOK_DEV = 128
SEQLEN = 4096
TOKENS = 16384
BUCKETS = 32
MOST = 8


def shard_levels(stream_key, shape, cuts, low, high):
    loudness, own = 1.0, jax.random.fold_in(stream_key, 6)
    for dim, parts in cuts:
        steps = jnp.exp(jax.random.uniform(jax.random.fold_in(own, dim), (parts,), jnp.float32, low / len(cuts), high / len(cuts)))
        loudness = loudness * jnp.repeat(steps, shape[dim] // parts).reshape([-1 if axis == dim else 1 for axis in range(len(shape))])
    return loudness


def routed_block(own_key, own, number, rows, number_of, top, limit, slope):
    ranking = jax.random.permutation(own_key, number_of)
    heavy_load, usual = shares(number_of, rows * top, limit, slope, True), shares(number_of, rows * top, limit, slope, False)
    places = jnp.arange(number_of)

    def named(lengths, turn):
        used = int((lengths > 0).sum())
        fixed = max(1, used // 4)
        shifted = fixed + (places - fixed + turn * (used - fixed)) % max(1, number_of - fixed)
        return jnp.zeros((number_of,), jnp.int32).at[ranking[jnp.where(places < fixed, places, shifted)]].set(jnp.asarray(lengths, jnp.int32))

    lengths = jnp.where(number % 4 == 0, named(heavy_load, number // 4), named(usual, number - number // 4 - 1))
    mixed = jax.random.permutation(jax.random.fold_in(own, 3), number_of)
    source_of, taker = mixed[0:number_of // 2 * 2:2], mixed[1:number_of // 2 * 2:2]
    slack = jnp.minimum(lengths[source_of] - 1, limit - lengths[taker]) // 2
    slack = jnp.where((source_of == ranking[0]) | (taker == ranking[0]) | (lengths[taker] == 0), 0, jnp.maximum(slack, 0))
    shifted = jax.random.randint(jax.random.fold_in(own, 4), (number_of // 2,), 0, 1 << 20) % (slack + 1)
    lengths = lengths.at[source_of].add(-shifted).at[taker].add(shifted)
    members = jnp.searchsorted(jnp.cumsum(lengths), jnp.arange(rows * top), side="right").astype(jnp.int32)
    listing = members.reshape(top, rows).T
    listing = listing[jax.random.permutation(jax.random.fold_in(own, 1), rows)]
    turn = jax.random.randint(jax.random.fold_in(own, 2), (rows, 1), 0, top)
    return jnp.take_along_axis(listing, (jnp.arange(top)[None, :] + turn) % top, axis=1)


def shares(amount, total, reach, skew, full):
    loads = [(1 << 20) // math.isqrt(rank ** skew) + 1 for rank in range(1, amount + 1)]
    largest = reach if full else min(reach, max(-(-total // amount), total * loads[0] // sum(loads)))
    least = 1 if total - largest >= amount - 1 else 0
    counts, surplus = [largest] + [least] * (amount - 1), total - largest - least * (amount - 1)
    while surplus > 0:
        free = [i for i in range(1, amount) if counts[i] < largest] or [i for i in range(1, amount) if counts[i] < reach]
        mass, budget = sum([loads[i] for i in free]), surplus
        for i in free:
            more = min(reach - counts[i], max(1, budget * loads[i] // mass), surplus)
            counts[i] = counts[i] + more
            surplus = surplus - more
    return np.array(counts)


def centred(own_key, dims, scale, most, cuts=(), held_as=jnp.bfloat16):
    factor_of = shard_levels(own_key, dims, cuts, -0.22, 0.18) if cuts else 1.0
    result = jax.random.normal(own_key, dims, jnp.float32) * scale * factor_of
    return jnp.minimum(jnp.maximum(result, -most), most).astype(held_as)


def setup_inputs(seed: int = 0) -> dict:
    seeds = jax.random.split(jax.random.key(seed), 17)
    first_in = centred(seeds[0], (TOKENS, D), 1.0, 6.0, ((0, 128),))
    second_in = centred(seeds[1], (TOKENS, D), 1.0, 6.0, ((0, 128),))
    attn_gain = jnp.clip(1.0 + 0.1 * jax.random.normal(seeds[2], (D,), jnp.float32), 0.5, 1.5).astype(jnp.bfloat16)
    attn_shift = centred(seeds[3], (D,), 0.5, 3.0, ((0, 128),))
    w_joint = centred(seeds[4], (D, D), (D // 4) ** -0.5, 0.375, ((0, 128),))
    w_value = centred(seeds[5], (D, D), D ** -0.5, 0.1875, ((0, 128),))
    w_output = centred(seeds[6], (D, D), (D // 16) ** -0.5, 0.75, ((0, 128),))
    ffn_gain = jnp.clip(1.0 + 0.1 * jax.random.normal(seeds[7], (D,), jnp.float32), 0.5, 1.5).astype(jnp.bfloat16)
    ffn_shift = centred(seeds[8], (D,), 0.5, 3.0, ((0, 128),))
    w_inner = centred(seeds[9], (D, FF), D ** -0.5, 0.1875, ((0, 128),))
    b_inner = centred(seeds[10], (FF,), 0.5, 3.0, ((0, 128),))
    w_outer = centred(seeds[11], (FF, D), FF ** -0.5, 0.09375, ((0, 128),))
    b_outer = centred(seeds[12], (D,), 0.5, 3.0, ((0, 128),))
    buckets_keys = jax.random.split(jax.random.fold_in(seeds[13], 1), ROUNDS * TOKENS // TOK_DEV)
    buckets_turns = jax.random.permutation(jax.random.fold_in(seeds[13], 3), ROUNDS * TOKENS // TOK_DEV)
    buckets = jax.vmap(lambda own, number: routed_block(jax.random.fold_in(seeds[13], 2), own, number, TOK_DEV, BUCKETS, 1, MOST, 2))(buckets_keys, buckets_turns).reshape((ROUNDS, TOKENS, 1))
    cot_first = centred(seeds[14], (TOKENS, D), 1.0, 6.0, ((0, 128),))
    cot_second = centred(seeds[15], (TOKENS, D), 1.0, 6.0, ((0, 128),))
    return dict(first_in=first_in, second_in=second_in, attn_gain=attn_gain, attn_shift=attn_shift, w_joint=w_joint, w_value=w_value, w_output=w_output, ffn_gain=ffn_gain, ffn_shift=ffn_shift, w_inner=w_inner, b_inner=b_inner, w_outer=w_outer, b_outer=b_outer, buckets=buckets, cot_first=cot_first, cot_second=cot_second)


@jax.custom_vjp
def low(v):
    return lax.optimization_barrier(v.astype(jnp.bfloat16)).astype(jnp.float32)

@jax.custom_vjp
def low_back(v):
    return v

def low_keep(v):
    return (low(v), None)

def low_pass(kept, grad):
    return (grad,)

def back_keep(v):
    return (v, None)

def back_low(kept, grad):
    return (low(grad),)
low.defvjp(low_keep, low_pass)
low_back.defvjp(back_keep, back_low)
EPS_NORM = 1e-05
EPS_KEY = 1e-06
SELF_SCORE = -10000.0
MASKED_SCORE = -1000000000.0
HIGHEST = lax.Precision.HIGHEST

def norm_apply(values, gain, shift):
    row_mean = lax.optimization_barrier(jnp.mean(values, axis=-1, keepdims=True))
    centered = values - row_mean
    spread = lax.optimization_barrier(jnp.mean(centered * centered, axis=-1, keepdims=True))
    return centered * lax.rsqrt(spread + EPS_NORM) * gain + shift

def unit_keys(joint_proj):
    shaped = joint_proj.reshape(joint_proj.shape[:-1] + (HEADS, HEAD_DIM))
    inverse_norm = lax.rsqrt(lax.optimization_barrier(jnp.sum(shaped * shaped, axis=-1, keepdims=True)) + EPS_KEY)
    return (shaped * inverse_norm).reshape(joint_proj.shape)

def combine_rounds(outputs, totals):
    weights = jax.nn.softmax(totals, axis=0)
    shaped = outputs.reshape(outputs.shape[:-1] + (HEADS, HEAD_DIM))
    mixed_heads = lax.optimization_barrier(jnp.sum(weights[..., None] * shaped, axis=0))
    return mixed_heads.reshape(mixed_heads.shape[:-2] + (HEADS * HEAD_DIM,))

def round_attention(queries, keys, values, chosen):
    length = queries.shape[0]
    block_rows = min(512, length)
    block_count = length // block_rows
    shape3 = (length, HEADS, HEAD_DIM)
    key_rows = keys.reshape(shape3)
    value_rows = values.reshape(shape3)
    places = jnp.arange(length, dtype=jnp.int32)

    def one_block(pieces):
        query_block, chosen_block, place_block = pieces
        scores = jnp.einsum('qhd,khd->hqk', query_block, key_rows, precision=HIGHEST)
        scores = low_back(scores)
        allowed = (chosen_block[:, None] == chosen[None, :]) & (places[None, :] <= place_block[:, None])
        itself = places[None, :] == place_block[:, None]
        scores = jnp.where(itself[None], SELF_SCORE, jnp.where(allowed[None], scores, MASKED_SCORE))
        row_peak = lax.optimization_barrier(jnp.max(scores, axis=-1, keepdims=True))
        exponent = jnp.exp(scores - row_peak)
        row_total = lax.optimization_barrier(jnp.sum(exponent, axis=-1, keepdims=True))
        probabilities = low(exponent / row_total)
        attended = jnp.einsum('hqk,khd->qhd', probabilities, value_rows, precision=HIGHEST)
        log_total = jnp.transpose((row_peak + jnp.log(row_total))[:, :, 0])
        return (attended.reshape(attended.shape[0], HEADS * HEAD_DIM), log_total)
    blocks = (queries.reshape(block_count, block_rows, HEADS, HEAD_DIM), chosen.reshape(block_count, block_rows), places.reshape(block_count, block_rows))
    attended, log_total = lax.map(jax.checkpoint(one_block), blocks)
    return (attended.reshape(length, HEADS * HEAD_DIM), log_total.reshape(length, HEADS))

def layer_forward(first_in, second_in, params, chosen_all):
    attn_gain, attn_shift, w_joint, w_value, w_output, ffn_gain, ffn_shift, w_inner, b_inner, w_outer, b_outer = params
    normed = low(norm_apply(second_in, attn_gain, attn_shift))
    joint_proj = low_back(jnp.dot(normed, w_joint, precision=HIGHEST))
    value_proj = low_back(jnp.dot(normed, w_value, precision=HIGHEST))
    queries = low(joint_proj)
    values_low = low(value_proj)
    outputs = []
    totals = []
    for round_index in range(ROUNDS):
        round_queries = low_back(queries)
        round_keys = low(unit_keys(round_queries))
        round_values = low_back(values_low)
        attended, log_total = round_attention(round_queries, round_keys, round_values, chosen_all[round_index])
        outputs.append(low_back(low(attended)))
        totals.append(low_back(low(log_total)))
    mixed_heads = low(combine_rounds(jnp.stack(outputs), jnp.stack(totals)))
    first_sum = first_in + low_back(jnp.dot(mixed_heads, w_output, precision=HIGHEST))
    ffn_input = low(norm_apply(first_sum, ffn_gain, ffn_shift))
    hidden = low_back(jnp.dot(ffn_input, w_inner, precision=HIGHEST) + b_inner)
    active = low(jax.nn.gelu(hidden))
    second_sum = second_in + low_back(jnp.dot(active, w_outer, precision=HIGHEST) + b_outer)
    return (first_sum, second_sum)

def reference(first_in, second_in, attn_gain, attn_shift, w_joint, w_value, w_output, ffn_gain, ffn_shift, w_inner, b_inner, w_outer, b_outer, buckets, cot_first, cot_second):
    length = SEQLEN
    seq_count = first_in.shape[0] // length
    params = tuple((weight.astype(jnp.float32) for weight in (attn_gain, attn_shift, w_joint, w_value, w_output, ffn_gain, ffn_shift, w_inner, b_inner, w_outer, b_outer)))
    chosen_seqs = jnp.transpose(buckets[:, :, 0].reshape(ROUNDS, seq_count, length), (1, 0, 2))

    def by_sequence(array):
        return array.astype(jnp.float32).reshape(seq_count, length, array.shape[-1])

    def one_sequence(grad_sums, pieces):
        first_seq, second_seq, chosen_seq, cot_one, cot_two = pieces

        def forward_only(first_arg, second_arg, param_arg):
            return layer_forward(first_arg, second_arg, param_arg, chosen_seq)
        results, pullback = jax.vjp(forward_only, first_seq, second_seq, params)
        grad_one, grad_two, grad_params = pullback((cot_one, cot_two))
        grad_sums = tuple((total + extra for total, extra in zip(grad_sums, grad_params)))
        return (grad_sums, (results[0].astype(jnp.bfloat16), results[1].astype(jnp.bfloat16), grad_one.astype(jnp.bfloat16), grad_two.astype(jnp.bfloat16)))
    zero_sums = tuple((jnp.zeros_like(weight) for weight in params))
    grad_sums, stacked = lax.scan(one_sequence, zero_sums, (by_sequence(first_in), by_sequence(second_in), chosen_seqs, by_sequence(cot_first), by_sequence(cot_second)))
    flattened = tuple((item.reshape(seq_count * length, D) for item in stacked))
    return (flattened[0], flattened[1], flattened[2], flattened[3], grad_sums[0], grad_sums[1], grad_sums[2], grad_sums[3], grad_sums[4], grad_sums[5], grad_sums[6], grad_sums[7], grad_sums[8], grad_sums[9], grad_sums[10])
```

```python
import jax
import jax.numpy as jnp
from jax import lax
from jax.experimental import pallas as pl
from jax.experimental.pallas import tpu as pltpu
from jax.sharding import Mesh, PartitionSpec as P

HEADS = 8
HEAD_DIM = 128
ROUNDS = 4
BUCKETS = 32
MOST = 8
TOK = 128
D = 1024
FF = 4096

EPS_NORM = 1e-05
EPS_KEY = 1e-06
SELF_SCORE = -10000.0
MASKED_SCORE = -1000000000.0

BF = jnp.bfloat16
F32 = jnp.float32

AXES = ("y", "z", "x", "c")
CHIPS = ("y", "z", "x")


def send(piece, axis, k):
    return lax.ppermute(piece, axis, [(i, (i + k) % 4) for i in range(4)])


def swap(piece):
    return lax.ppermute(piece, "c", [(0, 1), (1, 0)])


def gather(piece, axis):
    back, front, far = send(piece, axis, 3), send(piece, axis, 1), send(piece, axis, 2)
    return [piece, back, far, front]


def scatter(pieces, axis):
    front, back, far = (
        send(pieces[1], axis, 1),
        send(pieces[3], axis, 3),
        send(pieces[2], axis, 2),
    )
    return [pieces[0], back, far, front]


def in_order(pieces, mine):
    return jnp.roll(jnp.stack(pieces), mine, axis=0)


def reduce_over(array, axis, dim):
    mine = lax.axis_index(axis)
    parts = [
        lax.dynamic_index_in_dim(array, (mine + k) % 4, dim, keepdims=False) for k in range(4)
    ]
    got = scatter(parts, axis)
    total = got[0].astype(F32)
    for extra in got[1:]:
        total = total + extra.astype(F32)
    return total


def reduce_chips(array, order):
    left = list(CHIPS)
    for step, axis in enumerate(order):
        array = reduce_over(array, axis, left.index(axis))
        left.remove(axis)
        if step < 2:
            array = array.astype(BF)
    return array


def dot(a, b):
    return jnp.dot(a, b, preferred_element_type=F32)


def dot_t(a, b):
    return lax.dot_general(a, b, (((1,), (1,)), ((), ())), preferred_element_type=F32)


def t_dot(a, b):
    return lax.dot_general(a, b, (((0,), (0,)), ((), ())), preferred_element_type=F32)


def cost(us):
    return pl.CostEstimate(flops=int(us * 1e9), bytes_accessed=0, transcendentals=0)


def params(mib):
    return pltpu.CompilerParams(vmem_limit_bytes=mib * 1024 * 1024)


SMEM = pl.BlockSpec(memory_space=pltpu.SMEM)
VMEM = pl.BlockSpec(memory_space=pltpu.VMEM)


def iota(shape, dim):
    return lax.broadcasted_iota(jnp.int32, shape, dim)


def whole_call(kernel, name, outs, us, mib=16):
    def call(where, *arrays):
        return pl.pallas_call(
            kernel,
            in_specs=[SMEM] + [VMEM] * len(arrays),
            out_specs=[VMEM] * len(outs),
            out_shape=[jax.ShapeDtypeStruct(s, t) for s, t in outs],
            compiler_params=params(mib),
            cost_estimate=cost(us),
            name=name,
        )(where, *arrays)

    return call


def fixed(shape):
    return pl.BlockSpec(shape, lambda r: (0,) * len(shape))


def per_round(shape):
    return pl.BlockSpec((1,) + shape, lambda r: (r,) + (0,) * len(shape))


PAIRS = BUCKETS // 2


def pack_kernel(where, slab_ref, vec_ref, bucket_ref, keep_a, give_a, keep_b, give_b):
    low_core = where[3] == 0
    slab = slab_ref[...].astype(F32)
    heads = []
    for core in range(2):
        rows = []
        for h in range(4):
            cols = slice((core * 4 + h) * 128, (core * 4 + h + 1) * 128)
            rows += [slab[0:8, cols], slab[8:16, cols]]
        heads.append(jnp.concatenate(rows, axis=0))

    row, lane = iota((8, 128), 0), iota((8, 128), 1)
    vec = jnp.broadcast_to(vec_ref[0:1, :], (8, 128))
    par = jnp.zeros((8, 128), F32)
    for v in range(5):
        col = jnp.sum(jnp.where(lane == 8 * v + row, vec, 0.0), axis=1, keepdims=True)
        par = jnp.where(lane == v, col, par)
    for v in range(4):
        col = jnp.sum(jnp.where(lane == 40 + 4 * row + v, vec, 0.0), axis=1, keepdims=True)
        par = jnp.where(lane == 5 + v, col, par)

    sub, along = iota((128, 128), 0), iota((128, 128), 1)
    targets, counts = [], []
    for r in range(ROUNDS):
        chosen = jnp.broadcast_to(bucket_ref[r : r + 1, :].astype(F32), (128, 128))
        column = jnp.sum(jnp.where(sub == along, chosen, 0.0), axis=1, keepdims=True)
        earlier = (column == chosen) & (sub < along)
        rank = jnp.sum(earlier.astype(F32), axis=0, keepdims=True)
        targets.append(chosen[0:1] * MOST + rank)
        counts.append(jnp.sum((column == along.astype(F32)).astype(F32), axis=0, keepdims=True))
    aux = jnp.concatenate([par] + targets + counts, axis=0)
    keep_a[...] = jnp.concatenate([jnp.where(low_core, *heads), aux], axis=0).astype(BF)
    give_a[...] = jnp.concatenate([jnp.where(low_core, *heads[::-1]), aux], axis=0).astype(BF)

    chunks = []
    for i in range(4):
        for u in range(4):
            chunks.append(slab[24 + 8 * i : 32 + 8 * i, u * 256 : (u + 1) * 256])
    src, dst = iota((256, 256), 0), iota((256, 256), 1)
    wanted = 64 * ((dst % 128) // 32) + 32 * (dst // 128) + dst % 32
    picked = dot(jnp.concatenate(chunks, axis=0).astype(BF), (src == wanted).astype(F32).astype(BF))
    inner = []
    for core in range(2):
        halves = [
            jnp.concatenate(
                [
                    picked[t * 8 : (t + 1) * 8, core * 128 : (core + 1) * 128]
                    for t in range(half * 8, half * 8 + 8)
                ],
                axis=1,
            )
            for half in range(2)
        ]
        inner.append(jnp.concatenate(halves, axis=0))
    rest = jnp.concatenate([slab[16:24], jnp.zeros((8, D), F32)], axis=0)
    keep_b[...] = jnp.concatenate([jnp.where(low_core, *inner), rest], axis=0).astype(BF)
    give_b[...] = jnp.concatenate([jnp.where(low_core, *inner[::-1]), rest], axis=0).astype(BF)


pack = whole_call(
    pack_kernel, "pack", [((80, 128), BF)] * 2 + [((32, D), BF)] * 2, 3
)


def messages_kernel(where, keep_ref, got_ref, *outs):
    low_core = where[3] == 0
    keep, got = keep_ref[...].astype(F32), got_ref[...].astype(F32)
    first, second = jnp.where(low_core, keep, got), jnp.where(low_core, got, keep)
    aux = jnp.concatenate([first[64:72], second[64:72], first[72:80], second[72:80]], axis=0)
    heads = [
        jnp.concatenate(
            [
                first[h * 16 : h * 16 + 8], second[h * 16 : h * 16 + 8],
                first[h * 16 + 8 : h * 16 + 16], second[h * 16 + 8 : h * 16 + 16],
            ],
            axis=0,
        )
        for h in range(4)
    ]
    for k in range(4):
        head = (where[1] + k) % 4
        rows = heads[0]
        for h in range(1, 4):
            rows = jnp.where(head == h, heads[h], rows)
        outs[k][...] = jnp.concatenate([rows, aux], axis=0).astype(BF)


messages = whole_call(messages_kernel, "messages", [((64, 128), BF)] * 4, 1)


def payload_kernel(where, keep_ref, got_ref, outer_ref, out_ref):
    low_core = where[3] == 0
    keep, got = keep_ref[...].astype(F32), got_ref[...].astype(F32)
    first, second = jnp.where(low_core, keep, got), jnp.where(low_core, got, keep)
    for at, to in ((0, 0), (8, 16), (16, 64)):
        out_ref[to : to + 16, :] = jnp.concatenate(
            [first[at : at + 8], second[at : at + 8]], axis=0
        ).astype(BF)
    out_ref[32:64, :] = outer_ref[...]


payload = whole_call(payload_kernel, "payload", [((80, D), BF)], 1)


def assemble_kernel(where, x0, x1, x2, x3, w_ref, par_ref, tgt_ref, tgt_t_ref, count_ref, par_rows):
    for m, piece in enumerate((x0, x1, x2, x3)):
        for n in range(4):
            for k in range(4):
                chip = ((where[0] + n) % 4 * 4 + (where[1] + k) % 4) * 4 + (where[2] + m) % 4
                to = pl.ds(pl.multiple_of(chip * 16, 16), 16)
                at = (n * 4 + k) * 48
                w_ref[to, :128] = piece[at : at + 16, :]
                w_ref[to, 128:] = piece[at + 16 : at + 32, :]
                par_rows[to, :] = piece[at + 32 : at + 48, :]
    par_t = jnp.transpose(par_rows[...].astype(F32))
    par_ref[...] = par_t[:16, :]
    empty = jnp.zeros((96, 128), F32)
    slots = [piece[768:832, :].astype(F32) for piece in (x0, x1, x2, x3)]
    for r in range(ROUNDS):
        rows = jnp.concatenate(
            [slots[m][s * 8 + r : s * 8 + r + 1] for m in range(4) for s in range(8)], axis=0
        )
        tgt_ref[r] = rows.astype(jnp.int32)
        tgt_t_ref[r] = jnp.transpose(jnp.concatenate([rows, empty], axis=0)).astype(jnp.int32)
        count_ref[r] = jnp.concatenate(
            [slots[m][s * 8 + 4 + r : s * 8 + 5 + r] for m in range(4) for s in range(8)], axis=0
        )


def assemble(where, *pieces):
    shapes = [
        ((D, 256), BF), ((16, D), F32), ((ROUNDS, 32, 128), jnp.int32),
        ((ROUNDS, 128, 128), jnp.int32), ((ROUNDS, 32, 128), F32),
    ]
    return pl.pallas_call(
        assemble_kernel,
        in_specs=[SMEM] + [VMEM] * 4,
        out_specs=[VMEM] * 5,
        out_shape=[jax.ShapeDtypeStruct(s, t) for s, t in shapes],
        scratch_shapes=[pltpu.VMEM((D, 128), BF)],
        compiler_params=params(16),
        cost_estimate=cost(2),
        name="assemble",
    )(where, *pieces)


def mask_kernel(where, count_ref, mask_ref):
    z, x, c = where[1], where[2], where[3]
    shape = (256, 128)
    row, lane = iota(shape, 0), iota(shape, 1)
    source, rank = row >> 3, row & 7
    of_chip = lambda z_of, x_of, core: ((z_of & 3) * 8 + (x_of & 3) * 2 + core) * 8
    kpos = of_chip(z + ((source >> 1) & 3), x + (source >> 3), source & 1) + rank
    asker = (lane >> 3) & 7
    qpos = of_chip(z + (asker >> 1), x, asker & 1) + (lane & 7)
    code = jnp.where(kpos == qpos, -1.0, jnp.where(kpos < qpos, 0.0, -1e5))
    rank_f = rank.astype(F32)
    expand = (iota((256, 32), 0) >> 3) == iota((256, 32), 1)
    by_slot = dot(expand.astype(F32).astype(BF), count_ref[0].astype(BF)).astype(BF)
    bucket, side = iota((128, 128), 0), iota((128, 128), 1) >> 6

    @pl.loop(0, PAIRS, unroll=4)
    def _(p):
        select = (bucket == 2 * p + side).astype(F32).astype(BF)
        live = rank_f < dot(by_slot, select)
        mask_ref[0, p] = jnp.where(live, code, -1e5).astype(BF)


def make_mask(where, counts):
    return pl.pallas_call(
        mask_kernel,
        grid=(ROUNDS,),
        in_specs=[SMEM, per_round((32, 128))],
        out_specs=per_round((PAIRS, 256, 128)),
        out_shape=jax.ShapeDtypeStruct((ROUNDS, PAIRS, 256, 128), BF),
        compiler_params=params(16),
        cost_estimate=cost(6),
        name="make_mask",
    )(where, counts)


def token_rows(where, own0, own3, sib0, sib3):
    step = pl.program_id(0)
    own = step % 2 == where[3]
    near = jnp.where(own, own0[...].astype(F32), sib0[0].astype(F32))
    far = jnp.where(own, own3[0].astype(F32), sib3[0].astype(F32))
    return jnp.where(step < 2, near, far), own


def token_specs():
    far = pl.BlockSpec((1, TOK, D), lambda i: (jnp.maximum(i // 2 - 1, 0), 0, 0))
    return [
        pl.BlockSpec((TOK, D), lambda i: (0, 0)),
        far,
        pl.BlockSpec((1, TOK, D), lambda i: (0, 0, 0)),
        far,
    ]


def project_kernel(where, own0, own3, sib0, sib3, par_ref, w_ref, normed_ref, qv_ref):
    rows, _ = token_rows(where, own0, own3, sib0, sib3)
    centered = rows - jnp.mean(rows, axis=-1, keepdims=True)
    spread = jnp.mean(centered * centered, axis=-1, keepdims=True)
    normed = centered * lax.rsqrt(spread + EPS_NORM) * par_ref[0:1, :] + par_ref[1:2, :]
    normed = normed.astype(BF)
    normed_ref[...] = normed
    qv_ref[...] = dot(normed, w_ref[...]).astype(BF)


def project(where, tokens, par, w):
    whole = lambda i: (0, 0)
    return pl.pallas_call(
        project_kernel,
        grid=(8,),
        in_specs=[SMEM] + token_specs()
        + [pl.BlockSpec((16, D), whole), pl.BlockSpec((D, 256), whole)],
        out_specs=[
            pl.BlockSpec((TOK, D), lambda i: (i, 0)),
            pl.BlockSpec((TOK, 256), lambda i: (i, 0)),
        ],
        out_shape=[
            jax.ShapeDtypeStruct((8 * TOK, D), BF),
            jax.ShapeDtypeStruct((8 * TOK, 256), BF),
        ],
        compiler_params=params(24),
        cost_estimate=cost(4),
        name="project",
    )(where, *tokens, par, w)


def project_back_kernel(
    where, own0, own3, sib0, sib3, par_ref, w_ref, normed_ref, qv_ref, gq_ref, g0, g1, g2, g3,
    own_out, sib_out, wg_ref, total, sums,
):
    step = pl.program_id(0)
    x, own = token_rows(where, own0, own3, sib0, sib3)
    q = qv_ref[:, :HEAD_DIM].astype(F32)
    inv = lax.rsqrt(jnp.sum(q * q, axis=-1, keepdims=True) + EPS_KEY)
    grad = g0[...].astype(F32) + g1[...].astype(F32) + g2[...].astype(F32) + g3[...].astype(F32)
    gk = grad[:, :HEAD_DIM]
    along = jnp.sum(q * gk, axis=-1, keepdims=True)
    gq = gq_ref[...] + gk * inv - q * (inv * inv * inv * along)
    rows = jnp.concatenate([gq.astype(BF), grad[:, HEAD_DIM:].astype(BF)], axis=1)
    back = dot_t(rows, w_ref[...])

    @pl.when(own)
    def _():
        own_out[0] = back.astype(BF)

    @pl.when(jnp.logical_not(own))
    def _():
        sib_out[0] = back.astype(BF)

    centered = x - jnp.mean(x, axis=-1, keepdims=True)
    spread = jnp.mean(centered * centered, axis=-1, keepdims=True)
    xhat = centered * lax.rsqrt(spread + EPS_NORM)
    gain_part = jnp.sum((back * xhat).reshape(TOK // 8, 8, D), axis=0)
    shift_part = jnp.sum(back.reshape(TOK // 8, 8, D), axis=0)
    weight_part = t_dot(normed_ref[...], rows)

    @pl.when(step == 0)
    def _():
        total[...] = weight_part
        sums[0:8, :] = gain_part
        sums[8:16, :] = shift_part

    @pl.when(step > 0)
    def _():
        total[...] += weight_part
        sums[0:8, :] += gain_part
        sums[8:16, :] += shift_part

    @pl.when(step == 7)
    def _():
        wg_ref[:, :256] = total[...].astype(BF)
        gain_sum = jnp.sum(sums[0:8, :], axis=0, keepdims=True)
        shift_sum = jnp.sum(sums[8:16, :], axis=0, keepdims=True)
        both = jnp.where(iota((HEAD_DIM, D), 0) < 64, gain_sum, shift_sum)
        wg_ref[:, 256:] = jnp.transpose(both).astype(BF)


def project_back(where, tokens, par, w, normed, qv, gq, pieces):
    token_block = pl.BlockSpec((1, TOK, D), lambda i: (i // 2, 0, 0))
    whole = lambda i: (0, 0)
    row_block = lambda width: pl.BlockSpec((TOK, width), lambda i: (i, 0))
    return pl.pallas_call(
        project_back_kernel,
        grid=(8,),
        in_specs=[SMEM] + token_specs()
        + [
            pl.BlockSpec((16, D), whole),
            pl.BlockSpec((D, 256), whole),
            row_block(D),
            row_block(256),
            row_block(HEAD_DIM),
        ]
        + [row_block(256)] * 4,
        out_specs=[token_block, token_block, pl.BlockSpec((D, 384), whole)],
        out_shape=[
            jax.ShapeDtypeStruct((4, TOK, D), BF),
            jax.ShapeDtypeStruct((4, TOK, D), BF),
            jax.ShapeDtypeStruct((D, 384), BF),
        ],
        scratch_shapes=[pltpu.VMEM((D, 256), F32), pltpu.VMEM((16, D), F32)],
        compiler_params=params(32),
        cost_estimate=cost(8),
        name="project_back",
    )(where, *tokens, par, w, normed, qv, gq, *pieces)


def chip_rows(where, own, sib):
    low_core = where[3] == 0
    return jnp.concatenate([jnp.where(low_core, own, sib), jnp.where(low_core, sib, own)], axis=0)


def normalized(values):
    centered = values - jnp.mean(values, axis=-1, keepdims=True)
    spread = jnp.mean(centered * centered, axis=-1, keepdims=True)
    scale = lax.rsqrt(spread + EPS_NORM)
    return centered * scale, scale


def norm_back(u, xhat, scale):
    mean_u = jnp.mean(u, axis=-1, keepdims=True)
    mean_ux = jnp.mean(u * xhat, axis=-1, keepdims=True)
    return (u - mean_u - xhat * mean_ux) * scale


def head_rows(w_ref, head):
    return w_ref[pl.ds(head * 8, 8)].reshape(HEAD_DIM, D)


def heads_of(where):
    for side in range(2):
        core = where[3] if side == 0 else 1 - where[3]
        for m in range(4):
            yield side, m, core * 4 + (where[1] + m) % 4


GELU_IN = 0.7978845608028654
GELU_CUBE = 0.044715


def feed_kernel(
    where, mix_own, mix_sib, first_own, first_sib, cot_own, cot_sib, par_ref, bias_ref,
    out_w, inner_ref, outer_ref,
    sum_ref, first_out, input_t_ref, active_ref, grad_ref, back_ref, hid_sum_ref,
    ffn_in, cot_t, back_t,
):
    step = pl.program_id(0)

    @pl.when(step == 0)
    def _():
        total = chip_rows(where, first_own[...].astype(F32), first_sib[0].astype(F32))
        mixes = (mix_own, mix_sib)
        for side, m, head in heads_of(where):
            total = total + dot(mixes[side][:, m * 128 : m * 128 + 128], head_rows(out_w, head))
        sum_ref[...] = total
        own = jnp.where(where[3] == 0, total[:TOK], total[TOK:])
        first_out[...] = own.astype(BF)
        xhat, _ = normalized(total)
        rows = xhat * par_ref[2:3, :] + par_ref[3:4, :]
        ffn_in[...] = rows.astype(BF)
        input_t_ref[...] = jnp.transpose(rows).astype(BF)
        cot = chip_rows(where, cot_own[...].astype(F32), cot_sib[0].astype(F32))
        cot_t[...] = jnp.transpose(cot).astype(BF)

    inner = inner_ref[...].reshape(D, 256)
    outer = outer_ref[...].reshape(256, D)
    hidden = dot(ffn_in[...], inner) + bias_ref[0:1, :]
    square = hidden * hidden
    bent = jnp.tanh(GELU_IN * hidden * (1.0 + GELU_CUBE * square))
    half = 0.5 * (1.0 + bent)
    active_ref[...] = (hidden * half).astype(BF)
    slope = half + 0.5 * hidden * (1.0 - bent * bent) * GELU_IN * (
        1.0 + 3.0 * GELU_CUBE * square
    )
    grad_active = jnp.transpose(dot(outer, cot_t[...]))
    grad = (grad_active * slope).astype(BF)
    grad_ref[...] = grad
    hid_sum_ref[...] = jnp.broadcast_to(
        jnp.sum(grad.astype(F32), axis=0, keepdims=True), (8, 256)
    )
    part = dot(inner, jnp.transpose(grad))

    @pl.when(step == 0)
    def _():
        back_t[...] = part

    @pl.when(step > 0)
    def _():
        back_t[...] += part

    @pl.when(step == 7)
    def _():
        back_ref[...] = jnp.transpose(back_t[...])


def feed(where, mix_own, mix_sib, first_in, cot_second, sib_rows, par, bias, gathered):
    whole = lambda i: (0, 0)
    two = 2 * TOK
    return pl.pallas_call(
        feed_kernel,
        grid=(8,),
        in_specs=[
            SMEM,
            pl.BlockSpec((two, 512), whole),
            pl.BlockSpec((two, 512), whole),
            pl.BlockSpec((TOK, D), whole),
            pl.BlockSpec((1, TOK, D), lambda i: (1, 0, 0)),
            pl.BlockSpec((TOK, D), whole),
            pl.BlockSpec((1, TOK, D), lambda i: (3, 0, 0)),
            pl.BlockSpec((16, D), whole),
            pl.BlockSpec((8, 256), lambda i: (0, i)),
            pl.BlockSpec((64, 16, D), lambda i: (0, 4, 0)),
            pl.BlockSpec((64, 16, 256), lambda i: (0, i // 4, i % 4)),
            pl.BlockSpec((8, 32, D), lambda i: (i, 1, 0)),
        ],
        out_specs=[
            pl.BlockSpec((two, D), whole),
            pl.BlockSpec((TOK, D), whole),
            pl.BlockSpec((D, two), whole),
            pl.BlockSpec((two, 256), lambda i: (0, i)),
            pl.BlockSpec((two, 256), lambda i: (0, i)),
            pl.BlockSpec((two, D), whole),
            pl.BlockSpec((8, 256), lambda i: (0, i)),
        ],
        out_shape=[
            jax.ShapeDtypeStruct((two, D), F32),
            jax.ShapeDtypeStruct((TOK, D), BF),
            jax.ShapeDtypeStruct((D, two), BF),
            jax.ShapeDtypeStruct((two, 2048), BF),
            jax.ShapeDtypeStruct((two, 2048), BF),
            jax.ShapeDtypeStruct((two, D), F32),
            jax.ShapeDtypeStruct((8, 2048), F32),
        ],
        scratch_shapes=[
            pltpu.VMEM((two, D), BF),
            pltpu.VMEM((D, two), BF),
            pltpu.VMEM((D, two), F32),
        ],
        compiler_params=params(40),
        cost_estimate=cost(16),
        name="feed",
    )(
        where, mix_own, mix_sib, first_in, sib_rows, cot_second, sib_rows, par, bias,
        gathered, gathered, gathered,
    )


def first_back_kernel(
    where, back_own, back_sib, sum_ref, cot_own, cot_sib, par_ref, out_w,
    grad_first, branch_ref, m0, m1, m2, m3, sums_ref,
):
    back = back_own[...] + back_sib[...]
    xhat, scale = normalized(sum_ref[...])
    total = chip_rows(where, cot_own[...].astype(F32), cot_sib[0].astype(F32))
    total = total + norm_back(back * par_ref[2:3, :], xhat, scale)
    branch = total.astype(BF)
    branch_ref[...] = branch
    grad_first[...] = jnp.where(where[3] == 0, total[:TOK], total[TOK:]).astype(BF)
    outs = (m0, m1, m2, m3)
    for side, m, head in heads_of(where):
        if side == 0:
            outs[m][...] = dot_t(branch, head_rows(out_w, head)).astype(BF)
    gain = jnp.sum(back * xhat, axis=0, keepdims=True)
    shift = jnp.sum(back, axis=0, keepdims=True)
    sums_ref[...] = jnp.concatenate([gain, shift, jnp.zeros((6, D), F32)], axis=0)


def first_back(where, back_own, back_sib, first_sum, cot_first, sib_rows, par, gathered):
    two = 2 * TOK
    one = lambda shape: pl.BlockSpec(shape, lambda i: (0,) * len(shape))
    return pl.pallas_call(
        first_back_kernel,
        grid=(1,),
        in_specs=[
            SMEM, one((two, D)), one((two, D)), one((two, D)), one((TOK, D)),
            pl.BlockSpec((1, TOK, D), lambda i: (2, 0, 0)),
            one((16, D)),
            pl.BlockSpec((64, 16, D), lambda i: (0, 4, 0)),
        ],
        out_specs=[one((TOK, D)), one((two, D))] + [one((two, 128))] * 4 + [one((8, D))],
        out_shape=[jax.ShapeDtypeStruct((TOK, D), BF), jax.ShapeDtypeStruct((two, D), BF)]
        + [jax.ShapeDtypeStruct((two, 128), BF)] * 4
        + [jax.ShapeDtypeStruct((8, D), F32)],
        compiler_params=params(40),
        cost_estimate=cost(6),
        name="first_back",
    )(where, back_own, back_sib, first_sum, cot_first, sib_rows, par, gathered)


def weights_kernel(
    where, active_ref, grad_ref, input_t, cot_own, cot_sib, mix_own, mix_sib, branch_ref, outer_ref,
    gi_ref, go_ref, gw_ref, own_ref, give_ref, cot_sum_ref, cot, total,
):
    step = pl.program_id(0)

    @pl.when(step == 0)
    def _():
        rows = chip_rows(where, cot_own[...].astype(F32), cot_sib[0].astype(F32))
        cot[...] = rows.astype(BF)
        cot_sum_ref[...] = jnp.broadcast_to(jnp.sum(rows, axis=0, keepdims=True), (8, D))
        total[...] = jnp.zeros_like(total)
        low_core = where[3] == 0
        cols = jnp.where(
            low_core, branch_ref[:, :512].astype(F32), branch_ref[:, 512:].astype(F32)
        ).astype(BF)
        mixes = (mix_own, mix_sib)
        for side, m, head in heads_of(where):
            rows = t_dot(mixes[side][:, m * 128 : m * 128 + 128], cols)
            gw_ref[pl.ds(head * 8, 8)] = rows.astype(BF).reshape(8, 16, 512)

    active = active_ref[...]
    total[...] += dot(active, outer_ref[...].reshape(256, D))
    gi_ref[...] = dot(input_t[...], grad_ref[...]).astype(BF).reshape(64, 16, 256)
    go_ref[...] = t_dot(active, cot[...]).astype(BF).reshape(8, 32, D)

    @pl.when(step == 7)
    def _():
        low_core = where[3] == 0
        own_ref[...] = jnp.where(low_core, total[:TOK], total[TOK:])
        give_ref[...] = jnp.where(low_core, total[TOK:], total[:TOK])


def weight_grads(
    where, active, grad, input_t, cot_second, sib_rows, mix_own, mix_sib, branch, gathered
):
    two = 2 * TOK
    whole = lambda i: (0, 0)
    return pl.pallas_call(
        weights_kernel,
        grid=(8,),
        in_specs=[
            SMEM,
            pl.BlockSpec((two, 256), lambda i: (0, i)),
            pl.BlockSpec((two, 256), lambda i: (0, i)),
            pl.BlockSpec((D, two), whole),
            pl.BlockSpec((TOK, D), whole),
            pl.BlockSpec((1, TOK, D), lambda i: (3, 0, 0)),
            pl.BlockSpec((two, 512), whole),
            pl.BlockSpec((two, 512), whole),
            pl.BlockSpec((two, D), whole),
            pl.BlockSpec((8, 32, D), lambda i: (i, 1, 0)),
        ],
        out_specs=[
            pl.BlockSpec((64, 16, 256), lambda i: (0, 0, i)),
            pl.BlockSpec((8, 32, D), lambda i: (i, 0, 0)),
            pl.BlockSpec((64, 16, 512), lambda i: (0, 0, 0)),
            pl.BlockSpec((TOK, D), whole),
            pl.BlockSpec((TOK, D), whole),
            pl.BlockSpec((8, D), whole),
        ],
        out_shape=[
            jax.ShapeDtypeStruct((64, 16, 2048), BF),
            jax.ShapeDtypeStruct((64, 32, D), BF),
            jax.ShapeDtypeStruct((64, 16, 512), BF),
            jax.ShapeDtypeStruct((TOK, D), F32),
            jax.ShapeDtypeStruct((TOK, D), F32),
            jax.ShapeDtypeStruct((8, D), F32),
        ],
        scratch_shapes=[pltpu.VMEM((two, D), BF), pltpu.VMEM((two, D), F32)],
        compiler_params=params(40),
        cost_estimate=cost(14),
        name="weight_grads",
    )(where, active, grad, input_t, cot_second, sib_rows, mix_own, mix_sib, branch, gathered)


def make_keys(pieces, kv_rows):
    for m, piece in enumerate(pieces):

        @pl.loop(0, 8)
        def _(s, m=m, piece=piece):
            rows = pl.ds(pl.multiple_of(s * TOK, TOK), TOK)
            to = pl.ds(pl.multiple_of(m * 8 * TOK + s * TOK, TOK), TOK)
            q = piece[rows, :HEAD_DIM].astype(F32)
            inv = lax.rsqrt(jnp.sum(q * q, axis=-1, keepdims=True) + EPS_KEY)
            kv_rows[to, :HEAD_DIM] = (q * inv).astype(BF)
            kv_rows[to, HEAD_DIM:] = piece[rows, HEAD_DIM:]


def round_weights(lt_ref, at):
    totals = [lt_ref[r, at, :].astype(F32) for r in range(ROUNDS)]
    peak = jnp.maximum(jnp.maximum(totals[0], totals[1]), jnp.maximum(totals[2], totals[3]))
    exps = [jnp.exp(t - peak) for t in totals]
    scale = 1.0 / (exps[0] + exps[1] + exps[2] + exps[3])
    return [e * scale for e in exps]


def hot_slots(tgt_ref, source):
    slots = lax.broadcasted_iota(jnp.int32, (BUCKETS * MOST, TOK), 0)
    return (slots == tgt_ref[0, pl.ds(source, 1), :]).astype(F32).astype(BF)


def hot_tokens(tgt_t_ref, source):
    slots = lax.broadcasted_iota(jnp.int32, (TOK, BUCKETS * MOST), 1)
    return (slots == tgt_t_ref[0, :, source : source + 1]).astype(F32).astype(BF)


def spread(first, second):
    width = first.shape[-1]
    both = [a.reshape(PAIRS, 2, MOST, width) for a in (first, second)]
    return jnp.concatenate(both, axis=2).astype(BF)


def two_sources(pair):
    return pl.ds(pl.multiple_of(pair * 16, 16), 16)


def fill_keys(pieces, tgt_ref, kv_rows, kv_ref):
    @pl.loop(0, 16, unroll=4)
    def _(pair):
        placed = []
        for half in range(2):
            source = pair * 2 + half
            rows = kv_rows[pl.ds(pl.multiple_of(source * TOK, TOK), TOK), :]
            placed.append(dot(hot_slots(tgt_ref, source), rows))
        both = spread(*placed)
        at = two_sources(pair)
        for low in range(2):
            kv_ref[0, :, at, low * 128 : low * 128 + 128] = both[:, low, :, :128]
            kv_ref[0, :, at, 256 + low * 128 : 384 + low * 128] = both[:, low, :, 128:]


def place_diagonal(both, ref, pair):
    at = pl.multiple_of(pair * 16, 16)
    empty = jnp.zeros((PAIRS, 16, 128), BF)
    ref[:, pl.ds(at, 16), :128] = both[:, 0]
    ref[:, pl.ds(at, 16), 128:] = empty
    ref[:, pl.ds(64 + at, 16), :128] = empty
    ref[:, pl.ds(64 + at, 16), 128:] = both[:, 1]


def eye():
    return lax.broadcasted_iota(jnp.int32, (128, 128), 0) == lax.broadcasted_iota(
        jnp.int32, (128, 128), 1
    )


def pair_softmax(keys, queries, code):
    scores = dot_t(keys, queries)
    scores = jnp.where(code == 0.0, scores, code * 1e4)
    peak = jnp.max(scores, axis=0, keepdims=True)
    exponent = jnp.exp(scores - peak)
    total = jnp.sum(exponent, axis=0, keepdims=True)
    return exponent * (1.0 / total), peak + jnp.log(total)


def attend_kernel(
    p0, p1, p2, p3, tgt_ref, tgt_t_ref, mask_ref,
    mixed_ref, ro_ref, lt_ref, kv_ref, qm_ref, kv_rows, att,
):
    this_round = pl.program_id(0)
    pieces = (p0, p1, p2, p3)

    @pl.when(this_round == 0)
    def _():
        make_keys(pieces, kv_rows)

    fill_keys(pieces, tgt_ref, kv_rows, kv_ref)

    @pl.loop(0, 4, unroll=4)
    def _(pair):
        placed = []
        for half in range(2):
            source = pair * 2 + half
            rows = p0[pl.ds(pl.multiple_of(source * TOK, TOK), TOK), :HEAD_DIM]
            placed.append(dot(hot_slots(tgt_ref, source), rows))
        place_diagonal(spread(*placed), qm_ref.at[0], pair)

    ones = jnp.ones((128, 128), BF)

    @pl.loop(0, PAIRS, unroll=16)
    def _(p):
        code = mask_ref[0, p].astype(F32)
        probs, log_total = pair_softmax(kv_ref[0, p, :, :256], qm_ref[0, p], code)
        out = t_dot(probs.astype(BF), kv_ref[0, p, :, 256:])
        logs = dot(jnp.where(eye(), log_total, 0.0).astype(BF), ones)
        att[p, 0, :, :128] = out[:64, :128]
        att[p, 1, :, :128] = out[64:, 128:]
        att[p, 0, :, 128:] = logs[:64]
        att[p, 1, :, 128:] = logs[64:]

    for s in range(8):
        slots = att[:, :, s * MOST : (s + 1) * MOST, :].reshape(256, 256)
        rows = dot(hot_tokens(tgt_t_ref, s), slots.astype(BF)).astype(BF)
        ro_ref[this_round, s * TOK : (s + 1) * TOK, :] = rows[:, :HEAD_DIM]
        lt_ref[this_round, s * TOK : (s + 1) * TOK, :] = rows[:, HEAD_DIM:]

    @pl.when(this_round == ROUNDS - 1)
    def _():
        @pl.loop(0, 8)
        def _(s):
            at = pl.ds(pl.multiple_of(s * TOK, TOK), TOK)
            weights = round_weights(lt_ref, at)
            mixed = weights[0] * ro_ref[0, at, :].astype(F32)
            for r in range(1, ROUNDS):
                mixed = mixed + weights[r] * ro_ref[r, at, :].astype(F32)
            mixed_ref[at, :] = mixed.astype(BF)


def attend(pieces, tgt, tgt_t, mask):
    rows = 8 * TOK
    return pl.pallas_call(
        attend_kernel,
        grid=(ROUNDS,),
        in_specs=[fixed((rows, 256))] * 4
        + [per_round((32, TOK)), per_round((TOK, 128)), per_round((PAIRS, 256, 128))],
        out_specs=[
            fixed((rows, HEAD_DIM)),
            fixed((ROUNDS, rows, HEAD_DIM)),
            fixed((ROUNDS, rows, HEAD_DIM)),
            per_round((PAIRS, 256, 512)),
            per_round((PAIRS, 128, 256)),
        ],
        out_shape=[
            jax.ShapeDtypeStruct((rows, HEAD_DIM), BF),
            jax.ShapeDtypeStruct((ROUNDS, rows, HEAD_DIM), BF),
            jax.ShapeDtypeStruct((ROUNDS, rows, HEAD_DIM), BF),
            jax.ShapeDtypeStruct((ROUNDS, PAIRS, 256, 512), BF),
            jax.ShapeDtypeStruct((ROUNDS, PAIRS, 128, 256), BF),
        ],
        scratch_shapes=[
            pltpu.VMEM((4 * rows, 256), BF),
            pltpu.VMEM((PAIRS, 2, 64, 256), F32),
        ],
        compiler_params=params(40),
        cost_estimate=cost(24),
        name="attend",
    )(*pieces, tgt, tgt_t, mask)


def attend_back_kernel(
    tgt_ref, tgt_t_ref, mask_ref, kv_ref, qm_ref, ro_ref, lt_ref, gm_ref,
    gq_ref, gkv_ref, gd, gt_slots, gq_slots, gkv_slots, gkv_rows,
):
    this_round = pl.program_id(0)

    @pl.when(this_round == 0)
    def _():
        gq_ref[...] = jnp.zeros_like(gq_ref)
        gkv_rows[...] = jnp.zeros_like(gkv_rows)

    @pl.loop(0, 4, unroll=4)
    def _(pair):
        placed = []
        for half in range(2):
            source = pair * 2 + half
            at = pl.ds(pl.multiple_of(source * TOK, TOK), TOK)
            weights = round_weights(lt_ref, at)
            grad = gm_ref[at, :].astype(F32)
            agree = [
                jnp.sum(grad * ro_ref[r, at, :].astype(F32), axis=-1, keepdims=True)
                for r in range(ROUNDS)
            ]
            mean = weights[0] * agree[0]
            for r in range(1, ROUNDS):
                mean = mean + weights[r] * agree[r]
            weight, mine = weights[0], agree[0]
            for r in range(1, ROUNDS):
                weight = jnp.where(this_round == r, weights[r], weight)
                mine = jnp.where(this_round == r, agree[r], mine)
            rows = jnp.concatenate(
                [(weight * grad).astype(BF), (weight * (mine - mean)).astype(BF)], axis=1
            )
            placed.append(dot(hot_slots(tgt_ref, source), rows))
        both = spread(*placed)
        place_diagonal(both[..., :128], gd, pair)
        at = pl.multiple_of(pair * 16, 16)
        gt_slots[:, pl.ds(at, 16), :] = both[:, 0, :, 128:]
        gt_slots[:, pl.ds(64 + at, 16), :] = both[:, 1, :, 128:]

    @pl.loop(0, PAIRS, unroll=16)
    def _(p):
        code = mask_ref[0, p].astype(F32)
        keys, values = kv_ref[0, p, :, :256], kv_ref[0, p, :, 256:]
        queries, grads = qm_ref[0, p], gd[p]
        probs, _ = pair_softmax(keys, queries, code)
        grad_probs = dot_t(values, grads)
        agreement = jnp.sum(probs * grad_probs, axis=0, keepdims=True)
        grad_log = jnp.sum(jnp.where(eye(), gt_slots[p].astype(F32), 0.0), axis=0, keepdims=True)
        grad_scores = probs * (grad_probs + (grad_log - agreement))
        grad_scores = jnp.where(code == 0.0, grad_scores, 0.0).astype(BF)
        grad_keys = dot(grad_scores, queries)
        grad_values = dot(probs.astype(BF), grads)
        grad_queries = t_dot(grad_scores, keys)
        gq_slots[p, 0] = grad_queries[:64, :128]
        gq_slots[p, 1] = grad_queries[64:, 128:]
        for low in range(2):
            gkv_slots[p, low, :, :128] = grad_keys[:, low * 128 : low * 128 + 128]
            gkv_slots[p, low, :, 128:] = grad_values[:, low * 128 : low * 128 + 128]

    for s in range(32):
        slots = gkv_slots[:, :, s * MOST : (s + 1) * MOST, :].reshape(256, 256)
        gkv_rows[s * TOK : (s + 1) * TOK, :] += dot(hot_tokens(tgt_t_ref, s), slots.astype(BF))
    for s in range(8):
        slots = gq_slots[:, :, s * MOST : (s + 1) * MOST, :].reshape(256, HEAD_DIM)
        gq_ref[s * TOK : (s + 1) * TOK, :] += dot(hot_tokens(tgt_t_ref, s), slots.astype(BF))

    @pl.when(this_round == ROUNDS - 1)
    def _():
        for m in range(4):
            gkv_ref[m] = gkv_rows[m * 8 * TOK : (m + 1) * 8 * TOK, :].astype(BF)


def attend_back(tgt, tgt_t, mask, kv, qm, ro, lt, gm):
    rows = 8 * TOK
    return pl.pallas_call(
        attend_back_kernel,
        grid=(ROUNDS,),
        in_specs=[
            per_round((32, TOK)),
            per_round((TOK, 128)),
            per_round((PAIRS, 256, 128)),
            per_round((PAIRS, 256, 512)),
            per_round((PAIRS, 128, 256)),
            fixed((ROUNDS, rows, HEAD_DIM)),
            fixed((ROUNDS, rows, HEAD_DIM)),
            fixed((rows, HEAD_DIM)),
        ],
        out_specs=[fixed((rows, HEAD_DIM)), fixed((4, rows, 256))],
        out_shape=[
            jax.ShapeDtypeStruct((rows, HEAD_DIM), F32),
            jax.ShapeDtypeStruct((4, rows, 256), BF),
        ],
        scratch_shapes=[
            pltpu.VMEM((PAIRS, 128, 256), BF),
            pltpu.VMEM((PAIRS, 128, 128), BF),
            pltpu.VMEM((PAIRS, 2, 64, HEAD_DIM), F32),
            pltpu.VMEM((PAIRS, 2, 256, 256), F32),
            pltpu.VMEM((4 * rows, 256), F32),
        ],
        compiler_params=params(56),
        cost_estimate=cost(38),
        name="attend_back",
    )(tgt, tgt_t, mask, kv, qm, ro, lt, gm)


def local(
    first_in, second_in, attn_gain, attn_shift, w_joint, w_value, w_output, ffn_gain, ffn_shift,
    w_inner, b_inner, w_outer, b_outer, buckets, cot_first, cot_second,
):
    y, z, x, c = (lax.axis_index(a) for a in AXES)
    where = jnp.stack([y, z, x, c]).astype(jnp.int32)
    low_core = c == 0

    def by_core(first, second):
        return jnp.where(low_core, first, second)

    sib_rows = swap(jnp.stack([second_in, first_in, cot_first, cot_second]))
    tok_far = jnp.stack(gather(second_in, "z")[1:])
    tokens = (second_in, tok_far, sib_rows, swap(tok_far))

    slab = jnp.concatenate(
        [w_joint, w_value, w_output]
        + [w_inner[:, i * D : (i + 1) * D] for i in range(4)]
        + [jnp.zeros((8, D), BF)]
    )
    vec = jnp.concatenate(
        [attn_gain, attn_shift, ffn_gain, ffn_shift, b_outer, b_inner, jnp.zeros((56,), BF)]
    ).astype(F32)
    keep_a, give_a, keep_b, give_b = pack(where, slab, vec.reshape(1, 128), buckets[:, :, 0])
    got_a, got_b = swap(give_a), swap(give_b)
    gathered = lax.all_gather(
        payload(where, keep_b, got_b, w_outer)[0], CHIPS, axis=0, tiled=False
    ).reshape(64, 80, D)
    z_got = scatter(messages(where, keep_a, got_a), "z")
    y_got = gather(jnp.concatenate([piece[:48] for piece in z_got]), "y")
    x_got = gather(jnp.concatenate(y_got + [piece[48:] for piece in z_got]), "x")
    w_qv, par, tgt, tgt_t, counts = assemble(where, *x_got)
    bias_inner = par[5:9].reshape(4, 64, 2, 8)
    bias_inner = by_core(bias_inner[:, :, 0], bias_inner[:, :, 1])
    bias_inner = jnp.transpose(bias_inner, (1, 2, 0)).reshape(1, 2048)
    bias_inner = jnp.broadcast_to(bias_inner, (8, 2048))

    normed, qv = project(where, tokens, par, w_qv)
    pieces = gather(qv, "x")
    mask = make_mask(where, counts)
    mixed_head, round_out, round_total, kv, qm = attend(pieces, tgt, tgt_t, mask)

    mix_own = jnp.concatenate(
        scatter([mixed_head[k * 256 : (k + 1) * 256] for k in range(4)], "z"), axis=1
    )
    mix_sib = swap(mix_own)
    first_sum, first_out, input_t, active, grad_hidden, back, hid_sum = feed(
        where, mix_own, mix_sib, first_in, cot_second, sib_rows, par, bias_inner, gathered
    )
    back_sib = swap(back)
    grad_first, branch, g0, g1, g2, g3, norm_sums = first_back(
        where, back, back_sib, first_sum, cot_first, sib_rows, par, gathered
    )
    grad_mixed = jnp.concatenate(scatter([g0, g1, g2, g3], "z"))
    grad_inner, grad_outer, grad_output, second_own, second_give, cot_sum = weight_grads(
        where, active, grad_hidden, input_t, cot_second, sib_rows, mix_own, mix_sib, branch,
        gathered,
    )
    second_out = (
        second_in.astype(F32) + second_own + swap(second_give) + par[4]
    ).astype(BF)

    grad_inner = grad_inner.reshape(4, 4, 4, 16, 2048)
    grad_outer = grad_outer.reshape(4, 4, 4, 32, D)
    grad_output = grad_output.reshape(4, 4, 4, 16, 512)
    sums = jnp.stack([norm_sums[0], norm_sums[1], cot_sum[0]]).reshape(3, 64, 16)
    sums = jnp.pad(jnp.transpose(sums, (1, 0, 2)), ((0, 0), (0, 0), (0, 16)))
    sums = jnp.concatenate([sums, hid_sum[0].reshape(64, 1, 32)], axis=1).astype(BF)
    sums = jnp.pad(sums, ((0, 0), (0, 4), (0, D - 32))).reshape(4, 4, 4, 8, D)
    part_a = grad_inner[..., :1536]
    part_b = grad_outer[:, :, :, :24]
    part_c = jnp.concatenate(
        [
            jnp.concatenate([grad_inner[..., 1536:], grad_output], axis=4),
            grad_outer[:, :, :, 24:],
            sums,
        ],
        axis=3,
    )
    part_a = reduce_chips(part_a, ("x", "y", "z"))
    part_b = reduce_chips(part_b, ("y", "z", "x"))
    part_c = reduce_chips(part_c, ("z", "x", "y"))
    grad_outer = jnp.concatenate([part_b, part_c[16:24]], axis=0)
    inner_sum = jnp.concatenate([part_a, part_c[:16, :512]], axis=1).astype(BF)
    output_sum = part_c[:16, 512:].astype(BF)
    chip_sum = jnp.concatenate([inner_sum, output_sum], axis=1)
    rows_keep = by_core(chip_sum[:8], chip_sum[8:])
    rows_got = swap(by_core(chip_sum[8:], chip_sum[:8]))
    rows_low = by_core(rows_keep, rows_got)
    rows_high = by_core(rows_got, rows_keep)
    grad_inner = jnp.stack(
        [rows_low[:, :2048].reshape(8, 64, 32), rows_high[:, :2048].reshape(8, 64, 32)], axis=2
    ).reshape(8, FF).astype(F32)
    grad_output = jnp.concatenate([rows_low[:, 2048:], rows_high[:, 2048:]], axis=1).astype(F32)
    small = part_c[24:28, :32]
    mine16 = by_core(small[:3, :8], small[:3, 8:16])
    grad_ffn_gain, grad_ffn_shift, grad_b_outer = mine16[0], mine16[1], mine16[2]
    grad_b_inner = small[3]

    gq, gkv = attend_back(tgt, tgt_t, mask, kv, qm, round_out, round_total, grad_mixed)
    gkv_got = scatter([gkv[m] for m in range(4)], "x")
    back_own, back_give, w_grad = project_back(
        where, tokens, par, w_qv, normed, qv, gq, gkv_got
    )
    back_chip = (back_own.astype(F32) + swap(back_give).astype(F32)).astype(BF)
    back_parts = scatter([back_chip[k] for k in range(4)], "z")
    grad_normed = back_parts[0].astype(F32)
    for part in back_parts[1:]:
        grad_normed = grad_normed + part.astype(F32)
    attn_xhat, attn_scale = normalized(second_in.astype(F32))
    attn_back = norm_back(grad_normed * par[0], attn_xhat, attn_scale)
    grad_second = (cot_second.astype(F32) + attn_back).astype(BF)

    w_grad = w_grad.reshape(4, 4, 4, 2, 8, 384)
    w_grad = reduce_over(w_grad, "y", 0).astype(BF)
    w_grad = reduce_over(w_grad, "x", 1).astype(BF)
    w_rows = [
        lax.dynamic_index_in_dim(w_grad, (z + k) % 4, 0, keepdims=False) for k in range(4)
    ]
    w_rows = in_order(scatter(w_rows, "z"), z)
    rows_keep = by_core(w_rows[:, 0], w_rows[:, 1])
    rows_got = swap(by_core(w_rows[:, 1], w_rows[:, 0]))
    heads = by_core(
        jnp.concatenate([rows_keep, rows_got]), jnp.concatenate([rows_got, rows_keep])
    ).astype(F32)
    grad_joint = jnp.transpose(heads[:, :, :128], (1, 0, 2)).reshape(8, D)
    grad_value = jnp.transpose(heads[:, :, 128:256], (1, 0, 2)).reshape(8, D)
    grad_attn_gain = jnp.sum(heads[:, :, 256], axis=0)
    grad_attn_shift = jnp.sum(heads[:, :, 320], axis=0)

    return (
        first_out, second_out, grad_first, grad_second, grad_attn_gain, grad_attn_shift,
        grad_joint, grad_value, grad_output, grad_ffn_gain, grad_ffn_shift, grad_inner,
        grad_b_inner, grad_outer, grad_b_outer,
    )


def solution(mesh):
    chips = Mesh(mesh.devices.reshape(4, 4, 4, 2), AXES)
    rows, flat = P(AXES, None), P(AXES)
    return jax.shard_map(
        local,
        mesh=chips,
        in_specs=(
            rows, rows, flat, flat, rows, rows, rows, flat, flat, rows, flat, rows, flat,
            P(None, AXES, None), rows, rows,
        ),
        out_specs=(
            rows, rows, rows, rows, flat, flat, rows, rows, rows, flat, flat, rows, flat, rows,
            flat,
        ),
        check_vma=False,
    )
```

```python
import functools

import jax
import jax.numpy as jnp
from jax import lax
from jax.experimental import pallas as pl
from jax.experimental.pallas import tpu as pltpu
from jax.sharding import Mesh, PartitionSpec as P

HEADS = 8
HEAD_DIM = 128
ROUNDS = 4
BUCKETS = 32
MOST = 8
TOK = 128
D = 1024
FF = 4096

EPS_NORM = 1e-05
EPS_KEY = 1e-06
SELF_SCORE = -10000.0
MASKED_SCORE = -1000000000.0

BF = jnp.bfloat16
F32 = jnp.float32

AXES = ("y", "z", "x", "c")
CHIPS = ("y", "z", "x")


def send(piece, axis, k):
    return lax.ppermute(piece, axis, [(i, (i + k) % 4) for i in range(4)])


def swap(piece):
    return lax.ppermute(piece, "c", [(0, 1), (1, 0)])


def gather(piece, axis):
    back, front, far = send(piece, axis, 3), send(piece, axis, 1), send(piece, axis, 2)
    return [piece, back, far, front]


def scatter(pieces, axis):
    front, back, far = (
        send(pieces[1], axis, 1),
        send(pieces[3], axis, 3),
        send(pieces[2], axis, 2),
    )
    return [pieces[0], back, far, front]


def in_order(pieces, mine):
    return jnp.roll(jnp.stack(pieces), mine, axis=0)


def cut(array, mine, dim):
    return [
        lax.dynamic_index_in_dim(array, (mine + k) % 4, dim, keepdims=False) for k in range(4)
    ]


def add_up(parts):
    total = parts[0].astype(F32)
    for extra in parts[1:]:
        total = total + extra.astype(F32)
    return total


def reduce_over(array, axis, dim):
    return add_up(scatter(cut(array, lax.axis_index(axis), dim), axis))


def sync(*groups):
    return lax.optimization_barrier(groups)


def dot(a, b):
    return jnp.dot(a, b, preferred_element_type=F32)


def dot_t(a, b):
    return lax.dot_general(a, b, (((1,), (1,)), ((), ())), preferred_element_type=F32)


def t_dot(a, b):
    return lax.dot_general(a, b, (((0,), (0,)), ((), ())), preferred_element_type=F32)


def cost(us):
    return pl.CostEstimate(flops=int(us * 1e9), bytes_accessed=0, transcendentals=0)


def params(mib):
    return pltpu.CompilerParams(vmem_limit_bytes=mib * 1024 * 1024)


SMEM = pl.BlockSpec(memory_space=pltpu.SMEM)


def iota(shape, dim):
    return lax.broadcasted_iota(jnp.int32, shape, dim)


def whole_call(kernel, name, outs, us, mib=16):
    def call(where, *arrays):
        return pl.pallas_call(
            kernel,
            grid=(1,),
            in_specs=[SMEM] + [fixed(a.shape) for a in arrays],
            out_specs=[fixed(s) for s, _ in outs],
            out_shape=[jax.ShapeDtypeStruct(s, t) for s, t in outs],
            compiler_params=params(mib),
            cost_estimate=cost(us),
            name=name,
        )(where, *arrays)

    return call


def fixed(shape):
    return pl.BlockSpec(shape, lambda r: (0,) * len(shape))


def per_round(shape):
    return pl.BlockSpec((1,) + shape, lambda r: (r,) + (0,) * len(shape))


PAIRS = BUCKETS // 2


def pack_kernel(
    where, joint_ref, value_ref, output_ref, inner_ref, vec_ref, bucket_ref,
    keep_a, give_a, keep_b, give_b,
):
    low_core = where[3] == 0
    joint, value = joint_ref[...].astype(F32), value_ref[...].astype(F32)
    inner_rows = inner_ref[...].astype(F32)
    heads = []
    for core in range(2):
        rows = []
        for h in range(4):
            cols = slice((core * 4 + h) * 128, (core * 4 + h + 1) * 128)
            rows += [joint[:, cols], value[:, cols]]
        heads.append(jnp.concatenate(rows, axis=0))

    row, lane = iota((8, 128), 0), iota((8, 128), 1)
    vec = jnp.broadcast_to(vec_ref[0:1, :], (8, 128))
    par = jnp.zeros((8, 128), F32)
    for v in range(5):
        col = jnp.sum(jnp.where(lane == 8 * v + row, vec, 0.0), axis=1, keepdims=True)
        par = jnp.where(lane == v, col, par)
    for v in range(4):
        col = jnp.sum(jnp.where(lane == 40 + 4 * row + v, vec, 0.0), axis=1, keepdims=True)
        par = jnp.where(lane == 5 + v, col, par)

    sub, along = iota((128, 128), 0), iota((128, 128), 1)
    targets, counts = [], []
    for r in range(ROUNDS):
        chosen = jnp.broadcast_to(bucket_ref[r : r + 1, :].astype(F32), (128, 128))
        column = jnp.sum(jnp.where(sub == along, chosen, 0.0), axis=1, keepdims=True)
        earlier = (column == chosen) & (sub < along)
        rank = jnp.sum(earlier.astype(F32), axis=0, keepdims=True)
        targets.append(chosen[0:1] * MOST + rank)
        counts.append(jnp.sum((column == along.astype(F32)).astype(F32), axis=0, keepdims=True))
    aux = jnp.concatenate([par] + targets + counts, axis=0)
    keep_a[...] = jnp.concatenate([jnp.where(low_core, *heads), aux], axis=0).astype(BF)
    give_a[...] = jnp.concatenate([jnp.where(low_core, *heads[::-1]), aux], axis=0).astype(BF)

    chunks = [inner_rows[:, t * 256 : (t + 1) * 256] for t in range(16)]
    src, dst = iota((256, 256), 0), iota((256, 256), 1)
    wanted = 64 * ((dst % 128) // 32) + 32 * (dst // 128) + dst % 32
    picked = dot(jnp.concatenate(chunks, axis=0).astype(BF), (src == wanted).astype(F32).astype(BF))
    inner = []
    for core in range(2):
        halves = [
            jnp.concatenate(
                [
                    picked[t * 8 : (t + 1) * 8, core * 128 : (core + 1) * 128]
                    for t in range(half * 8, half * 8 + 8)
                ],
                axis=1,
            )
            for half in range(2)
        ]
        inner.append(jnp.concatenate(halves, axis=0))
    rest = jnp.concatenate([output_ref[...].astype(F32), jnp.zeros((8, D), F32)], axis=0)
    keep_b[...] = jnp.concatenate([jnp.where(low_core, *inner), rest], axis=0).astype(BF)
    give_b[...] = jnp.concatenate([jnp.where(low_core, *inner[::-1]), rest], axis=0).astype(BF)


pack = whole_call(
    pack_kernel, "pack", [((80, 128), BF)] * 2 + [((32, D), BF)] * 2, 3
)


def chip_message_kernel(where, keep_ref, got_ref, out_ref):
    low_core = where[3] == 0
    keep, got = keep_ref[...].astype(F32), got_ref[...].astype(F32)
    first, second = jnp.where(low_core, keep, got), jnp.where(low_core, got, keep)
    rows = []
    for at in range(0, 80, 8):
        rows += [first[at : at + 8], second[at : at + 8]]
    out_ref[...] = jnp.concatenate(rows, axis=0).astype(BF)


chip_message = whole_call(chip_message_kernel, "chip_message", [((160, 128), BF)], 1)


def head_messages_kernel(where, y0, y1, y2, y3, *outs):
    for k in range(4):
        head = (where[1] + k) % 4
        for n, piece in enumerate((y0, y1, y2, y3)):
            outs[k][n * 48 : n * 48 + 32, :] = piece[
                pl.ds(pl.multiple_of(head * 32, 32), 32), :
            ]
            outs[k][n * 48 + 32 : n * 48 + 48, :] = piece[128:144, :]
        outs[k][192:208, :] = y0[144:160, :]


head_messages = whole_call(
    head_messages_kernel, "head_messages", [((208, 128), BF)] * 4, 1
)


def payload_kernel(where, keep_ref, got_ref, outer_ref, out_ref):
    low_core = where[3] == 0
    keep, got = keep_ref[...].astype(F32), got_ref[...].astype(F32)
    first, second = jnp.where(low_core, keep, got), jnp.where(low_core, got, keep)
    for at, to in ((0, 0), (8, 16), (16, 64)):
        out_ref[to : to + 16, :] = jnp.concatenate(
            [first[at : at + 8], second[at : at + 8]], axis=0
        ).astype(BF)
    out_ref[32:64, :] = outer_ref[...]


payload = whole_call(payload_kernel, "payload", [((80, D), BF)], 1)


def assemble_kernel(where, x0, x1, x2, x3, w_ref, par_ref, tgt_ref, tgt_t_ref, count_ref, par_rows):
    for m, piece in enumerate((x0, x1, x2, x3)):
        for n in range(4):
            for k in range(4):
                chip = ((where[0] + n) % 4 * 4 + (where[1] + k) % 4) * 4 + (where[2] + m) % 4
                to = pl.ds(pl.multiple_of(chip * 16, 16), 16)
                at = k * 208 + n * 48
                w_ref[to, :128] = piece[at : at + 16, :]
                w_ref[to, 128:] = piece[at + 16 : at + 32, :]
                par_rows[to, :] = piece[at + 32 : at + 48, :]
    par_t = jnp.transpose(par_rows[...].astype(F32))
    par_ref[...] = par_t[:16, :]
    empty = jnp.zeros((96, 128), F32)
    slots = [
        jnp.concatenate(
            [piece[k * 208 + 192 : k * 208 + 208, :] for k in range(4)], axis=0
        ).astype(F32)
        for piece in (x0, x1, x2, x3)
    ]
    for r in range(ROUNDS):
        rows = jnp.concatenate(
            [slots[m][s * 8 + r : s * 8 + r + 1] for m in range(4) for s in range(8)], axis=0
        )
        tgt_ref[r] = rows.astype(jnp.int32)
        tgt_t_ref[r] = jnp.transpose(jnp.concatenate([rows, empty], axis=0)).astype(jnp.int32)
        count_ref[r] = jnp.concatenate(
            [slots[m][s * 8 + 4 + r : s * 8 + 5 + r] for m in range(4) for s in range(8)], axis=0
        )


def assemble(where, *pieces):
    shapes = [
        ((D, 256), BF), ((16, D), F32), ((ROUNDS, 32, 128), jnp.int32),
        ((ROUNDS, 128, 128), jnp.int32), ((ROUNDS, 32, 128), F32),
    ]
    return pl.pallas_call(
        assemble_kernel,
        grid=(1,),
        in_specs=[SMEM] + [fixed(p.shape) for p in pieces],
        out_specs=[fixed(s) for s, _ in shapes],
        out_shape=[jax.ShapeDtypeStruct(s, t) for s, t in shapes],
        scratch_shapes=[pltpu.VMEM((D, 128), BF)],
        compiler_params=params(16),
        cost_estimate=cost(2),
        name="assemble",
    )(where, *pieces)


def mask_kernel(where, count_ref, mask_ref):
    z, x, c = where[1], where[2], where[3]
    shape = (256, 128)
    row, lane = iota(shape, 0), iota(shape, 1)
    source, rank = row >> 3, row & 7
    of_chip = lambda z_of, x_of, core: ((z_of & 3) * 8 + (x_of & 3) * 2 + core) * 8
    kpos = of_chip(z + ((source >> 1) & 3), x + (source >> 3), source & 1) + rank
    asker = (lane >> 3) & 7
    qpos = of_chip(z + (asker >> 1), x, asker & 1) + (lane & 7)
    code = jnp.where(kpos == qpos, -1.0, jnp.where(kpos < qpos, 0.0, -1e5))
    rank_f = rank.astype(F32)
    expand = (iota((256, 32), 0) >> 3) == iota((256, 32), 1)
    by_slot = dot(expand.astype(F32).astype(BF), count_ref[0].astype(BF)).astype(BF)
    bucket, side = iota((128, 128), 0), iota((128, 128), 1) >> 6

    @pl.loop(0, PAIRS, unroll=4)
    def _(p):
        select = (bucket == 2 * p + side).astype(F32).astype(BF)
        live = rank_f < dot(by_slot, select)
        mask_ref[0, p] = jnp.where(live, code, -1e5).astype(BF)


def make_mask(where, counts):
    return pl.pallas_call(
        mask_kernel,
        grid=(ROUNDS,),
        in_specs=[SMEM, per_round((32, 128))],
        out_specs=per_round((PAIRS, 256, 128)),
        out_shape=jax.ShapeDtypeStruct((ROUNDS, PAIRS, 256, 128), BF),
        compiler_params=params(16),
        cost_estimate=cost(6),
        name="make_mask",
    )(where, counts)


def token_rows(where, own0, own3, sib):
    step = pl.program_id(0)
    own = step % 2 == where[3]
    rows = jnp.where(step < 2, own0[...].astype(F32), own3[0].astype(F32))
    return jnp.where(own, rows, sib[0].astype(F32)), own


def token_specs():
    far = pl.BlockSpec((1, TOK, D), lambda i: (jnp.maximum(i // 2 - 1, 0), 0, 0))
    return [
        pl.BlockSpec((TOK, D), lambda i: (0, 0)),
        far,
        pl.BlockSpec((1, TOK, D), lambda i: (i // 2, 0, 0)),
    ]


def project_kernel(where, own0, own3, sib, par_ref, w_ref, normed_ref, q_ref, v_ref):
    rows, _ = token_rows(where, own0, own3, sib)
    centered = rows - jnp.mean(rows, axis=-1, keepdims=True)
    spread = jnp.mean(centered * centered, axis=-1, keepdims=True)
    normed = centered * lax.rsqrt(spread + EPS_NORM) * par_ref[0:1, :] + par_ref[1:2, :]
    normed = normed.astype(BF)
    normed_ref[...] = normed
    both = dot(normed, w_ref[...]).astype(BF)
    q_ref[...] = both[:, :HEAD_DIM]
    v_ref[...] = both[:, HEAD_DIM:]


def project(where, tokens, par, w):
    whole = lambda i: (0, 0)
    return pl.pallas_call(
        project_kernel,
        grid=(8,),
        in_specs=[SMEM] + token_specs()
        + [pl.BlockSpec((16, D), whole), pl.BlockSpec((D, 256), whole)],
        out_specs=[
            pl.BlockSpec((TOK, D), lambda i: (i, 0)),
            pl.BlockSpec((TOK, HEAD_DIM), lambda i: (i, 0)),
            pl.BlockSpec((TOK, HEAD_DIM), lambda i: (i, 0)),
        ],
        out_shape=[
            jax.ShapeDtypeStruct((8 * TOK, D), BF),
            jax.ShapeDtypeStruct((8 * TOK, HEAD_DIM), BF),
            jax.ShapeDtypeStruct((8 * TOK, HEAD_DIM), BF),
        ],
        compiler_params=params(24),
        cost_estimate=cost(4),
        name="project",
    )(where, *tokens, par, w)


def project_back_kernel(
    where, own0, own3, sib, par_ref, w_ref, normed_ref, q_ref, gq_ref,
    k0, k1, k2, k3, v0, v1, v2, v3, own_out, sib_out, wg_ref, total, sums,
):
    step = pl.program_id(0)
    x, own = token_rows(where, own0, own3, sib)
    q = q_ref[...].astype(F32)
    inv = lax.rsqrt(jnp.sum(q * q, axis=-1, keepdims=True) + EPS_KEY)
    gk = k0[...].astype(F32) + k1[...].astype(F32) + k2[...].astype(F32) + k3[...].astype(F32)
    gv = v0[...].astype(F32) + v1[...].astype(F32) + v2[...].astype(F32) + v3[...].astype(F32)
    along = jnp.sum(q * gk, axis=-1, keepdims=True)
    gq = gq_ref[...] + gk * inv - q * (inv * inv * inv * along)
    rows = jnp.concatenate([gq.astype(BF), gv.astype(BF)], axis=1)
    back = dot_t(rows, w_ref[...])

    @pl.when(own)
    def _():
        own_out[0] = back.astype(BF)

    @pl.when(jnp.logical_not(own))
    def _():
        sib_out[0] = back.astype(BF)

    centered = x - jnp.mean(x, axis=-1, keepdims=True)
    spread = jnp.mean(centered * centered, axis=-1, keepdims=True)
    xhat = centered * lax.rsqrt(spread + EPS_NORM)
    gain_part = jnp.sum((back * xhat).reshape(TOK // 8, 8, D), axis=0)
    shift_part = jnp.sum(back.reshape(TOK // 8, 8, D), axis=0)
    weight_part = t_dot(normed_ref[...], rows)

    @pl.when(step == 0)
    def _():
        total[...] = weight_part
        sums[0:8, :] = gain_part
        sums[8:16, :] = shift_part

    @pl.when(step > 0)
    def _():
        total[...] += weight_part
        sums[0:8, :] += gain_part
        sums[8:16, :] += shift_part

    @pl.when(step == 7)
    def _():
        wg_ref[:, :256] = total[...].astype(BF)
        gain_sum = jnp.sum(sums[0:8, :], axis=0, keepdims=True)
        shift_sum = jnp.sum(sums[8:16, :], axis=0, keepdims=True)
        both = jnp.where(iota((HEAD_DIM, D), 0) < 64, gain_sum, shift_sum)
        wg_ref[:, 256:] = jnp.transpose(both).astype(BF)


def project_back(where, tokens, par, w, normed, q, gq, k_pieces, v_pieces):
    token_block = pl.BlockSpec((1, TOK, D), lambda i: (i // 2, 0, 0))
    whole = lambda i: (0, 0)
    row_block = lambda width: pl.BlockSpec((TOK, width), lambda i: (i, 0))
    return pl.pallas_call(
        project_back_kernel,
        grid=(8,),
        in_specs=[SMEM] + token_specs()
        + [
            pl.BlockSpec((16, D), whole),
            pl.BlockSpec((D, 256), whole),
            row_block(D),
            row_block(HEAD_DIM),
            row_block(HEAD_DIM),
        ]
        + [row_block(HEAD_DIM)] * 8,
        out_specs=[token_block, token_block, pl.BlockSpec((D, 384), whole)],
        out_shape=[
            jax.ShapeDtypeStruct((4, TOK, D), BF),
            jax.ShapeDtypeStruct((4, TOK, D), BF),
            jax.ShapeDtypeStruct((D, 384), BF),
        ],
        scratch_shapes=[pltpu.VMEM((D, 256), F32), pltpu.VMEM((16, D), F32)],
        compiler_params=params(32),
        cost_estimate=cost(8),
        name="project_back",
    )(where, *tokens, par, w, normed, q, gq, *k_pieces, *v_pieces)


def chip_rows(where, own, sib):
    low_core = where[3] == 0
    return jnp.concatenate([jnp.where(low_core, own, sib), jnp.where(low_core, sib, own)], axis=0)


def normalized(values):
    centered = values - jnp.mean(values, axis=-1, keepdims=True)
    spread = jnp.mean(centered * centered, axis=-1, keepdims=True)
    scale = lax.rsqrt(spread + EPS_NORM)
    return centered * scale, scale


def norm_back(u, xhat, scale):
    mean_u = jnp.mean(u, axis=-1, keepdims=True)
    mean_ux = jnp.mean(u * xhat, axis=-1, keepdims=True)
    return (u - mean_u - xhat * mean_ux) * scale


def head_rows(w_ref, head):
    return w_ref[pl.ds(head * 8, 8)].reshape(HEAD_DIM, D)


def heads_of(where):
    for side in range(2):
        core = where[3] if side == 0 else 1 - where[3]
        for m in range(4):
            yield side, m, core * 4 + (where[1] + m) % 4


GELU_IN = 0.7978845608028654
GELU_CUBE = 0.044715


def feed_kernel(
    where, mix_own, mix_sib, first_own, first_sib, cot_own, cot_sib, par_ref, bias_ref,
    out_w, inner_ref, outer_ref,
    sum_ref, first_out, input_t_ref, active_ref, grad_ref, back_ref, hid_sum_ref, cot_sum_ref,
    ffn_in, cot_t, back_t,
):
    step = pl.program_id(0)

    @pl.when(step == 0)
    def _():
        total = chip_rows(where, first_own[...].astype(F32), first_sib[0].astype(F32))
        mixes = (mix_own, mix_sib)
        for side, m, head in heads_of(where):
            total = total + dot(mixes[side][:, m * 128 : m * 128 + 128], head_rows(out_w, head))
        sum_ref[...] = total
        own = jnp.where(where[3] == 0, total[:TOK], total[TOK:])
        first_out[...] = own.astype(BF)
        xhat, _ = normalized(total)
        rows = xhat * par_ref[2:3, :] + par_ref[3:4, :]
        ffn_in[...] = rows.astype(BF)
        input_t_ref[...] = jnp.transpose(rows).astype(BF)
        cot = chip_rows(where, cot_own[...].astype(F32), cot_sib[0].astype(F32))
        cot_t[...] = jnp.transpose(cot).astype(BF)
        cot_sum_ref[...] = jnp.broadcast_to(jnp.sum(cot, axis=0, keepdims=True), (8, D))

    inner = inner_ref[...].reshape(D, 256)
    outer = outer_ref[...].reshape(256, D)
    hidden = dot(ffn_in[...], inner) + bias_ref[0:1, :]
    square = hidden * hidden
    bent = jnp.tanh(GELU_IN * hidden * (1.0 + GELU_CUBE * square))
    half = 0.5 * (1.0 + bent)
    active_ref[...] = (hidden * half).astype(BF)
    slope = half + 0.5 * hidden * (1.0 - bent * bent) * GELU_IN * (
        1.0 + 3.0 * GELU_CUBE * square
    )
    grad_active = jnp.transpose(dot(outer, cot_t[...]))
    grad = (grad_active * slope).astype(BF)
    grad_ref[...] = grad
    hid_sum_ref[...] = jnp.broadcast_to(
        jnp.sum(grad.astype(F32), axis=0, keepdims=True), (8, 256)
    )
    part = dot(inner, jnp.transpose(grad))

    @pl.when(step == 0)
    def _():
        back_t[...] = part

    @pl.when(step > 0)
    def _():
        back_t[...] += part

    @pl.when(step == 7)
    def _():
        back_ref[...] = jnp.transpose(back_t[...])


def feed(where, mix_own, mix_sib, first_in, cot_second, sib_rows, par, bias, gathered):
    whole = lambda i: (0, 0)
    two = 2 * TOK
    return pl.pallas_call(
        feed_kernel,
        grid=(8,),
        in_specs=[
            SMEM,
            pl.BlockSpec((two, 512), whole),
            pl.BlockSpec((two, 512), whole),
            pl.BlockSpec((TOK, D), whole),
            pl.BlockSpec((1, TOK, D), lambda i: (0, 0, 0)),
            pl.BlockSpec((TOK, D), whole),
            pl.BlockSpec((1, TOK, D), lambda i: (2, 0, 0)),
            pl.BlockSpec((16, D), whole),
            pl.BlockSpec((8, 256), lambda i: (0, i)),
            pl.BlockSpec((64, 16, D), lambda i: (0, 4, 0)),
            pl.BlockSpec((64, 16, 256), lambda i: (0, i // 4, i % 4)),
            pl.BlockSpec((8, 32, D), lambda i: (i, 1, 0)),
        ],
        out_specs=[
            pl.BlockSpec((two, D), whole),
            pl.BlockSpec((TOK, D), whole),
            pl.BlockSpec((D, two), whole),
            pl.BlockSpec((two, 256), lambda i: (0, i)),
            pl.BlockSpec((two, 256), lambda i: (0, i)),
            pl.BlockSpec((two, D), whole),
            pl.BlockSpec((8, 256), lambda i: (0, i)),
            pl.BlockSpec((8, D), whole),
        ],
        out_shape=[
            jax.ShapeDtypeStruct((two, D), F32),
            jax.ShapeDtypeStruct((TOK, D), BF),
            jax.ShapeDtypeStruct((D, two), BF),
            jax.ShapeDtypeStruct((two, 2048), BF),
            jax.ShapeDtypeStruct((two, 2048), BF),
            jax.ShapeDtypeStruct((two, D), F32),
            jax.ShapeDtypeStruct((8, 2048), F32),
            jax.ShapeDtypeStruct((8, D), F32),
        ],
        scratch_shapes=[
            pltpu.VMEM((two, D), BF),
            pltpu.VMEM((D, two), BF),
            pltpu.VMEM((D, two), F32),
        ],
        compiler_params=params(40),
        cost_estimate=cost(16),
        name="feed",
    )(
        where, mix_own, mix_sib, first_in, sib_rows, cot_second, sib_rows, par, bias,
        gathered, gathered, gathered,
    )


def first_back_kernel(
    where, back_own, back_sib, sum_ref, cot_own, cot_sib, par_ref, out_w,
    grad_first, branch_ref, m0, m1, m2, m3, sums_ref,
):
    back = back_own[...] + back_sib[...]
    xhat, scale = normalized(sum_ref[...])
    total = chip_rows(where, cot_own[...].astype(F32), cot_sib[0].astype(F32))
    total = total + norm_back(back * par_ref[2:3, :], xhat, scale)
    branch = total.astype(BF)
    branch_ref[...] = branch
    grad_first[...] = jnp.where(where[3] == 0, total[:TOK], total[TOK:]).astype(BF)
    outs = (m0, m1, m2, m3)
    for side, m, head in heads_of(where):
        if side == 0:
            outs[m][...] = dot_t(branch, head_rows(out_w, head)).astype(BF)
    gain = jnp.sum(back * xhat, axis=0, keepdims=True)
    shift = jnp.sum(back, axis=0, keepdims=True)
    sums_ref[...] = jnp.concatenate([gain, shift, jnp.zeros((6, D), F32)], axis=0)


def first_back(where, back_own, back_sib, first_sum, cot_first, sib_rows, par, gathered):
    two = 2 * TOK
    one = lambda shape: pl.BlockSpec(shape, lambda i: (0,) * len(shape))
    return pl.pallas_call(
        first_back_kernel,
        grid=(1,),
        in_specs=[
            SMEM, one((two, D)), one((two, D)), one((two, D)), one((TOK, D)),
            pl.BlockSpec((1, TOK, D), lambda i: (1, 0, 0)),
            one((16, D)),
            pl.BlockSpec((64, 16, D), lambda i: (0, 4, 0)),
        ],
        out_specs=[one((TOK, D)), one((two, D))] + [one((two, 128))] * 4 + [one((8, D))],
        out_shape=[jax.ShapeDtypeStruct((TOK, D), BF), jax.ShapeDtypeStruct((two, D), BF)]
        + [jax.ShapeDtypeStruct((two, 128), BF)] * 4
        + [jax.ShapeDtypeStruct((8, D), F32)],
        compiler_params=params(40),
        cost_estimate=cost(6),
        name="first_back",
    )(where, back_own, back_sib, first_sum, cot_first, sib_rows, par, gathered)


def weights_kernel(
    where, active_ref, grad_ref, input_t, cot_own, cot_sib, mix_own, mix_sib, branch_ref, sums_ref,
    outer_ref, a_ref, b_ref, own_ref, give_ref, cot, total,
):
    step = pl.program_id(0)

    @pl.when(step == 0)
    def _():
        cot[...] = chip_rows(where, cot_own[...].astype(F32), cot_sib[0].astype(F32)).astype(BF)
        total[...] = jnp.zeros_like(total)
        cols = jnp.where(
            where[3] == 0, branch_ref[:, :512].astype(F32), branch_ref[:, 512:].astype(F32)
        ).astype(BF)
        mixes = (mix_own, mix_sib)
        for side, m, head in heads_of(where):
            rows = t_dot(mixes[side][:, m * 128 : m * 128 + 128], cols).astype(BF)
            at = pl.ds(head * 8, 8)
            b_ref[at, 0:16, D:] = rows[:, :256].reshape(8, 16, 256)
            b_ref[at, 16:32, D:] = rows[:, 256:].reshape(8, 16, 256)
        a_ref[:, :, 2048:] = sums_ref[...]

    active = active_ref[...]
    total[...] += dot(active, outer_ref[...].reshape(256, D))
    a_ref[:, :, pl.ds(pl.multiple_of(step * 256, 256), 256)] = (
        dot(input_t[...], grad_ref[...]).astype(BF).reshape(64, 16, 256)
    )
    b_ref[pl.ds(step * 8, 8), :, :D] = t_dot(active, cot[...]).astype(BF).reshape(8, 32, D)

    @pl.when(step == 7)
    def _():
        low_core = where[3] == 0
        own_ref[...] = jnp.where(low_core, total[:TOK], total[TOK:])
        give_ref[...] = jnp.where(low_core, total[TOK:], total[:TOK])


def weight_grads(
    where, active, grad, input_t, cot_second, sib_rows, mix_own, mix_sib, branch, sums, gathered
):
    two = 2 * TOK
    whole = lambda i: (0, 0)
    whole3 = lambda i: (0, 0, 0)
    return pl.pallas_call(
        weights_kernel,
        grid=(8,),
        in_specs=[
            SMEM,
            pl.BlockSpec((two, 256), lambda i: (0, i)),
            pl.BlockSpec((two, 256), lambda i: (0, i)),
            pl.BlockSpec((D, two), whole),
            pl.BlockSpec((TOK, D), whole),
            pl.BlockSpec((1, TOK, D), lambda i: (2, 0, 0)),
            pl.BlockSpec((two, 512), whole),
            pl.BlockSpec((two, 512), whole),
            pl.BlockSpec((two, D), whole),
            pl.BlockSpec((64, 16, 128), whole3),
            pl.BlockSpec((8, 32, D), lambda i: (i, 1, 0)),
        ],
        out_specs=[
            pl.BlockSpec((64, 16, 2176), whole3),
            pl.BlockSpec((64, 32, 1280), whole3),
            pl.BlockSpec((TOK, D), whole),
            pl.BlockSpec((TOK, D), whole),
        ],
        out_shape=[
            jax.ShapeDtypeStruct((64, 16, 2176), BF),
            jax.ShapeDtypeStruct((64, 32, 1280), BF),
            jax.ShapeDtypeStruct((TOK, D), F32),
            jax.ShapeDtypeStruct((TOK, D), F32),
        ],
        scratch_shapes=[pltpu.VMEM((two, D), BF), pltpu.VMEM((two, D), F32)],
        compiler_params=params(48),
        cost_estimate=cost(12),
        name="weight_grads",
    )(
        where, active, grad, input_t, cot_second, sib_rows, mix_own, mix_sib, branch, sums,
        gathered,
    )


def make_keys(pieces, rows_ref):
    for m, piece in enumerate(pieces):

        @pl.loop(0, 8, unroll=4)
        def _(s, m=m, piece=piece):
            rows = pl.ds(pl.multiple_of(s * TOK, TOK), TOK)
            to = pl.ds(pl.multiple_of(m * 8 * TOK + s * TOK, TOK), TOK)
            q = piece[rows, :].astype(F32)
            inv = lax.rsqrt(jnp.sum(q * q, axis=-1, keepdims=True) + EPS_KEY)
            rows_ref[to, :] = (q * inv).astype(BF)


def round_weights(lt_ref, at):
    totals = [lt_ref[r, at, :].astype(F32) for r in range(ROUNDS)]
    peak = jnp.maximum(jnp.maximum(totals[0], totals[1]), jnp.maximum(totals[2], totals[3]))
    exps = [jnp.exp(t - peak) for t in totals]
    scale = 1.0 / (exps[0] + exps[1] + exps[2] + exps[3])
    return [e * scale for e in exps]


def hot_slots(tgt_ref, source):
    slots = iota((BUCKETS * MOST, TOK), 0)
    return (slots == tgt_ref[0, pl.ds(source, 1), :]).astype(F32).astype(BF)


def hot_tokens(tgt_t_ref, source):
    slots = iota((TOK, BUCKETS * MOST), 1)
    return (slots == tgt_t_ref[0, :, source : source + 1]).astype(F32).astype(BF)


def spread(first, second):
    width = first.shape[-1]
    both = [a.reshape(PAIRS, 2, MOST, width) for a in (first, second)]
    return jnp.concatenate(both, axis=2).astype(BF)


def fill(tgt_ref, read_rows, ref):
    @pl.loop(0, 16, unroll=4)
    def _(pair):
        placed = [
            dot(hot_slots(tgt_ref, pair * 2 + half), read_rows(pair * 2 + half))
            for half in range(2)
        ]
        both = spread(*placed)
        at = pl.ds(pl.multiple_of(pair * 16, 16), 16)
        ref[0, :, at, :128] = both[:, 0]
        ref[0, :, at, 128:] = both[:, 1]


def place_diagonal(both, ref, pair):
    at = pl.multiple_of(pair * 16, 16)
    empty = jnp.zeros((PAIRS, 16, 128), BF)
    ref[:, pl.ds(at, 16), :128] = both[:, 0]
    ref[:, pl.ds(at, 16), 128:] = empty
    ref[:, pl.ds(64 + at, 16), :128] = empty
    ref[:, pl.ds(64 + at, 16), 128:] = both[:, 1]


def eye():
    return iota((128, 128), 0) == iota((128, 128), 1)


def token_block(s):
    return pl.ds(pl.multiple_of(s * TOK, TOK), TOK)


def scores_kernel(q0, q1, q2, q3, tgt_ref, mask_ref, probs_ref, keys_ref, qm_ref, log_ref, k_rows):
    @pl.when(pl.program_id(0) == 0)
    def _():
        make_keys((q0, q1, q2, q3), k_rows)

    fill(tgt_ref, lambda source: k_rows[token_block(source), :], keys_ref)

    @pl.loop(0, 4, unroll=4)
    def _(pair):
        placed = [
            dot(hot_slots(tgt_ref, pair * 2 + half), q0[token_block(pair * 2 + half), :])
            for half in range(2)
        ]
        place_diagonal(spread(*placed), qm_ref.at[0], pair)

    @pl.loop(0, PAIRS, unroll=16)
    def _(p):
        code = mask_ref[0, p].astype(F32)
        scores = dot_t(keys_ref[0, p], qm_ref[0, p])
        scores = jnp.where(code == 0.0, scores, code * 1e4)
        peak = jnp.max(scores, axis=0, keepdims=True)
        exponent = jnp.exp(scores - peak)
        total = jnp.sum(exponent, axis=0, keepdims=True)
        probs_ref[0, p] = (exponent * (1.0 / total)).astype(BF)
        log_ref[0, pl.ds(p, 1), :] = peak + jnp.log(total)


def attend_scores(q_pieces, tgt, mask):
    rows = 8 * TOK
    outs = [(PAIRS, 256, 128), (PAIRS, 256, 256), (PAIRS, 128, 256), (PAIRS, 128)]
    types = [BF, BF, BF, F32]
    return pl.pallas_call(
        scores_kernel,
        grid=(ROUNDS,),
        in_specs=[fixed((rows, HEAD_DIM))] * 4
        + [per_round((32, TOK)), per_round((PAIRS, 256, 128))],
        out_specs=[per_round(shape) for shape in outs],
        out_shape=[
            jax.ShapeDtypeStruct((ROUNDS,) + shape, t) for shape, t in zip(outs, types)
        ],
        scratch_shapes=[pltpu.VMEM((4 * rows, HEAD_DIM), BF)],
        compiler_params=params(40),
        cost_estimate=cost(18),
        name="attend_scores",
    )(*q_pieces, tgt, mask)


def values_kernel(
    v0, v1, v2, v3, tgt_ref, tgt_t_ref, probs_ref, log_ref, mixed_ref, ro_ref, lt_ref, values_ref, att
):
    this_round = pl.program_id(0)
    for m, piece in enumerate((v0, v1, v2, v3)):

        @pl.loop(0, 4, unroll=4)
        def _(pair, m=m, piece=piece):
            placed = [
                dot(
                    hot_slots(tgt_ref, m * 8 + pair * 2 + half),
                    piece[token_block(pair * 2 + half), :],
                )
                for half in range(2)
            ]
            both = spread(*placed)
            at = pl.ds(pl.multiple_of((m * 4 + pair) * 16, 16), 16)
            values_ref[0, :, at, :128] = both[:, 0]
            values_ref[0, :, at, 128:] = both[:, 1]

    ones = jnp.ones((128, 128), BF)

    @pl.loop(0, PAIRS, unroll=16)
    def _(p):
        out = t_dot(probs_ref[0, p], values_ref[0, p])
        log_total = log_ref[0, pl.ds(p, 1), :]
        logs = dot(jnp.where(eye(), log_total, 0.0).astype(BF), ones)
        att[p, 0, :, :128] = out[:64, :128]
        att[p, 1, :, :128] = out[64:, 128:]
        att[p, 0, :, 128:] = logs[:64]
        att[p, 1, :, 128:] = logs[64:]

    for s in range(8):
        slots = att[:, :, s * MOST : (s + 1) * MOST, :].reshape(256, 256)
        rows = dot(hot_tokens(tgt_t_ref, s), slots.astype(BF)).astype(BF)
        ro_ref[this_round, s * TOK : (s + 1) * TOK, :] = rows[:, :HEAD_DIM]
        lt_ref[this_round, s * TOK : (s + 1) * TOK, :] = rows[:, HEAD_DIM:]

    @pl.when(this_round == ROUNDS - 1)
    def _():
        @pl.loop(0, 8)
        def _(s):
            at = token_block(s)
            weights = round_weights(lt_ref, at)
            mixed = weights[0] * ro_ref[0, at, :].astype(F32)
            for r in range(1, ROUNDS):
                mixed = mixed + weights[r] * ro_ref[r, at, :].astype(F32)
            mixed_ref[at, :] = mixed.astype(BF)


def attend_values(v_pieces, tgt, tgt_t, probs, logs):
    rows = 8 * TOK
    return pl.pallas_call(
        values_kernel,
        grid=(ROUNDS,),
        in_specs=[fixed((rows, HEAD_DIM))] * 4
        + [
            per_round((32, TOK)), per_round((TOK, 128)), per_round((PAIRS, 256, 128)),
            per_round((PAIRS, 128)),
        ],
        out_specs=[
            fixed((rows, HEAD_DIM)),
            fixed((ROUNDS, rows, HEAD_DIM)),
            fixed((ROUNDS, rows, HEAD_DIM)),
            per_round((PAIRS, 256, 256)),
        ],
        out_shape=[
            jax.ShapeDtypeStruct((rows, HEAD_DIM), BF),
            jax.ShapeDtypeStruct((ROUNDS, rows, HEAD_DIM), BF),
            jax.ShapeDtypeStruct((ROUNDS, rows, HEAD_DIM), BF),
            jax.ShapeDtypeStruct((ROUNDS, PAIRS, 256, 256), BF),
        ],
        scratch_shapes=[pltpu.VMEM((PAIRS, 2, 64, 256), F32)],
        compiler_params=params(40),
        cost_estimate=cost(14),
        name="attend_values",
    )(*v_pieces, tgt, tgt_t, probs, logs)


def take_slots(tgt_t_ref, slots_ref, rows_ref, sources):
    for s in range(sources):
        slots = slots_ref[:, :, s * MOST : (s + 1) * MOST, :].reshape(256, HEAD_DIM)
        rows_ref[s * TOK : (s + 1) * TOK, :] += dot(hot_tokens(tgt_t_ref, s), slots.astype(BF))


def values_back_kernel(
    tgt_ref, tgt_t_ref, probs_ref, ro_ref, lt_ref, gm_ref,
    o0, o1, o2, o3, gd_ref, gt_ref, gt_slots, slots, rows,
):
    this_round = pl.program_id(0)

    @pl.when(this_round == 0)
    def _():
        rows[...] = jnp.zeros_like(rows)

    @pl.loop(0, 4, unroll=4)
    def _(pair):
        placed = []
        for half in range(2):
            source = pair * 2 + half
            at = token_block(source)
            weights = round_weights(lt_ref, at)
            grad = gm_ref[at, :].astype(F32)
            agree = [
                jnp.sum(grad * ro_ref[r, at, :].astype(F32), axis=-1, keepdims=True)
                for r in range(ROUNDS)
            ]
            mean = weights[0] * agree[0]
            for r in range(1, ROUNDS):
                mean = mean + weights[r] * agree[r]
            weight, mine = weights[0], agree[0]
            for r in range(1, ROUNDS):
                weight = jnp.where(this_round == r, weights[r], weight)
                mine = jnp.where(this_round == r, agree[r], mine)
            both = jnp.concatenate(
                [(weight * grad).astype(BF), (weight * (mine - mean)).astype(BF)], axis=1
            )
            placed.append(dot(hot_slots(tgt_ref, source), both))
        both = spread(*placed)
        place_diagonal(both[..., :128], gd_ref.at[0], pair)
        at = pl.multiple_of(pair * 16, 16)
        gt_slots[:, pl.ds(at, 16), :] = both[:, 0, :, 128:]
        gt_slots[:, pl.ds(64 + at, 16), :] = both[:, 1, :, 128:]

    @pl.loop(0, PAIRS, unroll=16)
    def _(p):
        grad_values = dot(probs_ref[0, p], gd_ref[0, p])
        slots[p, 0] = grad_values[:, :128]
        slots[p, 1] = grad_values[:, 128:]
        gt_ref[0, pl.ds(p, 1), :] = jnp.sum(
            jnp.where(eye(), gt_slots[p].astype(F32), 0.0), axis=0, keepdims=True
        )

    take_slots(tgt_t_ref, slots, rows, 32)

    @pl.when(this_round == ROUNDS - 1)
    def _():
        for m, out in enumerate((o0, o1, o2, o3)):
            out[...] = rows[m * 8 * TOK : (m + 1) * 8 * TOK, :].astype(BF)


def attend_values_back(tgt, tgt_t, probs, ro, lt, gm):
    rows = 8 * TOK
    return pl.pallas_call(
        values_back_kernel,
        grid=(ROUNDS,),
        in_specs=[
            per_round((32, TOK)),
            per_round((TOK, 128)),
            per_round((PAIRS, 256, 128)),
            fixed((ROUNDS, rows, HEAD_DIM)),
            fixed((ROUNDS, rows, HEAD_DIM)),
            fixed((rows, HEAD_DIM)),
        ],
        out_specs=[fixed((rows, HEAD_DIM))] * 4
        + [per_round((PAIRS, 128, 256)), per_round((PAIRS, 128))],
        out_shape=[jax.ShapeDtypeStruct((rows, HEAD_DIM), BF)] * 4
        + [
            jax.ShapeDtypeStruct((ROUNDS, PAIRS, 128, 256), BF),
            jax.ShapeDtypeStruct((ROUNDS, PAIRS, 128), F32),
        ],
        scratch_shapes=[
            pltpu.VMEM((PAIRS, 128, 128), BF),
            pltpu.VMEM((PAIRS, 2, 256, HEAD_DIM), F32),
            pltpu.VMEM((4 * rows, HEAD_DIM), F32),
        ],
        compiler_params=params(48),
        cost_estimate=cost(16),
        name="attend_values_back",
    )(tgt, tgt_t, probs, ro, lt, gm)


def scores_back_kernel(
    half, tgt_t_ref, mask_ref, probs_ref, keys_ref, values_ref, qm_ref, gd_ref, gt_ref, *refs
):
    if half == 0:
        gq_ref, rows_out, gq_slots, slots, rows = refs
    else:
        gq_in, rows_in, gq_ref, o0, o1, o2, o3, gq_slots, slots, rows = refs
    step = pl.program_id(0)

    @pl.when(step == 0)
    def _():
        if half == 0:
            gq_ref[...] = jnp.zeros_like(gq_ref)
            rows[...] = jnp.zeros_like(rows)
        else:
            gq_ref[...] = gq_in[...]
            rows[...] = rows_in[...]

    @pl.loop(0, PAIRS, unroll=16)
    def _(p):
        probs = probs_ref[0, p].astype(F32)
        grad_probs = dot_t(values_ref[0, p], gd_ref[0, p])
        agreement = jnp.sum(probs * grad_probs, axis=0, keepdims=True)
        grad_scores = probs * (grad_probs + (gt_ref[0, pl.ds(p, 1), :] - agreement))
        seen = mask_ref[0, p].astype(F32) == 0.0
        grad_scores = jnp.where(seen, grad_scores, 0.0).astype(BF)
        grad_keys = dot(grad_scores, qm_ref[0, p])
        grad_queries = t_dot(grad_scores, keys_ref[0, p])
        gq_slots[p, 0] = grad_queries[:64, :128]
        gq_slots[p, 1] = grad_queries[64:, 128:]
        slots[p, 0] = grad_keys[:, :128]
        slots[p, 1] = grad_keys[:, 128:]

    take_slots(tgt_t_ref, slots, rows, 32)
    take_slots(tgt_t_ref, gq_slots, gq_ref, 8)

    @pl.when(step == 1)
    def _():
        if half == 0:
            rows_out[...] = rows[...]
        else:
            for m, out in enumerate((o0, o1, o2, o3)):
                out[...] = rows[m * 8 * TOK : (m + 1) * 8 * TOK, :].astype(BF)


def attend_scores_back(half, arrays, begun):
    rows = 8 * TOK
    shapes = [
        (TOK, 128), (PAIRS, 256, 128), (PAIRS, 256, 128), (PAIRS, 256, 256), (PAIRS, 256, 256),
        (PAIRS, 128, 256), (PAIRS, 128, 256), (PAIRS, 128),
    ]
    this_half = lambda shape: pl.BlockSpec(
        (1,) + shape, lambda r: (2 * half + r,) + (0,) * len(shape)
    )
    if half == 0:
        outs = [((rows, HEAD_DIM), F32), ((4 * rows, HEAD_DIM), F32)]
    else:
        outs = [((rows, HEAD_DIM), F32)] + [((rows, HEAD_DIM), BF)] * 4
    return pl.pallas_call(
        functools.partial(scores_back_kernel, half),
        grid=(2,),
        in_specs=[this_half(shape) for shape in shapes] + [fixed(a.shape) for a in begun],
        out_specs=[fixed(shape) for shape, _ in outs],
        out_shape=[jax.ShapeDtypeStruct(shape, t) for shape, t in outs],
        scratch_shapes=[
            pltpu.VMEM((PAIRS, 2, 64, HEAD_DIM), F32),
            pltpu.VMEM((PAIRS, 2, 256, HEAD_DIM), F32),
            pltpu.VMEM((4 * rows, HEAD_DIM), F32),
        ],
        compiler_params=params(56),
        cost_estimate=cost(14),
        name=f"attend_scores_back_{half}",
    )(*arrays, *begun)


def local(
    first_in, second_in, attn_gain, attn_shift, w_joint, w_value, w_output, ffn_gain, ffn_shift,
    w_inner, b_inner, w_outer, b_outer, buckets, cot_first, cot_second,
):
    y, z, x, c = (lax.axis_index(a) for a in AXES)
    where = jnp.stack([y, z, x, c]).astype(jnp.int32)
    low_core = c == 0

    def by_core(first, second):
        return jnp.where(low_core, first, second)

    vec = jnp.concatenate(
        [attn_gain, attn_shift, ffn_gain, ffn_shift, b_outer, b_inner, jnp.zeros((56,), BF)]
    ).astype(F32)
    keep_a, give_a, keep_b, give_b = pack(
        where, w_joint, w_value, w_output, w_inner, vec.reshape(1, 128), buckets[:, :, 0]
    )
    tok_near = [send(second_in, "z", 3), send(second_in, "z", 1)]
    got_b, got_a = swap(give_b), swap(give_a)
    gathered = lax.all_gather(
        payload(where, keep_b, got_b, w_outer)[0], CHIPS, axis=0, tiled=False
    ).reshape(64, 80, D)
    y_got = gather(chip_message(where, keep_a, got_a)[0], "y")
    heads_out, second_late, tok_near = sync(
        head_messages(where, *y_got), second_in, tok_near
    )
    z_got = scatter(heads_out, "z")
    tok_last = send(second_late, "z", 2)
    z_got, tok_last = sync(z_got, tok_last)
    tok_far = jnp.stack([tok_near[0], tok_last, tok_near[1]])
    sib_tok = swap(jnp.concatenate([second_in[None], tok_far]))
    tokens = (second_in, tok_far, sib_tok)
    x_got = gather(jnp.concatenate(z_got), "x")
    w_qv, par, tgt, tgt_t, counts = assemble(where, *x_got)
    bias_inner = par[5:9].reshape(4, 64, 2, 8)
    bias_inner = by_core(bias_inner[:, :, 0], bias_inner[:, :, 1])
    bias_inner = jnp.transpose(bias_inner, (1, 2, 0)).reshape(1, 2048)
    bias_inner = jnp.broadcast_to(bias_inner, (8, 2048))

    normed, queries, values = project(where, tokens, par, w_qv)
    q_pieces = gather(queries, "x")
    q_pieces, values, first_late = sync(q_pieces, values, (first_in, cot_first, cot_second))
    v_pieces = gather(values, "x")
    sib_rows = swap(jnp.stack(first_late))
    mask = make_mask(where, counts)
    probs, key_slots, query_slots, logs = attend_scores(q_pieces, tgt, mask)
    mixed_head, round_out, round_total, value_slots = attend_values(
        v_pieces, tgt, tgt_t, probs, logs
    )

    mix_own = jnp.concatenate(
        scatter([mixed_head[k * 256 : (k + 1) * 256] for k in range(4)], "z"), axis=1
    )
    mix_sib = swap(mix_own)
    first_sum, first_out, input_t, active, grad_hidden, back, hid_sum, cot_sum = feed(
        where, mix_own, mix_sib, first_in, cot_second, sib_rows, par, bias_inner, gathered
    )
    back_sib = swap(back)
    grad_first, branch, g0, g1, g2, g3, norm_sums = first_back(
        where, back, back_sib, first_sum, cot_first, sib_rows, par, gathered
    )
    grad_mixed = jnp.concatenate(scatter([g0, g1, g2, g3], "z"))
    sums = jnp.stack([norm_sums[0], norm_sums[1], cot_sum[0]]).reshape(3, 64, 16)
    sums = jnp.pad(jnp.transpose(sums, (1, 0, 2)), ((0, 0), (0, 0), (0, 16)))
    sums = jnp.concatenate([sums, hid_sum[0].reshape(64, 1, 32)], axis=1).astype(BF)
    sums = jnp.pad(sums, ((0, 0), (0, 12), (0, 96)))
    grad_a, grad_b, second_own, second_give = weight_grads(
        where, active, grad_hidden, input_t, cot_second, sib_rows, mix_own, mix_sib, branch,
        sums, gathered,
    )
    second_out = (
        second_in.astype(F32) + second_own + swap(second_give) + par[4]
    ).astype(BF)

    grad_a = grad_a.reshape(4, 4, 4, 16, 2176)
    grad_b = grad_b.reshape(4, 4, 4, 32, 1280)
    a_parts, b_parts = cut(grad_a, y, 0), cut(grad_b, z, 1)

    grad_mixed, a_parts, b_parts = sync(grad_mixed, a_parts, b_parts)
    a_got = [send(a_parts[1], "y", 1), send(a_parts[3], "y", 3)]
    b_got = [send(b_parts[1], "z", 1), send(b_parts[3], "z", 3)]
    v0, v1, v2, v3, grad_slots, log_slots = attend_values_back(
        tgt, tgt_t, probs, round_out, round_total, grad_mixed
    )

    gv_got = [v0, send(v1, "x", 1)]
    back_in = (tgt_t, mask, probs, key_slots, value_slots, query_slots, grad_slots, log_slots)
    half = attend_scores_back(0, back_in, ())
    half, a_got, b_got, gv_got, v2, v3, a_far, b_far = sync(
        half, a_got, b_got, gv_got, v2, v3, a_parts[2], b_parts[2]
    )

    gv_got = gv_got + [send(v3, "x", 3), send(v2, "x", 2)]
    a_far, b_far = send(a_far, "y", 2), send(b_far, "z", 2)
    gq, k0, k1, k2, k3 = attend_scores_back(1, back_in, half)

    gv_got, k1, k2, k3 = sync(gv_got, k1, k2, k3)
    gk_got = scatter([k0, k1, k2, k3], "x")
    a_sum = add_up([a_parts[0], a_far] + a_got).astype(BF)
    b_sum = add_up([b_parts[0], b_far] + b_got).astype(BF)

    gk_got, a_sum, b_sum = sync(gk_got, a_sum, b_sum)
    a_sum = reduce_over(a_sum, "z", 0).astype(BF)
    b_sum = reduce_over(b_sum, "x", 1).astype(BF)

    back_own, back_give, w_grad = project_back(
        where, tokens, par, w_qv, normed, queries, gq, gk_got, gv_got
    )
    back_chip = (back_own.astype(F32) + swap(back_give).astype(F32)).astype(BF)
    back_parts = scatter([back_chip[k] for k in range(4)], "z")
    grad_normed = back_parts[0].astype(F32)
    for part in back_parts[1:]:
        grad_normed = grad_normed + part.astype(F32)
    attn_xhat, attn_scale = normalized(second_in.astype(F32))
    attn_back = norm_back(grad_normed * par[0], attn_xhat, attn_scale)
    grad_second = (cot_second.astype(F32) + attn_back).astype(BF)

    w_grad = w_grad.reshape(4, 4, 4, 2, 8, 384)
    w_grad = reduce_over(w_grad, "y", 0).astype(BF)
    joined = jnp.concatenate(
        [
            jnp.transpose(w_grad, (1, 0, 2, 3, 4)).reshape(4, 64, 3, 128).reshape(4, -1, 128),
            a_sum.reshape(4, -1, 128),
        ],
        axis=1,
    )
    joined = reduce_over(joined, "x", 0)
    w_grad = joined[:192].astype(BF).reshape(4, 2, 8, 384)
    a_total = joined[192:].reshape(16, 2176)
    b_total = reduce_over(b_sum, "y", 0)
    grad_outer = b_total[:, :D]
    output_sum = jnp.concatenate([b_total[:16, D:], b_total[16:, D:]], axis=1)
    small = a_total[:4, 2048:2080]
    mine16 = by_core(small[:3, :8], small[:3, 8:16])
    grad_ffn_gain, grad_ffn_shift, grad_b_outer = mine16[0], mine16[1], mine16[2]
    grad_b_inner = small[3]

    w_rows = [
        lax.dynamic_index_in_dim(w_grad, (z + k) % 4, 0, keepdims=False) for k in range(4)
    ]
    w_rows = in_order(scatter(w_rows, "z"), z)
    chip_sum = jnp.concatenate([a_total[:, :2048], output_sum], axis=1).astype(BF)
    last_keep = by_core(w_rows[:, 0], w_rows[:, 1])
    last_give = by_core(w_rows[:, 1], w_rows[:, 0])
    rows_keep = by_core(chip_sum[:8], chip_sum[8:])
    rows_got = swap(by_core(chip_sum[8:], chip_sum[:8]))
    last_got = swap(last_give)
    rows_low = by_core(rows_keep, rows_got)
    rows_high = by_core(rows_got, rows_keep)
    grad_inner = jnp.stack(
        [rows_low[:, :2048].reshape(8, 64, 32), rows_high[:, :2048].reshape(8, 64, 32)], axis=2
    ).reshape(8, FF).astype(F32)
    grad_output = jnp.concatenate([rows_low[:, 2048:], rows_high[:, 2048:]], axis=1).astype(F32)
    heads = by_core(
        jnp.concatenate([last_keep, last_got]), jnp.concatenate([last_got, last_keep])
    ).astype(F32)
    grad_joint = jnp.transpose(heads[:, :, :128], (1, 0, 2)).reshape(8, D)
    grad_value = jnp.transpose(heads[:, :, 128:256], (1, 0, 2)).reshape(8, D)
    grad_attn_gain = jnp.sum(heads[:, :, 256], axis=0)
    grad_attn_shift = jnp.sum(heads[:, :, 320], axis=0)

    return (
        first_out, second_out, grad_first, grad_second, grad_attn_gain, grad_attn_shift,
        grad_joint, grad_value, grad_output, grad_ffn_gain, grad_ffn_shift, grad_inner,
        grad_b_inner, grad_outer, grad_b_outer,
    )


def solution(mesh):
    chips = Mesh(mesh.devices.reshape(4, 4, 4, 2), AXES)
    rows, flat = P(AXES, None), P(AXES)
    return jax.shard_map(
        local,
        mesh=chips,
        in_specs=(
            rows, rows, flat, flat, rows, rows, rows, flat, flat, rows, flat, rows, flat,
            P(None, AXES, None), rows, rows,
        ),
        out_specs=(
            rows, rows, rows, rows, flat, flat, rows, rows, rows, flat, flat, rows, flat, rows,
            flat,
        ),
        check_vma=False,
    )
```

```python
import functools

import jax
import jax.numpy as jnp
from jax import lax
from jax.experimental import pallas as pl
from jax.experimental.pallas import tpu as pltpu
from jax.sharding import Mesh, PartitionSpec as P

HEADS = 8
HEAD_DIM = 128
ROUNDS = 4
BUCKETS = 32
MOST = 8
TOK = 128
D = 1024
FF = 4096

EPS_NORM = 1e-05
EPS_KEY = 1e-06
SELF_SCORE = -10000.0
MASKED_SCORE = -1000000000.0

BF = jnp.bfloat16
F32 = jnp.float32

AXES = ("y", "z", "x", "c")
CHIPS = ("y", "z", "x")


def send(piece, axis, k):
    return lax.ppermute(piece, axis, [(i, (i + k) % 4) for i in range(4)])


def swap(piece):
    return lax.ppermute(piece, "c", [(0, 1), (1, 0)])


def gather(piece, axis):
    back, front, far = send(piece, axis, 3), send(piece, axis, 1), send(piece, axis, 2)
    return [piece, back, far, front]


def scatter(pieces, axis):
    front, back, far = (
        send(pieces[1], axis, 1),
        send(pieces[3], axis, 3),
        send(pieces[2], axis, 2),
    )
    return [pieces[0], back, far, front]


def sync(*groups):
    return lax.optimization_barrier(groups)


def dot(a, b):
    return jnp.dot(a, b, preferred_element_type=F32)


def dot_t(a, b):
    return lax.dot_general(a, b, (((1,), (1,)), ((), ())), preferred_element_type=F32)


def t_dot(a, b):
    return lax.dot_general(a, b, (((0,), (0,)), ((), ())), preferred_element_type=F32)


def cost(us):
    return pl.CostEstimate(flops=int(us * 1e9), bytes_accessed=0, transcendentals=0)


def params(mib):
    return pltpu.CompilerParams(vmem_limit_bytes=mib * 1024 * 1024)


SMEM = pl.BlockSpec(memory_space=pltpu.SMEM)


def kernel_call(kernel, *, out_shape, far_in=(), far_out=(), **rest):
    inner = pl.pallas_call(
        kernel,
        out_shape=[
            pltpu.HBM(o.shape, o.dtype) if at in far_out else o for at, o in enumerate(out_shape)
        ],
        **rest,
    )

    def run(*arrays):
        return inner(
            *[
                pltpu.with_memory_space_constraint(a, pltpu.HBM) if at in far_in else a
                for at, a in enumerate(arrays)
            ]
        )

    return run


def iota(shape, dim):
    return lax.broadcasted_iota(jnp.int32, shape, dim)


def whole_call(kernel, name, outs, us, mib=16, scratch=(), far_in=(), far_out=()):
    def call(where, *arrays):
        return kernel_call(
            kernel,
            grid=(1,),
            in_specs=[SMEM] + [fixed(a.shape) for a in arrays],
            out_specs=[fixed(s) for s, _ in outs],
            out_shape=[jax.ShapeDtypeStruct(s, t) for s, t in outs],
            scratch_shapes=list(scratch),
            compiler_params=params(mib),
            cost_estimate=cost(us),
            far_in=far_in,
            far_out=far_out,
            name=name,
        )(where, *arrays)

    return call


def fixed(shape):
    return pl.BlockSpec(shape, lambda r: (0,) * len(shape))


def per_round(shape):
    return pl.BlockSpec((1,) + shape, lambda r: (r,) + (0,) * len(shape))


PAIRS = BUCKETS // 2


def exchange(stacked, axis):
    return lax.all_to_all(stacked, axis, split_axis=0, concat_axis=0, tiled=True)


def total_of(parts):
    total = parts[0].astype(F32)
    for extra in parts[1:]:
        total = total + extra.astype(F32)
    return total


def pack_kernel(
    where, joint_ref, value_ref, output_ref, inner_ref, vec_ref, bucket_ref,
    keep_a, give_a, keep_b, give_b,
):
    low_core = where[3] == 0
    joint, value = joint_ref[...].astype(F32), value_ref[...].astype(F32)
    inner_rows = inner_ref[...].astype(F32)
    heads = []
    for core in range(2):
        rows = []
        for h in range(4):
            cols = slice((core * 4 + h) * 128, (core * 4 + h + 1) * 128)
            rows += [joint[:, cols], value[:, cols]]
        heads.append(jnp.concatenate(rows, axis=0))

    row, lane = iota((8, 128), 0), iota((8, 128), 1)
    vec = jnp.broadcast_to(vec_ref[0:1, :], (8, 128))
    par = jnp.zeros((8, 128), F32)
    for v in range(5):
        col = jnp.sum(jnp.where(lane == 8 * v + row, vec, 0.0), axis=1, keepdims=True)
        par = jnp.where(lane == v, col, par)
    for v in range(4):
        col = jnp.sum(jnp.where(lane == 40 + 4 * row + v, vec, 0.0), axis=1, keepdims=True)
        par = jnp.where(lane == 5 + v, col, par)

    sub, along = iota((128, 128), 0), iota((128, 128), 1)
    targets, counts = [], []
    for r in range(ROUNDS):
        chosen = jnp.broadcast_to(bucket_ref[r : r + 1, :].astype(F32), (128, 128))
        column = jnp.sum(jnp.where(sub == along, chosen, 0.0), axis=1, keepdims=True)
        earlier = (column == chosen) & (sub < along)
        rank = jnp.sum(earlier.astype(F32), axis=0, keepdims=True)
        targets.append(chosen[0:1] * MOST + rank)
        counts.append(jnp.sum((column == along.astype(F32)).astype(F32), axis=0, keepdims=True))
    aux = jnp.concatenate([par] + targets + counts, axis=0)
    keep_a[...] = jnp.concatenate([jnp.where(low_core, *heads), aux], axis=0).astype(BF)
    give_a[...] = jnp.concatenate([jnp.where(low_core, *heads[::-1]), aux], axis=0).astype(BF)

    chunks = [inner_rows[:, t * 256 : (t + 1) * 256] for t in range(16)]
    src, dst = iota((256, 256), 0), iota((256, 256), 1)
    wanted = 64 * ((dst % 128) // 32) + 32 * (dst // 128) + dst % 32
    picked = dot(jnp.concatenate(chunks, axis=0).astype(BF), (src == wanted).astype(F32).astype(BF))
    inner = []
    for core in range(2):
        halves = [
            jnp.concatenate(
                [
                    picked[t * 8 : (t + 1) * 8, core * 128 : (core + 1) * 128]
                    for t in range(half * 8, half * 8 + 8)
                ],
                axis=1,
            )
            for half in range(2)
        ]
        inner.append(jnp.concatenate(halves, axis=0))
    rest = jnp.concatenate([output_ref[...].astype(F32), jnp.zeros((8, D), F32)], axis=0)
    keep_b[...] = jnp.concatenate([jnp.where(low_core, *inner), rest], axis=0).astype(BF)
    give_b[...] = jnp.concatenate([jnp.where(low_core, *inner[::-1]), rest], axis=0).astype(BF)


pack = whole_call(
    pack_kernel, "pack", [((80, 128), BF)] * 2 + [((32, D), BF)] * 2, 3, far_in=(1, 2, 3, 4, 6)
)


def chip_message_kernel(where, keep_ref, got_ref, out_ref):
    low_core = where[3] == 0
    keep, got = keep_ref[...].astype(F32), got_ref[...].astype(F32)
    first, second = jnp.where(low_core, keep, got), jnp.where(low_core, got, keep)
    rows = []
    for at in range(0, 80, 8):
        rows += [first[at : at + 8], second[at : at + 8]]
    out_ref[...] = jnp.concatenate(rows, axis=0).astype(BF)


chip_message = whole_call(chip_message_kernel, "chip_message", [((160, 128), BF)], 1)


def head_messages_kernel(where, y0, y1, y2, y3, *outs):
    for k in range(4):
        head = (where[1] + k) % 4
        for n, piece in enumerate((y0, y1, y2, y3)):
            outs[k][n * 48 : n * 48 + 32, :] = piece[
                pl.ds(pl.multiple_of(head * 32, 32), 32), :
            ]
            outs[k][n * 48 + 32 : n * 48 + 48, :] = piece[128:144, :]
        outs[k][192:208, :] = y0[144:160, :]


head_messages = whole_call(
    head_messages_kernel, "head_messages", [((208, 128), BF)] * 4, 1
)


def payload_kernel(where, keep_ref, got_ref, outer_ref, out_ref):
    low_core = where[3] == 0
    keep, got = keep_ref[...].astype(F32), got_ref[...].astype(F32)
    first, second = jnp.where(low_core, keep, got), jnp.where(low_core, got, keep)
    for at, to in ((0, 0), (8, 16), (16, 64)):
        out_ref[to : to + 16, :] = jnp.concatenate(
            [first[at : at + 8], second[at : at + 8]], axis=0
        ).astype(BF)
    out_ref[32:64, :] = outer_ref[...]


payload = whole_call(payload_kernel, "payload", [((80, D), BF)], 1)


def assemble_kernel(where, x0, x1, x2, x3, w_ref, par_ref, tgt_ref, tgt_t_ref, count_ref, par_rows):
    for m, piece in enumerate((x0, x1, x2, x3)):
        for n in range(4):
            for k in range(4):
                chip = ((where[0] + n) % 4 * 4 + (where[1] + k) % 4) * 4 + (where[2] + m) % 4
                to = pl.ds(pl.multiple_of(chip * 16, 16), 16)
                at = k * 208 + n * 48
                w_ref[to, :128] = piece[at : at + 16, :]
                w_ref[to, 128:] = piece[at + 16 : at + 32, :]
                par_rows[to, :] = piece[at + 32 : at + 48, :]
    par_t = jnp.transpose(par_rows[...].astype(F32))
    par_ref[...] = par_t[:16, :]
    empty = jnp.zeros((96, 128), F32)
    slots = [
        jnp.concatenate(
            [piece[k * 208 + 192 : k * 208 + 208, :] for k in range(4)], axis=0
        ).astype(F32)
        for piece in (x0, x1, x2, x3)
    ]
    for r in range(ROUNDS):
        rows = jnp.concatenate(
            [slots[m][s * 8 + r : s * 8 + r + 1] for m in range(4) for s in range(8)], axis=0
        )
        tgt_ref[r] = rows.astype(jnp.int32)
        tgt_t_ref[r] = jnp.transpose(jnp.concatenate([rows, empty], axis=0)).astype(jnp.int32)
        count_ref[r] = jnp.concatenate(
            [slots[m][s * 8 + 4 + r : s * 8 + 5 + r] for m in range(4) for s in range(8)], axis=0
        )


def assemble(where, *pieces):
    shapes = [
        ((D, 256), BF), ((16, D), F32), ((ROUNDS, 32, 128), jnp.int32),
        ((ROUNDS, 128, 128), jnp.int32), ((ROUNDS, 32, 128), F32),
    ]
    return kernel_call(
        assemble_kernel,
        grid=(1,),
        in_specs=[SMEM] + [fixed(p.shape) for p in pieces],
        out_specs=[fixed(s) for s, _ in shapes],
        out_shape=[jax.ShapeDtypeStruct(s, t) for s, t in shapes],
        scratch_shapes=[pltpu.VMEM((D, 128), BF)],
        compiler_params=params(16),
        cost_estimate=cost(2),
        far_out=(2, 3),
        name="assemble",
    )(where, *pieces)


def mask_kernel(where, count_ref, mask_ref):
    z, x, c = where[1], where[2], where[3]
    shape = (256, 128)
    row, lane = iota(shape, 0), iota(shape, 1)
    source, rank = row >> 3, row & 7
    of_chip = lambda z_of, x_of, core: ((z_of & 3) * 8 + (x_of & 3) * 2 + core) * 8
    kpos = of_chip(z + ((source >> 1) & 3), x + (source >> 3), source & 1) + rank
    asker = (lane >> 3) & 7
    qpos = of_chip(z + (asker >> 1), x, asker & 1) + (lane & 7)
    code = jnp.where(kpos == qpos, -1.0, jnp.where(kpos < qpos, 0.0, -1e5))
    rank_f = rank.astype(F32)
    expand = (iota((256, 32), 0) >> 3) == iota((256, 32), 1)
    by_slot = dot(expand.astype(F32).astype(BF), count_ref[0].astype(BF)).astype(BF)
    bucket, side = iota((128, 128), 0), iota((128, 128), 1) >> 6

    @pl.loop(0, PAIRS, unroll=4)
    def _(p):
        select = (bucket == 2 * p + side).astype(F32).astype(BF)
        live = rank_f < dot(by_slot, select)
        mask_ref[0, p] = jnp.where(live, code, -1e5).astype(BF)


def make_mask(where, counts):
    return kernel_call(
        mask_kernel,
        grid=(ROUNDS,),
        in_specs=[SMEM, per_round((32, 128))],
        out_specs=[per_round((PAIRS, 256, 128))],
        out_shape=[jax.ShapeDtypeStruct((ROUNDS, PAIRS, 256, 128), BF)],
        far_out=(0,),
        compiler_params=params(16),
        cost_estimate=cost(6),
        name="make_mask",
    )(where, counts)[0]


def token_rows(where, own0, own3, sib):
    step = pl.program_id(0)
    own = step % 2 == where[3]
    rows = jnp.where(step < 2, own0[...].astype(F32), own3[0].astype(F32))
    return jnp.where(own, rows, sib[0].astype(F32)), own


def token_specs():
    far = pl.BlockSpec((1, TOK, D), lambda i: (jnp.maximum(i // 2 - 1, 0), 0, 0))
    return [
        pl.BlockSpec((TOK, D), lambda i: (0, 0)),
        far,
        pl.BlockSpec((1, TOK, D), lambda i: (i // 2, 0, 0)),
    ]


def project_kernel(where, own0, own3, sib, par_ref, w_ref, normed_ref, q_ref, v_ref):
    rows, _ = token_rows(where, own0, own3, sib)
    centered = rows - jnp.mean(rows, axis=-1, keepdims=True)
    spread = jnp.mean(centered * centered, axis=-1, keepdims=True)
    normed = centered * lax.rsqrt(spread + EPS_NORM) * par_ref[0:1, :] + par_ref[1:2, :]
    normed = normed.astype(BF)
    normed_ref[...] = normed
    both = dot(normed, w_ref[...]).astype(BF)
    q_ref[...] = both[:, :HEAD_DIM]
    v_ref[...] = both[:, HEAD_DIM:]


def project(where, tokens, par, w):
    whole = lambda i: (0, 0)
    return kernel_call(
        project_kernel,
        grid=(8,),
        in_specs=[SMEM] + token_specs()
        + [pl.BlockSpec((16, D), whole), pl.BlockSpec((D, 256), whole)],
        out_specs=[
            pl.BlockSpec((TOK, D), lambda i: (i, 0)),
            pl.BlockSpec((TOK, HEAD_DIM), lambda i: (i, 0)),
            pl.BlockSpec((TOK, HEAD_DIM), lambda i: (i, 0)),
        ],
        out_shape=[
            jax.ShapeDtypeStruct((8 * TOK, D), BF),
            jax.ShapeDtypeStruct((8 * TOK, HEAD_DIM), BF),
            jax.ShapeDtypeStruct((8 * TOK, HEAD_DIM), BF),
        ],
        compiler_params=params(16),
        cost_estimate=cost(4),
        far_out=(0,),
        name="project",
    )(where, *tokens, par, w)


def project_back_kernel(
    where, own0, own3, sib, par_ref, w_ref, normed_ref, q_ref, gq_ref,
    gk_ref, gv_ref, own_out, sib_out, wg0, wg1, wg2, wg3, total, sums,
):
    step = pl.program_id(0)
    x, own = token_rows(where, own0, own3, sib)
    q = q_ref[...].astype(F32)
    inv = lax.rsqrt(jnp.sum(q * q, axis=-1, keepdims=True) + EPS_KEY)
    gk = total_of([gk_ref[m] for m in range(4)])
    gv = total_of([gv_ref[m] for m in range(4)])
    along = jnp.sum(q * gk, axis=-1, keepdims=True)
    gq = gq_ref[...] + gk * inv - q * (inv * inv * inv * along)
    rows = jnp.concatenate([gq.astype(BF), gv.astype(BF)], axis=1)
    back = dot_t(rows, w_ref[...])

    @pl.when(own)
    def _():
        own_out[0] = back.astype(BF)

    @pl.when(jnp.logical_not(own))
    def _():
        sib_out[0] = back.astype(BF)

    centered = x - jnp.mean(x, axis=-1, keepdims=True)
    spread = jnp.mean(centered * centered, axis=-1, keepdims=True)
    xhat = centered * lax.rsqrt(spread + EPS_NORM)
    gain_part = jnp.sum((back * xhat).reshape(TOK // 8, 8, D), axis=0)
    shift_part = jnp.sum(back.reshape(TOK // 8, 8, D), axis=0)
    weight_part = t_dot(normed_ref[...], rows)

    @pl.when(step == 0)
    def _():
        total[:, :256] = weight_part
        sums[0:8, :] = gain_part
        sums[8:16, :] = shift_part

    @pl.when(step > 0)
    def _():
        total[:, :256] += weight_part
        sums[0:8, :] += gain_part
        sums[8:16, :] += shift_part

    @pl.when(step == 7)
    def _():
        gain_sum = jnp.sum(sums[0:8, :], axis=0, keepdims=True)
        shift_sum = jnp.sum(sums[8:16, :], axis=0, keepdims=True)
        both = jnp.where(iota((HEAD_DIM, D), 0) < 64, gain_sum, shift_sum)
        total[:, 256:] = jnp.transpose(both)
        for k, out in enumerate((wg0, wg1, wg2, wg3)):
            rows = pl.ds(pl.multiple_of(((where[0] + k) & 3) * 256, 256), 256)
            out[...] = total[rows, :].astype(BF)


def project_back(where, tokens, par, w, normed, q, gq, gk, gv):
    token_block = pl.BlockSpec((1, TOK, D), lambda i: (i // 2, 0, 0))
    whole = lambda i: (0, 0)
    row_block = lambda width: pl.BlockSpec((TOK, width), lambda i: (i, 0))
    return kernel_call(
        project_back_kernel,
        grid=(8,),
        in_specs=[SMEM] + token_specs()
        + [
            pl.BlockSpec((16, D), whole),
            pl.BlockSpec((D, 256), whole),
            row_block(D),
            row_block(HEAD_DIM),
            row_block(HEAD_DIM),
        ]
        + [pl.BlockSpec((4, TOK, HEAD_DIM), lambda i: (0, i, 0))] * 2,
        out_specs=[token_block, token_block] + [pl.BlockSpec((256, 384), whole)] * 4,
        out_shape=[
            jax.ShapeDtypeStruct((4, TOK, D), BF),
            jax.ShapeDtypeStruct((4, TOK, D), BF),
        ]
        + [jax.ShapeDtypeStruct((256, 384), BF)] * 4,
        scratch_shapes=[pltpu.VMEM((D, 384), F32), pltpu.VMEM((16, D), F32)],
        compiler_params=params(22),
        cost_estimate=cost(8),
        far_in=(2, 3, 5, 6, 7, 8),
        name="project_back",
    )(where, *tokens, par, w, normed, q, gq, gk, gv)


def chip_rows(where, own, sib):
    low_core = where[3] == 0
    return jnp.concatenate([jnp.where(low_core, own, sib), jnp.where(low_core, sib, own)], axis=0)


def normalized(values):
    centered = values - jnp.mean(values, axis=-1, keepdims=True)
    spread = jnp.mean(centered * centered, axis=-1, keepdims=True)
    scale = lax.rsqrt(spread + EPS_NORM)
    return centered * scale, scale


def norm_back(u, xhat, scale):
    mean_u = jnp.mean(u, axis=-1, keepdims=True)
    mean_ux = jnp.mean(u * xhat, axis=-1, keepdims=True)
    return (u - mean_u - xhat * mean_ux) * scale


def head_rows(w_ref, head):
    return w_ref[pl.ds(head * 8, 8)].reshape(HEAD_DIM, D)


def heads_of(where):
    for side in range(2):
        core = where[3] if side == 0 else 1 - where[3]
        for m in range(4):
            yield side, m, core * 4 + (where[1] + m) % 4


GELU_IN = 0.7978845608028654
GELU_CUBE = 0.044715


def feed_kernel(
    where, mix_own, mix_sib, first_own, first_sib, cot_own, cot_sib, par_ref, bias_ref,
    out_w, inner_ref, outer_ref,
    sum_ref, first_out, input_t_ref, active_ref, grad_ref, back_ref, hid_sum_ref, cot_sum_ref,
    ffn_in, cot_t, back_t,
):
    step = pl.program_id(0)

    @pl.when(step == 0)
    def _():
        total = chip_rows(where, first_own[...].astype(F32), first_sib[0].astype(F32))
        mixes = (mix_own, mix_sib)
        for side, m, head in heads_of(where):
            total = total + dot(mixes[side][:, m * 128 : m * 128 + 128], head_rows(out_w, head))
        sum_ref[...] = total
        own = jnp.where(where[3] == 0, total[:TOK], total[TOK:])
        first_out[...] = own.astype(BF)
        xhat, _ = normalized(total)
        rows = xhat * par_ref[2:3, :] + par_ref[3:4, :]
        ffn_in[...] = rows.astype(BF)
        input_t_ref[...] = jnp.transpose(rows).astype(BF)
        cot = chip_rows(where, cot_own[...].astype(F32), cot_sib[0].astype(F32))
        cot_t[...] = jnp.transpose(cot).astype(BF)
        cot_sum_ref[...] = jnp.broadcast_to(jnp.sum(cot, axis=0, keepdims=True), (8, D))

    inner = inner_ref[...].reshape(D, 256)
    outer = outer_ref[...].reshape(256, D)
    hidden = dot(ffn_in[...], inner) + bias_ref[0:1, :]
    square = hidden * hidden
    bent = jnp.tanh(GELU_IN * hidden * (1.0 + GELU_CUBE * square))
    half = 0.5 * (1.0 + bent)
    active_ref[...] = (hidden * half).astype(BF)
    slope = half + 0.5 * hidden * (1.0 - bent * bent) * GELU_IN * (
        1.0 + 3.0 * GELU_CUBE * square
    )
    grad_active = jnp.transpose(dot(outer, cot_t[...]))
    grad = (grad_active * slope).astype(BF)
    grad_ref[...] = grad
    hid_sum_ref[...] = jnp.broadcast_to(
        jnp.sum(grad.astype(F32), axis=0, keepdims=True), (8, 256)
    )
    part = dot(inner, jnp.transpose(grad))

    @pl.when(step == 0)
    def _():
        back_t[...] = part

    @pl.when(step > 0)
    def _():
        back_t[...] += part

    @pl.when(step == 7)
    def _():
        back_ref[...] = jnp.transpose(back_t[...])


def feed(where, mix_own, mix_sib, first_in, cot_second, sib_rows, par, bias, gathered):
    whole = lambda i: (0, 0)
    two = 2 * TOK
    return kernel_call(
        feed_kernel,
        grid=(8,),
        in_specs=[
            SMEM,
            pl.BlockSpec((two, 512), whole),
            pl.BlockSpec((two, 512), whole),
            pl.BlockSpec((TOK, D), whole),
            pl.BlockSpec((1, TOK, D), lambda i: (0, 0, 0)),
            pl.BlockSpec((TOK, D), whole),
            pl.BlockSpec((1, TOK, D), lambda i: (2, 0, 0)),
            pl.BlockSpec((16, D), whole),
            pl.BlockSpec((8, 256), lambda i: (0, i)),
            pl.BlockSpec((64, 16, D), lambda i: (0, 4, 0)),
            pl.BlockSpec((64, 16, 256), lambda i: (0, i // 4, i % 4)),
            pl.BlockSpec((8, 32, D), lambda i: (i, 1, 0)),
        ],
        out_specs=[
            pl.BlockSpec((two, D), whole),
            pl.BlockSpec((TOK, D), whole),
            pl.BlockSpec((D, two), whole),
            pl.BlockSpec((two, 256), lambda i: (0, i)),
            pl.BlockSpec((two, 256), lambda i: (0, i)),
            pl.BlockSpec((two, D), whole),
            pl.BlockSpec((8, 256), lambda i: (0, i)),
            pl.BlockSpec((8, D), whole),
        ],
        out_shape=[
            jax.ShapeDtypeStruct((two, D), F32),
            jax.ShapeDtypeStruct((TOK, D), BF),
            jax.ShapeDtypeStruct((D, two), BF),
            jax.ShapeDtypeStruct((two, 2048), BF),
            jax.ShapeDtypeStruct((two, 2048), BF),
            jax.ShapeDtypeStruct((two, D), F32),
            jax.ShapeDtypeStruct((8, 2048), F32),
            jax.ShapeDtypeStruct((8, D), F32),
        ],
        scratch_shapes=[
            pltpu.VMEM((two, D), BF),
            pltpu.VMEM((D, two), BF),
            pltpu.VMEM((D, two), F32),
        ],
        compiler_params=params(26),
        cost_estimate=cost(16),
        far_in=(2, 4, 6, 9, 10, 11),
        far_out=(0, 2, 3, 4, 5),
        name="feed",
    )(
        where, mix_own, mix_sib, first_in, sib_rows, cot_second, sib_rows, par, bias,
        gathered, gathered, gathered,
    )


def first_back_kernel(
    where, back_own, back_sib, sum_ref, cot_own, cot_sib, par_ref, out_w,
    grad_first, branch_ref, m0, m1, m2, m3, sums_ref,
):
    back = back_own[...] + back_sib[...]
    xhat, scale = normalized(sum_ref[...])
    total = chip_rows(where, cot_own[...].astype(F32), cot_sib[0].astype(F32))
    total = total + norm_back(back * par_ref[2:3, :], xhat, scale)
    branch = total.astype(BF)
    branch_ref[...] = branch
    grad_first[...] = jnp.where(where[3] == 0, total[:TOK], total[TOK:]).astype(BF)
    outs = (m0, m1, m2, m3)
    for side, m, head in heads_of(where):
        if side == 0:
            outs[m][...] = dot_t(branch, head_rows(out_w, head)).astype(BF)
    gain = jnp.sum(back * xhat, axis=0, keepdims=True)
    shift = jnp.sum(back, axis=0, keepdims=True)
    sums_ref[...] = jnp.concatenate([gain, shift, jnp.zeros((6, D), F32)], axis=0)


def first_back(where, back_own, back_sib, first_sum, cot_first, sib_rows, par, gathered):
    two = 2 * TOK
    one = lambda shape: pl.BlockSpec(shape, lambda i: (0,) * len(shape))
    return kernel_call(
        first_back_kernel,
        grid=(1,),
        in_specs=[
            SMEM, one((two, D)), one((two, D)), one((two, D)), one((TOK, D)),
            pl.BlockSpec((1, TOK, D), lambda i: (1, 0, 0)),
            one((16, D)),
            pl.BlockSpec((64, 16, D), lambda i: (0, 4, 0)),
        ],
        out_specs=[one((TOK, D)), one((two, D))] + [one((two, 128))] * 4 + [one((8, D))],
        out_shape=[jax.ShapeDtypeStruct((TOK, D), BF), jax.ShapeDtypeStruct((two, D), BF)]
        + [jax.ShapeDtypeStruct((two, 128), BF)] * 4
        + [jax.ShapeDtypeStruct((8, D), F32)],
        compiler_params=params(24),
        cost_estimate=cost(6),
        far_in=(1, 2, 3, 5, 7),
        far_out=(1, 2, 3, 4, 5),
        name="first_back",
    )(where, back_own, back_sib, first_sum, cot_first, sib_rows, par, gathered)


FIVE = (16, 16, 8, 8, 16)


def inner_grads_kernel(where, active_ref, grad_ref, input_t, cot_own, cot_sib, a0, a1, far_low, far_high, a3, far, cot):
    step = pl.program_id(0)

    @pl.when(step == 0)
    def _():
        cot[...] = chip_rows(
            where, cot_own[:, :512].astype(F32), cot_sib[0, :, :512].astype(F32)
        ).astype(BF)

    lanes = pl.ds(pl.multiple_of(step * 256, 256), 256)
    outs = (a0, a1, far, a3)
    for k, out in enumerate(outs):
        rows = pl.ds(pl.multiple_of(((where[0] + k) & 3) * 256, 256), 256)
        out[:, :, lanes] = dot(input_t[rows, :], grad_ref[...]).astype(BF).reshape(16, 16, 256)
    outer = t_dot(active_ref[...], cot[...]).astype(BF).reshape(8, 32, 512)
    near = ((step >> 1) - where[0]) & 3
    for k, out in enumerate(outs):

        @pl.when(near == k)
        def _(out=out):
            chips = pl.ds((step & 1) * 8, 8)
            out[chips, :, 2048:2560] = outer[:, :16]
            out[chips, :, 2560:] = outer[:, 16:]

    @pl.when(step == 7)
    def _():
        far_low[...] = far[:8]
        far_high[...] = far[8:]


def inner_grads(where, active, grad, input_t, cot_second, sib_rows):
    two = 2 * TOK
    whole = lambda i: (0, 0)
    return kernel_call(
        inner_grads_kernel,
        grid=(8,),
        in_specs=[
            SMEM,
            pl.BlockSpec((two, 256), lambda i: (0, i)),
            pl.BlockSpec((two, 256), lambda i: (0, i)),
            pl.BlockSpec((D, two), whole),
            pl.BlockSpec((TOK, D), whole),
            pl.BlockSpec((1, TOK, D), lambda i: (2, 0, 0)),
        ],
        out_specs=[pl.BlockSpec((n, 16, 3072), lambda i: (0, 0, 0)) for n in FIVE],
        out_shape=[jax.ShapeDtypeStruct((n, 16, 3072), BF) for n in FIVE],
        scratch_shapes=[pltpu.VMEM((16, 16, 3072), BF), pltpu.VMEM((two, 512), BF)],
        compiler_params=params(28),
        cost_estimate=cost(9),
        far_in=(1, 2, 3, 5),
        far_out=(0, 1, 2, 3, 4),
        name="inner_grads",
    )(where, active, grad, input_t, cot_second, sib_rows)


def outer_grads_kernel(
    where, active_ref, cot_own, cot_sib, mix_own, mix_sib, branch_ref, sums_ref, outer_ref,
    b0, b1, far_low, far_high, b3, own_ref, give_ref, far, cot, total,
):
    step = pl.program_id(0)
    outs = (b0, b1, far, b3)

    @pl.when(step == 0)
    def _():
        cot[...] = chip_rows(
            where, cot_own[:, 512:].astype(F32), cot_sib[0, :, 512:].astype(F32)
        ).astype(BF)
        total[...] = jnp.zeros_like(total)
        cols = jnp.where(
            where[3] == 0, branch_ref[:, :512].astype(F32), branch_ref[:, 512:].astype(F32)
        ).astype(BF)
        mixes = (mix_own, mix_sib)
        for side, m, head in heads_of(where):
            rows = t_dot(mixes[side][:, m * 128 : m * 128 + 128], cols).astype(BF)
            rows = rows.reshape(2, 4, 16, 512)
            at = pl.ds((head >> 1) * 4, 4)
            for part in range(2):
                near = (2 * (head & 1) + part - where[1]) & 3
                for k, out in enumerate(outs):

                    @pl.when(near == k)
                    def _(part=part, out=out, rows=rows, at=at):
                        out[at, 0:16, :256] = rows[part, :, :, :256]
                        out[at, 16:32, :256] = rows[part, :, :, 256:]

        for k, out in enumerate(outs):
            near = (where[1] + k) & 3
            for y in range(4):
                out[y * 4 : y * 4 + 4, 0:16, 256:384] = sums_ref[pl.ds(y * 16 + near * 4, 4)]
                out[y * 4 : y * 4 + 4, 16:32, 256:384] = jnp.zeros((4, 16, 128), BF)

    active = active_ref[...]
    total[...] += dot(active, outer_ref[...].reshape(256, D))
    outer = t_dot(active, cot[...]).astype(BF).reshape(2, 4, 32, 512)
    for side in range(2):
        near = (2 * (step & 1) + side - where[1]) & 3
        for k, out in enumerate(outs):

            @pl.when(near == k)
            def _(side=side, out=out):
                out[pl.ds((step >> 1) * 4, 4), :, 384:] = outer[side]

    @pl.when(step == 7)
    def _():
        far_low[...] = far[:8]
        far_high[...] = far[8:]
        low_core = where[3] == 0
        own_ref[...] = jnp.where(low_core, total[:TOK], total[TOK:])
        give_ref[...] = jnp.where(low_core, total[TOK:], total[:TOK])


def outer_grads(where, active, cot_second, sib_rows, mix_own, mix_sib, branch, sums, gathered):
    two = 2 * TOK
    whole = lambda i: (0, 0)
    whole3 = lambda i: (0, 0, 0)
    return kernel_call(
        outer_grads_kernel,
        grid=(8,),
        in_specs=[
            SMEM,
            pl.BlockSpec((two, 256), lambda i: (0, i)),
            pl.BlockSpec((TOK, D), whole),
            pl.BlockSpec((1, TOK, D), lambda i: (2, 0, 0)),
            pl.BlockSpec((two, 512), whole),
            pl.BlockSpec((two, 512), whole),
            pl.BlockSpec((two, D), whole),
            pl.BlockSpec((64, 16, 128), whole3),
            pl.BlockSpec((8, 32, D), lambda i: (i, 1, 0)),
        ],
        out_specs=[pl.BlockSpec((n, 32, 896), whole3) for n in FIVE]
        + [pl.BlockSpec((TOK, D), whole)] * 2,
        out_shape=[jax.ShapeDtypeStruct((n, 32, 896), BF) for n in FIVE]
        + [jax.ShapeDtypeStruct((TOK, D), F32)] * 2,
        scratch_shapes=[
            pltpu.VMEM((16, 32, 896), BF), pltpu.VMEM((two, 512), BF), pltpu.VMEM((two, D), F32),
        ],
        compiler_params=params(28),
        cost_estimate=cost(10),
        far_in=(1, 3, 5, 6, 8),
        far_out=tuple(range(7)),
        name="outer_grads",
    )(where, active, cot_second, sib_rows, mix_own, mix_sib, branch, sums, gathered)


def pass_on_kernel(*refs):
    pieces, outs = refs[:8], refs[8:]
    for at, out in enumerate(outs):
        out[...] = total_of([pieces[2 * at][...], pieces[2 * at + 1][...]]).astype(BF)


def pass_on(*parts):
    specs, outs, shapes, arrays = [], [], [], []
    for piece, low, last_piece, high in parts:
        block = (2,) + low.shape[1:]
        near = pl.BlockSpec(block, lambda i: (i, 0, 0))
        second = pl.BlockSpec(block, lambda i: (i + 4, 0, 0))
        specs += [near, near, second, near]
        outs += [near, second]
        shapes += [jax.ShapeDtypeStruct(piece.shape, BF)] * 2
        arrays += [piece, low, last_piece, high]
    return kernel_call(
        pass_on_kernel,
        grid=(4,),
        in_specs=specs,
        out_specs=outs,
        out_shape=shapes,
        input_output_aliases={0: 0, 2: 1, 4: 2, 6: 3},
        compiler_params=params(16),
        cost_estimate=cost(4),
        far_in=(0, 2, 4, 6),
        far_out=(0, 1, 2, 3),
        name="pass_on",
    )(*arrays)


def recut_kernel(axis, where, *refs):
    parts, outs = refs[:3], refs[3:]
    for k, out in enumerate(outs):
        mine = (where[axis] + k) & 3
        out[...] = total_of([part[mine] for part in parts]).astype(BF)


recut_a = whole_call(
    functools.partial(recut_kernel, 1), "recut_a", [((4, 16, 3072), BF)] * 4, 4, mib=32,
    far_in=(1,), far_out=(0, 1, 2, 3),
)
recut_b = whole_call(
    functools.partial(recut_kernel, 0), "recut_b", [((4, 32, 896), BF)] * 4, 3, mib=24,
    far_in=(1,), far_out=(0, 1, 2, 3),
)


def join_kernel(where, *refs):
    w, a, b, outs = refs[:4], refs[4:8], refs[8:12], refs[12:]
    for k, out in enumerate(outs):
        x = (where[2] + k) & 3
        for z in range(4):
            rows = pl.ds(pl.multiple_of(z * 64 + x * 16, 16), 16)
            total = total_of([part[rows, :] for part in w]).astype(BF)
            for j in range(3):
                at = (z * 3 + j) * 16
                out[at : at + 16, :] = total[:, j * 128 : j * 128 + 128]
        total = total_of([part[x] for part in a]).astype(BF)
        for j in range(24):
            out[192 + j * 16 : 208 + j * 16, :] = total[:, j * 128 : j * 128 + 128]
        total = total_of([part[x] for part in b]).astype(BF)
        for j in range(7):
            out[576 + j * 32 : 608 + j * 32, :] = total[:, j * 128 : j * 128 + 128]


join = whole_call(join_kernel, "join", [((800, 128), BF)] * 4, 3)


def divide_kernel(where, x0, x1, x2, x3, w0, w1, w2, w3, keep_ref, give_ref, outer_ref, small_ref, total):
    low_core = where[3] == 0
    total[...] = total_of([part[...] for part in (x0, x1, x2, x3)])
    for k, out in enumerate((w0, w1, w2, w3)):
        z = (where[1] + k) & 3
        for j in range(3):
            rows = pl.ds(pl.multiple_of((z * 3 + j) * 16, 16), 16)
            out[:, j * 128 : j * 128 + 128] = total[rows, :].astype(BF)
    blocks = [total[192 + j * 16 : 208 + j * 16, :] for j in range(16)]
    for at in (576, 592):
        blocks += [total[at : at + 16, :], total[at + 32 : at + 48, :]]
    low = jnp.concatenate([block[:8] for block in blocks], axis=0)
    high = jnp.concatenate([block[8:] for block in blocks], axis=0)
    keep_ref[...] = jnp.where(low_core, low, high)
    give_ref[...] = jnp.where(low_core, high, low).astype(BF)
    for j in range(4):
        lanes = slice(j * 128, j * 128 + 128)
        outer_ref[:16, lanes] = total[448 + j * 16 : 464 + j * 16, :]
        outer_ref[16:, lanes] = total[512 + j * 16 : 528 + j * 16, :]
        lanes = slice(512 + j * 128, 640 + j * 128)
        outer_ref[:, lanes] = total[672 + j * 32 : 704 + j * 32, :]
    small_ref[...] = total[640:648, :]


divide = whole_call(
    divide_kernel, "divide",
    [((16, 384), BF)] * 4 + [((160, 128), F32), ((160, 128), BF), ((32, D), F32), ((8, 128), F32)],
    2, scratch=[pltpu.VMEM((800, 128), F32)],
)


def last_kernel(where, w0, w1, w2, w3, give_ref, keep_w, out_ref, kept, given):
    low_core = where[3] == 0
    for m, piece in enumerate((w0, w1, w2, w3)):
        z = (where[1] + m) & 3
        rows = piece[...].astype(F32)
        mine = jnp.where(low_core, rows[:8], rows[8:])
        other = jnp.where(low_core, rows[8:], rows[:8])
        for j in range(3):
            at = pl.ds(pl.multiple_of((z * 3 + j) * 8, 8), 8)
            kept[at, :] = mine[:, j * 128 : j * 128 + 128]
            given[at, :] = other[:, j * 128 : j * 128 + 128]
    keep_w[...] = kept[...]
    out_ref[:96, :] = given[...].astype(BF)
    out_ref[96:, :] = give_ref[...]


last = whole_call(
    last_kernel, "last", [((96, 128), F32), ((256, 128), BF)], 1,
    scratch=[pltpu.VMEM((96, 128), F32)] * 2,
)


def finish_kernel(
    where, keep_w, keep_ref, got_ref, joint_ref, value_ref, norm_ref, inner_ref, output_ref
):
    low_core = where[3] == 0
    got = got_ref[...].astype(F32)
    mine, other = keep_w[...], got[:96]
    norm = jnp.zeros((8, 128), F32)
    for core in range(2):
        rows = jnp.where(low_core, *((mine, other) if core == 0 else (other, mine)))
        for z in range(4):
            lanes = slice((core * 4 + z) * 128, (core * 4 + z + 1) * 128)
            joint_ref[:, lanes] = rows[z * 24 : z * 24 + 8]
            value_ref[:, lanes] = rows[z * 24 + 8 : z * 24 + 16]
            norm = norm + rows[z * 24 + 16 : z * 24 + 24]
    norm_ref[...] = norm
    mine, other = keep_ref[...], got[96:]
    low, high = jnp.where(low_core, mine, other), jnp.where(low_core, other, mine)
    both = jnp.concatenate([low[:128], high[:128]], axis=1).astype(BF)
    dst, src = iota((256, 256), 1), iota((256, 256), 0)
    wanted = 128 * ((dst >> 5) & 1) + 32 * (dst >> 6) + (dst & 31)
    mixed = dot(both, (src == wanted).astype(F32).astype(BF))
    for t in range(16):
        inner_ref[:, t * 256 : (t + 1) * 256] = mixed[t * 8 : t * 8 + 8, :]
    for core, rows in enumerate((low, high)):
        for at, lane in enumerate((0, 128, 256, 384)):
            lanes = slice(core * 512 + lane, core * 512 + lane + 128)
            output_ref[:, lanes] = rows[128 + at * 8 : 136 + at * 8]


finish = whole_call(
    finish_kernel, "finish",
    [((8, D), F32), ((8, D), F32), ((8, 128), F32), ((8, FF), F32), ((8, D), F32)], 1,
)


def make_keys(pieces, rows_ref):
    for m, piece in enumerate(pieces):

        @pl.loop(0, 8, unroll=4)
        def _(s, m=m, piece=piece):
            rows = pl.ds(pl.multiple_of(s * TOK, TOK), TOK)
            to = pl.ds(pl.multiple_of(m * 8 * TOK + s * TOK, TOK), TOK)
            q = piece[rows, :].astype(F32)
            inv = lax.rsqrt(jnp.sum(q * q, axis=-1, keepdims=True) + EPS_KEY)
            rows_ref[to, :] = (q * inv).astype(BF)


def round_weights(lt_ref, at):
    totals = [lt_ref[r, at, :].astype(F32) for r in range(ROUNDS)]
    peak = jnp.maximum(jnp.maximum(totals[0], totals[1]), jnp.maximum(totals[2], totals[3]))
    exps = [jnp.exp(t - peak) for t in totals]
    scale = 1.0 / (exps[0] + exps[1] + exps[2] + exps[3])
    return [e * scale for e in exps]


def hot_slots(tgt_ref, source):
    slots = iota((BUCKETS * MOST, TOK), 0)
    return (slots == tgt_ref[0, pl.ds(source, 1), :]).astype(F32).astype(BF)


def hot_tokens(tgt_t_ref, source):
    slots = iota((TOK, BUCKETS * MOST), 1)
    return (slots == tgt_t_ref[0, :, source : source + 1]).astype(F32).astype(BF)


def spread(first, second):
    width = first.shape[-1]
    both = [a.reshape(PAIRS, 2, MOST, width) for a in (first, second)]
    return jnp.concatenate(both, axis=2).astype(BF)


def fill(tgt_ref, read_rows, ref):
    @pl.loop(0, 16, unroll=4)
    def _(pair):
        placed = [
            dot(hot_slots(tgt_ref, pair * 2 + half), read_rows(pair * 2 + half))
            for half in range(2)
        ]
        both = spread(*placed)
        at = pl.ds(pl.multiple_of(pair * 16, 16), 16)
        ref[0, :, at, :128] = both[:, 0]
        ref[0, :, at, 128:] = both[:, 1]


def place(both, ref, pair):
    at = pl.multiple_of(pair * 16, 16)
    ref[:, pl.ds(at, 16), :] = both[:, 0]
    ref[:, pl.ds(64 + at, 16), :] = both[:, 1]


def diagonal(rows):
    first = iota((128, 128), 0) < 64
    none = jnp.zeros((128, 128), BF)
    return jnp.concatenate([jnp.where(first, rows, none), jnp.where(first, none, rows)], axis=1)


def diagonal_t(rows):
    turned = jnp.transpose(rows)
    first = iota((128, 128), 1) < 64
    none = jnp.zeros((128, 128), BF)
    return jnp.concatenate([jnp.where(first, turned, none), jnp.where(first, none, turned)], axis=0)


def eye():
    return iota((128, 128), 0) == iota((128, 128), 1)


def token_block(s):
    return pl.ds(pl.multiple_of(s * TOK, TOK), TOK)


def scores_kernel(q0, q1, q2, q3, tgt_ref, mask_ref, probs_ref, keys_ref, qm_ref, log_ref, k_rows):
    @pl.when(pl.program_id(0) == 0)
    def _():
        make_keys((q0, q1, q2, q3), k_rows)

    fill(tgt_ref, lambda source: k_rows[token_block(source), :], keys_ref)

    @pl.loop(0, 4, unroll=4)
    def _(pair):
        placed = [
            dot(hot_slots(tgt_ref, pair * 2 + half), q0[token_block(pair * 2 + half), :])
            for half in range(2)
        ]
        place(spread(*placed), qm_ref.at[0], pair)

    @pl.loop(0, PAIRS, unroll=16)
    def _(p):
        code = mask_ref[0, p].astype(F32)
        scores = dot(keys_ref[0, p], diagonal_t(qm_ref[0, p]))
        scores = jnp.where(code == 0.0, scores, code * 1e4)
        peak = jnp.max(scores, axis=0, keepdims=True)
        exponent = jnp.exp(scores - peak)
        total = jnp.sum(exponent, axis=0, keepdims=True)
        probs_ref[0, p] = (exponent * (1.0 / total)).astype(BF)
        log_ref[0, pl.ds(p, 1), :] = peak + jnp.log(total)


def attend_scores(q_pieces, tgt, mask):
    rows = 8 * TOK
    outs = [(PAIRS, 256, 128), (PAIRS, 256, 256), (PAIRS, 128, 128), (PAIRS, 128)]
    types = [BF, BF, BF, F32]
    return kernel_call(
        scores_kernel,
        grid=(ROUNDS,),
        in_specs=[fixed((rows, HEAD_DIM))] * 4
        + [per_round((32, TOK)), per_round((PAIRS, 256, 128))],
        out_specs=[per_round(shape) for shape in outs],
        out_shape=[
            jax.ShapeDtypeStruct((ROUNDS,) + shape, t) for shape, t in zip(outs, types)
        ],
        scratch_shapes=[pltpu.VMEM((4 * rows, HEAD_DIM), BF)],
        compiler_params=params(20),
        cost_estimate=cost(18),
        far_in=(5,),
        far_out=(0, 1, 2),
        name="attend_scores",
    )(*q_pieces, tgt, mask)


def values_kernel(
    v0, v1, v2, v3, tgt_ref, tgt_t_ref, probs_ref, log_ref, mixed_ref, ro_ref, lt_ref, values_ref, att
):
    this_round = pl.program_id(0)
    for m, piece in enumerate((v0, v1, v2, v3)):

        @pl.loop(0, 4, unroll=4)
        def _(pair, m=m, piece=piece):
            placed = [
                dot(
                    hot_slots(tgt_ref, m * 8 + pair * 2 + half),
                    piece[token_block(pair * 2 + half), :],
                )
                for half in range(2)
            ]
            both = spread(*placed)
            at = pl.ds(pl.multiple_of((m * 4 + pair) * 16, 16), 16)
            values_ref[0, :, at, :128] = both[:, 0]
            values_ref[0, :, at, 128:] = both[:, 1]

    ones = jnp.ones((128, 128), BF)

    @pl.loop(0, PAIRS, unroll=16)
    def _(p):
        out = t_dot(probs_ref[0, p], values_ref[0, p])
        log_total = log_ref[0, pl.ds(p, 1), :]
        logs = dot(jnp.where(eye(), log_total, 0.0).astype(BF), ones)
        att[p, 0, :, :128] = out[:64, :128]
        att[p, 1, :, :128] = out[64:, 128:]
        att[p, 0, :, 128:] = logs[:64]
        att[p, 1, :, 128:] = logs[64:]

    for s in range(8):
        slots = att[:, :, s * MOST : (s + 1) * MOST, :].reshape(256, 256)
        rows = dot(hot_tokens(tgt_t_ref, s), slots.astype(BF)).astype(BF)
        ro_ref[this_round, s * TOK : (s + 1) * TOK, :] = rows[:, :HEAD_DIM]
        lt_ref[this_round, s * TOK : (s + 1) * TOK, :] = rows[:, HEAD_DIM:]

    @pl.when(this_round == ROUNDS - 1)
    def _():
        @pl.loop(0, 8)
        def _(s):
            at = token_block(s)
            weights = round_weights(lt_ref, at)
            mixed = weights[0] * ro_ref[0, at, :].astype(F32)
            for r in range(1, ROUNDS):
                mixed = mixed + weights[r] * ro_ref[r, at, :].astype(F32)
            mixed_ref[at, :] = mixed.astype(BF)


def attend_values(v_pieces, tgt, tgt_t, probs, logs):
    rows = 8 * TOK
    return kernel_call(
        values_kernel,
        grid=(ROUNDS,),
        in_specs=[fixed((rows, HEAD_DIM))] * 4
        + [
            per_round((32, TOK)), per_round((TOK, 128)), per_round((PAIRS, 256, 128)),
            per_round((PAIRS, 128)),
        ],
        out_specs=[
            fixed((rows, HEAD_DIM)),
            fixed((ROUNDS, rows, HEAD_DIM)),
            fixed((ROUNDS, rows, HEAD_DIM)),
            per_round((PAIRS, 256, 256)),
        ],
        out_shape=[
            jax.ShapeDtypeStruct((rows, HEAD_DIM), BF),
            jax.ShapeDtypeStruct((ROUNDS, rows, HEAD_DIM), BF),
            jax.ShapeDtypeStruct((ROUNDS, rows, HEAD_DIM), BF),
            jax.ShapeDtypeStruct((ROUNDS, PAIRS, 256, 256), BF),
        ],
        scratch_shapes=[pltpu.VMEM((PAIRS, 2, 64, 256), F32)],
        compiler_params=params(22),
        cost_estimate=cost(14),
        far_in=(6,),
        far_out=(1, 2, 3),
        name="attend_values",
    )(*v_pieces, tgt, tgt_t, probs, logs)


def take_slots(tgt_t_ref, slots_ref, rows_ref, sources):
    for s in range(sources):
        slots = slots_ref[:, :, s * MOST : (s + 1) * MOST, :].reshape(256, HEAD_DIM)
        rows_ref[s * TOK : (s + 1) * TOK, :] += dot(hot_tokens(tgt_t_ref, s), slots.astype(BF))


def values_back_kernel(
    where, tgt_ref, tgt_t_ref, probs_ref, ro_ref, lt_ref, gm_ref, out_ref, gd_ref, gt_ref, gt_slots, slots, rows, token_rows,
):
    this_round = pl.program_id(0)

    @pl.when(this_round == 0)
    def _():
        rows[...] = jnp.zeros_like(rows)

        @pl.loop(0, 8, unroll=2)
        def _(s):
            at = token_block(s)
            weights = round_weights(lt_ref, at)
            grad = gm_ref[at, :].astype(F32)
            agree = [
                jnp.sum(grad * ro_ref[r, at, :].astype(F32), axis=-1, keepdims=True)
                for r in range(ROUNDS)
            ]
            mean = total_of([weights[r] * agree[r] for r in range(ROUNDS)])
            for r in range(ROUNDS):
                token_rows[r, at, :HEAD_DIM] = (weights[r] * grad).astype(BF)
                token_rows[r, at, HEAD_DIM:] = (weights[r] * (agree[r] - mean)).astype(BF)

    @pl.loop(0, 4, unroll=4)
    def _(pair):
        placed = [
            dot(
                hot_slots(tgt_ref, pair * 2 + half),
                token_rows[this_round, token_block(pair * 2 + half), :],
            )
            for half in range(2)
        ]
        both = spread(*placed)
        place(both[..., :HEAD_DIM], gd_ref.at[0], pair)
        place(both[..., HEAD_DIM:], gt_slots, pair)

    @pl.loop(0, PAIRS, unroll=16)
    def _(p):
        grad_values = dot(probs_ref[0, p], diagonal(gd_ref[0, p]))
        slots[p, 0] = grad_values[:, :128]
        slots[p, 1] = grad_values[:, 128:]
        gt_ref[0, pl.ds(p, 1), :] = jnp.sum(
            jnp.where(eye(), gt_slots[p].astype(F32), 0.0), axis=0, keepdims=True
        )

    take_slots(tgt_t_ref, slots, rows, 32)

    @pl.when(this_round == ROUNDS - 1)
    def _():
        for m in range(4):
            out_ref[(where[2] + m) & 3] = rows[m * 8 * TOK : (m + 1) * 8 * TOK, :].astype(BF)


def attend_values_back(where, tgt, tgt_t, probs, ro, lt, gm):
    rows = 8 * TOK
    return kernel_call(
        values_back_kernel,
        grid=(ROUNDS,),
        in_specs=[
            SMEM,
            per_round((32, TOK)),
            per_round((TOK, 128)),
            per_round((PAIRS, 256, 128)),
            fixed((ROUNDS, rows, HEAD_DIM)),
            fixed((ROUNDS, rows, HEAD_DIM)),
            fixed((rows, HEAD_DIM)),
        ],
        out_specs=[
            fixed((4, rows, HEAD_DIM)), per_round((PAIRS, 128, 128)), per_round((PAIRS, 128)),
        ],
        out_shape=[
            jax.ShapeDtypeStruct((4, rows, HEAD_DIM), BF),
            jax.ShapeDtypeStruct((ROUNDS, PAIRS, 128, 128), BF),
            jax.ShapeDtypeStruct((ROUNDS, PAIRS, 128), F32),
        ],
        scratch_shapes=[
            pltpu.VMEM((PAIRS, 128, 128), BF),
            pltpu.VMEM((PAIRS, 2, 256, HEAD_DIM), F32),
            pltpu.VMEM((4 * rows, HEAD_DIM), F32),
            pltpu.VMEM((ROUNDS, rows, 256), BF),
        ],
        compiler_params=params(26),
        cost_estimate=cost(12),
        far_in=(1, 2, 3, 4, 5),
        far_out=(0, 1, 2),
        name="attend_values_back",
    )(where, tgt, tgt_t, probs, ro, lt, gm)


def scores_back_kernel(
    where, tgt_t_ref, mask_ref, probs_ref, values_ref, qm_ref, gd_ref, gt_ref,
    gs_ref, out_ref, slots, rows,
):
    this_round = pl.program_id(0)

    @pl.when(this_round == 0)
    def _():
        rows[...] = jnp.zeros_like(rows)

    @pl.loop(0, PAIRS, unroll=16)
    def _(p):
        probs = probs_ref[0, p].astype(F32)
        grad_probs = dot(values_ref[0, p], diagonal_t(gd_ref[0, p]))
        agreement = jnp.sum(probs * grad_probs, axis=0, keepdims=True)
        grad_scores = probs * (grad_probs + (gt_ref[0, pl.ds(p, 1), :] - agreement))
        seen = mask_ref[0, p].astype(F32) == 0.0
        grad_scores = jnp.where(seen, grad_scores, 0.0).astype(BF)
        gs_ref[0, p] = grad_scores
        grad_keys = dot(grad_scores, diagonal(qm_ref[0, p]))
        slots[p, 0] = grad_keys[:, :128]
        slots[p, 1] = grad_keys[:, 128:]

    take_slots(tgt_t_ref, slots, rows, 32)

    @pl.when(this_round == ROUNDS - 1)
    def _():
        for m in range(4):
            out_ref[(where[2] + m) & 3] = rows[m * 8 * TOK : (m + 1) * 8 * TOK, :].astype(BF)


def attend_scores_back(where, *arrays):
    rows = 8 * TOK
    slots = (PAIRS, 256, 128)
    return kernel_call(
        scores_back_kernel,
        grid=(ROUNDS,),
        in_specs=[SMEM] + [per_round(a.shape[1:]) for a in arrays],
        out_specs=[per_round(slots), fixed((4, rows, HEAD_DIM))],
        out_shape=[
            jax.ShapeDtypeStruct((ROUNDS,) + slots, BF),
            jax.ShapeDtypeStruct((4, rows, HEAD_DIM), BF),
        ],
        scratch_shapes=[
            pltpu.VMEM((PAIRS, 2, 256, HEAD_DIM), F32),
            pltpu.VMEM((4 * rows, HEAD_DIM), F32),
        ],
        compiler_params=params(28),
        cost_estimate=cost(20),
        far_in=tuple(range(1, 8)),
        far_out=(0, 1),
        name="attend_scores_back",
    )(where, *arrays)


def queries_back_kernel(tgt_t_ref, gs_ref, keys_ref, gq_ref, slots):
    @pl.when(pl.program_id(0) == 0)
    def _():
        gq_ref[...] = jnp.zeros_like(gq_ref)

    @pl.loop(0, PAIRS, unroll=16)
    def _(p):
        grad_queries = t_dot(gs_ref[0, p], keys_ref[0, p])
        slots[p, 0] = grad_queries[:64, :128]
        slots[p, 1] = grad_queries[64:, 128:]

    take_slots(tgt_t_ref, slots, gq_ref, 8)


def attend_queries_back(*arrays):
    rows = 8 * TOK
    return kernel_call(
        queries_back_kernel,
        grid=(ROUNDS,),
        in_specs=[per_round(a.shape[1:]) for a in arrays],
        out_specs=[fixed((rows, HEAD_DIM))],
        out_shape=[jax.ShapeDtypeStruct((rows, HEAD_DIM), F32)],
        scratch_shapes=[pltpu.VMEM((PAIRS, 2, 64, HEAD_DIM), F32)],
        compiler_params=params(20),
        cost_estimate=cost(8),
        far_in=(0, 1, 2),
        far_out=(0,),
        name="attend_queries_back",
    )(*arrays)[0]


def local(
    first_in, second_in, attn_gain, attn_shift, w_joint, w_value, w_output, ffn_gain, ffn_shift,
    w_inner, b_inner, w_outer, b_outer, buckets, cot_first, cot_second,
):
    y, z, x, c = (lax.axis_index(a) for a in AXES)
    where = jnp.stack([y, z, x, c]).astype(jnp.int32)
    low_core = c == 0

    def by_core(first, second):
        return jnp.where(low_core, first, second)

    vec = jnp.concatenate(
        [attn_gain, attn_shift, ffn_gain, ffn_shift, b_outer, b_inner, jnp.zeros((56,), BF)]
    ).astype(F32)
    keep_a, give_a, keep_b, give_b = pack(
        where, w_joint, w_value, w_output, w_inner, vec.reshape(1, 128), buckets[:, :, 0]
    )
    tok_near = [send(second_in, "z", 3), send(second_in, "z", 1)]
    got_a, got_b = swap(give_a), swap(give_b)
    gathered = lax.all_gather(
        payload(where, keep_b, got_b, w_outer)[0], CHIPS, axis=0, tiled=False
    ).reshape(64, 80, D)
    y_got = gather(chip_message(where, keep_a, got_a)[0], "y")
    heads_out, second_late, tok_near = sync(
        head_messages(where, *y_got), second_in, tok_near
    )
    z_got = scatter(heads_out, "z")
    tok_last = send(second_late, "z", 2)
    z_got, tok_last = sync(z_got, tok_last)
    tok_far = jnp.stack([tok_near[0], tok_last, tok_near[1]])
    sib_tok = swap(jnp.concatenate([second_in[None], tok_far]))
    tokens = (second_in, tok_far, sib_tok)
    x_got = gather(jnp.concatenate(z_got), "x")
    w_qv, par, tgt, tgt_t, counts = assemble(where, *x_got)
    bias_inner = par[5:9].reshape(4, 64, 2, 8)
    bias_inner = by_core(bias_inner[:, :, 0], bias_inner[:, :, 1])
    bias_inner = jnp.transpose(bias_inner, (1, 2, 0)).reshape(1, 2048)
    bias_inner = jnp.broadcast_to(bias_inner, (8, 2048))

    normed, queries, values = project(where, tokens, par, w_qv)
    q_pieces = gather(queries, "x")
    q_pieces[1], q_pieces[3], values = sync(q_pieces[1], q_pieces[3], values)
    v_near = [send(values, "x", 3), send(values, "x", 1)]
    q_pieces, values, first_late = sync(
        q_pieces, values, jnp.stack([first_in, cot_first, cot_second])
    )
    v_pieces = [values, v_near[0], send(values, "x", 2), v_near[1]]
    sib_rows = swap(first_late)
    mask = make_mask(where, counts)
    probs, key_slots, query_slots, logs = attend_scores(q_pieces, tgt, mask)
    v_pieces, bias_inner = sync(v_pieces, bias_inner)
    mixed_head, round_out, round_total, value_slots = attend_values(
        v_pieces, tgt, tgt_t, probs, logs
    )

    mix_own = jnp.concatenate(
        scatter([mixed_head[k * 256 : (k + 1) * 256] for k in range(4)], "z"), axis=1
    )
    mix_sib = swap(mix_own)
    first_sum, first_out, input_t, active, grad_hidden, back, hid_sum, cot_sum = feed(
        where, mix_own, mix_sib, first_in, cot_second, sib_rows, par, bias_inner, gathered
    )
    a_parts = inner_grads(where, active, grad_hidden, input_t, cot_second, sib_rows)
    back_sib, a_parts = sync(swap(back), a_parts)
    grad_first, branch, g0, g1, g2, g3, norm_sums = first_back(
        where, back, back_sib, first_sum, cot_first, sib_rows, par, gathered
    )
    grad_mixed = scatter([g0, g1, g2, g3], "z")
    a_low, a_high = send(a_parts[2], "y", 1), send(a_parts[3], "y", 3)
    sums = jnp.stack([norm_sums[0], norm_sums[1], cot_sum[0]]).reshape(3, 64, 16)
    sums = jnp.pad(jnp.transpose(sums, (1, 0, 2)), ((0, 0), (0, 0), (0, 16)))
    sums = jnp.concatenate([sums, hid_sum[0].reshape(64, 1, 32)], axis=1).astype(BF)
    sums = jnp.pad(sums, ((0, 0), (0, 12), (0, 96)))
    *b_parts, second_own, second_give = outer_grads(
        where, active, cot_second, sib_rows, mix_own, mix_sib, branch, sums, gathered
    )
    grad_mixed, b_parts, second_give = sync(grad_mixed, b_parts, second_give)

    b_low, b_high = send(b_parts[2], "z", 1), send(b_parts[3], "z", 3)
    second_got = swap(second_give)
    gv, grad_slots, log_slots = attend_values_back(
        where, tgt, tgt_t, probs, round_out, round_total, jnp.concatenate(grad_mixed)
    )
    a_low, a_high, b_low, b_high, second_got, gv, grad_slots = sync(
        a_low, a_high, b_low, b_high, second_got, gv, grad_slots
    )

    a_next, a_last, b_next, b_last = pass_on(
        (a_parts[1], a_low, a_parts[4], a_high), (b_parts[1], b_low, b_parts[4], b_high)
    )
    grad_slots, a_next, b_next = sync(grad_slots, a_next, b_next)
    a_got = [send(a_next, "y", 1), send(a_last, "y", 3)]
    b_got = [send(b_next, "z", 1), send(b_last, "z", 3)]
    gv_got = exchange(gv, "x")
    grad_scores, gk = attend_scores_back(
        where, tgt_t, mask, probs, value_slots, query_slots, grad_slots, log_slots
    )
    gv_got, b_got, gk, grad_scores = sync(gv_got, b_got, gk, grad_scores)

    gk_got = exchange(gk, "x")
    gq = attend_queries_back(tgt_t, grad_scores, key_slots)
    b_parts = recut_b(
        where, *[part.reshape(4, 4, 32, 896) for part in [b_parts[0]] + b_got]
    )
    b_got = [b_parts[0], send(b_parts[1], "y", 1), send(b_parts[3], "y", 3)]
    a_parts = recut_a(
        where, *[part.reshape(4, 4, 16, 3072) for part in [a_parts[0]] + a_got]
    )
    gk_got, a_parts, b_far, b_got, gq = sync(gk_got, a_parts, b_parts[2], b_got, gq)

    a_got = scatter(a_parts, "z")
    b_got = b_got + [send(b_far, "y", 2)]
    back_own, back_give, *w_parts = project_back(
        where, tokens, par, w_qv, normed, queries, gq, gk_got, gv_got
    )

    back_give, w_parts, a_got[1], a_got[3], b_got = sync(
        back_give, w_parts, a_got[1], a_got[3], b_got
    )
    w_got = scatter(w_parts, "y")
    back_chip = (back_own.astype(F32) + swap(back_give).astype(F32)).astype(BF)
    back_parts = [back_chip[k] for k in range(4)]
    back_far = send(back_parts[2], "z", 2)
    back_parts, w_got, a_got, b_got = sync(back_parts, w_got, a_got, b_got)

    second_out = (second_in.astype(F32) + second_own + second_got + par[4]).astype(BF)

    x_parts = scatter(join(where, *w_got, *a_got, *b_got), "x")
    back_sum = [
        back_parts[0], send(back_parts[1], "z", 1), send(back_parts[3], "z", 3), back_far
    ]
    x_parts, back_sum = sync(x_parts, back_sum)

    *z_parts, chip_keep, chip_give, grad_outer, small = divide(where, *x_parts)
    w_got = scatter(z_parts, "z")
    w_keep, last_give = last(where, *w_got, chip_give)
    grad_joint, grad_value, norm, grad_inner, grad_output = finish(
        where, w_keep, chip_keep, swap(last_give)
    )
    grad_attn_gain, grad_attn_shift = norm[:, 0], norm[:, 64]
    mine16 = by_core(small[:3, :8], small[:3, 8:16])
    grad_ffn_gain, grad_ffn_shift, grad_b_outer = mine16[0], mine16[1], mine16[2]
    grad_b_inner = small[3, :32]

    attn_xhat, attn_scale = normalized(second_in.astype(F32))
    attn_back = norm_back(total_of(back_sum) * par[0], attn_xhat, attn_scale)
    grad_second = (cot_second.astype(F32) + attn_back).astype(BF)

    return (
        first_out, second_out, grad_first, grad_second, grad_attn_gain, grad_attn_shift,
        grad_joint, grad_value, grad_output, grad_ffn_gain, grad_ffn_shift, grad_inner,
        grad_b_inner, grad_outer, grad_b_outer,
    )


def solution(mesh):
    chips = Mesh(mesh.devices.reshape(4, 4, 4, 2), AXES)
    rows, flat = P(AXES, None), P(AXES)
    return jax.shard_map(
        local,
        mesh=chips,
        in_specs=(
            rows, rows, flat, flat, rows, rows, rows, flat, flat, rows, flat, rows, flat,
            P(None, AXES, None), rows, rows,
        ),
        out_specs=(
            rows, rows, rows, rows, flat, flat, rows, rows, rows, flat, flat, rows, flat, rows,
            flat,
        ),
        check_vma=False,
    )
```

```python
import functools

import jax
import jax.numpy as jnp
from jax import lax
from jax.experimental import pallas as pl
from jax.experimental.pallas import tpu as pltpu
from jax.sharding import Mesh, PartitionSpec as P

HEADS = 8
HEAD_DIM = 128
ROUNDS = 4
BUCKETS = 32
MOST = 8
TOK = 128
D = 1024
FF = 4096

EPS_NORM = 1e-05
EPS_KEY = 1e-06
SELF_SCORE = -10000.0
MASKED_SCORE = -1000000000.0

BF = jnp.bfloat16
F32 = jnp.float32

AXES = ("y", "z", "x", "c")
CHIPS = ("y", "z", "x")


def send(piece, axis, k):
    return lax.ppermute(piece, axis, [(i, (i + k) % 4) for i in range(4)])


def swap(piece):
    return lax.ppermute(piece, "c", [(0, 1), (1, 0)])


def gather(piece, axis):
    back, front, far = send(piece, axis, 3), send(piece, axis, 1), send(piece, axis, 2)
    return [piece, back, far, front]


def scatter(pieces, axis):
    front, back, far = (
        send(pieces[1], axis, 1),
        send(pieces[3], axis, 3),
        send(pieces[2], axis, 2),
    )
    return [pieces[0], back, far, front]


def sync(*groups):
    return lax.optimization_barrier(groups)


def dot(a, b):
    return jnp.dot(a, b, preferred_element_type=F32)


def dot_t(a, b):
    return lax.dot_general(a, b, (((1,), (1,)), ((), ())), preferred_element_type=F32)


def t_dot(a, b):
    return lax.dot_general(a, b, (((0,), (0,)), ((), ())), preferred_element_type=F32)


def cost(us):
    return pl.CostEstimate(flops=int(us * 0.35e9), bytes_accessed=0, transcendentals=0)


def params(mib):
    return pltpu.CompilerParams(vmem_limit_bytes=mib * 1024 * 1024)


SMEM = pl.BlockSpec(memory_space=pltpu.SMEM)


def kernel_call(kernel, *, out_shape, far_in=(), far_out=(), **rest):
    inner = pl.pallas_call(
        kernel,
        out_shape=[
            pltpu.HBM(o.shape, o.dtype) if at in far_out else o for at, o in enumerate(out_shape)
        ],
        **rest,
    )

    def run(*arrays):
        return inner(
            *[
                pltpu.with_memory_space_constraint(a, pltpu.HBM) if at in far_in else a
                for at, a in enumerate(arrays)
            ]
        )

    return run


def iota(shape, dim):
    return lax.broadcasted_iota(jnp.int32, shape, dim)


def whole_call(kernel, name, outs, us, mib=16, scratch=(), far_in=(), far_out=()):
    def call(where, *arrays):
        return kernel_call(
            kernel,
            grid=(1,),
            in_specs=[SMEM] + [fixed(a.shape) for a in arrays],
            out_specs=[fixed(s) for s, _ in outs],
            out_shape=[jax.ShapeDtypeStruct(s, t) for s, t in outs],
            scratch_shapes=list(scratch),
            compiler_params=params(mib),
            cost_estimate=cost(us),
            far_in=far_in,
            far_out=far_out,
            name=name,
        )(where, *arrays)

    return call


def fixed(shape):
    return pl.BlockSpec(shape, lambda r: (0,) * len(shape))


def per_round(shape):
    return pl.BlockSpec((1,) + shape, lambda r: (r,) + (0,) * len(shape))


PAIRS = BUCKETS // 2


def exchange(stacked, axis):
    return lax.all_to_all(stacked, axis, split_axis=0, concat_axis=0, tiled=True)


def total_of(parts):
    total = parts[0].astype(F32)
    for extra in parts[1:]:
        total = total + extra.astype(F32)
    return total


def pack_kernel(
    where, joint_ref, value_ref, output_ref, inner_ref, vec_ref, bucket_ref,
    keep_a, give_a, keep_b, give_b,
):
    low_core = where[3] == 0
    joint, value = joint_ref[...].astype(F32), value_ref[...].astype(F32)
    inner_rows = inner_ref[...].astype(F32)
    heads = []
    for core in range(2):
        rows = []
        for h in range(4):
            cols = slice((core * 4 + h) * 128, (core * 4 + h + 1) * 128)
            rows += [joint[:, cols], value[:, cols]]
        heads.append(jnp.concatenate(rows, axis=0))

    sub, along = iota((128, 128), 0), iota((128, 128), 1)
    targets, counts = [], []
    for r in range(ROUNDS):
        chosen = jnp.broadcast_to(bucket_ref[r : r + 1, :].astype(F32), (128, 128))
        column = jnp.sum(jnp.where(sub == along, chosen, 0.0), axis=1, keepdims=True)
        earlier = (column == chosen) & (sub < along)
        rank = jnp.sum(earlier.astype(F32), axis=0, keepdims=True)
        targets.append(chosen[0:1] * MOST + rank)
        counts.append(jnp.sum((column == along.astype(F32)).astype(F32), axis=0, keepdims=True))
    vec = jnp.concatenate([vec_ref[...], jnp.zeros((7, 128), F32)], axis=0)
    aux = jnp.concatenate([vec] + targets + counts, axis=0)
    keep_a[...] = jnp.concatenate([jnp.where(low_core, *heads), aux], axis=0).astype(BF)
    give_a[...] = jnp.concatenate([jnp.where(low_core, *heads[::-1]), aux], axis=0).astype(BF)

    chunks = [inner_rows[:, t * 256 : (t + 1) * 256] for t in range(16)]
    src, dst = iota((256, 256), 0), iota((256, 256), 1)
    wanted = 64 * ((dst % 128) // 32) + 32 * (dst // 128) + dst % 32
    picked = dot(jnp.concatenate(chunks, axis=0).astype(BF), (src == wanted).astype(F32).astype(BF))
    inner = []
    for core in range(2):
        halves = [
            jnp.concatenate(
                [
                    picked[t * 8 : (t + 1) * 8, core * 128 : (core + 1) * 128]
                    for t in range(half * 8, half * 8 + 8)
                ],
                axis=1,
            )
            for half in range(2)
        ]
        inner.append(jnp.concatenate(halves, axis=0))
    rest = jnp.concatenate([output_ref[...].astype(F32), jnp.zeros((8, D), F32)], axis=0)
    keep_b[...] = jnp.concatenate([jnp.where(low_core, *inner), rest], axis=0).astype(BF)
    give_b[...] = jnp.concatenate([jnp.where(low_core, *inner[::-1]), rest], axis=0).astype(BF)


pack = whole_call(
    pack_kernel, "pack", [((80, 128), BF)] * 2 + [((32, D), BF)] * 2, 3, far_in=(1, 2, 3, 4, 6)
)


def chip_message_kernel(where, keep_ref, got_ref, out_ref):
    low_core = where[3] == 0
    keep, got = keep_ref[...].astype(F32), got_ref[...].astype(F32)
    first, second = jnp.where(low_core, keep, got), jnp.where(low_core, got, keep)
    rows = []
    for at in (0, 16, 32, 48, 8, 24, 40, 56, 64, 72):
        rows += [first[at : at + 8], second[at : at + 8]]
    out_ref[...] = jnp.concatenate(rows, axis=0).astype(BF)


chip_message = whole_call(chip_message_kernel, "chip_message", [((160, 128), BF)], 1)


def head_messages_kernel(where, y0, y1, y2, y3, *outs):
    pieces = (y0, y1, y2, y3)
    vec = []
    for piece in pieces:
        rows = piece[128:144, :].astype(F32)
        vec += [rows[0:1], rows[8:9]]
    vec = jnp.concatenate(vec + [jnp.zeros((8, 128), F32)], axis=0).astype(BF)
    for k in range(4):
        head = (where[1] + k) & 3
        q_rows = pl.ds(pl.multiple_of(head * 16, 16), 16)
        v_rows = pl.ds(pl.multiple_of(64 + head * 16, 16), 16)
        for n, piece in enumerate(pieces):
            outs[k][n * 16 : n * 16 + 16, :] = piece[q_rows, :]
            outs[k][96 + n * 16 : 112 + n * 16, :] = piece[v_rows, :]
        outs[k][64:80, :] = vec
        outs[k][80:96, :] = y0[144:160, :]


head_messages = whole_call(
    head_messages_kernel, "head_messages", [((160, 128), BF)] * 4, 1
)


def payload_kernel(where, keep_ref, got_ref, outer_ref, out_ref):
    low_core = where[3] == 0
    keep, got = keep_ref[...].astype(F32), got_ref[...].astype(F32)
    first, second = jnp.where(low_core, keep, got), jnp.where(low_core, got, keep)
    for at, to in ((0, 0), (8, 16), (16, 64)):
        out_ref[to : to + 16, :] = jnp.concatenate(
            [first[at : at + 8], second[at : at + 8]], axis=0
        ).astype(BF)
    out_ref[32:64, :] = outer_ref[...]


payload = whole_call(payload_kernel, "payload", [((80, D), BF)], 1)


def by_rows(where, pieces, ref):
    for m, rows in enumerate(pieces):
        for n in range(4):
            for k in range(4):
                chip = ((where[0] + n) % 4 * 4 + (where[1] + k) % 4) * 4 + (where[2] + m) % 4
                ref[pl.ds(pl.multiple_of(chip * 16, 16), 16), :] = rows(k, n)


def device_of(where, shape):
    row = iota(shape, 0)
    x, z, y = (where[2] + (row >> 5)) & 3, (where[1] + (row >> 3)) & 3, (where[0] + (row >> 1)) & 3
    return ((y * 4 + z) * 4 + x) * 2 + (row & 1)


def parameter(where, vec, v):
    shape = (128, D)
    lane = iota(shape, 1)
    picked = dot(vec, (iota(shape, 0) == 8 * v + (lane & 7)).astype(F32).astype(BF))
    mine = device_of(where, shape) == (lane >> 3)
    return jnp.sum(jnp.where(mine, picked, 0.0), axis=0, keepdims=True)


def assemble_kernel(where, x0, x1, x2, x3, w_ref, par_ref, tgt_ref, tgt_t_ref, count_ref, vec_ref):
    pieces = (x0, x1, x2, x3)
    by_rows(
        where,
        [
            lambda k, n, piece=piece: piece[k * 160 + n * 16 : k * 160 + n * 16 + 16, :]
            for piece in pieces
        ],
        w_ref,
    )
    vec = jnp.concatenate(
        [
            piece[k * 160 + 64 : k * 160 + 80, :].astype(F32)[:8]
            for piece in pieces
            for k in range(4)
        ],
        axis=0,
    ).astype(BF)
    vec_ref[...] = vec
    par_ref[...] = jnp.concatenate(
        [parameter(where, vec, 0), parameter(where, vec, 1), jnp.zeros((6, D), F32)], axis=0
    )
    empty = jnp.zeros((96, 128), F32)
    slots = [
        jnp.concatenate(
            [piece[k * 160 + 80 : k * 160 + 96, :] for k in range(4)], axis=0
        ).astype(F32)
        for piece in pieces
    ]
    for r in range(ROUNDS):
        rows = jnp.concatenate(
            [slots[m][s * 8 + r : s * 8 + r + 1] for m in range(4) for s in range(8)], axis=0
        )
        tgt_ref[r] = rows.astype(jnp.int32)
        tgt_t_ref[r] = jnp.transpose(jnp.concatenate([rows, empty], axis=0)).astype(jnp.int32)
        count_ref[r] = jnp.concatenate(
            [slots[m][s * 8 + 4 + r : s * 8 + 5 + r] for m in range(4) for s in range(8)], axis=0
        )


assemble = whole_call(
    assemble_kernel, "assemble",
    [
        ((D, 128), BF), ((8, D), F32), ((ROUNDS, 32, 128), jnp.int32),
        ((ROUNDS, 128, 128), jnp.int32), ((ROUNDS, 32, 128), F32), ((128, 128), BF),
    ],
    2, far_out=(2, 3),
)


def mask_kernel(where, count_ref, vec_ref, mask_ref, par_ref, bias_ref):
    z, x, c = where[1], where[2], where[3]

    @pl.when(pl.program_id(0) == 0)
    def _():
        vec = vec_ref[...]
        par_ref[...] = jnp.concatenate(
            [parameter(where, vec, v) for v in (2, 3, 4)] + [jnp.zeros((5, D), F32)], axis=0
        )
        wide = (128, 2048)
        lane = iota(wide, 1)
        picked = dot(vec, (iota(wide, 0) == 40 + (lane & 31)).astype(F32).astype(BF))
        mine = device_of(where, wide) == 2 * (lane >> 5) + c
        bias = jnp.sum(jnp.where(mine, picked, 0.0), axis=0, keepdims=True)
        bias_ref[...] = jnp.broadcast_to(bias, (8, 2048))

    shape = (256, 128)
    row, lane = iota(shape, 0), iota(shape, 1)
    source, rank = row >> 3, row & 7
    of_chip = lambda z_of, x_of, core: ((z_of & 3) * 8 + (x_of & 3) * 2 + core) * 8
    kpos = of_chip(z + ((source >> 1) & 3), x + (source >> 3), source & 1) + rank
    asker = (lane >> 3) & 7
    qpos = of_chip(z + (asker >> 1), x, asker & 1) + (lane & 7)
    code = jnp.where(kpos == qpos, -1.0, jnp.where(kpos < qpos, 0.0, -1e5))
    rank_f = rank.astype(F32)
    expand = (iota((256, 32), 0) >> 3) == iota((256, 32), 1)
    by_slot = dot(expand.astype(F32).astype(BF), count_ref[0].astype(BF)).astype(BF)
    bucket, side = iota((128, 128), 0), iota((128, 128), 1) >> 6

    @pl.loop(0, PAIRS, unroll=4)
    def _(p):
        select = (bucket == 2 * p + side).astype(F32).astype(BF)
        live = rank_f < dot(by_slot, select)
        mask_ref[0, p] = jnp.where(live, code, -1e5).astype(BF)


def make_mask(where, counts, vec):
    return kernel_call(
        mask_kernel,
        grid=(ROUNDS,),
        in_specs=[SMEM, per_round((32, 128)), fixed((128, 128))],
        out_specs=[per_round((PAIRS, 256, 128)), fixed((8, D)), fixed((8, 2048))],
        out_shape=[
            jax.ShapeDtypeStruct((ROUNDS, PAIRS, 256, 128), BF),
            jax.ShapeDtypeStruct((8, D), F32),
            jax.ShapeDtypeStruct((8, 2048), F32),
        ],
        far_out=(0,),
        compiler_params=params(16),
        cost_estimate=cost(7),
        name="make_mask",
    )(where, counts, vec)


def chip_rows(where, own, sib):
    low_core = where[3] == 0
    return jnp.concatenate([jnp.where(low_core, own, sib), jnp.where(low_core, sib, own)], axis=0)


def token_rows(where, own0, own3, sib):
    near = pl.program_id(0) == 0
    own = jnp.where(near, own0[...].astype(F32), own3[0].astype(F32))
    return chip_rows(where, own, sib[0].astype(F32))


def token_specs():
    return [
        pl.BlockSpec((TOK, D), lambda i: (0, 0)),
        pl.BlockSpec((1, TOK, D), lambda i: (jnp.maximum(i - 1, 0), 0, 0)),
        pl.BlockSpec((1, TOK, D), lambda i: (i, 0, 0)),
    ]


def project_kernel(where, own0, own3, sib, par_ref, w_ref, normed_ref, q_ref):
    rows = token_rows(where, own0, own3, sib)
    centered = rows - jnp.mean(rows, axis=-1, keepdims=True)
    spread = jnp.mean(centered * centered, axis=-1, keepdims=True)
    normed = centered * lax.rsqrt(spread + EPS_NORM) * par_ref[0:1, :] + par_ref[1:2, :]
    normed = normed.astype(BF)
    normed_ref[...] = normed
    q_ref[...] = dot(normed, w_ref[...]).astype(BF)


def project(where, tokens, par, w):
    whole = lambda i: (0, 0)
    return kernel_call(
        project_kernel,
        grid=(4,),
        in_specs=[SMEM] + token_specs()
        + [pl.BlockSpec((8, D), whole), pl.BlockSpec((D, HEAD_DIM), whole)],
        out_specs=[
            pl.BlockSpec((2 * TOK, D), lambda i: (i, 0)),
            pl.BlockSpec((2 * TOK, HEAD_DIM), lambda i: (i, 0)),
        ],
        out_shape=[
            jax.ShapeDtypeStruct((8 * TOK, D), BF),
            jax.ShapeDtypeStruct((8 * TOK, HEAD_DIM), BF),
        ],
        compiler_params=params(20),
        cost_estimate=cost(4),
        far_out=(0,),
        name="project",
    )(where, *tokens, par, w)


def project_values_kernel(where, x0, x1, x2, x3, normed_ref, v_ref, w_ref):
    @pl.when(pl.program_id(0) == 0)
    def _():
        by_rows(
            where,
            [
                lambda k, n, piece=piece: piece[k * 160 + n * 16 + 96 : k * 160 + n * 16 + 112, :]
                for piece in (x0, x1, x2, x3)
            ],
            w_ref,
        )

    v_ref[...] = dot(normed_ref[...], w_ref[...]).astype(BF)


def project_values(where, pieces, normed):
    return kernel_call(
        project_values_kernel,
        grid=(4,),
        in_specs=[SMEM] + [fixed(p.shape) for p in pieces]
        + [pl.BlockSpec((2 * TOK, D), lambda i: (i, 0))],
        out_specs=[
            pl.BlockSpec((2 * TOK, HEAD_DIM), lambda i: (i, 0)), fixed((D, HEAD_DIM)),
        ],
        out_shape=[
            jax.ShapeDtypeStruct((8 * TOK, HEAD_DIM), BF),
            jax.ShapeDtypeStruct((D, HEAD_DIM), BF),
        ],
        compiler_params=params(16),
        cost_estimate=cost(3),
        far_in=(5,),
        name="project_values",
    )(where, *pieces, normed)


def project_back_kernel(
    where, own0, own3, sib, wq_ref, wv_ref, normed_ref, q_ref, gq_ref,
    gk_ref, gv_ref, own_out, sib_out, wg0, wg1, wg2, wg3, total, sums,
):
    step = pl.program_id(0)
    x = token_rows(where, own0, own3, sib)
    q = q_ref[...].astype(F32)
    inv = lax.rsqrt(jnp.sum(q * q, axis=-1, keepdims=True) + EPS_KEY)
    gk = total_of([gk_ref[m] for m in range(4)])
    gv = total_of([gv_ref[m] for m in range(4)])
    along = jnp.sum(q * gk, axis=-1, keepdims=True)
    gq = gq_ref[...] + gk * inv - q * (inv * inv * inv * along)
    rows = jnp.concatenate([gq.astype(BF), gv.astype(BF)], axis=1)
    back = dot_t(rows[:, :HEAD_DIM], wq_ref[...]) + dot_t(rows[:, HEAD_DIM:], wv_ref[...])

    low_core = where[3] == 0
    own_out[0] = jnp.where(low_core, back[:TOK], back[TOK:]).astype(BF)
    sib_out[0] = jnp.where(low_core, back[TOK:], back[:TOK]).astype(BF)
    centered = x - jnp.mean(x, axis=-1, keepdims=True)
    spread = jnp.mean(centered * centered, axis=-1, keepdims=True)
    xhat = centered * lax.rsqrt(spread + EPS_NORM)
    gain_part = jnp.sum((back * xhat).reshape(TOK // 4, 8, D), axis=0)
    shift_part = jnp.sum(back.reshape(TOK // 4, 8, D), axis=0)
    weight_part = t_dot(normed_ref[...], rows)

    @pl.when(step == 0)
    def _():
        total[:, :256] = weight_part
        sums[0:8, :] = gain_part
        sums[8:16, :] = shift_part

    @pl.when(step > 0)
    def _():
        total[:, :256] += weight_part
        sums[0:8, :] += gain_part
        sums[8:16, :] += shift_part

    @pl.when(step == 3)
    def _():
        gain_sum = jnp.sum(sums[0:8, :], axis=0, keepdims=True)
        shift_sum = jnp.sum(sums[8:16, :], axis=0, keepdims=True)
        both = jnp.where(iota((HEAD_DIM, D), 0) < 64, gain_sum, shift_sum)
        total[:, 256:] = jnp.transpose(both)
        for k, out in enumerate((wg0, wg1, wg2, wg3)):
            rows = pl.ds(pl.multiple_of(((where[0] + k) & 3) * 256, 256), 256)
            out[...] = total[rows, :].astype(BF)


def project_back(where, tokens, wq, wv, normed, q, gq, gk, gv):
    token_block = pl.BlockSpec((1, TOK, D), lambda i: (i, 0, 0))
    whole = lambda i: (0, 0)
    row_block = lambda width: pl.BlockSpec((2 * TOK, width), lambda i: (i, 0))
    return kernel_call(
        project_back_kernel,
        grid=(4,),
        in_specs=[SMEM] + token_specs()
        + [
            pl.BlockSpec((D, HEAD_DIM), whole),
            pl.BlockSpec((D, HEAD_DIM), whole),
            row_block(D),
            row_block(HEAD_DIM),
            row_block(HEAD_DIM),
        ]
        + [pl.BlockSpec((4, 2 * TOK, HEAD_DIM), lambda i: (0, i, 0))] * 2,
        out_specs=[token_block, token_block] + [pl.BlockSpec((256, 384), whole)] * 4,
        out_shape=[
            jax.ShapeDtypeStruct((4, TOK, D), BF),
            jax.ShapeDtypeStruct((4, TOK, D), BF),
        ]
        + [jax.ShapeDtypeStruct((256, 384), BF)] * 4,
        scratch_shapes=[pltpu.VMEM((D, 384), F32), pltpu.VMEM((16, D), F32)],
        compiler_params=params(30),
        cost_estimate=cost(8),
        far_in=(2, 3, 4, 5, 6, 7, 8),
        far_out=(0, 1, 2, 3, 4, 5),
        name="project_back",
    )(where, *tokens, wq, wv, normed, q, gq, gk, gv)


def normalized(values):
    centered = values - jnp.mean(values, axis=-1, keepdims=True)
    spread = jnp.mean(centered * centered, axis=-1, keepdims=True)
    scale = lax.rsqrt(spread + EPS_NORM)
    return centered * scale, scale


def norm_back(u, xhat, scale):
    mean_u = jnp.mean(u, axis=-1, keepdims=True)
    mean_ux = jnp.mean(u * xhat, axis=-1, keepdims=True)
    return (u - mean_u - xhat * mean_ux) * scale


def head_rows(w_ref, head):
    return w_ref[pl.ds(head * 8, 8)].reshape(HEAD_DIM, D)


def heads_of(where):
    for side in range(2):
        core = where[3] if side == 0 else 1 - where[3]
        for m in range(4):
            yield side, m, core * 4 + (where[1] + m) % 4


GELU_IN = 0.7978845608028654
GELU_CUBE = 0.044715


def feed_kernel(
    where, mix_own, mix_sib, first_own, first_sib, cot_own, cot_sib, par_ref, bias_ref,
    out_w, inner_ref, outer_ref,
    sum_ref, first_out, input_t_ref, active_ref, grad_ref, back_ref, hid_sum_ref, cot_sum_ref,
    ffn_in, cot_t, back_t,
):
    step = pl.program_id(0)

    @pl.when(step == 0)
    def _():
        total = chip_rows(where, first_own[...].astype(F32), first_sib[0].astype(F32))
        mixes = (mix_own, mix_sib)
        for side, m, head in heads_of(where):
            total = total + dot(mixes[side][:, m * 128 : m * 128 + 128], head_rows(out_w, head))
        sum_ref[...] = total
        own = jnp.where(where[3] == 0, total[:TOK], total[TOK:])
        first_out[...] = own.astype(BF)
        xhat, _ = normalized(total)
        rows = xhat * par_ref[0:1, :] + par_ref[1:2, :]
        ffn_in[...] = rows.astype(BF)
        input_t_ref[...] = jnp.transpose(rows).astype(BF)
        cot = chip_rows(where, cot_own[...].astype(F32), cot_sib[0].astype(F32))
        cot_t[...] = jnp.transpose(cot).astype(BF)
        cot_sum_ref[...] = jnp.broadcast_to(jnp.sum(cot, axis=0, keepdims=True), (8, D))

    inner = inner_ref[...].reshape(D, 512)
    outer = outer_ref[...].reshape(512, D)
    hidden = dot(ffn_in[...], inner) + bias_ref[0:1, :]
    square = hidden * hidden
    bent = jnp.tanh(GELU_IN * hidden * (1.0 + GELU_CUBE * square))
    half = 0.5 * (1.0 + bent)
    active_ref[...] = (hidden * half).astype(BF)
    slope = half + 0.5 * hidden * (1.0 - bent * bent) * GELU_IN * (
        1.0 + 3.0 * GELU_CUBE * square
    )
    grad_active = jnp.transpose(dot(outer, cot_t[...]))
    grad = (grad_active * slope).astype(BF)
    grad_ref[...] = grad
    hid_sum_ref[...] = jnp.broadcast_to(
        jnp.sum(grad.astype(F32), axis=0, keepdims=True), (8, 512)
    )
    part = dot(inner, jnp.transpose(grad))

    @pl.when(step == 0)
    def _():
        back_t[...] = part

    @pl.when(step > 0)
    def _():
        back_t[...] += part

    @pl.when(step == 3)
    def _():
        back_ref[...] = jnp.transpose(back_t[...])


def feed(where, mix_own, mix_sib, first_in, cot_second, sib_rows, par, bias, gathered):
    whole = lambda i: (0, 0)
    two = 2 * TOK
    return kernel_call(
        feed_kernel,
        grid=(4,),
        in_specs=[
            SMEM,
            pl.BlockSpec((two, 512), whole),
            pl.BlockSpec((two, 512), whole),
            pl.BlockSpec((TOK, D), whole),
            pl.BlockSpec((1, TOK, D), lambda i: (0, 0, 0)),
            pl.BlockSpec((TOK, D), whole),
            pl.BlockSpec((1, TOK, D), lambda i: (2, 0, 0)),
            pl.BlockSpec((8, D), whole),
            pl.BlockSpec((8, 512), lambda i: (0, i)),
            pl.BlockSpec((64, 16, D), lambda i: (0, 4, 0)),
            pl.BlockSpec((64, 16, 512), lambda i: (0, i // 2, i % 2)),
            pl.BlockSpec((16, 32, D), lambda i: (i, 1, 0)),
        ],
        out_specs=[
            pl.BlockSpec((two, D), whole),
            pl.BlockSpec((TOK, D), whole),
            pl.BlockSpec((D, two), whole),
            pl.BlockSpec((two, 512), lambda i: (0, i)),
            pl.BlockSpec((two, 512), lambda i: (0, i)),
            pl.BlockSpec((two, D), whole),
            pl.BlockSpec((8, 512), lambda i: (0, i)),
            pl.BlockSpec((8, D), whole),
        ],
        out_shape=[
            jax.ShapeDtypeStruct((two, D), F32),
            jax.ShapeDtypeStruct((TOK, D), BF),
            jax.ShapeDtypeStruct((D, two), BF),
            jax.ShapeDtypeStruct((two, 2048), BF),
            jax.ShapeDtypeStruct((two, 2048), BF),
            jax.ShapeDtypeStruct((two, D), F32),
            jax.ShapeDtypeStruct((8, 2048), F32),
            jax.ShapeDtypeStruct((8, D), F32),
        ],
        scratch_shapes=[
            pltpu.VMEM((two, D), BF),
            pltpu.VMEM((D, two), BF),
            pltpu.VMEM((D, two), F32),
        ],
        compiler_params=params(32),
        cost_estimate=cost(16),
        far_in=(2, 4, 6, 9, 10, 11),
        far_out=(0, 2, 3, 4, 5),
        name="feed",
    )(
        where, mix_own, mix_sib, first_in, sib_rows, cot_second, sib_rows, par, bias,
        gathered, gathered, gathered,
    )


def first_back_kernel(
    where, back_own, back_sib, sum_ref, cot_own, cot_sib, par_ref, out_w,
    grad_first, branch_ref, m0, m1, m2, m3, sums_ref,
):
    back = back_own[...] + back_sib[...]
    xhat, scale = normalized(sum_ref[...])
    total = chip_rows(where, cot_own[...].astype(F32), cot_sib[0].astype(F32))
    total = total + norm_back(back * par_ref[0:1, :], xhat, scale)
    branch = total.astype(BF)
    branch_ref[...] = branch
    grad_first[...] = jnp.where(where[3] == 0, total[:TOK], total[TOK:]).astype(BF)
    outs = (m0, m1, m2, m3)
    for side, m, head in heads_of(where):
        if side == 0:
            outs[m][...] = dot_t(branch, head_rows(out_w, head)).astype(BF)
    gain = jnp.sum(back * xhat, axis=0, keepdims=True)
    shift = jnp.sum(back, axis=0, keepdims=True)
    sums_ref[...] = jnp.concatenate([gain, shift, jnp.zeros((6, D), F32)], axis=0)


def first_back(where, back_own, back_sib, first_sum, cot_first, sib_rows, par, gathered):
    two = 2 * TOK
    one = lambda shape: pl.BlockSpec(shape, lambda i: (0,) * len(shape))
    return kernel_call(
        first_back_kernel,
        grid=(1,),
        in_specs=[
            SMEM, one((two, D)), one((two, D)), one((two, D)), one((TOK, D)),
            pl.BlockSpec((1, TOK, D), lambda i: (1, 0, 0)),
            one((8, D)),
            pl.BlockSpec((64, 16, D), lambda i: (0, 4, 0)),
        ],
        out_specs=[one((TOK, D)), one((two, D))] + [one((two, 128))] * 4 + [one((8, D))],
        out_shape=[jax.ShapeDtypeStruct((TOK, D), BF), jax.ShapeDtypeStruct((two, D), BF)]
        + [jax.ShapeDtypeStruct((two, 128), BF)] * 4
        + [jax.ShapeDtypeStruct((8, D), F32)],
        compiler_params=params(24),
        cost_estimate=cost(6),
        far_in=(1, 2, 3, 5, 7),
        far_out=(1, 2, 3, 4, 5),
        name="first_back",
    )(where, back_own, back_sib, first_sum, cot_first, sib_rows, par, gathered)


def inner_grads_kernel(where, active_ref, grad_ref, input_t, cot_own, cot_sib, a0, a1, a2, a3, cot):
    step = pl.program_id(0)

    @pl.when(step == 0)
    def _():
        cot[...] = chip_rows(
            where, cot_own[:, :256].astype(F32), cot_sib[0, :, :256].astype(F32)
        ).astype(BF)

    lanes = pl.ds(pl.multiple_of(step * 512, 512), 512)
    outs = (a0, a1, a2, a3)
    inner = dot(input_t[...], grad_ref[...]).astype(BF).reshape(4, 16, 16, 512)
    outer = t_dot(active_ref[...], cot[...]).astype(BF).reshape(16, 32, 256)
    for k, out in enumerate(outs):
        for y in range(4):

            @pl.when(((y - where[0]) & 3) == k)
            def _(out=out, y=y):
                out[:, :, lanes] = inner[y]

        @pl.when(((step - where[0]) & 3) == k)
        def _(out=out):
            out[:, :, 2048:2304] = outer[:, :16]
            out[:, :, 2304:] = outer[:, 16:]


def inner_grads(where, active, grad, input_t, cot_second, sib_rows):
    two = 2 * TOK
    whole = lambda i: (0, 0)
    return kernel_call(
        inner_grads_kernel,
        grid=(4,),
        in_specs=[
            SMEM,
            pl.BlockSpec((two, 512), lambda i: (0, i)),
            pl.BlockSpec((two, 512), lambda i: (0, i)),
            pl.BlockSpec((D, two), whole),
            pl.BlockSpec((TOK, D), whole),
            pl.BlockSpec((1, TOK, D), lambda i: (2, 0, 0)),
        ],
        out_specs=[pl.BlockSpec((16, 16, 2560), lambda i: (0, 0, 0))] * 4,
        out_shape=[jax.ShapeDtypeStruct((16, 16, 2560), BF)] * 4,
        scratch_shapes=[pltpu.VMEM((two, 256), BF)],
        compiler_params=params(32),
        cost_estimate=cost(9),
        far_in=(1, 2, 3, 5),
        far_out=(0, 1, 2, 3),
        name="inner_grads",
    )(where, active, grad, input_t, cot_second, sib_rows)


def outer_grads_kernel(
    where, active_ref, cot_own, cot_sib, mix_own, mix_sib, branch_ref, sums_ref, outer_ref,
    b0, b1, b2, b3, own_ref, give_ref, cot, total,
):
    step = pl.program_id(0)
    outs = (b0, b1, b2, b3)

    @pl.when(step == 0)
    def _():
        cot[...] = chip_rows(
            where, cot_own[:, 256:].astype(F32), cot_sib[0, :, 256:].astype(F32)
        ).astype(BF)
        total[...] = jnp.zeros_like(total)
        cols = jnp.where(
            where[3] == 0, branch_ref[:, :512].astype(F32), branch_ref[:, 512:].astype(F32)
        ).astype(BF)
        mixes = (mix_own, mix_sib)
        for side, m, head in heads_of(where):
            rows = t_dot(mixes[side][:, m * 128 : m * 128 + 128], cols).astype(BF)
            rows = rows.reshape(2, 4, 16, 512)
            at = pl.ds((head >> 1) * 4, 4)
            for part in range(2):
                near = (2 * (head & 1) + part - where[1]) & 3
                for k, out in enumerate(outs):

                    @pl.when(near == k)
                    def _(part=part, out=out, rows=rows, at=at):
                        out[at, 0:16, :256] = rows[part, :, :, :256]
                        out[at, 16:32, :256] = rows[part, :, :, 256:]

        for k, out in enumerate(outs):
            near = (where[1] + k) & 3
            for y in range(4):
                out[y * 4 : y * 4 + 4, 0:16, 256:384] = sums_ref[pl.ds(y * 16 + near * 4, 4)]
                out[y * 4 : y * 4 + 4, 16:32, 256:384] = jnp.zeros((4, 16, 128), BF)

    active = active_ref[...]
    total[...] += dot(active, outer_ref[...].reshape(512, D))
    outer = t_dot(active, cot[...]).astype(BF).reshape(4, 4, 32, 768)
    for z in range(4):
        for k, out in enumerate(outs):

            @pl.when(((z - where[1]) & 3) == k)
            def _(z=z, out=out):
                out[pl.ds(step * 4, 4), :, 384:] = outer[z]

    @pl.when(step == 3)
    def _():
        low_core = where[3] == 0
        own_ref[...] = jnp.where(low_core, total[:TOK], total[TOK:])
        give_ref[...] = jnp.where(low_core, total[TOK:], total[:TOK])


def outer_grads(where, active, cot_second, sib_rows, mix_own, mix_sib, branch, sums, gathered):
    two = 2 * TOK
    whole = lambda i: (0, 0)
    whole3 = lambda i: (0, 0, 0)
    return kernel_call(
        outer_grads_kernel,
        grid=(4,),
        in_specs=[
            SMEM,
            pl.BlockSpec((two, 512), lambda i: (0, i)),
            pl.BlockSpec((TOK, D), whole),
            pl.BlockSpec((1, TOK, D), lambda i: (2, 0, 0)),
            pl.BlockSpec((two, 512), whole),
            pl.BlockSpec((two, 512), whole),
            pl.BlockSpec((two, D), whole),
            pl.BlockSpec((64, 16, 128), whole3),
            pl.BlockSpec((16, 32, D), lambda i: (i, 1, 0)),
        ],
        out_specs=[pl.BlockSpec((16, 32, 1152), whole3)] * 4
        + [pl.BlockSpec((TOK, D), whole)] * 2,
        out_shape=[jax.ShapeDtypeStruct((16, 32, 1152), BF)] * 4
        + [jax.ShapeDtypeStruct((TOK, D), F32)] * 2,
        scratch_shapes=[
            pltpu.VMEM((two, 768), BF), pltpu.VMEM((two, D), F32),
        ],
        compiler_params=params(32),
        cost_estimate=cost(10),
        far_in=(1, 3, 5, 6, 8),
        far_out=tuple(range(6)),
        name="outer_grads",
    )(where, active, cot_second, sib_rows, mix_own, mix_sib, branch, sums, gathered)


def recut_kernel(axis, where, *refs):
    parts, outs = refs[:4], refs[4:]
    for k, out in enumerate(outs):
        mine = (where[axis] + k) & 3
        out[...] = total_of([part[mine] for part in parts]).astype(BF)


recut_a = whole_call(
    functools.partial(recut_kernel, 1), "recut_a", [((4, 16, 2560), BF)] * 4, 4, mib=32,
    far_in=(1,), far_out=(0, 1, 2, 3),
)
recut_b = whole_call(
    functools.partial(recut_kernel, 0), "recut_b", [((4, 32, 1152), BF)] * 4, 3, mib=24,
    far_in=(1,), far_out=(0, 1, 2, 3),
)


def join_kernel(where, *refs):
    w, a, b, outs = refs[:4], refs[4:8], refs[8:12], refs[12:]
    for k, out in enumerate(outs):
        x = (where[2] + k) & 3
        for z in range(4):
            rows = pl.ds(pl.multiple_of(z * 64 + x * 16, 16), 16)
            total = total_of([part[rows, :] for part in w]).astype(BF)
            for j in range(3):
                at = (z * 3 + j) * 16
                out[at : at + 16, :] = total[:, j * 128 : j * 128 + 128]
        total = total_of([part[x] for part in a]).astype(BF)
        for j in range(20):
            out[192 + j * 16 : 208 + j * 16, :] = total[:, j * 128 : j * 128 + 128]
        total = total_of([part[x] for part in b]).astype(BF)
        for j in range(9):
            out[512 + j * 32 : 544 + j * 32, :] = total[:, j * 128 : j * 128 + 128]


join = whole_call(join_kernel, "join", [((800, 128), BF)] * 4, 3)


def divide_kernel(where, x0, x1, x2, x3, w0, w1, w2, w3, keep_ref, give_ref, outer_ref, small_ref, total):
    low_core = where[3] == 0
    total[...] = total_of([part[...] for part in (x0, x1, x2, x3)])
    for k, out in enumerate((w0, w1, w2, w3)):
        z = (where[1] + k) & 3
        for j in range(3):
            rows = pl.ds(pl.multiple_of((z * 3 + j) * 16, 16), 16)
            out[:, j * 128 : j * 128 + 128] = total[rows, :].astype(BF)
    blocks = [total[192 + j * 16 : 208 + j * 16, :] for j in range(16)]
    for at in (512, 528):
        blocks += [total[at : at + 16, :], total[at + 32 : at + 48, :]]
    low = jnp.concatenate([block[:8] for block in blocks], axis=0)
    high = jnp.concatenate([block[8:] for block in blocks], axis=0)
    keep_ref[...] = jnp.where(low_core, low, high)
    give_ref[...] = jnp.where(low_core, high, low).astype(BF)
    for j in range(2):
        lanes = slice(j * 128, j * 128 + 128)
        outer_ref[:16, lanes] = total[448 + j * 16 : 464 + j * 16, :]
        outer_ref[16:, lanes] = total[480 + j * 16 : 496 + j * 16, :]
    for j in range(6):
        lanes = slice(256 + j * 128, 384 + j * 128)
        outer_ref[:, lanes] = total[608 + j * 32 : 640 + j * 32, :]
    small_ref[...] = total[576:584, :]


divide = whole_call(
    divide_kernel, "divide",
    [((16, 384), BF)] * 4 + [((160, 128), F32), ((160, 128), BF), ((32, D), F32), ((8, 128), F32)],
    2, scratch=[pltpu.VMEM((800, 128), F32)],
)


def last_kernel(where, w0, w1, w2, w3, give_ref, keep_w, out_ref, kept, given):
    low_core = where[3] == 0
    for m, piece in enumerate((w0, w1, w2, w3)):
        z = (where[1] + m) & 3
        rows = piece[...].astype(F32)
        mine = jnp.where(low_core, rows[:8], rows[8:])
        other = jnp.where(low_core, rows[8:], rows[:8])
        for j in range(3):
            at = pl.ds(pl.multiple_of((z * 3 + j) * 8, 8), 8)
            kept[at, :] = mine[:, j * 128 : j * 128 + 128]
            given[at, :] = other[:, j * 128 : j * 128 + 128]
    keep_w[...] = kept[...]
    out_ref[:96, :] = given[...].astype(BF)
    out_ref[96:, :] = give_ref[...]


last = whole_call(
    last_kernel, "last", [((96, 128), F32), ((256, 128), BF)], 1,
    scratch=[pltpu.VMEM((96, 128), F32)] * 2,
)


def finish_kernel(
    where, keep_w, keep_ref, got_ref, joint_ref, value_ref, norm_ref, inner_ref, output_ref
):
    low_core = where[3] == 0
    got = got_ref[...].astype(F32)
    mine, other = keep_w[...], got[:96]
    norm = jnp.zeros((8, 128), F32)
    for core in range(2):
        rows = jnp.where(low_core, *((mine, other) if core == 0 else (other, mine)))
        for z in range(4):
            lanes = slice((core * 4 + z) * 128, (core * 4 + z + 1) * 128)
            joint_ref[:, lanes] = rows[z * 24 : z * 24 + 8]
            value_ref[:, lanes] = rows[z * 24 + 8 : z * 24 + 16]
            norm = norm + rows[z * 24 + 16 : z * 24 + 24]
    norm_ref[...] = norm
    mine, other = keep_ref[...], got[96:]
    low, high = jnp.where(low_core, mine, other), jnp.where(low_core, other, mine)
    both = jnp.concatenate([low[:128], high[:128]], axis=1).astype(BF)
    dst, src = iota((256, 256), 1), iota((256, 256), 0)
    wanted = 128 * ((dst >> 5) & 1) + 32 * (dst >> 6) + (dst & 31)
    mixed = dot(both, (src == wanted).astype(F32).astype(BF))
    for t in range(16):
        inner_ref[:, t * 256 : (t + 1) * 256] = mixed[t * 8 : t * 8 + 8, :]
    for core, rows in enumerate((low, high)):
        for at, lane in enumerate((0, 128, 256, 384)):
            lanes = slice(core * 512 + lane, core * 512 + lane + 128)
            output_ref[:, lanes] = rows[128 + at * 8 : 136 + at * 8]


finish = whole_call(
    finish_kernel, "finish",
    [((8, D), F32), ((8, D), F32), ((8, 128), F32), ((8, FF), F32), ((8, D), F32)], 1,
)


def make_keys(pieces, rows_ref):
    for m, piece in enumerate(pieces):

        @pl.loop(0, 8, unroll=4)
        def _(s, m=m, piece=piece):
            rows = pl.ds(pl.multiple_of(s * TOK, TOK), TOK)
            to = pl.ds(pl.multiple_of(m * 8 * TOK + s * TOK, TOK), TOK)
            q = piece[rows, :].astype(F32)
            inv = lax.rsqrt(jnp.sum(q * q, axis=-1, keepdims=True) + EPS_KEY)
            rows_ref[to, :] = (q * inv).astype(BF)


def round_weights(lt_ref, at):
    totals = [lt_ref[r, at, :].astype(F32) for r in range(ROUNDS)]
    peak = jnp.maximum(jnp.maximum(totals[0], totals[1]), jnp.maximum(totals[2], totals[3]))
    exps = [jnp.exp(t - peak) for t in totals]
    scale = 1.0 / (exps[0] + exps[1] + exps[2] + exps[3])
    return [e * scale for e in exps]


def hot_slots(tgt_ref, source):
    slots = iota((BUCKETS * MOST, TOK), 0)
    return (slots == tgt_ref[0, pl.ds(source, 1), :]).astype(F32).astype(BF)


def hot_tokens(tgt_t_ref, source):
    slots = iota((TOK, BUCKETS * MOST), 1)
    return (slots == tgt_t_ref[0, :, source : source + 1]).astype(F32).astype(BF)


def spread(first, second):
    width = first.shape[-1]
    both = [a.reshape(PAIRS, 2, MOST, width) for a in (first, second)]
    return jnp.concatenate(both, axis=2).astype(BF)


def fill(tgt_ref, read_rows, ref):
    @pl.loop(0, 16, unroll=4)
    def _(pair):
        placed = [
            dot(hot_slots(tgt_ref, pair * 2 + half), read_rows(pair * 2 + half))
            for half in range(2)
        ]
        both = spread(*placed)
        at = pl.ds(pl.multiple_of(pair * 16, 16), 16)
        ref[0, :, at, :128] = both[:, 0]
        ref[0, :, at, 128:] = both[:, 1]


def place(both, ref, pair):
    at = pl.multiple_of(pair * 16, 16)
    ref[:, pl.ds(at, 16), :] = both[:, 0]
    ref[:, pl.ds(64 + at, 16), :] = both[:, 1]


def diagonal(rows):
    first = iota((128, 128), 0) < 64
    none = jnp.zeros((128, 128), BF)
    return jnp.concatenate([jnp.where(first, rows, none), jnp.where(first, none, rows)], axis=1)


def diagonal_t(rows):
    turned = jnp.transpose(rows)
    first = iota((128, 128), 1) < 64
    none = jnp.zeros((128, 128), BF)
    return jnp.concatenate([jnp.where(first, turned, none), jnp.where(first, none, turned)], axis=0)


def eye():
    return iota((128, 128), 0) == iota((128, 128), 1)


def token_block(s):
    return pl.ds(pl.multiple_of(s * TOK, TOK), TOK)


def scores_kernel(q0, q1, q2, q3, tgt_ref, mask_ref, probs_ref, keys_ref, qm_ref, log_ref, k_rows):
    @pl.when(pl.program_id(0) == 0)
    def _():
        make_keys((q0, q1, q2, q3), k_rows)

    fill(tgt_ref, lambda source: k_rows[token_block(source), :], keys_ref)

    @pl.loop(0, 4, unroll=4)
    def _(pair):
        placed = [
            dot(hot_slots(tgt_ref, pair * 2 + half), q0[token_block(pair * 2 + half), :])
            for half in range(2)
        ]
        place(spread(*placed), qm_ref.at[0], pair)

    @pl.loop(0, PAIRS, unroll=16)
    def _(p):
        code = mask_ref[0, p].astype(F32)
        scores = dot(keys_ref[0, p], diagonal_t(qm_ref[0, p]))
        scores = jnp.where(code == 0.0, scores, code * 1e4)
        peak = jnp.max(scores, axis=0, keepdims=True)
        exponent = jnp.exp(scores - peak)
        total = jnp.sum(exponent, axis=0, keepdims=True)
        probs_ref[0, p] = (exponent * (1.0 / total)).astype(BF)
        log_ref[0, pl.ds(p, 1), :] = peak + jnp.log(total)


def attend_scores(q_pieces, tgt, mask):
    rows = 8 * TOK
    outs = [(PAIRS, 256, 128), (PAIRS, 256, 256), (PAIRS, 128, 128), (PAIRS, 128)]
    types = [BF, BF, BF, F32]
    return kernel_call(
        scores_kernel,
        grid=(ROUNDS,),
        in_specs=[fixed((rows, HEAD_DIM))] * 4
        + [per_round((32, TOK)), per_round((PAIRS, 256, 128))],
        out_specs=[per_round(shape) for shape in outs],
        out_shape=[
            jax.ShapeDtypeStruct((ROUNDS,) + shape, t) for shape, t in zip(outs, types)
        ],
        scratch_shapes=[pltpu.VMEM((4 * rows, HEAD_DIM), BF)],
        compiler_params=params(20),
        cost_estimate=cost(18),
        far_in=(5,),
        far_out=(0, 1, 2),
        name="attend_scores",
    )(*q_pieces, tgt, mask)


def values_kernel(
    v0, v1, v2, v3, tgt_ref, tgt_t_ref, probs_ref, log_ref, mixed_ref, ro_ref, lt_ref, values_ref, att
):
    this_round = pl.program_id(0)
    for m, piece in enumerate((v0, v1, v2, v3)):

        @pl.loop(0, 4, unroll=4)
        def _(pair, m=m, piece=piece):
            placed = [
                dot(
                    hot_slots(tgt_ref, m * 8 + pair * 2 + half),
                    piece[token_block(pair * 2 + half), :],
                )
                for half in range(2)
            ]
            both = spread(*placed)
            at = pl.ds(pl.multiple_of((m * 4 + pair) * 16, 16), 16)
            values_ref[0, :, at, :128] = both[:, 0]
            values_ref[0, :, at, 128:] = both[:, 1]

    ones = jnp.ones((128, 128), BF)

    @pl.loop(0, PAIRS, unroll=16)
    def _(p):
        out = t_dot(probs_ref[0, p], values_ref[0, p])
        log_total = log_ref[0, pl.ds(p, 1), :]
        logs = dot(jnp.where(eye(), log_total, 0.0).astype(BF), ones)
        att[p, 0, :, :128] = out[:64, :128]
        att[p, 1, :, :128] = out[64:, 128:]
        att[p, 0, :, 128:] = logs[:64]
        att[p, 1, :, 128:] = logs[64:]

    for s in range(8):
        slots = att[:, :, s * MOST : (s + 1) * MOST, :].reshape(256, 256)
        rows = dot(hot_tokens(tgt_t_ref, s), slots.astype(BF)).astype(BF)
        ro_ref[this_round, s * TOK : (s + 1) * TOK, :] = rows[:, :HEAD_DIM]
        lt_ref[this_round, s * TOK : (s + 1) * TOK, :] = rows[:, HEAD_DIM:]

    @pl.when(this_round == ROUNDS - 1)
    def _():
        @pl.loop(0, 8)
        def _(s):
            at = token_block(s)
            weights = round_weights(lt_ref, at)
            mixed = weights[0] * ro_ref[0, at, :].astype(F32)
            for r in range(1, ROUNDS):
                mixed = mixed + weights[r] * ro_ref[r, at, :].astype(F32)
            mixed_ref[at, :] = mixed.astype(BF)


def attend_values(v_pieces, tgt, tgt_t, probs, logs):
    rows = 8 * TOK
    return kernel_call(
        values_kernel,
        grid=(ROUNDS,),
        in_specs=[fixed((rows, HEAD_DIM))] * 4
        + [
            per_round((32, TOK)), per_round((TOK, 128)), per_round((PAIRS, 256, 128)),
            per_round((PAIRS, 128)),
        ],
        out_specs=[
            fixed((rows, HEAD_DIM)),
            fixed((ROUNDS, rows, HEAD_DIM)),
            fixed((ROUNDS, rows, HEAD_DIM)),
            per_round((PAIRS, 256, 256)),
        ],
        out_shape=[
            jax.ShapeDtypeStruct((rows, HEAD_DIM), BF),
            jax.ShapeDtypeStruct((ROUNDS, rows, HEAD_DIM), BF),
            jax.ShapeDtypeStruct((ROUNDS, rows, HEAD_DIM), BF),
            jax.ShapeDtypeStruct((ROUNDS, PAIRS, 256, 256), BF),
        ],
        scratch_shapes=[pltpu.VMEM((PAIRS, 2, 64, 256), F32)],
        compiler_params=params(22),
        cost_estimate=cost(14),
        far_in=(6,),
        far_out=(1, 2, 3),
        name="attend_values",
    )(*v_pieces, tgt, tgt_t, probs, logs)


def take_slots(tgt_t_ref, slots_ref, rows_ref, sources):
    for s in range(sources):
        slots = slots_ref[:, :, s * MOST : (s + 1) * MOST, :].reshape(256, HEAD_DIM)
        rows_ref[s * TOK : (s + 1) * TOK, :] += dot(hot_tokens(tgt_t_ref, s), slots.astype(BF))


def values_back_kernel(
    where, tgt_ref, tgt_t_ref, probs_ref, ro_ref, lt_ref, gm_ref, out_ref, gd_ref, gt_ref, gt_slots, slots, rows, token_rows,
):
    this_round = pl.program_id(0)

    @pl.when(this_round == 0)
    def _():
        rows[...] = jnp.zeros_like(rows)

        @pl.loop(0, 8, unroll=2)
        def _(s):
            at = token_block(s)
            weights = round_weights(lt_ref, at)
            grad = gm_ref[at, :].astype(F32)
            agree = [
                jnp.sum(grad * ro_ref[r, at, :].astype(F32), axis=-1, keepdims=True)
                for r in range(ROUNDS)
            ]
            mean = total_of([weights[r] * agree[r] for r in range(ROUNDS)])
            for r in range(ROUNDS):
                token_rows[r, at, :HEAD_DIM] = (weights[r] * grad).astype(BF)
                token_rows[r, at, HEAD_DIM:] = (weights[r] * (agree[r] - mean)).astype(BF)

    @pl.loop(0, 4, unroll=4)
    def _(pair):
        placed = [
            dot(
                hot_slots(tgt_ref, pair * 2 + half),
                token_rows[this_round, token_block(pair * 2 + half), :],
            )
            for half in range(2)
        ]
        both = spread(*placed)
        place(both[..., :HEAD_DIM], gd_ref.at[0], pair)
        place(both[..., HEAD_DIM:], gt_slots, pair)

    @pl.loop(0, PAIRS, unroll=16)
    def _(p):
        grad_values = dot(probs_ref[0, p], diagonal(gd_ref[0, p]))
        slots[p, 0] = grad_values[:, :128]
        slots[p, 1] = grad_values[:, 128:]
        gt_ref[0, pl.ds(p, 1), :] = jnp.sum(
            jnp.where(eye(), gt_slots[p].astype(F32), 0.0), axis=0, keepdims=True
        )

    take_slots(tgt_t_ref, slots, rows, 32)

    @pl.when(this_round == ROUNDS - 1)
    def _():
        for m in range(4):
            out_ref[(where[2] + m) & 3] = rows[m * 8 * TOK : (m + 1) * 8 * TOK, :].astype(BF)


def attend_values_back(where, tgt, tgt_t, probs, ro, lt, gm):
    rows = 8 * TOK
    return kernel_call(
        values_back_kernel,
        grid=(ROUNDS,),
        in_specs=[
            SMEM,
            per_round((32, TOK)),
            per_round((TOK, 128)),
            per_round((PAIRS, 256, 128)),
            fixed((ROUNDS, rows, HEAD_DIM)),
            fixed((ROUNDS, rows, HEAD_DIM)),
            fixed((rows, HEAD_DIM)),
        ],
        out_specs=[
            fixed((4, rows, HEAD_DIM)), per_round((PAIRS, 128, 128)), per_round((PAIRS, 128)),
        ],
        out_shape=[
            jax.ShapeDtypeStruct((4, rows, HEAD_DIM), BF),
            jax.ShapeDtypeStruct((ROUNDS, PAIRS, 128, 128), BF),
            jax.ShapeDtypeStruct((ROUNDS, PAIRS, 128), F32),
        ],
        scratch_shapes=[
            pltpu.VMEM((PAIRS, 128, 128), BF),
            pltpu.VMEM((PAIRS, 2, 256, HEAD_DIM), F32),
            pltpu.VMEM((4 * rows, HEAD_DIM), F32),
            pltpu.VMEM((ROUNDS, rows, 256), BF),
        ],
        compiler_params=params(26),
        cost_estimate=cost(12),
        far_in=(1, 2, 3, 4, 5),
        far_out=(0, 1, 2),
        name="attend_values_back",
    )(where, tgt, tgt_t, probs, ro, lt, gm)


def scores_back_kernel(
    half, where, tgt_t_ref, mask_ref, probs_ref, values_ref, qm_ref, gd_ref, gt_ref, *refs
):
    if half == 0:
        gs_ref, rows_out, slots, rows = refs
    else:
        rows_in, gs_ref, out_ref, slots, rows = refs
    step = pl.program_id(0)

    @pl.when(step == 0)
    def _():
        if half == 0:
            rows[...] = jnp.zeros_like(rows)
        else:
            rows[...] = rows_in[...]

    @pl.loop(0, PAIRS, unroll=16)
    def _(p):
        probs = probs_ref[0, p].astype(F32)
        grad_probs = dot(values_ref[0, p], diagonal_t(gd_ref[0, p]))
        agreement = jnp.sum(probs * grad_probs, axis=0, keepdims=True)
        grad_scores = probs * (grad_probs + (gt_ref[0, pl.ds(p, 1), :] - agreement))
        seen = mask_ref[0, p].astype(F32) == 0.0
        grad_scores = jnp.where(seen, grad_scores, 0.0).astype(BF)
        gs_ref[0, p] = grad_scores
        grad_keys = dot(grad_scores, diagonal(qm_ref[0, p]))
        slots[p, 0] = grad_keys[:, :128]
        slots[p, 1] = grad_keys[:, 128:]

    take_slots(tgt_t_ref, slots, rows, 32)

    @pl.when(step == 1)
    def _():
        if half == 0:
            rows_out[...] = rows[...]
        else:
            for m in range(4):
                out_ref[(where[2] + m) & 3] = rows[m * 8 * TOK : (m + 1) * 8 * TOK, :].astype(BF)


def attend_scores_back(half, where, arrays, begun):
    rows = 8 * TOK
    shapes = [
        (TOK, 128), (PAIRS, 256, 128), (PAIRS, 256, 128), (PAIRS, 256, 256),
        (PAIRS, 128, 128), (PAIRS, 128, 128), (PAIRS, 128),
    ]
    this_half = lambda shape: pl.BlockSpec(
        (1,) + shape, lambda r: (2 * half + r,) + (0,) * len(shape)
    )
    slots = (PAIRS, 256, 128)
    if half == 0:
        outs = [((4 * rows, HEAD_DIM), F32)]
    else:
        outs = [((4, rows, HEAD_DIM), BF)]
    return kernel_call(
        functools.partial(scores_back_kernel, half),
        grid=(2,),
        in_specs=[SMEM] + [this_half(shape) for shape in shapes] + [fixed(a.shape) for a in begun],
        out_specs=[per_round(slots)] + [fixed(shape) for shape, _ in outs],
        out_shape=[jax.ShapeDtypeStruct((2,) + slots, BF)]
        + [jax.ShapeDtypeStruct(shape, t) for shape, t in outs],
        scratch_shapes=[
            pltpu.VMEM((PAIRS, 2, 256, HEAD_DIM), F32),
            pltpu.VMEM((4 * rows, HEAD_DIM), F32),
        ],
        compiler_params=params(30),
        cost_estimate=cost(10),
        far_in=tuple(range(1, 8)),
        far_out=(0,),
        name=f"attend_scores_back_{half}",
    )(where, *arrays, *begun)


def queries_back_kernel(tgt_t_ref, first_ref, second_ref, keys_ref, gq_ref, slots):
    step = pl.program_id(0)

    @pl.when(step == 0)
    def _():
        gq_ref[...] = jnp.zeros_like(gq_ref)

    def one_round(gs_ref):
        @pl.loop(0, PAIRS, unroll=16)
        def _(p):
            grad_queries = t_dot(gs_ref[0, p], keys_ref[0, p])
            slots[p, 0] = grad_queries[:64, :128]
            slots[p, 1] = grad_queries[64:, 128:]

    @pl.when(step < 2)
    def _():
        one_round(first_ref)

    @pl.when(step >= 2)
    def _():
        one_round(second_ref)

    take_slots(tgt_t_ref, slots, gq_ref, 8)


def attend_queries_back(tgt_t, first, second, keys):
    rows, slots = 8 * TOK, (1, PAIRS, 256, 128)
    return kernel_call(
        queries_back_kernel,
        grid=(ROUNDS,),
        in_specs=[
            per_round((TOK, 128)),
            pl.BlockSpec(slots, lambda r: (jnp.minimum(r, 1), 0, 0, 0)),
            pl.BlockSpec(slots, lambda r: (jnp.maximum(r, 2) - 2, 0, 0, 0)),
            per_round((PAIRS, 256, 256)),
        ],
        out_specs=[fixed((rows, HEAD_DIM))],
        out_shape=[jax.ShapeDtypeStruct((rows, HEAD_DIM), F32)],
        scratch_shapes=[pltpu.VMEM((PAIRS, 2, 64, HEAD_DIM), F32)],
        compiler_params=params(20),
        cost_estimate=cost(8),
        far_in=(0, 1, 2, 3),
        far_out=(0,),
        name="attend_queries_back",
    )(tgt_t, first, second, keys)[0]


def local(
    first_in, second_in, attn_gain, attn_shift, w_joint, w_value, w_output, ffn_gain, ffn_shift,
    w_inner, b_inner, w_outer, b_outer, buckets, cot_first, cot_second,
):
    y, z, x, c = (lax.axis_index(a) for a in AXES)
    where = jnp.stack([y, z, x, c]).astype(jnp.int32)
    low_core = c == 0

    def by_core(first, second):
        return jnp.where(low_core, first, second)

    vec = jnp.concatenate(
        [attn_gain, attn_shift, ffn_gain, ffn_shift, b_outer, b_inner, jnp.zeros((56,), BF)]
    ).astype(F32)
    keep_a, give_a, keep_b, give_b = pack(
        where, w_joint, w_value, w_output, w_inner, vec.reshape(1, 128), buckets[:, :, 0]
    )
    tok_near = [send(second_in, "z", 3), send(second_in, "z", 1)]
    got_a, got_b = swap(give_a), swap(give_b)
    gathered = lax.all_gather(
        payload(where, keep_b, got_b, w_outer)[0], CHIPS, axis=0, tiled=False
    ).reshape(64, 80, D)
    y_got = gather(chip_message(where, keep_a, got_a)[0], "y")
    heads_out, second_late, tok_near = sync(
        head_messages(where, *y_got), second_in, tok_near
    )
    z_got = scatter(heads_out, "z")
    tok_last = send(second_late, "z", 2)
    z_got, tok_last = sync(z_got, tok_last)
    tok_far = jnp.stack([tok_near[0], tok_last, tok_near[1]])
    sib_tok = swap(jnp.concatenate([second_in[None], tok_far]))
    tokens = (second_in, tok_far, sib_tok)
    x_got = gather(jnp.concatenate(z_got), "x")
    wq, par, tgt, tgt_t, counts, vec = assemble(where, *x_got)

    normed, queries = project(where, tokens, par, wq)
    queries, counts, vec = sync(queries, counts, vec)
    q_pieces = gather(queries, "x")
    mask, par_ffn, bias_inner = make_mask(where, counts, vec)
    values, wv = project_values(where, x_got, normed)
    values, q_pieces[1], q_pieces[3] = sync(values, q_pieces[1], q_pieces[3])
    v_pieces = gather(values, "x")
    sib_rows = swap(jnp.stack([first_in, cot_first, cot_second]))
    probs, key_slots, query_slots, logs = attend_scores(q_pieces, tgt, mask)
    mixed_head, round_out, round_total, value_slots = attend_values(
        v_pieces, tgt, tgt_t, probs, logs
    )

    mix_own = jnp.concatenate(
        scatter([mixed_head[k * 256 : (k + 1) * 256] for k in range(4)], "z"), axis=1
    )
    mix_sib = swap(mix_own)
    first_sum, first_out, input_t, active, grad_hidden, back, hid_sum, cot_sum = feed(
        where, mix_own, mix_sib, first_in, cot_second, sib_rows, par_ffn, bias_inner, gathered
    )
    a_parts = inner_grads(where, active, grad_hidden, input_t, cot_second, sib_rows)
    back_sib, a_parts = sync(swap(back), a_parts)
    grad_first, branch, g0, g1, g2, g3, norm_sums = first_back(
        where, back, back_sib, first_sum, cot_first, sib_rows, par_ffn, gathered
    )
    grad_mixed = scatter([g0, g1, g2, g3], "z")
    a_got = [send(a_parts[1], "y", 1), send(a_parts[3], "y", 3)]
    sums = jnp.stack([norm_sums[0], norm_sums[1], cot_sum[0]]).reshape(3, 64, 16)
    sums = jnp.pad(jnp.transpose(sums, (1, 0, 2)), ((0, 0), (0, 0), (0, 16)))
    sums = jnp.concatenate([sums, hid_sum[0].reshape(64, 1, 32)], axis=1).astype(BF)
    sums = jnp.pad(sums, ((0, 0), (0, 12), (0, 96)))
    *b_parts, second_own, second_give = outer_grads(
        where, active, cot_second, sib_rows, mix_own, mix_sib, branch, sums, gathered
    )
    grad_mixed, b_parts, second_give = sync(grad_mixed, b_parts, second_give)

    b_got = [send(b_parts[1], "z", 1), send(b_parts[3], "z", 3)]
    gv, grad_slots, log_slots = attend_values_back(
        where, tgt, tgt_t, probs, round_out, round_total, jnp.concatenate(grad_mixed)
    )

    gv, grad_slots, a_far = sync(gv, grad_slots, a_parts[2])
    gv_got = exchange(gv, "x")
    a_far = send(a_far, "y", 2)
    back_in = (tgt_t, mask, probs, value_slots, query_slots, grad_slots, log_slots)
    gs_first, half = attend_scores_back(0, where, back_in, ())
    a_got, b_got, b_far, half = sync(a_got, b_got, b_parts[2], half)
    b_far = send(b_far, "z", 2)
    gs_second, gk = attend_scores_back(1, where, back_in, (half,))
    gv_got, gk, gs_second, second_give = sync(gv_got, gk, gs_second, second_give)

    gk_got = exchange(gk, "x")
    second_got = swap(second_give)
    gq = attend_queries_back(tgt_t, gs_first, gs_second, key_slots)
    a_far, gq = sync(a_far, gq)
    a_parts = recut_a(
        where, *[part.reshape(4, 4, 16, 2560) for part in [a_parts[0], a_far] + a_got]
    )
    a_parts, b_far = sync(a_parts, b_far)
    a_got = scatter(a_parts, "z")
    b_parts = recut_b(
        where, *[part.reshape(4, 4, 32, 1152) for part in [b_parts[0], b_far] + b_got]
    )
    gk_got, second_got, b_parts = sync(gk_got, second_got, b_parts)

    b_got = scatter(b_parts, "y")
    back_own, back_give, *w_parts = project_back(
        where, tokens, wq, wv, normed, queries, gq, gk_got, gv_got
    )

    back_give, w_parts, a_got, b_got[1], b_got[3] = sync(
        back_give, w_parts, a_got, b_got[1], b_got[3]
    )
    w_got = scatter(w_parts, "y")
    back_chip = (back_own.astype(F32) + swap(back_give).astype(F32)).astype(BF)
    back_parts = [back_chip[k] for k in range(4)]
    back_far = send(back_parts[2], "z", 2)
    back_parts, w_got, a_got, b_got = sync(back_parts, w_got, a_got, b_got)

    second_out = (second_in.astype(F32) + second_own + second_got + par_ffn[2]).astype(BF)

    x_parts = scatter(join(where, *w_got, *a_got, *b_got), "x")
    x_parts[1], back_parts, back_far = sync(x_parts[1], back_parts, back_far)
    back_sum = [
        back_parts[0], send(back_parts[1], "z", 1), send(back_parts[3], "z", 3), back_far
    ]

    *z_parts, chip_keep, chip_give, grad_outer, small = divide(where, *x_parts)
    w_got = scatter(z_parts, "z")
    w_keep, last_give = last(where, *w_got, chip_give)
    grad_joint, grad_value, norm, grad_inner, grad_output = finish(
        where, w_keep, chip_keep, swap(last_give)
    )
    grad_attn_gain, grad_attn_shift = norm[:, 0], norm[:, 64]
    mine16 = by_core(small[:3, :8], small[:3, 8:16])
    grad_ffn_gain, grad_ffn_shift, grad_b_outer = mine16[0], mine16[1], mine16[2]
    grad_b_inner = small[3, :32]

    attn_xhat, attn_scale = normalized(second_in.astype(F32))
    attn_back = norm_back(total_of(back_sum) * par[0], attn_xhat, attn_scale)
    grad_second = (cot_second.astype(F32) + attn_back).astype(BF)

    return (
        first_out, second_out, grad_first, grad_second, grad_attn_gain, grad_attn_shift,
        grad_joint, grad_value, grad_output, grad_ffn_gain, grad_ffn_shift, grad_inner,
        grad_b_inner, grad_outer, grad_b_outer,
    )


def solution(mesh):
    chips = Mesh(mesh.devices.reshape(4, 4, 4, 2), AXES)
    rows, flat = P(AXES, None), P(AXES)
    return jax.shard_map(
        local,
        mesh=chips,
        in_specs=(
            rows, rows, flat, flat, rows, rows, rows, flat, flat, rows, flat, rows, flat,
            P(None, AXES, None), rows, rows,
        ),
        out_specs=(
            rows, rows, rows, rows, flat, flat, rows, rows, rows, flat, flat, rows, flat, rows,
            flat,
        ),
        check_vma=False,
    )
```

```python
import functools

import jax
import jax.numpy as jnp
from jax import lax
from jax.experimental import pallas as pl
from jax.experimental.pallas import tpu as pltpu
from jax.sharding import Mesh, PartitionSpec as P

HEADS = 8
HEAD_DIM = 128
ROUNDS = 4
BUCKETS = 32
MOST = 8
TOK = 128
D = 1024
FF = 4096

EPS_NORM = 1e-05
EPS_KEY = 1e-06
SELF_SCORE = -10000.0
MASKED_SCORE = -1000000000.0

BF = jnp.bfloat16
F32 = jnp.float32

AXES = ("y", "z", "x", "c")
CHIPS = ("y", "z", "x")


def send(piece, axis, k):
    return lax.ppermute(piece, axis, [(i, (i + k) % 4) for i in range(4)])


def swap(piece):
    return lax.ppermute(piece, "c", [(0, 1), (1, 0)])


def gather(piece, axis):
    back, front, far = send(piece, axis, 3), send(piece, axis, 1), send(piece, axis, 2)
    return [piece, back, far, front]


def scatter(pieces, axis):
    front, back, far = (
        send(pieces[1], axis, 1),
        send(pieces[3], axis, 3),
        send(pieces[2], axis, 2),
    )
    return [pieces[0], back, far, front]


def sync(*groups):
    return lax.optimization_barrier(groups)


def dot(a, b):
    return jnp.dot(a, b, preferred_element_type=F32)


def dot_t(a, b):
    return lax.dot_general(a, b, (((1,), (1,)), ((), ())), preferred_element_type=F32)


def t_dot(a, b):
    return lax.dot_general(a, b, (((0,), (0,)), ((), ())), preferred_element_type=F32)


def cost(us):
    return pl.CostEstimate(flops=int(us * 0.35e9), bytes_accessed=0, transcendentals=0)


def params(mib):
    return pltpu.CompilerParams(vmem_limit_bytes=mib * 1024 * 1024)


SMEM = pl.BlockSpec(memory_space=pltpu.SMEM)


def kernel_call(kernel, *, out_shape, far_in=(), far_out=(), **rest):
    inner = pl.pallas_call(
        kernel,
        out_shape=[
            pltpu.HBM(o.shape, o.dtype) if at in far_out else o for at, o in enumerate(out_shape)
        ],
        **rest,
    )

    def run(*arrays):
        return inner(
            *[
                pltpu.with_memory_space_constraint(a, pltpu.HBM) if at in far_in else a
                for at, a in enumerate(arrays)
            ]
        )

    return run


def iota(shape, dim):
    return lax.broadcasted_iota(jnp.int32, shape, dim)


def whole_call(kernel, name, outs, us, mib=16, scratch=(), far_in=(), far_out=()):
    def call(where, *arrays):
        return kernel_call(
            kernel,
            grid=(1,),
            in_specs=[SMEM] + [fixed(a.shape) for a in arrays],
            out_specs=[fixed(s) for s, _ in outs],
            out_shape=[jax.ShapeDtypeStruct(s, t) for s, t in outs],
            scratch_shapes=list(scratch),
            compiler_params=params(mib),
            cost_estimate=cost(us),
            far_in=far_in,
            far_out=far_out,
            name=name,
        )(where, *arrays)

    return call


def fixed(shape):
    return pl.BlockSpec(shape, lambda r: (0,) * len(shape))


def per_round(shape):
    return pl.BlockSpec((1,) + shape, lambda r: (r,) + (0,) * len(shape))


PAIRS = BUCKETS // 2


def exchange(stacked, axis):
    return lax.all_to_all(stacked, axis, split_axis=0, concat_axis=0, tiled=True)


def total_of(parts):
    total = parts[0].astype(F32)
    for extra in parts[1:]:
        total = total + extra.astype(F32)
    return total


def pack_kernel(
    where, joint_ref, value_ref, output_ref, inner_ref, vec_ref, bucket_ref,
    keep_ref, give_ref,
):
    low_core = where[3] == 0
    joint, value = joint_ref[...].astype(F32), value_ref[...].astype(F32)
    inner_rows = inner_ref[...].astype(F32)
    heads = []
    for core in range(2):
        rows = []
        for h in range(4):
            cols = slice((core * 4 + h) * 128, (core * 4 + h + 1) * 128)
            rows += [joint[:, cols], value[:, cols]]
        heads.append(jnp.concatenate(rows, axis=0))

    sub, along = iota((128, 128), 0), iota((128, 128), 1)
    targets, counts = [], []
    for r in range(ROUNDS):
        chosen = jnp.broadcast_to(bucket_ref[r : r + 1, :].astype(F32), (128, 128))
        column = jnp.sum(jnp.where(sub == along, chosen, 0.0), axis=1, keepdims=True)
        earlier = (column == chosen) & (sub < along)
        rank = jnp.sum(earlier.astype(F32), axis=0, keepdims=True)
        targets.append(chosen[0:1] * MOST + rank)
        counts.append(jnp.sum((column == along.astype(F32)).astype(F32), axis=0, keepdims=True))
    vec = jnp.concatenate([vec_ref[...], jnp.zeros((7, 128), F32)], axis=0)
    aux = jnp.concatenate([vec] + targets + counts, axis=0)
    keep_ref[:80, :] = jnp.concatenate([jnp.where(low_core, *heads), aux], axis=0).astype(BF)
    give_ref[:80, :] = jnp.concatenate([jnp.where(low_core, *heads[::-1]), aux], axis=0).astype(BF)

    chunks = [inner_rows[:, t * 256 : (t + 1) * 256] for t in range(16)]
    src, dst = iota((256, 256), 0), iota((256, 256), 1)
    wanted = 64 * ((dst % 128) // 32) + 32 * (dst // 128) + dst % 32
    picked = dot(jnp.concatenate(chunks, axis=0).astype(BF), (src == wanted).astype(F32).astype(BF))
    inner = []
    for core in range(2):
        halves = [
            jnp.concatenate(
                [
                    picked[t * 8 : (t + 1) * 8, core * 128 : (core + 1) * 128]
                    for t in range(half * 8, half * 8 + 8)
                ],
                axis=1,
            )
            for half in range(2)
        ]
        inner.append(jnp.concatenate(halves, axis=0))
    rest = jnp.concatenate([output_ref[...].astype(F32), jnp.zeros((8, D), F32)], axis=0)
    keep = jnp.concatenate([jnp.where(low_core, *inner), rest], axis=0).astype(BF)
    give = jnp.concatenate([jnp.where(low_core, *inner[::-1]), rest], axis=0).astype(BF)
    for j in range(8):
        lanes = slice(j * 128, j * 128 + 128)
        keep_ref[80 + j * 32 : 112 + j * 32, :] = keep[:, lanes]
        give_ref[80 + j * 32 : 112 + j * 32, :] = give[:, lanes]


pack = whole_call(
    pack_kernel, "pack", [((336, 128), BF)] * 2, 3, far_in=(1, 2, 3, 4, 6)
)


def chip_message_kernel(where, keep_ref, got_ref, out_ref):
    low_core = where[3] == 0
    keep, got = keep_ref[:80, :].astype(F32), got_ref[:80, :].astype(F32)
    first, second = jnp.where(low_core, keep, got), jnp.where(low_core, got, keep)
    rows = []
    for at in (0, 16, 32, 48, 8, 24, 40, 56, 64, 72):
        rows += [first[at : at + 8], second[at : at + 8]]
    out_ref[...] = jnp.concatenate(rows, axis=0).astype(BF)


chip_message = whole_call(chip_message_kernel, "chip_message", [((160, 128), BF)], 1)


def head_messages_kernel(where, y0, y1, y2, y3, *outs):
    pieces = (y0, y1, y2, y3)
    vec = []
    for piece in pieces:
        rows = piece[128:144, :].astype(F32)
        vec += [rows[0:1], rows[8:9]]
    vec = jnp.concatenate(vec + [jnp.zeros((8, 128), F32)], axis=0).astype(BF)
    for k in range(4):
        head = (where[1] + k) & 3
        q_rows = pl.ds(pl.multiple_of(head * 16, 16), 16)
        v_rows = pl.ds(pl.multiple_of(64 + head * 16, 16), 16)
        for n, piece in enumerate(pieces):
            outs[k][n * 16 : n * 16 + 16, :] = piece[q_rows, :]
            outs[k][96 + n * 16 : 112 + n * 16, :] = piece[v_rows, :]
        outs[k][64:80, :] = vec
        outs[k][80:96, :] = y0[144:160, :]


head_messages = whole_call(
    head_messages_kernel, "head_messages", [((160, 128), BF)] * 4, 1
)


def payload_kernel(where, keep_ref, got_ref, outer_ref, out_ref):
    low_core = where[3] == 0
    for j in range(8):
        lanes = slice(j * 128, j * 128 + 128)
        block = slice(80 + j * 32, 112 + j * 32)
        keep, got = keep_ref[block, :].astype(F32), got_ref[block, :].astype(F32)
        first, second = jnp.where(low_core, keep, got), jnp.where(low_core, got, keep)
        for at, to in ((0, 0), (8, 16), (16, 64)):
            out_ref[to : to + 16, lanes] = jnp.concatenate(
                [first[at : at + 8], second[at : at + 8]], axis=0
            ).astype(BF)
    out_ref[32:64, :] = outer_ref[...]


payload = whole_call(payload_kernel, "payload", [((80, D), BF)], 1)


def by_rows(where, pieces, ref):
    for m, rows in enumerate(pieces):
        for n in range(4):
            for k in range(4):
                chip = ((where[0] + n) % 4 * 4 + (where[1] + k) % 4) * 4 + (where[2] + m) % 4
                ref[pl.ds(pl.multiple_of(chip * 16, 16), 16), :] = rows(k, n)


def device_of(where, shape):
    row = iota(shape, 0)
    x, z, y = (where[2] + (row >> 5)) & 3, (where[1] + (row >> 3)) & 3, (where[0] + (row >> 1)) & 3
    return ((y * 4 + z) * 4 + x) * 2 + (row & 1)


def parameter(where, vec, v):
    shape = (128, D)
    lane = iota(shape, 1)
    picked = dot(vec, (iota(shape, 0) == 8 * v + (lane & 7)).astype(F32).astype(BF))
    mine = device_of(where, shape) == (lane >> 3)
    return jnp.sum(jnp.where(mine, picked, 0.0), axis=0, keepdims=True)


def assemble_kernel(where, x0, x1, x2, x3, w_ref, par_ref, tgt_ref, tgt_t_ref, count_ref, vec_ref):
    pieces = (x0, x1, x2, x3)
    by_rows(
        where,
        [
            lambda k, n, piece=piece: piece[k * 160 + n * 16 : k * 160 + n * 16 + 16, :]
            for piece in pieces
        ],
        w_ref,
    )
    vec = jnp.concatenate(
        [
            piece[k * 160 + 64 : k * 160 + 80, :].astype(F32)[:8]
            for piece in pieces
            for k in range(4)
        ],
        axis=0,
    ).astype(BF)
    vec_ref[...] = vec
    par_ref[...] = jnp.concatenate(
        [parameter(where, vec, 0), parameter(where, vec, 1), jnp.zeros((6, D), F32)], axis=0
    )
    empty = jnp.zeros((96, 128), F32)
    slots = [
        jnp.concatenate(
            [piece[k * 160 + 80 : k * 160 + 96, :] for k in range(4)], axis=0
        ).astype(F32)
        for piece in pieces
    ]
    for r in range(ROUNDS):
        rows = jnp.concatenate(
            [slots[m][s * 8 + r : s * 8 + r + 1] for m in range(4) for s in range(8)], axis=0
        )
        tgt_ref[r] = rows.astype(jnp.int32)
        tgt_t_ref[r] = jnp.transpose(jnp.concatenate([rows, empty], axis=0)).astype(jnp.int32)
        count_ref[r] = jnp.concatenate(
            [slots[m][s * 8 + 4 + r : s * 8 + 5 + r] for m in range(4) for s in range(8)], axis=0
        )


assemble = whole_call(
    assemble_kernel, "assemble",
    [
        ((D, 128), BF), ((8, D), F32), ((ROUNDS, 32, 128), jnp.int32),
        ((ROUNDS, 128, 128), jnp.int32), ((ROUNDS, 32, 128), F32), ((128, 128), BF),
    ],
    2, far_out=(2, 3),
)


def mask_kernel(where, count_ref, vec_ref, mask_ref, par_ref, bias_ref):
    z, x, c = where[1], where[2], where[3]

    @pl.when(pl.program_id(0) == 0)
    def _():
        vec = vec_ref[...]
        par_ref[...] = jnp.concatenate(
            [parameter(where, vec, v) for v in (2, 3, 4)] + [jnp.zeros((5, D), F32)], axis=0
        )
        wide = (128, 2048)
        lane = iota(wide, 1)
        picked = dot(vec, (iota(wide, 0) == 40 + (lane & 31)).astype(F32).astype(BF))
        mine = device_of(where, wide) == 2 * (lane >> 5) + c
        bias = jnp.sum(jnp.where(mine, picked, 0.0), axis=0, keepdims=True)
        bias_ref[...] = jnp.broadcast_to(bias, (8, 2048))

    shape = (256, 128)
    row, lane = iota(shape, 0), iota(shape, 1)
    source, rank = row >> 3, row & 7
    of_chip = lambda z_of, x_of, core: ((z_of & 3) * 8 + (x_of & 3) * 2 + core) * 8
    kpos = of_chip(z + ((source >> 1) & 3), x + (source >> 3), source & 1) + rank
    asker = (lane >> 3) & 7
    qpos = of_chip(z + (asker >> 1), x, asker & 1) + (lane & 7)
    code = jnp.where(kpos == qpos, -1.0, jnp.where(kpos < qpos, 0.0, -1e5))
    rank_f = rank.astype(F32)
    expand = (iota((256, 32), 0) >> 3) == iota((256, 32), 1)
    by_slot = dot(expand.astype(F32).astype(BF), count_ref[0].astype(BF)).astype(BF)
    bucket, side = iota((128, 128), 0), iota((128, 128), 1) >> 6

    @pl.loop(0, PAIRS, unroll=4)
    def _(p):
        select = (bucket == 2 * p + side).astype(F32).astype(BF)
        live = rank_f < dot(by_slot, select)
        mask_ref[0, p] = jnp.where(live, code, -1e5).astype(BF)


def make_mask(where, counts, vec):
    return kernel_call(
        mask_kernel,
        grid=(ROUNDS,),
        in_specs=[SMEM, per_round((32, 128)), fixed((128, 128))],
        out_specs=[per_round((PAIRS, 256, 128)), fixed((8, D)), fixed((8, 2048))],
        out_shape=[
            jax.ShapeDtypeStruct((ROUNDS, PAIRS, 256, 128), BF),
            jax.ShapeDtypeStruct((8, D), F32),
            jax.ShapeDtypeStruct((8, 2048), F32),
        ],
        far_out=(0,),
        compiler_params=params(16),
        cost_estimate=cost(7),
        name="make_mask",
    )(where, counts, vec)


def chip_rows(where, own, sib):
    low_core = where[3] == 0
    return jnp.concatenate([jnp.where(low_core, own, sib), jnp.where(low_core, sib, own)], axis=0)


def token_rows(where, own0, own3, sib):
    near = pl.program_id(0) == 0
    own = jnp.where(near, own0[...].astype(F32), own3[0].astype(F32))
    return chip_rows(where, own, sib[0].astype(F32))


def token_specs():
    return [
        pl.BlockSpec((TOK, D), lambda i: (0, 0)),
        pl.BlockSpec((1, TOK, D), lambda i: (jnp.maximum(i - 1, 0), 0, 0)),
        pl.BlockSpec((1, TOK, D), lambda i: (i, 0, 0)),
    ]


def project_kernel(where, own0, own3, sib, par_ref, w_ref, normed_ref, q_ref):
    rows = token_rows(where, own0, own3, sib)
    centered = rows - jnp.mean(rows, axis=-1, keepdims=True)
    spread = jnp.mean(centered * centered, axis=-1, keepdims=True)
    normed = centered * lax.rsqrt(spread + EPS_NORM) * par_ref[0:1, :] + par_ref[1:2, :]
    normed = normed.astype(BF)
    normed_ref[...] = normed
    q_ref[...] = dot(normed, w_ref[...]).astype(BF)


def project(where, tokens, par, w):
    whole = lambda i: (0, 0)
    return kernel_call(
        project_kernel,
        grid=(4,),
        in_specs=[SMEM] + token_specs()
        + [pl.BlockSpec((8, D), whole), pl.BlockSpec((D, HEAD_DIM), whole)],
        out_specs=[
            pl.BlockSpec((2 * TOK, D), lambda i: (i, 0)),
            pl.BlockSpec((2 * TOK, HEAD_DIM), lambda i: (i, 0)),
        ],
        out_shape=[
            jax.ShapeDtypeStruct((8 * TOK, D), BF),
            jax.ShapeDtypeStruct((8 * TOK, HEAD_DIM), BF),
        ],
        compiler_params=params(20),
        cost_estimate=cost(4),
        far_out=(0,),
        name="project",
    )(where, *tokens, par, w)


def project_values_kernel(where, x0, x1, x2, x3, normed_ref, v_ref, w_ref):
    @pl.when(pl.program_id(0) == 0)
    def _():
        by_rows(
            where,
            [
                lambda k, n, piece=piece: piece[k * 160 + n * 16 + 96 : k * 160 + n * 16 + 112, :]
                for piece in (x0, x1, x2, x3)
            ],
            w_ref,
        )

    v_ref[...] = dot(normed_ref[...], w_ref[...]).astype(BF)


def project_values(where, pieces, normed):
    return kernel_call(
        project_values_kernel,
        grid=(4,),
        in_specs=[SMEM] + [fixed(p.shape) for p in pieces]
        + [pl.BlockSpec((2 * TOK, D), lambda i: (i, 0))],
        out_specs=[
            pl.BlockSpec((2 * TOK, HEAD_DIM), lambda i: (i, 0)), fixed((D, HEAD_DIM)),
        ],
        out_shape=[
            jax.ShapeDtypeStruct((8 * TOK, HEAD_DIM), BF),
            jax.ShapeDtypeStruct((D, HEAD_DIM), BF),
        ],
        compiler_params=params(16),
        cost_estimate=cost(3),
        far_in=(5,),
        name="project_values",
    )(where, *pieces, normed)


def project_back_kernel(
    where, own0, own3, sib, wq_ref, wv_ref, normed_ref, q_ref, gq_ref,
    gk_ref, gv_ref, own_out, sib_out, wg0, wg1, wg2, wg3, total, sums,
):
    step = pl.program_id(0)
    x = token_rows(where, own0, own3, sib)
    q = q_ref[...].astype(F32)
    inv = lax.rsqrt(jnp.sum(q * q, axis=-1, keepdims=True) + EPS_KEY)
    gk = total_of([gk_ref[m] for m in range(4)])
    gv = total_of([gv_ref[m] for m in range(4)])
    along = jnp.sum(q * gk, axis=-1, keepdims=True)
    gq = gq_ref[...] + gk * inv - q * (inv * inv * inv * along)
    rows = jnp.concatenate([gq.astype(BF), gv.astype(BF)], axis=1)
    back = dot_t(rows[:, :HEAD_DIM], wq_ref[...]) + dot_t(rows[:, HEAD_DIM:], wv_ref[...])

    low_core = where[3] == 0
    own_out[0] = jnp.where(low_core, back[:TOK], back[TOK:]).astype(BF)
    sib_out[0] = jnp.where(low_core, back[TOK:], back[:TOK]).astype(BF)
    centered = x - jnp.mean(x, axis=-1, keepdims=True)
    spread = jnp.mean(centered * centered, axis=-1, keepdims=True)
    xhat = centered * lax.rsqrt(spread + EPS_NORM)
    gain_part = jnp.sum((back * xhat).reshape(TOK // 4, 8, D), axis=0)
    shift_part = jnp.sum(back.reshape(TOK // 4, 8, D), axis=0)
    weight_part = t_dot(normed_ref[...], rows)

    @pl.when(step == 0)
    def _():
        total[:, :256] = weight_part
        sums[0:8, :] = gain_part
        sums[8:16, :] = shift_part

    @pl.when(step > 0)
    def _():
        total[:, :256] += weight_part
        sums[0:8, :] += gain_part
        sums[8:16, :] += shift_part

    @pl.when(step == 3)
    def _():
        gain_sum = jnp.sum(sums[0:8, :], axis=0, keepdims=True)
        shift_sum = jnp.sum(sums[8:16, :], axis=0, keepdims=True)
        both = jnp.where(iota((HEAD_DIM, D), 0) < 64, gain_sum, shift_sum)
        total[:, 256:] = jnp.transpose(both)
        for k, out in enumerate((wg0, wg1, wg2, wg3)):
            rows = pl.ds(pl.multiple_of(((where[0] + k) & 3) * 256, 256), 256)
            out[...] = total[rows, :].astype(BF)


def project_back(where, tokens, wq, wv, normed, q, gq, gk, gv):
    token_block = pl.BlockSpec((1, TOK, D), lambda i: (i, 0, 0))
    whole = lambda i: (0, 0)
    row_block = lambda width: pl.BlockSpec((2 * TOK, width), lambda i: (i, 0))
    return kernel_call(
        project_back_kernel,
        grid=(4,),
        in_specs=[SMEM] + token_specs()
        + [
            pl.BlockSpec((D, HEAD_DIM), whole),
            pl.BlockSpec((D, HEAD_DIM), whole),
            row_block(D),
            row_block(HEAD_DIM),
            row_block(HEAD_DIM),
        ]
        + [pl.BlockSpec((4, 2 * TOK, HEAD_DIM), lambda i: (0, i, 0))] * 2,
        out_specs=[token_block, token_block] + [pl.BlockSpec((256, 384), whole)] * 4,
        out_shape=[
            jax.ShapeDtypeStruct((4, TOK, D), BF),
            jax.ShapeDtypeStruct((4, TOK, D), BF),
        ]
        + [jax.ShapeDtypeStruct((256, 384), BF)] * 4,
        scratch_shapes=[pltpu.VMEM((D, 384), F32), pltpu.VMEM((16, D), F32)],
        compiler_params=params(30),
        cost_estimate=cost(8),
        far_in=(2, 3, 4, 5, 6, 7, 8),
        far_out=(0, 1, 2, 3, 4, 5),
        name="project_back",
    )(where, *tokens, wq, wv, normed, q, gq, gk, gv)


def normalized(values):
    centered = values - jnp.mean(values, axis=-1, keepdims=True)
    spread = jnp.mean(centered * centered, axis=-1, keepdims=True)
    scale = lax.rsqrt(spread + EPS_NORM)
    return centered * scale, scale


def norm_back(u, xhat, scale):
    mean_u = jnp.mean(u, axis=-1, keepdims=True)
    mean_ux = jnp.mean(u * xhat, axis=-1, keepdims=True)
    return (u - mean_u - xhat * mean_ux) * scale


def head_rows(w_ref, head):
    return w_ref[pl.ds(head * 8, 8)].reshape(HEAD_DIM, D)


def heads_of(where):
    for side in range(2):
        core = where[3] if side == 0 else 1 - where[3]
        for m in range(4):
            yield side, m, core * 4 + (where[1] + m) % 4


GELU_IN = 0.7978845608028654
GELU_CUBE = 0.044715


def feed_kernel(
    where, mix_own, mix_sib, first_own, first_sib, cot_own, cot_sib, par_ref, bias_ref,
    out_w, inner_ref, outer_ref,
    sum_ref, first_out, input_t_ref, active_ref, grad_ref, back_ref, hid_sum_ref, cot_sum_ref,
    ffn_in, cot_t, back_t,
):
    step = pl.program_id(0)

    @pl.when(step == 0)
    def _():
        total = chip_rows(where, first_own[...].astype(F32), first_sib[0].astype(F32))
        mixes = (mix_own, mix_sib)
        for side, m, head in heads_of(where):
            total = total + dot(mixes[side][:, m * 128 : m * 128 + 128], head_rows(out_w, head))
        sum_ref[...] = total
        own = jnp.where(where[3] == 0, total[:TOK], total[TOK:])
        first_out[...] = own.astype(BF)
        xhat, _ = normalized(total)
        rows = xhat * par_ref[0:1, :] + par_ref[1:2, :]
        ffn_in[...] = rows.astype(BF)
        input_t_ref[...] = jnp.transpose(rows).astype(BF)
        cot = chip_rows(where, cot_own[...].astype(F32), cot_sib[0].astype(F32))
        cot_t[...] = jnp.transpose(cot).astype(BF)
        cot_sum_ref[...] = jnp.broadcast_to(jnp.sum(cot, axis=0, keepdims=True), (8, D))

    inner = inner_ref[...].reshape(D, 512)
    outer = outer_ref[...].reshape(512, D)
    hidden = dot(ffn_in[...], inner) + bias_ref[0:1, :]
    square = hidden * hidden
    bent = jnp.tanh(GELU_IN * hidden * (1.0 + GELU_CUBE * square))
    half = 0.5 * (1.0 + bent)
    active_ref[...] = (hidden * half).astype(BF)
    slope = half + 0.5 * hidden * (1.0 - bent * bent) * GELU_IN * (
        1.0 + 3.0 * GELU_CUBE * square
    )
    grad_active = jnp.transpose(dot(outer, cot_t[...]))
    grad = (grad_active * slope).astype(BF)
    grad_ref[...] = grad
    hid_sum_ref[...] = jnp.broadcast_to(
        jnp.sum(grad.astype(F32), axis=0, keepdims=True), (8, 512)
    )
    part = dot(inner, jnp.transpose(grad))

    @pl.when(step == 0)
    def _():
        back_t[...] = part

    @pl.when(step > 0)
    def _():
        back_t[...] += part

    @pl.when(step == 3)
    def _():
        back_ref[...] = jnp.transpose(back_t[...])


def feed(where, mix_own, mix_sib, first_in, cot_second, sib_rows, par, bias, gathered):
    whole = lambda i: (0, 0)
    two = 2 * TOK
    return kernel_call(
        feed_kernel,
        grid=(4,),
        in_specs=[
            SMEM,
            pl.BlockSpec((two, 512), whole),
            pl.BlockSpec((two, 512), whole),
            pl.BlockSpec((TOK, D), whole),
            pl.BlockSpec((1, TOK, D), lambda i: (0, 0, 0)),
            pl.BlockSpec((TOK, D), whole),
            pl.BlockSpec((1, TOK, D), lambda i: (2, 0, 0)),
            pl.BlockSpec((8, D), whole),
            pl.BlockSpec((8, 512), lambda i: (0, i)),
            pl.BlockSpec((64, 16, D), lambda i: (0, 4, 0)),
            pl.BlockSpec((64, 16, 512), lambda i: (0, i // 2, i % 2)),
            pl.BlockSpec((16, 32, D), lambda i: (i, 1, 0)),
        ],
        out_specs=[
            pl.BlockSpec((two, D), whole),
            pl.BlockSpec((TOK, D), whole),
            pl.BlockSpec((D, two), whole),
            pl.BlockSpec((two, 512), lambda i: (0, i)),
            pl.BlockSpec((two, 512), lambda i: (0, i)),
            pl.BlockSpec((two, D), whole),
            pl.BlockSpec((8, 512), lambda i: (0, i)),
            pl.BlockSpec((8, D), whole),
        ],
        out_shape=[
            jax.ShapeDtypeStruct((two, D), F32),
            jax.ShapeDtypeStruct((TOK, D), BF),
            jax.ShapeDtypeStruct((D, two), BF),
            jax.ShapeDtypeStruct((two, 2048), BF),
            jax.ShapeDtypeStruct((two, 2048), BF),
            jax.ShapeDtypeStruct((two, D), F32),
            jax.ShapeDtypeStruct((8, 2048), F32),
            jax.ShapeDtypeStruct((8, D), F32),
        ],
        scratch_shapes=[
            pltpu.VMEM((two, D), BF),
            pltpu.VMEM((D, two), BF),
            pltpu.VMEM((D, two), F32),
        ],
        compiler_params=params(32),
        cost_estimate=cost(16),
        far_in=(4, 6, 9, 10, 11),
        far_out=(0, 2, 3, 4, 5),
        name="feed",
    )(
        where, mix_own, mix_sib, first_in, sib_rows, cot_second, sib_rows, par, bias,
        gathered, gathered, gathered,
    )


def first_back_kernel(
    where, back_own, back_sib, sum_ref, cot_own, cot_sib, par_ref, out_w,
    grad_first, branch_ref, m0, m1, m2, m3, sums_ref,
):
    back = back_own[...] + back_sib[...]
    xhat, scale = normalized(sum_ref[...])
    total = chip_rows(where, cot_own[...].astype(F32), cot_sib[0].astype(F32))
    total = total + norm_back(back * par_ref[0:1, :], xhat, scale)
    branch = total.astype(BF)
    branch_ref[...] = branch
    grad_first[...] = jnp.where(where[3] == 0, total[:TOK], total[TOK:]).astype(BF)
    outs = (m0, m1, m2, m3)
    for side, m, head in heads_of(where):
        if side == 0:
            outs[m][...] = dot_t(branch, head_rows(out_w, head)).astype(BF)
    gain = jnp.sum(back * xhat, axis=0, keepdims=True)
    shift = jnp.sum(back, axis=0, keepdims=True)
    sums_ref[...] = jnp.concatenate([gain, shift, jnp.zeros((6, D), F32)], axis=0)


def first_back(where, back_own, back_sib, first_sum, cot_first, sib_rows, par, gathered):
    two = 2 * TOK
    one = lambda shape: pl.BlockSpec(shape, lambda i: (0,) * len(shape))
    return kernel_call(
        first_back_kernel,
        grid=(1,),
        in_specs=[
            SMEM, one((two, D)), one((two, D)), one((two, D)), one((TOK, D)),
            pl.BlockSpec((1, TOK, D), lambda i: (1, 0, 0)),
            one((8, D)),
            pl.BlockSpec((64, 16, D), lambda i: (0, 4, 0)),
        ],
        out_specs=[one((TOK, D)), one((two, D))] + [one((two, 128))] * 4 + [one((8, D))],
        out_shape=[jax.ShapeDtypeStruct((TOK, D), BF), jax.ShapeDtypeStruct((two, D), BF)]
        + [jax.ShapeDtypeStruct((two, 128), BF)] * 4
        + [jax.ShapeDtypeStruct((8, D), F32)],
        compiler_params=params(24),
        cost_estimate=cost(6),
        far_in=(1, 3, 5, 7),
        far_out=(1,),
        name="first_back",
    )(where, back_own, back_sib, first_sum, cot_first, sib_rows, par, gathered)


def inner_grads_kernel(where, active_ref, grad_ref, input_t, cot_own, cot_sib, a0, a1, a2, a3, cot):
    step = pl.program_id(0)

    @pl.when(step == 0)
    def _():
        cot[...] = chip_rows(
            where, cot_own[:, :256].astype(F32), cot_sib[0, :, :256].astype(F32)
        ).astype(BF)

    lanes = pl.ds(pl.multiple_of(step * 512, 512), 512)
    outs = (a0, a1, a2, a3)
    inner = dot(input_t[...], grad_ref[...]).astype(BF).reshape(4, 16, 16, 512)
    outer = t_dot(active_ref[...], cot[...]).astype(BF).reshape(16, 32, 256)
    for k, out in enumerate(outs):
        for y in range(4):

            @pl.when(((y - where[0]) & 3) == k)
            def _(out=out, y=y):
                out[:, :, lanes] = inner[y]

        @pl.when(((step - where[0]) & 3) == k)
        def _(out=out):
            out[:, :, 2048:2304] = outer[:, :16]
            out[:, :, 2304:] = outer[:, 16:]


def inner_grads(where, active, grad, input_t, cot_second, sib_rows):
    two = 2 * TOK
    whole = lambda i: (0, 0)
    return kernel_call(
        inner_grads_kernel,
        grid=(4,),
        in_specs=[
            SMEM,
            pl.BlockSpec((two, 512), lambda i: (0, i)),
            pl.BlockSpec((two, 512), lambda i: (0, i)),
            pl.BlockSpec((D, two), whole),
            pl.BlockSpec((TOK, D), whole),
            pl.BlockSpec((1, TOK, D), lambda i: (2, 0, 0)),
        ],
        out_specs=[pl.BlockSpec((16, 16, 2560), lambda i: (0, 0, 0))] * 4,
        out_shape=[jax.ShapeDtypeStruct((16, 16, 2560), BF)] * 4,
        scratch_shapes=[pltpu.VMEM((two, 256), BF)],
        compiler_params=params(32),
        cost_estimate=cost(9),
        far_in=(1, 2, 3, 5),
        far_out=(0, 1, 2, 3),
        name="inner_grads",
    )(where, active, grad, input_t, cot_second, sib_rows)


def outer_grads_kernel(
    where, active_ref, cot_own, cot_sib, mix_own, mix_sib, branch_ref, sums_ref,
    b0, b1, b2, b3, cot,
):
    step = pl.program_id(0)
    outs = (b0, b1, b2, b3)

    @pl.when(step == 0)
    def _():
        cot[...] = chip_rows(
            where, cot_own[:, 256:].astype(F32), cot_sib[0, :, 256:].astype(F32)
        ).astype(BF)
        cols = jnp.where(
            where[3] == 0, branch_ref[:, :512].astype(F32), branch_ref[:, 512:].astype(F32)
        ).astype(BF)
        mixes = (mix_own, mix_sib)
        for side, m, head in heads_of(where):
            rows = t_dot(mixes[side][:, m * 128 : m * 128 + 128], cols).astype(BF)
            rows = rows.reshape(2, 4, 16, 512)
            at = pl.ds((head >> 1) * 4, 4)
            for part in range(2):
                near = (2 * (head & 1) + part - where[1]) & 3
                for k, out in enumerate(outs):

                    @pl.when(near == k)
                    def _(part=part, out=out, rows=rows, at=at):
                        out[at, 0:16, :256] = rows[part, :, :, :256]
                        out[at, 16:32, :256] = rows[part, :, :, 256:]

        for k, out in enumerate(outs):
            near = (where[1] + k) & 3
            for y in range(4):
                out[y * 4 : y * 4 + 4, 0:16, 256:384] = sums_ref[pl.ds(y * 16 + near * 4, 4)]
                out[y * 4 : y * 4 + 4, 16:32, 256:384] = jnp.zeros((4, 16, 128), BF)

    outer = t_dot(active_ref[...], cot[...]).astype(BF).reshape(4, 4, 32, 768)
    for z in range(4):
        for k, out in enumerate(outs):

            @pl.when(((z - where[1]) & 3) == k)
            def _(z=z, out=out):
                out[pl.ds(step * 4, 4), :, 384:] = outer[z]


def outer_grads(where, active, cot_second, sib_rows, mix_own, mix_sib, branch, sums):
    two = 2 * TOK
    whole = lambda i: (0, 0)
    whole3 = lambda i: (0, 0, 0)
    return kernel_call(
        outer_grads_kernel,
        grid=(4,),
        in_specs=[
            SMEM,
            pl.BlockSpec((two, 512), lambda i: (0, i)),
            pl.BlockSpec((TOK, D), whole),
            pl.BlockSpec((1, TOK, D), lambda i: (2, 0, 0)),
            pl.BlockSpec((two, 512), whole),
            pl.BlockSpec((two, 512), whole),
            pl.BlockSpec((two, D), whole),
            pl.BlockSpec((64, 16, 128), whole3),
        ],
        out_specs=[pl.BlockSpec((16, 32, 1152), whole3)] * 4,
        out_shape=[jax.ShapeDtypeStruct((16, 32, 1152), BF)] * 4,
        scratch_shapes=[pltpu.VMEM((two, 768), BF)],
        compiler_params=params(32),
        cost_estimate=cost(10),
        far_in=(1, 3, 5, 6),
        far_out=tuple(range(4)),
        name="outer_grads",
    )(where, active, cot_second, sib_rows, mix_own, mix_sib, branch, sums)


def second_kernel(where, active_ref, outer_ref, own_ref, give_ref, total):
    step = pl.program_id(0)
    part = dot(active_ref[...], outer_ref[...].reshape(512, D))

    @pl.when(step == 0)
    def _():
        total[...] = part

    @pl.when(step > 0)
    def _():
        total[...] += part

    @pl.when(step == 3)
    def _():
        low_core = where[3] == 0
        own_ref[...] = jnp.where(low_core, total[:TOK], total[TOK:])
        give_ref[...] = jnp.where(low_core, total[TOK:], total[:TOK])


def second_parts(where, active, gathered):
    two = 2 * TOK
    whole = lambda i: (0, 0)
    return kernel_call(
        second_kernel,
        grid=(4,),
        in_specs=[
            SMEM,
            pl.BlockSpec((two, 512), lambda i: (0, i)),
            pl.BlockSpec((16, 32, D), lambda i: (i, 1, 0)),
        ],
        out_specs=[pl.BlockSpec((TOK, D), whole)] * 2,
        out_shape=[jax.ShapeDtypeStruct((TOK, D), F32)] * 2,
        scratch_shapes=[pltpu.VMEM((two, D), F32)],
        compiler_params=params(20),
        cost_estimate=cost(4),
        far_in=(1, 2),
        name="second_parts",
    )(where, active, gathered)


def recut_kernel(axis, where, *refs):
    parts, outs = refs[:4], refs[4:]
    for k, out in enumerate(outs):
        mine = (where[axis] + k) & 3
        out[...] = total_of([part[mine] for part in parts]).astype(BF)


recut_a = whole_call(
    functools.partial(recut_kernel, 1), "recut_a", [((4, 16, 2560), BF)] * 4, 4, mib=32,
    far_in=(1,), far_out=(0, 1, 2, 3),
)
recut_b = whole_call(
    functools.partial(recut_kernel, 0), "recut_b", [((4, 32, 1152), BF)] * 4, 3, mib=24,
    far_in=(1,), far_out=(0, 1, 2, 3),
)


def join_kernel(where, *refs):
    w, a, b, outs = refs[:4], refs[4:8], refs[8:12], refs[12:]
    for k, out in enumerate(outs):
        x = (where[2] + k) & 3
        for z in range(4):
            rows = pl.ds(pl.multiple_of(z * 64 + x * 16, 16), 16)
            total = total_of([part[rows, :] for part in w]).astype(BF)
            for j in range(3):
                at = (z * 3 + j) * 16
                out[at : at + 16, :] = total[:, j * 128 : j * 128 + 128]
        total = total_of([part[x] for part in a]).astype(BF)
        for j in range(20):
            out[192 + j * 16 : 208 + j * 16, :] = total[:, j * 128 : j * 128 + 128]
        total = total_of([part[x] for part in b]).astype(BF)
        for j in range(9):
            out[512 + j * 32 : 544 + j * 32, :] = total[:, j * 128 : j * 128 + 128]


join = whole_call(join_kernel, "join", [((800, 128), BF)] * 4, 3)


def divide_kernel(where, x0, x1, x2, x3, w0, w1, w2, w3, keep_ref, give_ref, outer_ref, small_ref, total):
    low_core = where[3] == 0
    total[...] = total_of([part[...] for part in (x0, x1, x2, x3)])
    for k, out in enumerate((w0, w1, w2, w3)):
        z = (where[1] + k) & 3
        for j in range(3):
            rows = pl.ds(pl.multiple_of((z * 3 + j) * 16, 16), 16)
            out[:, j * 128 : j * 128 + 128] = total[rows, :].astype(BF)
    blocks = [total[192 + j * 16 : 208 + j * 16, :] for j in range(16)]
    for at in (512, 528):
        blocks += [total[at : at + 16, :], total[at + 32 : at + 48, :]]
    low = jnp.concatenate([block[:8] for block in blocks], axis=0)
    high = jnp.concatenate([block[8:] for block in blocks], axis=0)
    keep_ref[...] = jnp.where(low_core, low, high)
    give_ref[...] = jnp.where(low_core, high, low).astype(BF)
    for j in range(2):
        lanes = slice(j * 128, j * 128 + 128)
        outer_ref[:16, lanes] = total[448 + j * 16 : 464 + j * 16, :]
        outer_ref[16:, lanes] = total[480 + j * 16 : 496 + j * 16, :]
    for j in range(6):
        lanes = slice(256 + j * 128, 384 + j * 128)
        outer_ref[:, lanes] = total[608 + j * 32 : 640 + j * 32, :]
    small_ref[...] = total[576:584, :]


divide = whole_call(
    divide_kernel, "divide",
    [((16, 384), BF)] * 4 + [((160, 128), F32), ((160, 128), BF), ((32, D), F32), ((8, 128), F32)],
    2, scratch=[pltpu.VMEM((800, 128), F32)],
)


def last_kernel(where, w0, w1, w2, w3, give_ref, keep_w, out_ref, kept, given):
    low_core = where[3] == 0
    for m, piece in enumerate((w0, w1, w2, w3)):
        z = (where[1] + m) & 3
        rows = piece[...].astype(F32)
        mine = jnp.where(low_core, rows[:8], rows[8:])
        other = jnp.where(low_core, rows[8:], rows[:8])
        for j in range(3):
            at = pl.ds(pl.multiple_of((z * 3 + j) * 8, 8), 8)
            kept[at, :] = mine[:, j * 128 : j * 128 + 128]
            given[at, :] = other[:, j * 128 : j * 128 + 128]
    keep_w[...] = kept[...]
    out_ref[:96, :] = given[...].astype(BF)
    out_ref[96:, :] = give_ref[...]


last = whole_call(
    last_kernel, "last", [((96, 128), F32), ((256, 128), BF)], 1,
    scratch=[pltpu.VMEM((96, 128), F32)] * 2,
)


def finish_kernel(
    where, keep_w, keep_ref, got_ref, joint_ref, value_ref, norm_ref, inner_ref, output_ref
):
    low_core = where[3] == 0
    got = got_ref[...].astype(F32)
    mine, other = keep_w[...], got[:96]
    norm = jnp.zeros((8, 128), F32)
    for core in range(2):
        rows = jnp.where(low_core, *((mine, other) if core == 0 else (other, mine)))
        for z in range(4):
            lanes = slice((core * 4 + z) * 128, (core * 4 + z + 1) * 128)
            joint_ref[:, lanes] = rows[z * 24 : z * 24 + 8]
            value_ref[:, lanes] = rows[z * 24 + 8 : z * 24 + 16]
            norm = norm + rows[z * 24 + 16 : z * 24 + 24]
    norm_ref[...] = norm
    mine, other = keep_ref[...], got[96:]
    low, high = jnp.where(low_core, mine, other), jnp.where(low_core, other, mine)
    both = jnp.concatenate([low[:128], high[:128]], axis=1).astype(BF)
    dst, src = iota((256, 256), 1), iota((256, 256), 0)
    wanted = 128 * ((dst >> 5) & 1) + 32 * (dst >> 6) + (dst & 31)
    mixed = dot(both, (src == wanted).astype(F32).astype(BF))
    for t in range(16):
        inner_ref[:, t * 256 : (t + 1) * 256] = mixed[t * 8 : t * 8 + 8, :]
    for core, rows in enumerate((low, high)):
        for at, lane in enumerate((0, 128, 256, 384)):
            lanes = slice(core * 512 + lane, core * 512 + lane + 128)
            output_ref[:, lanes] = rows[128 + at * 8 : 136 + at * 8]


finish = whole_call(
    finish_kernel, "finish",
    [((8, D), F32), ((8, D), F32), ((8, 128), F32), ((8, FF), F32), ((8, D), F32)], 1,
)


def make_keys(pieces, rows_ref):
    for m, piece in enumerate(pieces):

        @pl.loop(0, 8, unroll=4)
        def _(s, m=m, piece=piece):
            rows = pl.ds(pl.multiple_of(s * TOK, TOK), TOK)
            to = pl.ds(pl.multiple_of(m * 8 * TOK + s * TOK, TOK), TOK)
            q = piece[rows, :].astype(F32)
            inv = lax.rsqrt(jnp.sum(q * q, axis=-1, keepdims=True) + EPS_KEY)
            rows_ref[to, :] = (q * inv).astype(BF)


def round_weights(lt_ref, at):
    totals = [lt_ref[r, at, :].astype(F32) for r in range(ROUNDS)]
    peak = jnp.maximum(jnp.maximum(totals[0], totals[1]), jnp.maximum(totals[2], totals[3]))
    exps = [jnp.exp(t - peak) for t in totals]
    scale = 1.0 / (exps[0] + exps[1] + exps[2] + exps[3])
    return [e * scale for e in exps]


def hot_slots(tgt_ref, source):
    slots = iota((BUCKETS * MOST, TOK), 0)
    return (slots == tgt_ref[0, pl.ds(source, 1), :]).astype(F32).astype(BF)


def hot_tokens(tgt_t_ref, source):
    slots = iota((TOK, BUCKETS * MOST), 1)
    return (slots == tgt_t_ref[0, :, source : source + 1]).astype(F32).astype(BF)


def spread(first, second):
    width = first.shape[-1]
    both = [a.reshape(PAIRS, 2, MOST, width) for a in (first, second)]
    return jnp.concatenate(both, axis=2).astype(BF)


def fill(tgt_ref, read_rows, ref):
    @pl.loop(0, 16, unroll=4)
    def _(pair):
        placed = [
            dot(hot_slots(tgt_ref, pair * 2 + half), read_rows(pair * 2 + half))
            for half in range(2)
        ]
        both = spread(*placed)
        at = pl.ds(pl.multiple_of(pair * 16, 16), 16)
        ref[0, :, at, :128] = both[:, 0]
        ref[0, :, at, 128:] = both[:, 1]


def place(both, ref, pair):
    at = pl.multiple_of(pair * 16, 16)
    ref[:, pl.ds(at, 16), :] = both[:, 0]
    ref[:, pl.ds(64 + at, 16), :] = both[:, 1]


def diagonal(rows):
    first = iota((128, 128), 0) < 64
    none = jnp.zeros((128, 128), BF)
    return jnp.concatenate([jnp.where(first, rows, none), jnp.where(first, none, rows)], axis=1)


def diagonal_t(rows):
    turned = jnp.transpose(rows)
    first = iota((128, 128), 1) < 64
    none = jnp.zeros((128, 128), BF)
    return jnp.concatenate([jnp.where(first, turned, none), jnp.where(first, none, turned)], axis=0)


def eye():
    return iota((128, 128), 0) == iota((128, 128), 1)


def token_block(s):
    return pl.ds(pl.multiple_of(s * TOK, TOK), TOK)


def scores_kernel(q0, q1, q2, q3, tgt_ref, mask_ref, probs_ref, keys_ref, qm_ref, log_ref, k_rows):
    @pl.when(pl.program_id(0) == 0)
    def _():
        make_keys((q0, q1, q2, q3), k_rows)

    fill(tgt_ref, lambda source: k_rows[token_block(source), :], keys_ref)

    @pl.loop(0, 4, unroll=4)
    def _(pair):
        placed = [
            dot(hot_slots(tgt_ref, pair * 2 + half), q0[token_block(pair * 2 + half), :])
            for half in range(2)
        ]
        place(spread(*placed), qm_ref.at[0], pair)

    @pl.loop(0, PAIRS, unroll=16)
    def _(p):
        code = mask_ref[0, p].astype(F32)
        scores = dot(keys_ref[0, p], diagonal_t(qm_ref[0, p]))
        scores = jnp.where(code == 0.0, scores, code * 1e4)
        peak = jnp.max(scores, axis=0, keepdims=True)
        exponent = jnp.exp(scores - peak)
        total = jnp.sum(exponent, axis=0, keepdims=True)
        probs_ref[0, p] = (exponent * (1.0 / total)).astype(BF)
        log_ref[0, pl.ds(p, 1), :] = peak + jnp.log(total)


def attend_scores(q_pieces, tgt, mask):
    rows = 8 * TOK
    outs = [(PAIRS, 256, 128), (PAIRS, 256, 256), (PAIRS, 128, 128), (PAIRS, 128)]
    types = [BF, BF, BF, F32]
    return kernel_call(
        scores_kernel,
        grid=(ROUNDS,),
        in_specs=[fixed((rows, HEAD_DIM))] * 4
        + [per_round((32, TOK)), per_round((PAIRS, 256, 128))],
        out_specs=[per_round(shape) for shape in outs],
        out_shape=[
            jax.ShapeDtypeStruct((ROUNDS,) + shape, t) for shape, t in zip(outs, types)
        ],
        scratch_shapes=[pltpu.VMEM((4 * rows, HEAD_DIM), BF)],
        compiler_params=params(20),
        cost_estimate=cost(18),
        far_in=(5,),
        far_out=(0, 1, 2),
        name="attend_scores",
    )(*q_pieces, tgt, mask)


def values_kernel(
    v0, v1, v2, v3, tgt_ref, tgt_t_ref, probs_ref, log_ref, mixed_ref, ro_ref, lt_ref, values_ref, att
):
    this_round = pl.program_id(0)
    for m, piece in enumerate((v0, v1, v2, v3)):

        @pl.loop(0, 4, unroll=4)
        def _(pair, m=m, piece=piece):
            placed = [
                dot(
                    hot_slots(tgt_ref, m * 8 + pair * 2 + half),
                    piece[token_block(pair * 2 + half), :],
                )
                for half in range(2)
            ]
            both = spread(*placed)
            at = pl.ds(pl.multiple_of((m * 4 + pair) * 16, 16), 16)
            values_ref[0, :, at, :128] = both[:, 0]
            values_ref[0, :, at, 128:] = both[:, 1]

    ones = jnp.ones((128, 128), BF)

    @pl.loop(0, PAIRS, unroll=16)
    def _(p):
        out = t_dot(probs_ref[0, p], values_ref[0, p])
        log_total = log_ref[0, pl.ds(p, 1), :]
        logs = dot(jnp.where(eye(), log_total, 0.0).astype(BF), ones)
        att[p, 0, :, :128] = out[:64, :128]
        att[p, 1, :, :128] = out[64:, 128:]
        att[p, 0, :, 128:] = logs[:64]
        att[p, 1, :, 128:] = logs[64:]

    for s in range(8):
        slots = att[:, :, s * MOST : (s + 1) * MOST, :].reshape(256, 256)
        rows = dot(hot_tokens(tgt_t_ref, s), slots.astype(BF)).astype(BF)
        ro_ref[this_round, s * TOK : (s + 1) * TOK, :] = rows[:, :HEAD_DIM]
        lt_ref[this_round, s * TOK : (s + 1) * TOK, :] = rows[:, HEAD_DIM:]

    @pl.when(this_round == ROUNDS - 1)
    def _():
        @pl.loop(0, 8)
        def _(s):
            at = token_block(s)
            weights = round_weights(lt_ref, at)
            mixed = weights[0] * ro_ref[0, at, :].astype(F32)
            for r in range(1, ROUNDS):
                mixed = mixed + weights[r] * ro_ref[r, at, :].astype(F32)
            mixed_ref[at, :] = mixed.astype(BF)


def attend_values(v_pieces, tgt, tgt_t, probs, logs):
    rows = 8 * TOK
    return kernel_call(
        values_kernel,
        grid=(ROUNDS,),
        in_specs=[fixed((rows, HEAD_DIM))] * 4
        + [
            per_round((32, TOK)), per_round((TOK, 128)), per_round((PAIRS, 256, 128)),
            per_round((PAIRS, 128)),
        ],
        out_specs=[
            fixed((rows, HEAD_DIM)),
            fixed((ROUNDS, rows, HEAD_DIM)),
            fixed((ROUNDS, rows, HEAD_DIM)),
            per_round((PAIRS, 256, 256)),
        ],
        out_shape=[
            jax.ShapeDtypeStruct((rows, HEAD_DIM), BF),
            jax.ShapeDtypeStruct((ROUNDS, rows, HEAD_DIM), BF),
            jax.ShapeDtypeStruct((ROUNDS, rows, HEAD_DIM), BF),
            jax.ShapeDtypeStruct((ROUNDS, PAIRS, 256, 256), BF),
        ],
        scratch_shapes=[pltpu.VMEM((PAIRS, 2, 64, 256), F32)],
        compiler_params=params(22),
        cost_estimate=cost(14),
        far_in=(6,),
        far_out=(1, 2, 3),
        name="attend_values",
    )(*v_pieces, tgt, tgt_t, probs, logs)


def take_slots(tgt_t_ref, slots_ref, rows_ref, sources):
    for s in range(sources):
        slots = slots_ref[:, :, s * MOST : (s + 1) * MOST, :].reshape(256, HEAD_DIM)
        rows_ref[s * TOK : (s + 1) * TOK, :] += dot(hot_tokens(tgt_t_ref, s), slots.astype(BF))


def values_back_kernel(
    where, tgt_ref, tgt_t_ref, probs_ref, ro_ref, lt_ref, gm_ref, out_ref, gd_ref, gt_ref, gt_slots, slots, rows, token_rows,
):
    this_round = pl.program_id(0)

    @pl.when(this_round == 0)
    def _():
        rows[...] = jnp.zeros_like(rows)

        @pl.loop(0, 8, unroll=2)
        def _(s):
            at = token_block(s)
            weights = round_weights(lt_ref, at)
            grad = gm_ref[at, :].astype(F32)
            agree = [
                jnp.sum(grad * ro_ref[r, at, :].astype(F32), axis=-1, keepdims=True)
                for r in range(ROUNDS)
            ]
            mean = total_of([weights[r] * agree[r] for r in range(ROUNDS)])
            for r in range(ROUNDS):
                token_rows[r, at, :HEAD_DIM] = (weights[r] * grad).astype(BF)
                token_rows[r, at, HEAD_DIM:] = (weights[r] * (agree[r] - mean)).astype(BF)

    @pl.loop(0, 4, unroll=4)
    def _(pair):
        placed = [
            dot(
                hot_slots(tgt_ref, pair * 2 + half),
                token_rows[this_round, token_block(pair * 2 + half), :],
            )
            for half in range(2)
        ]
        both = spread(*placed)
        place(both[..., :HEAD_DIM], gd_ref.at[0], pair)
        place(both[..., HEAD_DIM:], gt_slots, pair)

    @pl.loop(0, PAIRS, unroll=16)
    def _(p):
        grad_values = dot(probs_ref[0, p], diagonal(gd_ref[0, p]))
        slots[p, 0] = grad_values[:, :128]
        slots[p, 1] = grad_values[:, 128:]
        gt_ref[0, pl.ds(p, 1), :] = jnp.sum(
            jnp.where(eye(), gt_slots[p].astype(F32), 0.0), axis=0, keepdims=True
        )

    take_slots(tgt_t_ref, slots, rows, 32)

    @pl.when(this_round == ROUNDS - 1)
    def _():
        for m in range(4):
            out_ref[(where[2] + m) & 3] = rows[m * 8 * TOK : (m + 1) * 8 * TOK, :].astype(BF)


def attend_values_back(where, tgt, tgt_t, probs, ro, lt, gm):
    rows = 8 * TOK
    return kernel_call(
        values_back_kernel,
        grid=(ROUNDS,),
        in_specs=[
            SMEM,
            per_round((32, TOK)),
            per_round((TOK, 128)),
            per_round((PAIRS, 256, 128)),
            fixed((ROUNDS, rows, HEAD_DIM)),
            fixed((ROUNDS, rows, HEAD_DIM)),
            fixed((rows, HEAD_DIM)),
        ],
        out_specs=[
            fixed((4, rows, HEAD_DIM)), per_round((PAIRS, 128, 128)), per_round((PAIRS, 128)),
        ],
        out_shape=[
            jax.ShapeDtypeStruct((4, rows, HEAD_DIM), BF),
            jax.ShapeDtypeStruct((ROUNDS, PAIRS, 128, 128), BF),
            jax.ShapeDtypeStruct((ROUNDS, PAIRS, 128), F32),
        ],
        scratch_shapes=[
            pltpu.VMEM((PAIRS, 128, 128), BF),
            pltpu.VMEM((PAIRS, 2, 256, HEAD_DIM), F32),
            pltpu.VMEM((4 * rows, HEAD_DIM), F32),
            pltpu.VMEM((ROUNDS, rows, 256), BF),
        ],
        compiler_params=params(26),
        cost_estimate=cost(12),
        far_in=(1, 2, 3, 4, 5),
        far_out=(0, 1, 2),
        name="attend_values_back",
    )(where, tgt, tgt_t, probs, ro, lt, gm)


def scores_back_kernel(
    half, where, tgt_t_ref, mask_ref, probs_ref, values_ref, qm_ref, gd_ref, gt_ref, *refs
):
    if half == 0:
        gs_ref, rows_out, slots, rows = refs
    else:
        rows_in, gs_ref, out_ref, slots, rows = refs
    step = pl.program_id(0)

    @pl.when(step == 0)
    def _():
        if half == 0:
            rows[...] = jnp.zeros_like(rows)
        else:
            rows[...] = rows_in[...]

    @pl.loop(0, PAIRS, unroll=16)
    def _(p):
        probs = probs_ref[0, p].astype(F32)
        grad_probs = dot(values_ref[0, p], diagonal_t(gd_ref[0, p]))
        agreement = jnp.sum(probs * grad_probs, axis=0, keepdims=True)
        grad_scores = probs * (grad_probs + (gt_ref[0, pl.ds(p, 1), :] - agreement))
        seen = mask_ref[0, p].astype(F32) == 0.0
        grad_scores = jnp.where(seen, grad_scores, 0.0).astype(BF)
        gs_ref[0, p] = grad_scores
        grad_keys = dot(grad_scores, diagonal(qm_ref[0, p]))
        slots[p, 0] = grad_keys[:, :128]
        slots[p, 1] = grad_keys[:, 128:]

    take_slots(tgt_t_ref, slots, rows, 32)

    @pl.when(step == 1)
    def _():
        if half == 0:
            rows_out[...] = rows[...]
        else:
            for m in range(4):
                out_ref[(where[2] + m) & 3] = rows[m * 8 * TOK : (m + 1) * 8 * TOK, :].astype(BF)


def attend_scores_back(half, where, arrays, begun):
    rows = 8 * TOK
    shapes = [
        (TOK, 128), (PAIRS, 256, 128), (PAIRS, 256, 128), (PAIRS, 256, 256),
        (PAIRS, 128, 128), (PAIRS, 128, 128), (PAIRS, 128),
    ]
    this_half = lambda shape: pl.BlockSpec(
        (1,) + shape, lambda r: (2 * half + r,) + (0,) * len(shape)
    )
    slots = (PAIRS, 256, 128)
    if half == 0:
        outs = [((4 * rows, HEAD_DIM), F32)]
    else:
        outs = [((4, rows, HEAD_DIM), BF)]
    return kernel_call(
        functools.partial(scores_back_kernel, half),
        grid=(2,),
        in_specs=[SMEM] + [this_half(shape) for shape in shapes] + [fixed(a.shape) for a in begun],
        out_specs=[per_round(slots)] + [fixed(shape) for shape, _ in outs],
        out_shape=[jax.ShapeDtypeStruct((2,) + slots, BF)]
        + [jax.ShapeDtypeStruct(shape, t) for shape, t in outs],
        scratch_shapes=[
            pltpu.VMEM((PAIRS, 2, 256, HEAD_DIM), F32),
            pltpu.VMEM((4 * rows, HEAD_DIM), F32),
        ],
        compiler_params=params(30),
        cost_estimate=cost(10),
        far_in=tuple(range(1, 8)),
        far_out=(0,) if half == 0 else (0, 1),
        name=f"attend_scores_back_{half}",
    )(where, *arrays, *begun)


def queries_back_kernel(tgt_t_ref, first_ref, second_ref, keys_ref, gq_ref, slots):
    step = pl.program_id(0)

    @pl.when(step == 0)
    def _():
        gq_ref[...] = jnp.zeros_like(gq_ref)

    def one_round(gs_ref):
        @pl.loop(0, PAIRS, unroll=16)
        def _(p):
            grad_queries = t_dot(gs_ref[0, p], keys_ref[0, p])
            slots[p, 0] = grad_queries[:64, :128]
            slots[p, 1] = grad_queries[64:, 128:]

    @pl.when(step < 2)
    def _():
        one_round(first_ref)

    @pl.when(step >= 2)
    def _():
        one_round(second_ref)

    take_slots(tgt_t_ref, slots, gq_ref, 8)


def attend_queries_back(tgt_t, first, second, keys):
    rows, slots = 8 * TOK, (1, PAIRS, 256, 128)
    return kernel_call(
        queries_back_kernel,
        grid=(ROUNDS,),
        in_specs=[
            per_round((TOK, 128)),
            pl.BlockSpec(slots, lambda r: (jnp.minimum(r, 1), 0, 0, 0)),
            pl.BlockSpec(slots, lambda r: (jnp.maximum(r, 2) - 2, 0, 0, 0)),
            per_round((PAIRS, 256, 256)),
        ],
        out_specs=[fixed((rows, HEAD_DIM))],
        out_shape=[jax.ShapeDtypeStruct((rows, HEAD_DIM), F32)],
        scratch_shapes=[pltpu.VMEM((PAIRS, 2, 64, HEAD_DIM), F32)],
        compiler_params=params(20),
        cost_estimate=cost(8),
        far_in=(0, 1, 2, 3),
        far_out=(0,),
        name="attend_queries_back",
    )(tgt_t, first, second, keys)[0]


def local(
    first_in, second_in, attn_gain, attn_shift, w_joint, w_value, w_output, ffn_gain, ffn_shift,
    w_inner, b_inner, w_outer, b_outer, buckets, cot_first, cot_second,
):
    y, z, x, c = (lax.axis_index(a) for a in AXES)
    where = jnp.stack([y, z, x, c]).astype(jnp.int32)
    low_core = c == 0

    def by_core(first, second):
        return jnp.where(low_core, first, second)

    vec = jnp.concatenate(
        [attn_gain, attn_shift, ffn_gain, ffn_shift, b_outer, b_inner, jnp.zeros((56,), BF)]
    ).astype(F32)
    keep, give = pack(
        where, w_joint, w_value, w_output, w_inner, vec.reshape(1, 128), buckets[:, :, 0]
    )
    tok_near = [send(second_in, "z", 3), send(second_in, "z", 1)]
    got = swap(give)
    gathered = lax.all_gather(
        payload(where, keep, got, w_outer)[0], CHIPS, axis=0, tiled=False
    ).reshape(64, 80, D)
    y_got = gather(chip_message(where, keep, got)[0], "y")
    heads_out, second_late, tok_near = sync(
        head_messages(where, *y_got), second_in, tok_near
    )
    z_got = scatter(heads_out, "z")
    tok_last = send(second_late, "z", 2)
    z_got, tok_last = sync(z_got, tok_last)
    tok_far = jnp.stack([tok_near[0], tok_last, tok_near[1]])
    sib_tok = swap(jnp.concatenate([second_in[None], tok_far]))
    tokens = (second_in, tok_far, sib_tok)
    x_got = gather(jnp.concatenate(z_got), "x")
    wq, par, tgt, tgt_t, counts, vec = assemble(where, *x_got)

    normed, queries = project(where, tokens, par, wq)
    queries, counts, vec = sync(queries, counts, vec)
    q_pieces = gather(queries, "x")
    mask, par_ffn, bias_inner = make_mask(where, counts, vec)
    values, wv = project_values(where, x_got, normed)
    values, q_pieces[1], q_pieces[3], sib_rows = sync(
        values, q_pieces[1], q_pieces[3], jnp.stack([first_in, cot_first, cot_second])
    )
    v_pieces = gather(values, "x")
    sib_rows = swap(sib_rows)
    probs, key_slots, query_slots, logs = attend_scores(q_pieces, tgt, mask)
    mixed_head, round_out, round_total, value_slots = attend_values(
        v_pieces, tgt, tgt_t, probs, logs
    )

    mix_own = jnp.concatenate(
        scatter([mixed_head[k * 256 : (k + 1) * 256] for k in range(4)], "z"), axis=1
    )
    mix_sib = swap(mix_own)
    first_sum, first_out, input_t, active, grad_hidden, back, hid_sum, cot_sum = feed(
        where, mix_own, mix_sib, first_in, cot_second, sib_rows, par_ffn, bias_inner, gathered
    )
    a_parts = inner_grads(where, active, grad_hidden, input_t, cot_second, sib_rows)
    back_sib, a_parts = sync(swap(back), a_parts)
    grad_first, branch, g0, g1, g2, g3, norm_sums = first_back(
        where, back, back_sib, first_sum, cot_first, sib_rows, par_ffn, gathered
    )
    grad_mixed = scatter([g0, g1, g2, g3], "z")
    a_got = [send(a_parts[1], "y", 1), send(a_parts[3], "y", 3)]
    sums = jnp.stack([norm_sums[0], norm_sums[1], cot_sum[0]]).reshape(3, 64, 16)
    sums = jnp.pad(jnp.transpose(sums, (1, 0, 2)), ((0, 0), (0, 0), (0, 16)))
    sums = jnp.concatenate([sums, hid_sum[0].reshape(64, 1, 32)], axis=1).astype(BF)
    sums = jnp.pad(sums, ((0, 0), (0, 12), (0, 96)))
    b_parts = outer_grads(
        where, active, cot_second, sib_rows, mix_own, mix_sib, branch, sums
    )
    grad_mixed, b_parts = sync(grad_mixed, b_parts)

    b_got = [send(b_parts[1], "z", 1), send(b_parts[3], "z", 3)]
    gv, grad_slots, log_slots = attend_values_back(
        where, tgt, tgt_t, probs, round_out, round_total, jnp.concatenate(grad_mixed)
    )

    gv, grad_slots = sync(gv, grad_slots)
    gv_got = exchange(gv, "x")
    back_in = (tgt_t, mask, probs, value_slots, query_slots, grad_slots, log_slots)
    gs_first, half = attend_scores_back(0, where, back_in, ())
    a_got, b_got, a_far, b_far, half = sync(a_got, b_got, a_parts[2], b_parts[2], half)
    a_far, b_far = send(a_far, "y", 2), send(b_far, "z", 2)
    gs_second, gk = attend_scores_back(1, where, back_in, (half,))
    gv_got, gk, gs_second = sync(gv_got, gk, gs_second)

    gk_got = exchange(gk, "x")
    gq = attend_queries_back(tgt_t, gs_first, gs_second, key_slots)
    b_far, gq = sync(b_far, gq)
    b_parts = recut_b(
        where, *[part.reshape(4, 4, 32, 1152) for part in [b_parts[0], b_far] + b_got]
    )
    b_parts, a_far = sync(b_parts, a_far)
    b_got = scatter(b_parts, "y")
    a_parts = recut_a(
        where, *[part.reshape(4, 4, 16, 2560) for part in [a_parts[0], a_far] + a_got]
    )
    gk_got, a_parts = sync(gk_got, a_parts)

    a_got = scatter(a_parts, "z")
    back_own, back_give, *w_parts = project_back(
        where, tokens, wq, wv, normed, queries, gq, gk_got, gv_got
    )

    back_give, w_parts, b_got, a_got[1], a_got[3], active = sync(
        back_give, w_parts, b_got, a_got[1], a_got[3], active
    )
    second_own, second_give = second_parts(where, active, gathered)
    w_got = scatter(w_parts, "y")
    back_chip = (back_own.astype(F32) + swap(back_give).astype(F32)).astype(BF)
    back_parts = [back_chip[k] for k in range(4)]
    back_far = send(back_parts[2], "z", 2)
    back_parts, w_got, a_got, b_got, second_give = sync(
        back_parts, w_got, a_got, b_got, second_give
    )
    second_got = swap(second_give)


    x_parts = scatter(join(where, *w_got, *a_got, *b_got), "x")
    x_parts[1], back_parts, back_far = sync(x_parts[1], back_parts, back_far)
    back_sum = [
        back_parts[0], send(back_parts[1], "z", 1), send(back_parts[3], "z", 3), back_far
    ]

    second_out = (second_in.astype(F32) + second_own + second_got + par_ffn[2]).astype(BF)
    *z_parts, chip_keep, chip_give, grad_outer, small = divide(where, *x_parts)
    w_got = scatter(z_parts, "z")
    w_keep, last_give = last(where, *w_got, chip_give)
    grad_joint, grad_value, norm, grad_inner, grad_output = finish(
        where, w_keep, chip_keep, swap(last_give)
    )
    grad_attn_gain, grad_attn_shift = norm[:, 0], norm[:, 64]
    mine16 = by_core(small[:3, :8], small[:3, 8:16])
    grad_ffn_gain, grad_ffn_shift, grad_b_outer = mine16[0], mine16[1], mine16[2]
    grad_b_inner = small[3, :32]

    attn_xhat, attn_scale = normalized(second_in.astype(F32))
    attn_back = norm_back(total_of(back_sum) * par[0], attn_xhat, attn_scale)
    grad_second = (cot_second.astype(F32) + attn_back).astype(BF)

    return (
        first_out, second_out, grad_first, grad_second, grad_attn_gain, grad_attn_shift,
        grad_joint, grad_value, grad_output, grad_ffn_gain, grad_ffn_shift, grad_inner,
        grad_b_inner, grad_outer, grad_b_outer,
    )


def solution(mesh):
    chips = Mesh(mesh.devices.reshape(4, 4, 4, 2), AXES)
    rows, flat = P(AXES, None), P(AXES)
    return jax.shard_map(
        local,
        mesh=chips,
        in_specs=(
            rows, rows, flat, flat, rows, rows, rows, flat, flat, rows, flat, rows, flat,
            P(None, AXES, None), rows, rows,
        ),
        out_specs=(
            rows, rows, rows, rows, flat, flat, rows, rows, rows, flat, flat, rows, flat, rows,
            flat,
        ),
        check_vma=False,
    )
```

```python
import functools

import jax
import jax.numpy as jnp
from jax import lax
from jax.experimental import pallas as pl
from jax.experimental.pallas import tpu as pltpu
from jax.sharding import Mesh, PartitionSpec as P

HEADS = 8
HEAD_DIM = 128
ROUNDS = 4
BUCKETS = 32
MOST = 8
TOK = 128
D = 1024
FF = 4096

EPS_NORM = 1e-05
EPS_KEY = 1e-06
SELF_SCORE = -10000.0
MASKED_SCORE = -1000000000.0

BF = jnp.bfloat16
F32 = jnp.float32

AXES = ("y", "z", "x", "c")
CHIPS = ("y", "z", "x")


def send(piece, axis, k):
    return lax.ppermute(piece, axis, [(i, (i + k) % 4) for i in range(4)])


def swap(piece):
    return lax.ppermute(piece, "c", [(0, 1), (1, 0)])


def gather(piece, axis):
    back, front, far = send(piece, axis, 3), send(piece, axis, 1), send(piece, axis, 2)
    return [piece, back, far, front]


def scatter(pieces, axis):
    front, back, far = (
        send(pieces[1], axis, 1),
        send(pieces[3], axis, 3),
        send(pieces[2], axis, 2),
    )
    return [pieces[0], back, far, front]


def sync(*groups):
    return lax.optimization_barrier(groups)


def dot(a, b):
    return jnp.dot(a, b, preferred_element_type=F32)


def dot_t(a, b):
    return lax.dot_general(a, b, (((1,), (1,)), ((), ())), preferred_element_type=F32)


def t_dot(a, b):
    return lax.dot_general(a, b, (((0,), (0,)), ((), ())), preferred_element_type=F32)


def cost(us):
    return pl.CostEstimate(flops=int(us * 0.35e9), bytes_accessed=0, transcendentals=0)


def params(mib):
    return pltpu.CompilerParams(vmem_limit_bytes=mib * 1024 * 1024)


SMEM = pl.BlockSpec(memory_space=pltpu.SMEM)


def kernel_call(kernel, *, out_shape, far_in=(), far_out=(), **rest):
    inner = pl.pallas_call(
        kernel,
        out_shape=[
            pltpu.HBM(o.shape, o.dtype) if at in far_out else o for at, o in enumerate(out_shape)
        ],
        **rest,
    )

    def run(*arrays):
        return inner(
            *[
                pltpu.with_memory_space_constraint(a, pltpu.HBM) if at in far_in else a
                for at, a in enumerate(arrays)
            ]
        )

    return run


def iota(shape, dim):
    return lax.broadcasted_iota(jnp.int32, shape, dim)


def whole_call(kernel, name, outs, us, mib=16, scratch=(), far_in=(), far_out=()):
    def call(where, *arrays):
        return kernel_call(
            kernel,
            grid=(1,),
            in_specs=[SMEM] + [fixed(a.shape) for a in arrays],
            out_specs=[fixed(s) for s, _ in outs],
            out_shape=[jax.ShapeDtypeStruct(s, t) for s, t in outs],
            scratch_shapes=list(scratch),
            compiler_params=params(mib),
            cost_estimate=cost(us),
            far_in=far_in,
            far_out=far_out,
            name=name,
        )(where, *arrays)

    return call


def fixed(shape):
    return pl.BlockSpec(shape, lambda r: (0,) * len(shape))


def per_round(shape):
    return pl.BlockSpec((1,) + shape, lambda r: (r,) + (0,) * len(shape))


PAIRS = BUCKETS // 2


def exchange(stacked, axis):
    return lax.all_to_all(stacked, axis, split_axis=0, concat_axis=0, tiled=True)


def total_of(parts):
    total = parts[0].astype(F32)
    for extra in parts[1:]:
        total = total + extra.astype(F32)
    return total


def pack_kernel(
    where, joint_ref, value_ref, output_ref, inner_ref, vec_ref, bucket_ref,
    keep_ref, give_ref,
):
    low_core = where[3] == 0
    joint, value = joint_ref[...].astype(F32), value_ref[...].astype(F32)
    inner_rows = inner_ref[...].astype(F32)
    heads = []
    for core in range(2):
        rows = []
        for h in range(4):
            cols = slice((core * 4 + h) * 128, (core * 4 + h + 1) * 128)
            rows += [joint[:, cols], value[:, cols]]
        heads.append(jnp.concatenate(rows, axis=0))

    sub, along = iota((128, 128), 0), iota((128, 128), 1)
    targets, counts = [], []
    for r in range(ROUNDS):
        chosen = jnp.broadcast_to(bucket_ref[r : r + 1, :].astype(F32), (128, 128))
        column = jnp.sum(jnp.where(sub == along, chosen, 0.0), axis=1, keepdims=True)
        earlier = (column == chosen) & (sub < along)
        rank = jnp.sum(earlier.astype(F32), axis=0, keepdims=True)
        targets.append(chosen[0:1] * MOST + rank)
        counts.append(jnp.sum((column == along.astype(F32)).astype(F32), axis=0, keepdims=True))
    vec = jnp.concatenate([vec_ref[...], jnp.zeros((7, 128), F32)], axis=0)
    aux = jnp.concatenate([vec] + targets + counts, axis=0)
    keep_ref[:80, :] = jnp.concatenate([jnp.where(low_core, *heads), aux], axis=0).astype(BF)
    give_ref[:80, :] = jnp.concatenate([jnp.where(low_core, *heads[::-1]), aux], axis=0).astype(BF)

    chunks = [inner_rows[:, t * 256 : (t + 1) * 256] for t in range(16)]
    src, dst = iota((256, 256), 0), iota((256, 256), 1)
    wanted = 64 * ((dst % 128) // 32) + 32 * (dst // 128) + dst % 32
    picked = dot(jnp.concatenate(chunks, axis=0).astype(BF), (src == wanted).astype(F32).astype(BF))
    inner = []
    for core in range(2):
        halves = [
            jnp.concatenate(
                [
                    picked[t * 8 : (t + 1) * 8, core * 128 : (core + 1) * 128]
                    for t in range(half * 8, half * 8 + 8)
                ],
                axis=1,
            )
            for half in range(2)
        ]
        inner.append(jnp.concatenate(halves, axis=0))
    rest = jnp.concatenate([output_ref[...].astype(F32), jnp.zeros((8, D), F32)], axis=0)
    keep = jnp.concatenate([jnp.where(low_core, *inner), rest], axis=0).astype(BF)
    give = jnp.concatenate([jnp.where(low_core, *inner[::-1]), rest], axis=0).astype(BF)
    for j in range(8):
        lanes = slice(j * 128, j * 128 + 128)
        keep_ref[80 + j * 32 : 112 + j * 32, :] = keep[:, lanes]
        give_ref[80 + j * 32 : 112 + j * 32, :] = give[:, lanes]


pack = whole_call(
    pack_kernel, "pack", [((336, 128), BF)] * 2, 3, far_in=(1, 2, 3, 4, 6)
)


def chip_message_kernel(where, keep_ref, got_ref, out_ref):
    low_core = where[3] == 0
    keep, got = keep_ref[:80, :].astype(F32), got_ref[:80, :].astype(F32)
    first, second = jnp.where(low_core, keep, got), jnp.where(low_core, got, keep)
    rows = []
    for at in (0, 16, 32, 48, 8, 24, 40, 56, 64, 72):
        rows += [first[at : at + 8], second[at : at + 8]]
    out_ref[...] = jnp.concatenate(rows, axis=0).astype(BF)


chip_message = whole_call(chip_message_kernel, "chip_message", [((160, 128), BF)], 1)


def head_messages_kernel(where, y0, y1, y2, y3, *outs):
    pieces = (y0, y1, y2, y3)
    vec = []
    for piece in pieces:
        rows = piece[128:144, :].astype(F32)
        vec += [rows[0:1], rows[8:9]]
    vec = jnp.concatenate(vec + [jnp.zeros((8, 128), F32)], axis=0).astype(BF)
    for k in range(4):
        head = (where[1] + k) & 3
        q_rows = pl.ds(pl.multiple_of(head * 16, 16), 16)
        v_rows = pl.ds(pl.multiple_of(64 + head * 16, 16), 16)
        for n, piece in enumerate(pieces):
            outs[k][n * 16 : n * 16 + 16, :] = piece[q_rows, :]
            outs[k][96 + n * 16 : 112 + n * 16, :] = piece[v_rows, :]
        outs[k][64:80, :] = vec
        outs[k][80:96, :] = y0[144:160, :]


head_messages = whole_call(
    head_messages_kernel, "head_messages", [((160, 128), BF)] * 4, 1
)


def payload_kernel(where, keep_ref, got_ref, outer_ref, out_ref):
    low_core = where[3] == 0
    for j in range(8):
        lanes = slice(j * 128, j * 128 + 128)
        block = slice(80 + j * 32, 112 + j * 32)
        keep, got = keep_ref[block, :].astype(F32), got_ref[block, :].astype(F32)
        first, second = jnp.where(low_core, keep, got), jnp.where(low_core, got, keep)
        for at, to in ((0, 0), (8, 16), (16, 64)):
            out_ref[to : to + 16, lanes] = jnp.concatenate(
                [first[at : at + 8], second[at : at + 8]], axis=0
            ).astype(BF)
    out_ref[32:64, :] = outer_ref[...]


payload = whole_call(payload_kernel, "payload", [((80, D), BF)], 1)


def by_rows(where, pieces, ref):
    for m, rows in enumerate(pieces):
        for n in range(4):
            for k in range(4):
                chip = ((where[0] + n) % 4 * 4 + (where[1] + k) % 4) * 4 + (where[2] + m) % 4
                ref[pl.ds(pl.multiple_of(chip * 16, 16), 16), :] = rows(k, n)


def device_of(where, shape):
    row = iota(shape, 0)
    x, z, y = (where[2] + (row >> 5)) & 3, (where[1] + (row >> 3)) & 3, (where[0] + (row >> 1)) & 3
    return ((y * 4 + z) * 4 + x) * 2 + (row & 1)


def parameter(where, vec, v):
    shape = (128, D)
    lane = iota(shape, 1)
    picked = dot(vec, (iota(shape, 0) == 8 * v + (lane & 7)).astype(F32).astype(BF))
    mine = device_of(where, shape) == (lane >> 3)
    return jnp.sum(jnp.where(mine, picked, 0.0), axis=0, keepdims=True)


def assemble_kernel(where, x0, x1, x2, x3, w_ref, par_ref, tgt_ref, tgt_t_ref, count_ref, vec_ref):
    pieces = (x0, x1, x2, x3)
    by_rows(
        where,
        [
            lambda k, n, piece=piece: piece[k * 160 + n * 16 : k * 160 + n * 16 + 16, :]
            for piece in pieces
        ],
        w_ref,
    )
    vec = jnp.concatenate(
        [
            piece[k * 160 + 64 : k * 160 + 80, :].astype(F32)[:8]
            for piece in pieces
            for k in range(4)
        ],
        axis=0,
    ).astype(BF)
    vec_ref[...] = vec
    par_ref[...] = jnp.concatenate(
        [parameter(where, vec, 0), parameter(where, vec, 1), jnp.zeros((6, D), F32)], axis=0
    )
    empty = jnp.zeros((96, 128), F32)
    slots = [
        jnp.concatenate(
            [piece[k * 160 + 80 : k * 160 + 96, :] for k in range(4)], axis=0
        ).astype(F32)
        for piece in pieces
    ]
    for r in range(ROUNDS):
        rows = jnp.concatenate(
            [slots[m][s * 8 + r : s * 8 + r + 1] for m in range(4) for s in range(8)], axis=0
        )
        tgt_ref[r] = rows.astype(jnp.int32)
        tgt_t_ref[r] = jnp.transpose(jnp.concatenate([rows, empty], axis=0)).astype(jnp.int32)
        count_ref[r] = jnp.concatenate(
            [slots[m][s * 8 + 4 + r : s * 8 + 5 + r] for m in range(4) for s in range(8)], axis=0
        )


assemble = whole_call(
    assemble_kernel, "assemble",
    [
        ((D, 128), BF), ((8, D), F32), ((ROUNDS, 32, 128), jnp.int32),
        ((ROUNDS, 128, 128), jnp.int32), ((ROUNDS, 32, 128), F32), ((128, 128), BF),
    ],
    2, far_out=(2, 3),
)


def mask_kernel(where, count_ref, vec_ref, mask_ref, par_ref, bias_ref):
    z, x, c = where[1], where[2], where[3]

    @pl.when(pl.program_id(0) == 0)
    def _():
        vec = vec_ref[...]
        par_ref[...] = jnp.concatenate(
            [parameter(where, vec, v) for v in (2, 3, 4)] + [jnp.zeros((5, D), F32)], axis=0
        )
        wide = (128, 2048)
        lane = iota(wide, 1)
        picked = dot(vec, (iota(wide, 0) == 40 + (lane & 31)).astype(F32).astype(BF))
        mine = device_of(where, wide) == 2 * (lane >> 5) + c
        bias = jnp.sum(jnp.where(mine, picked, 0.0), axis=0, keepdims=True)
        bias_ref[...] = jnp.broadcast_to(bias, (8, 2048))

    shape = (256, 128)
    row, lane = iota(shape, 0), iota(shape, 1)
    source, rank = row >> 3, row & 7
    of_chip = lambda z_of, x_of, core: ((z_of & 3) * 8 + (x_of & 3) * 2 + core) * 8
    kpos = of_chip(z + ((source >> 1) & 3), x + (source >> 3), source & 1) + rank
    asker = (lane >> 3) & 7
    qpos = of_chip(z + (asker >> 1), x, asker & 1) + (lane & 7)
    code = jnp.where(kpos == qpos, -1.0, jnp.where(kpos < qpos, 0.0, -1e5))
    rank_f = rank.astype(F32)
    expand = (iota((256, 32), 0) >> 3) == iota((256, 32), 1)
    by_slot = dot(expand.astype(F32).astype(BF), count_ref[0].astype(BF)).astype(BF)
    bucket, side = iota((128, 128), 0), iota((128, 128), 1) >> 6

    @pl.loop(0, PAIRS, unroll=4)
    def _(p):
        select = (bucket == 2 * p + side).astype(F32).astype(BF)
        live = rank_f < dot(by_slot, select)
        mask_ref[0, p] = jnp.where(live, code, -1e5).astype(BF)


def make_mask(where, counts, vec):
    return kernel_call(
        mask_kernel,
        grid=(ROUNDS,),
        in_specs=[SMEM, per_round((32, 128)), fixed((128, 128))],
        out_specs=[per_round((PAIRS, 256, 128)), fixed((8, D)), fixed((8, 2048))],
        out_shape=[
            jax.ShapeDtypeStruct((ROUNDS, PAIRS, 256, 128), BF),
            jax.ShapeDtypeStruct((8, D), F32),
            jax.ShapeDtypeStruct((8, 2048), F32),
        ],
        far_out=(0,),
        compiler_params=params(16),
        cost_estimate=cost(7),
        name="make_mask",
    )(where, counts, vec)


def chip_rows(where, own, sib):
    low_core = where[3] == 0
    return jnp.concatenate([jnp.where(low_core, own, sib), jnp.where(low_core, sib, own)], axis=0)


def token_rows(where, own0, own3, sib):
    near = pl.program_id(0) == 0
    own = jnp.where(near, own0[...].astype(F32), own3[0].astype(F32))
    return chip_rows(where, own, sib[0].astype(F32))


def token_specs():
    return [
        pl.BlockSpec((TOK, D), lambda i: (0, 0)),
        pl.BlockSpec((1, TOK, D), lambda i: (jnp.maximum(i - 1, 0), 0, 0)),
        pl.BlockSpec((1, TOK, D), lambda i: (i, 0, 0)),
    ]


def project_kernel(where, own0, own3, sib, par_ref, w_ref, normed_ref, q_ref):
    rows = token_rows(where, own0, own3, sib)
    centered = rows - jnp.mean(rows, axis=-1, keepdims=True)
    spread = jnp.mean(centered * centered, axis=-1, keepdims=True)
    normed = centered * lax.rsqrt(spread + EPS_NORM) * par_ref[0:1, :] + par_ref[1:2, :]
    normed = normed.astype(BF)
    normed_ref[...] = normed
    q_ref[...] = dot(normed, w_ref[...]).astype(BF)


def project(where, tokens, par, w):
    whole = lambda i: (0, 0)
    return kernel_call(
        project_kernel,
        grid=(4,),
        in_specs=[SMEM] + token_specs()
        + [pl.BlockSpec((8, D), whole), pl.BlockSpec((D, HEAD_DIM), whole)],
        out_specs=[
            pl.BlockSpec((2 * TOK, D), lambda i: (i, 0)),
            pl.BlockSpec((2 * TOK, HEAD_DIM), lambda i: (i, 0)),
        ],
        out_shape=[
            jax.ShapeDtypeStruct((8 * TOK, D), BF),
            jax.ShapeDtypeStruct((8 * TOK, HEAD_DIM), BF),
        ],
        compiler_params=params(20),
        cost_estimate=cost(4),
        far_out=(0,),
        name="project",
    )(where, *tokens, par, w)


def project_values_kernel(where, x0, x1, x2, x3, normed_ref, v_ref, w_ref):
    @pl.when(pl.program_id(0) == 0)
    def _():
        by_rows(
            where,
            [
                lambda k, n, piece=piece: piece[k * 160 + n * 16 + 96 : k * 160 + n * 16 + 112, :]
                for piece in (x0, x1, x2, x3)
            ],
            w_ref,
        )

    v_ref[...] = dot(normed_ref[...], w_ref[...]).astype(BF)


def project_values(where, pieces, normed):
    return kernel_call(
        project_values_kernel,
        grid=(4,),
        in_specs=[SMEM] + [fixed(p.shape) for p in pieces]
        + [pl.BlockSpec((2 * TOK, D), lambda i: (i, 0))],
        out_specs=[
            pl.BlockSpec((2 * TOK, HEAD_DIM), lambda i: (i, 0)), fixed((D, HEAD_DIM)),
        ],
        out_shape=[
            jax.ShapeDtypeStruct((8 * TOK, HEAD_DIM), BF),
            jax.ShapeDtypeStruct((D, HEAD_DIM), BF),
        ],
        compiler_params=params(16),
        cost_estimate=cost(3),
        far_in=(5,),
        name="project_values",
    )(where, *pieces, normed)


def project_back_kernel(
    where, own0, own3, sib, wq_ref, wv_ref, normed_ref, q_ref, gq_ref,
    gk_ref, gv_ref, own_out, sib_out, wg0, wg1, wg2, wg3, total, sums,
):
    step = pl.program_id(0)
    x = token_rows(where, own0, own3, sib)
    q = q_ref[...].astype(F32)
    inv = lax.rsqrt(jnp.sum(q * q, axis=-1, keepdims=True) + EPS_KEY)
    gk = total_of([gk_ref[m] for m in range(4)])
    gv = total_of([gv_ref[m] for m in range(4)])
    along = jnp.sum(q * gk, axis=-1, keepdims=True)
    gq = gq_ref[...] + gk * inv - q * (inv * inv * inv * along)
    rows = jnp.concatenate([gq.astype(BF), gv.astype(BF)], axis=1)
    back = dot_t(rows[:, :HEAD_DIM], wq_ref[...]) + dot_t(rows[:, HEAD_DIM:], wv_ref[...])

    low_core = where[3] == 0
    own_out[0] = jnp.where(low_core, back[:TOK], back[TOK:]).astype(BF)
    sib_out[0] = jnp.where(low_core, back[TOK:], back[:TOK]).astype(BF)
    centered = x - jnp.mean(x, axis=-1, keepdims=True)
    spread = jnp.mean(centered * centered, axis=-1, keepdims=True)
    xhat = centered * lax.rsqrt(spread + EPS_NORM)
    gain_part = jnp.sum((back * xhat).reshape(TOK // 4, 8, D), axis=0)
    shift_part = jnp.sum(back.reshape(TOK // 4, 8, D), axis=0)
    weight_part = t_dot(normed_ref[...], rows)

    @pl.when(step == 0)
    def _():
        total[:, :256] = weight_part
        sums[0:8, :] = gain_part
        sums[8:16, :] = shift_part

    @pl.when(step > 0)
    def _():
        total[:, :256] += weight_part
        sums[0:8, :] += gain_part
        sums[8:16, :] += shift_part

    @pl.when(step == 3)
    def _():
        gain_sum = jnp.sum(sums[0:8, :], axis=0, keepdims=True)
        shift_sum = jnp.sum(sums[8:16, :], axis=0, keepdims=True)
        both = jnp.where(iota((HEAD_DIM, D), 0) < 64, gain_sum, shift_sum)
        total[:, 256:] = jnp.transpose(both)
        for k, out in enumerate((wg0, wg1, wg2, wg3)):
            rows = pl.ds(pl.multiple_of(((where[0] + k) & 3) * 256, 256), 256)
            out[...] = total[rows, :].astype(BF)


def project_back(where, tokens, wq, wv, normed, q, gq, gk, gv):
    token_block = pl.BlockSpec((1, TOK, D), lambda i: (i, 0, 0))
    whole = lambda i: (0, 0)
    row_block = lambda width: pl.BlockSpec((2 * TOK, width), lambda i: (i, 0))
    return kernel_call(
        project_back_kernel,
        grid=(4,),
        in_specs=[SMEM] + token_specs()
        + [
            pl.BlockSpec((D, HEAD_DIM), whole),
            pl.BlockSpec((D, HEAD_DIM), whole),
            row_block(D),
            row_block(HEAD_DIM),
            row_block(HEAD_DIM),
        ]
        + [pl.BlockSpec((4, 2 * TOK, HEAD_DIM), lambda i: (0, i, 0))] * 2,
        out_specs=[token_block, token_block] + [pl.BlockSpec((256, 384), whole)] * 4,
        out_shape=[
            jax.ShapeDtypeStruct((4, TOK, D), BF),
            jax.ShapeDtypeStruct((4, TOK, D), BF),
        ]
        + [jax.ShapeDtypeStruct((256, 384), BF)] * 4,
        scratch_shapes=[pltpu.VMEM((D, 384), F32), pltpu.VMEM((16, D), F32)],
        compiler_params=params(30),
        cost_estimate=cost(8),
        far_in=(2, 3, 4, 5, 6, 7, 8),
        far_out=(0, 1, 2, 3, 4, 5),
        name="project_back",
    )(where, *tokens, wq, wv, normed, q, gq, gk, gv)


def normalized(values):
    centered = values - jnp.mean(values, axis=-1, keepdims=True)
    spread = jnp.mean(centered * centered, axis=-1, keepdims=True)
    scale = lax.rsqrt(spread + EPS_NORM)
    return centered * scale, scale


def norm_back(u, xhat, scale):
    mean_u = jnp.mean(u, axis=-1, keepdims=True)
    mean_ux = jnp.mean(u * xhat, axis=-1, keepdims=True)
    return (u - mean_u - xhat * mean_ux) * scale


def head_rows(w_ref, head):
    return w_ref[pl.ds(head * 8, 8)].reshape(HEAD_DIM, D)


def heads_of(where):
    for side in range(2):
        core = where[3] if side == 0 else 1 - where[3]
        for m in range(4):
            yield side, m, core * 4 + (where[1] + m) % 4


GELU_IN = 0.7978845608028654
GELU_CUBE = 0.044715


def feed_kernel(
    where, mix_own, mix_sib, first_own, first_sib, cot_own, cot_sib, par_ref, bias_ref,
    out_w, inner_ref, outer_ref,
    sum_ref, first_out, input_t_ref, active_ref, grad_ref, back_ref, hid_sum_ref, cot_sum_ref,
    ffn_in, cot_t, back_t,
):
    step = pl.program_id(0)

    @pl.when(step == 0)
    def _():
        total = chip_rows(where, first_own[...].astype(F32), first_sib[0].astype(F32))
        mixes = (mix_own, mix_sib)
        for side, m, head in heads_of(where):
            total = total + dot(mixes[side][:, m * 128 : m * 128 + 128], head_rows(out_w, head))
        sum_ref[...] = total
        own = jnp.where(where[3] == 0, total[:TOK], total[TOK:])
        first_out[...] = own.astype(BF)
        xhat, _ = normalized(total)
        rows = xhat * par_ref[0:1, :] + par_ref[1:2, :]
        ffn_in[...] = rows.astype(BF)
        input_t_ref[...] = jnp.transpose(rows).astype(BF)
        cot = chip_rows(where, cot_own[...].astype(F32), cot_sib[0].astype(F32))
        cot_t[...] = jnp.transpose(cot).astype(BF)
        cot_sum_ref[...] = jnp.broadcast_to(jnp.sum(cot, axis=0, keepdims=True), (8, D))

    inner = inner_ref[...].reshape(D, 512)
    outer = outer_ref[...].reshape(512, D)
    hidden = dot(ffn_in[...], inner) + bias_ref[0:1, :]
    square = hidden * hidden
    bent = jnp.tanh(GELU_IN * hidden * (1.0 + GELU_CUBE * square))
    half = 0.5 * (1.0 + bent)
    active_ref[...] = (hidden * half).astype(BF)
    slope = half + 0.5 * hidden * (1.0 - bent * bent) * GELU_IN * (
        1.0 + 3.0 * GELU_CUBE * square
    )
    grad_active = jnp.transpose(dot(outer, cot_t[...]))
    grad = (grad_active * slope).astype(BF)
    grad_ref[...] = grad
    hid_sum_ref[...] = jnp.broadcast_to(
        jnp.sum(grad.astype(F32), axis=0, keepdims=True), (8, 512)
    )
    part = dot(inner, jnp.transpose(grad))

    @pl.when(step == 0)
    def _():
        back_t[...] = part

    @pl.when(step > 0)
    def _():
        back_t[...] += part

    @pl.when(step == 3)
    def _():
        back_ref[...] = jnp.transpose(back_t[...])


def feed(where, mix_own, mix_sib, first_in, cot_second, sib_rows, par, bias, gathered):
    whole = lambda i: (0, 0)
    two = 2 * TOK
    return kernel_call(
        feed_kernel,
        grid=(4,),
        in_specs=[
            SMEM,
            pl.BlockSpec((two, 512), whole),
            pl.BlockSpec((two, 512), whole),
            pl.BlockSpec((TOK, D), whole),
            pl.BlockSpec((1, TOK, D), lambda i: (0, 0, 0)),
            pl.BlockSpec((TOK, D), whole),
            pl.BlockSpec((1, TOK, D), lambda i: (2, 0, 0)),
            pl.BlockSpec((8, D), whole),
            pl.BlockSpec((8, 512), lambda i: (0, i)),
            pl.BlockSpec((64, 16, D), lambda i: (0, 4, 0)),
            pl.BlockSpec((64, 16, 512), lambda i: (0, i // 2, i % 2)),
            pl.BlockSpec((16, 32, D), lambda i: (i, 1, 0)),
        ],
        out_specs=[
            pl.BlockSpec((two, D), whole),
            pl.BlockSpec((TOK, D), whole),
            pl.BlockSpec((D, two), whole),
            pl.BlockSpec((two, 512), lambda i: (0, i)),
            pl.BlockSpec((two, 512), lambda i: (0, i)),
            pl.BlockSpec((two, D), whole),
            pl.BlockSpec((8, 512), lambda i: (0, i)),
            pl.BlockSpec((8, D), whole),
        ],
        out_shape=[
            jax.ShapeDtypeStruct((two, D), F32),
            jax.ShapeDtypeStruct((TOK, D), BF),
            jax.ShapeDtypeStruct((D, two), BF),
            jax.ShapeDtypeStruct((two, 2048), BF),
            jax.ShapeDtypeStruct((two, 2048), BF),
            jax.ShapeDtypeStruct((two, D), F32),
            jax.ShapeDtypeStruct((8, 2048), F32),
            jax.ShapeDtypeStruct((8, D), F32),
        ],
        scratch_shapes=[
            pltpu.VMEM((two, D), BF),
            pltpu.VMEM((D, two), BF),
            pltpu.VMEM((D, two), F32),
        ],
        compiler_params=params(32),
        cost_estimate=cost(16),
        far_in=(4, 6, 9, 10, 11),
        far_out=(0, 2, 3, 4, 5),
        name="feed",
    )(
        where, mix_own, mix_sib, first_in, sib_rows, cot_second, sib_rows, par, bias,
        gathered, gathered, gathered,
    )


def first_back_kernel(
    where, back_own, back_sib, sum_ref, cot_own, cot_sib, par_ref, out_w,
    grad_first, branch_ref, m0, m1, m2, m3, sums_ref,
):
    back = back_own[...] + back_sib[...]
    xhat, scale = normalized(sum_ref[...])
    total = chip_rows(where, cot_own[...].astype(F32), cot_sib[0].astype(F32))
    total = total + norm_back(back * par_ref[0:1, :], xhat, scale)
    branch = total.astype(BF)
    branch_ref[...] = branch
    grad_first[...] = jnp.where(where[3] == 0, total[:TOK], total[TOK:]).astype(BF)
    outs = (m0, m1, m2, m3)
    for side, m, head in heads_of(where):
        if side == 0:
            outs[m][...] = dot_t(branch, head_rows(out_w, head)).astype(BF)
    gain = jnp.sum(back * xhat, axis=0, keepdims=True)
    shift = jnp.sum(back, axis=0, keepdims=True)
    sums_ref[...] = jnp.concatenate([gain, shift, jnp.zeros((6, D), F32)], axis=0)


def first_back(where, back_own, back_sib, first_sum, cot_first, sib_rows, par, gathered):
    two = 2 * TOK
    one = lambda shape: pl.BlockSpec(shape, lambda i: (0,) * len(shape))
    return kernel_call(
        first_back_kernel,
        grid=(1,),
        in_specs=[
            SMEM, one((two, D)), one((two, D)), one((two, D)), one((TOK, D)),
            pl.BlockSpec((1, TOK, D), lambda i: (1, 0, 0)),
            one((8, D)),
            pl.BlockSpec((64, 16, D), lambda i: (0, 4, 0)),
        ],
        out_specs=[one((TOK, D)), one((two, D))] + [one((two, 128))] * 4 + [one((8, D))],
        out_shape=[jax.ShapeDtypeStruct((TOK, D), BF), jax.ShapeDtypeStruct((two, D), BF)]
        + [jax.ShapeDtypeStruct((two, 128), BF)] * 4
        + [jax.ShapeDtypeStruct((8, D), F32)],
        compiler_params=params(24),
        cost_estimate=cost(6),
        far_in=(1, 3, 5, 7),
        far_out=(1,),
        name="first_back",
    )(where, back_own, back_sib, first_sum, cot_first, sib_rows, par, gathered)


def inner_grads_kernel(where, active_ref, grad_ref, input_t, cot_own, cot_sib, a0, a1, a2, a3, cot):
    step = pl.program_id(0)

    @pl.when(step == 0)
    def _():
        cot[...] = chip_rows(
            where, cot_own[:, :256].astype(F32), cot_sib[0, :, :256].astype(F32)
        ).astype(BF)

    lanes = pl.ds(pl.multiple_of(step * 512, 512), 512)
    outs = (a0, a1, a2, a3)
    inner = dot(input_t[...], grad_ref[...]).astype(BF).reshape(4, 16, 16, 512)
    outer = t_dot(active_ref[...], cot[...]).astype(BF).reshape(16, 32, 256)
    for k, out in enumerate(outs):
        for y in range(4):

            @pl.when(((y - where[0]) & 3) == k)
            def _(out=out, y=y):
                out[:, :, lanes] = inner[y]

        @pl.when(((step - where[0]) & 3) == k)
        def _(out=out):
            out[:, :, 2048:2304] = outer[:, :16]
            out[:, :, 2304:] = outer[:, 16:]


def inner_grads(where, active, grad, input_t, cot_second, sib_rows):
    two = 2 * TOK
    whole = lambda i: (0, 0)
    return kernel_call(
        inner_grads_kernel,
        grid=(4,),
        in_specs=[
            SMEM,
            pl.BlockSpec((two, 512), lambda i: (0, i)),
            pl.BlockSpec((two, 512), lambda i: (0, i)),
            pl.BlockSpec((D, two), whole),
            pl.BlockSpec((TOK, D), whole),
            pl.BlockSpec((1, TOK, D), lambda i: (2, 0, 0)),
        ],
        out_specs=[pl.BlockSpec((16, 16, 2560), lambda i: (0, 0, 0))] * 4,
        out_shape=[jax.ShapeDtypeStruct((16, 16, 2560), BF)] * 4,
        scratch_shapes=[pltpu.VMEM((two, 256), BF)],
        compiler_params=params(32),
        cost_estimate=cost(9),
        far_in=(1, 2, 3, 5),
        far_out=(0, 1, 2, 3),
        name="inner_grads",
    )(where, active, grad, input_t, cot_second, sib_rows)


def outer_grads_kernel(
    where, active_ref, cot_own, cot_sib, mix_own, mix_sib, branch_ref, sums_ref,
    b0, b1, b2, b3, cot,
):
    step = pl.program_id(0)
    outs = (b0, b1, b2, b3)

    @pl.when(step == 0)
    def _():
        cot[...] = chip_rows(
            where, cot_own[:, 256:].astype(F32), cot_sib[0, :, 256:].astype(F32)
        ).astype(BF)
        cols = jnp.where(
            where[3] == 0, branch_ref[:, :512].astype(F32), branch_ref[:, 512:].astype(F32)
        ).astype(BF)
        mixes = (mix_own, mix_sib)
        for side, m, head in heads_of(where):
            rows = t_dot(mixes[side][:, m * 128 : m * 128 + 128], cols).astype(BF)
            rows = rows.reshape(2, 4, 16, 512)
            at = pl.ds((head >> 1) * 4, 4)
            for part in range(2):
                near = (2 * (head & 1) + part - where[1]) & 3
                for k, out in enumerate(outs):

                    @pl.when(near == k)
                    def _(part=part, out=out, rows=rows, at=at):
                        out[at, 0:16, :256] = rows[part, :, :, :256]
                        out[at, 16:32, :256] = rows[part, :, :, 256:]

        for k, out in enumerate(outs):
            near = (where[1] + k) & 3
            for y in range(4):
                out[y * 4 : y * 4 + 4, 0:16, 256:384] = sums_ref[pl.ds(y * 16 + near * 4, 4)]
                out[y * 4 : y * 4 + 4, 16:32, 256:384] = jnp.zeros((4, 16, 128), BF)

    outer = t_dot(active_ref[...], cot[...]).astype(BF).reshape(4, 4, 32, 768)
    for z in range(4):
        for k, out in enumerate(outs):

            @pl.when(((z - where[1]) & 3) == k)
            def _(z=z, out=out):
                out[pl.ds(step * 4, 4), :, 384:] = outer[z]


def outer_grads(where, active, cot_second, sib_rows, mix_own, mix_sib, branch, sums):
    two = 2 * TOK
    whole = lambda i: (0, 0)
    whole3 = lambda i: (0, 0, 0)
    return kernel_call(
        outer_grads_kernel,
        grid=(4,),
        in_specs=[
            SMEM,
            pl.BlockSpec((two, 512), lambda i: (0, i)),
            pl.BlockSpec((TOK, D), whole),
            pl.BlockSpec((1, TOK, D), lambda i: (2, 0, 0)),
            pl.BlockSpec((two, 512), whole),
            pl.BlockSpec((two, 512), whole),
            pl.BlockSpec((two, D), whole),
            pl.BlockSpec((64, 16, 128), whole3),
        ],
        out_specs=[pl.BlockSpec((16, 32, 1152), whole3)] * 4,
        out_shape=[jax.ShapeDtypeStruct((16, 32, 1152), BF)] * 4,
        scratch_shapes=[pltpu.VMEM((two, 768), BF)],
        compiler_params=params(32),
        cost_estimate=cost(10),
        far_in=(1, 3, 5, 6),
        far_out=tuple(range(4)),
        name="outer_grads",
    )(where, active, cot_second, sib_rows, mix_own, mix_sib, branch, sums)


def second_kernel(where, active_ref, outer_ref, own_ref, give_ref, total):
    step = pl.program_id(0)
    part = dot(active_ref[...], outer_ref[...].reshape(512, D))

    @pl.when(step == 0)
    def _():
        total[...] = part

    @pl.when(step > 0)
    def _():
        total[...] += part

    @pl.when(step == 3)
    def _():
        low_core = where[3] == 0
        own_ref[...] = jnp.where(low_core, total[:TOK], total[TOK:])
        give_ref[...] = jnp.where(low_core, total[TOK:], total[:TOK])


def second_parts(where, active, gathered):
    two = 2 * TOK
    whole = lambda i: (0, 0)
    return kernel_call(
        second_kernel,
        grid=(4,),
        in_specs=[
            SMEM,
            pl.BlockSpec((two, 512), lambda i: (0, i)),
            pl.BlockSpec((16, 32, D), lambda i: (i, 1, 0)),
        ],
        out_specs=[pl.BlockSpec((TOK, D), whole)] * 2,
        out_shape=[jax.ShapeDtypeStruct((TOK, D), F32)] * 2,
        scratch_shapes=[pltpu.VMEM((two, D), F32)],
        compiler_params=params(20),
        cost_estimate=cost(4),
        far_in=(1, 2),
        name="second_parts",
    )(where, active, gathered)


def recut_kernel(axis, where, *refs):
    parts, outs = refs[:4], refs[4:]
    for k, out in enumerate(outs):
        mine = (where[axis] + k) & 3
        out[...] = total_of([part[mine] for part in parts]).astype(BF)


recut_a = whole_call(
    functools.partial(recut_kernel, 1), "recut_a", [((4, 16, 2560), BF)] * 4, 4, mib=32,
    far_in=(1,), far_out=(0, 1, 2, 3),
)
recut_b = whole_call(
    functools.partial(recut_kernel, 0), "recut_b", [((4, 32, 1152), BF)] * 4, 3, mib=24,
    far_in=(1,), far_out=(0, 1, 2, 3),
)


def join_kernel(where, *refs):
    w, a, b, outs = refs[:4], refs[4:8], refs[8:12], refs[12:]
    for k, out in enumerate(outs):
        x = (where[2] + k) & 3
        for z in range(4):
            rows = pl.ds(pl.multiple_of(z * 64 + x * 16, 16), 16)
            total = total_of([part[rows, :] for part in w]).astype(BF)
            for j in range(3):
                at = (z * 3 + j) * 16
                out[at : at + 16, :] = total[:, j * 128 : j * 128 + 128]
        total = total_of([part[x] for part in a]).astype(BF)
        for j in range(20):
            out[192 + j * 16 : 208 + j * 16, :] = total[:, j * 128 : j * 128 + 128]
        total = total_of([part[x] for part in b]).astype(BF)
        for j in range(9):
            out[512 + j * 32 : 544 + j * 32, :] = total[:, j * 128 : j * 128 + 128]


join = whole_call(join_kernel, "join", [((800, 128), BF)] * 4, 3)


def divide_kernel(where, x0, x1, x2, x3, w0, w1, w2, w3, keep_ref, give_ref, outer_ref, small_ref, total):
    low_core = where[3] == 0
    total[...] = total_of([part[...] for part in (x0, x1, x2, x3)])
    for k, out in enumerate((w0, w1, w2, w3)):
        z = (where[1] + k) & 3
        for j in range(3):
            rows = pl.ds(pl.multiple_of((z * 3 + j) * 16, 16), 16)
            out[:, j * 128 : j * 128 + 128] = total[rows, :].astype(BF)
    blocks = [total[192 + j * 16 : 208 + j * 16, :] for j in range(16)]
    for at in (512, 528):
        blocks += [total[at : at + 16, :], total[at + 32 : at + 48, :]]
    low = jnp.concatenate([block[:8] for block in blocks], axis=0)
    high = jnp.concatenate([block[8:] for block in blocks], axis=0)
    keep_ref[...] = jnp.where(low_core, low, high)
    give_ref[...] = jnp.where(low_core, high, low).astype(BF)
    for j in range(2):
        lanes = slice(j * 128, j * 128 + 128)
        outer_ref[:16, lanes] = total[448 + j * 16 : 464 + j * 16, :]
        outer_ref[16:, lanes] = total[480 + j * 16 : 496 + j * 16, :]
    for j in range(6):
        lanes = slice(256 + j * 128, 384 + j * 128)
        outer_ref[:, lanes] = total[608 + j * 32 : 640 + j * 32, :]
    small_ref[...] = total[576:584, :]


divide = whole_call(
    divide_kernel, "divide",
    [((16, 384), BF)] * 4 + [((160, 128), F32), ((160, 128), BF), ((32, D), F32), ((8, 128), F32)],
    2, scratch=[pltpu.VMEM((800, 128), F32)],
)


def last_kernel(where, w0, w1, w2, w3, give_ref, keep_w, out_ref, kept, given):
    low_core = where[3] == 0
    for m, piece in enumerate((w0, w1, w2, w3)):
        z = (where[1] + m) & 3
        rows = piece[...].astype(F32)
        mine = jnp.where(low_core, rows[:8], rows[8:])
        other = jnp.where(low_core, rows[8:], rows[:8])
        for j in range(3):
            at = pl.ds(pl.multiple_of((z * 3 + j) * 8, 8), 8)
            kept[at, :] = mine[:, j * 128 : j * 128 + 128]
            given[at, :] = other[:, j * 128 : j * 128 + 128]
    keep_w[...] = kept[...]
    out_ref[:96, :] = given[...].astype(BF)
    out_ref[96:, :] = give_ref[...]


last = whole_call(
    last_kernel, "last", [((96, 128), F32), ((256, 128), BF)], 1,
    scratch=[pltpu.VMEM((96, 128), F32)] * 2,
)


def finish_kernel(
    where, keep_w, keep_ref, got_ref, joint_ref, value_ref, norm_ref, inner_ref, output_ref
):
    low_core = where[3] == 0
    got = got_ref[...].astype(F32)
    mine, other = keep_w[...], got[:96]
    norm = jnp.zeros((8, 128), F32)
    for core in range(2):
        rows = jnp.where(low_core, *((mine, other) if core == 0 else (other, mine)))
        for z in range(4):
            lanes = slice((core * 4 + z) * 128, (core * 4 + z + 1) * 128)
            joint_ref[:, lanes] = rows[z * 24 : z * 24 + 8]
            value_ref[:, lanes] = rows[z * 24 + 8 : z * 24 + 16]
            norm = norm + rows[z * 24 + 16 : z * 24 + 24]
    norm_ref[...] = norm
    mine, other = keep_ref[...], got[96:]
    low, high = jnp.where(low_core, mine, other), jnp.where(low_core, other, mine)
    both = jnp.concatenate([low[:128], high[:128]], axis=1).astype(BF)
    dst, src = iota((256, 256), 1), iota((256, 256), 0)
    wanted = 128 * ((dst >> 5) & 1) + 32 * (dst >> 6) + (dst & 31)
    mixed = dot(both, (src == wanted).astype(F32).astype(BF))
    for t in range(16):
        inner_ref[:, t * 256 : (t + 1) * 256] = mixed[t * 8 : t * 8 + 8, :]
    for core, rows in enumerate((low, high)):
        for at, lane in enumerate((0, 128, 256, 384)):
            lanes = slice(core * 512 + lane, core * 512 + lane + 128)
            output_ref[:, lanes] = rows[128 + at * 8 : 136 + at * 8]


finish = whole_call(
    finish_kernel, "finish",
    [((8, D), F32), ((8, D), F32), ((8, 128), F32), ((8, FF), F32), ((8, D), F32)], 1,
)


def make_keys(pieces, rows_ref):
    for m, piece in enumerate(pieces):

        @pl.loop(0, 8, unroll=4)
        def _(s, m=m, piece=piece):
            rows = pl.ds(pl.multiple_of(s * TOK, TOK), TOK)
            to = pl.ds(pl.multiple_of(m * 8 * TOK + s * TOK, TOK), TOK)
            q = piece[rows, :].astype(F32)
            inv = lax.rsqrt(jnp.sum(q * q, axis=-1, keepdims=True) + EPS_KEY)
            rows_ref[to, :] = (q * inv).astype(BF)


def round_weights(lt_ref, at):
    totals = [lt_ref[r, at, :].astype(F32) for r in range(ROUNDS)]
    peak = jnp.maximum(jnp.maximum(totals[0], totals[1]), jnp.maximum(totals[2], totals[3]))
    exps = [jnp.exp(t - peak) for t in totals]
    scale = 1.0 / (exps[0] + exps[1] + exps[2] + exps[3])
    return [e * scale for e in exps]


def hot_slots(tgt_ref, source):
    slots = iota((BUCKETS * MOST, TOK), 0)
    return (slots == tgt_ref[0, pl.ds(source, 1), :]).astype(F32).astype(BF)


def hot_tokens(tgt_t_ref, source):
    slots = iota((TOK, BUCKETS * MOST), 1)
    return (slots == tgt_t_ref[0, :, source : source + 1]).astype(F32).astype(BF)


def spread(first, second):
    width = first.shape[-1]
    both = [a.reshape(PAIRS, 2, MOST, width) for a in (first, second)]
    return jnp.concatenate(both, axis=2).astype(BF)


def fill(tgt_ref, read_rows, ref):
    @pl.loop(0, 16, unroll=4)
    def _(pair):
        placed = [
            dot(hot_slots(tgt_ref, pair * 2 + half), read_rows(pair * 2 + half))
            for half in range(2)
        ]
        both = spread(*placed)
        at = pl.ds(pl.multiple_of(pair * 16, 16), 16)
        ref[0, :, at, :128] = both[:, 0]
        ref[0, :, at, 128:] = both[:, 1]


def place(both, ref, pair):
    at = pl.multiple_of(pair * 16, 16)
    ref[:, pl.ds(at, 16), :] = both[:, 0]
    ref[:, pl.ds(64 + at, 16), :] = both[:, 1]


def diagonal(rows):
    first = iota((128, 128), 0) < 64
    none = jnp.zeros((128, 128), BF)
    return jnp.concatenate([jnp.where(first, rows, none), jnp.where(first, none, rows)], axis=1)


def diagonal_t(rows):
    turned = jnp.transpose(rows)
    first = iota((128, 128), 1) < 64
    none = jnp.zeros((128, 128), BF)
    return jnp.concatenate([jnp.where(first, turned, none), jnp.where(first, none, turned)], axis=0)


def eye():
    return iota((128, 128), 0) == iota((128, 128), 1)


def token_block(s):
    return pl.ds(pl.multiple_of(s * TOK, TOK), TOK)


def scores_kernel(q0, q1, q2, q3, tgt_ref, mask_ref, probs_ref, keys_ref, qm_ref, log_ref, k_rows):
    @pl.when(pl.program_id(0) == 0)
    def _():
        make_keys((q0, q1, q2, q3), k_rows)

    fill(tgt_ref, lambda source: k_rows[token_block(source), :], keys_ref)

    @pl.loop(0, 4, unroll=4)
    def _(pair):
        placed = [
            dot(hot_slots(tgt_ref, pair * 2 + half), q0[token_block(pair * 2 + half), :])
            for half in range(2)
        ]
        place(spread(*placed), qm_ref.at[0], pair)

    @pl.loop(0, PAIRS, unroll=16)
    def _(p):
        code = mask_ref[0, p].astype(F32)
        scores = dot(keys_ref[0, p], diagonal_t(qm_ref[0, p]))
        scores = jnp.where(code == 0.0, scores, code * 1e4)
        peak = jnp.max(scores, axis=0, keepdims=True)
        exponent = jnp.exp(scores - peak)
        total = jnp.sum(exponent, axis=0, keepdims=True)
        probs_ref[0, p] = (exponent * (1.0 / total)).astype(BF)
        log_ref[0, pl.ds(p, 1), :] = peak + jnp.log(total)


def attend_scores(q_pieces, tgt, mask):
    rows = 8 * TOK
    outs = [(PAIRS, 256, 128), (PAIRS, 256, 256), (PAIRS, 128, 128), (PAIRS, 128)]
    types = [BF, BF, BF, F32]
    return kernel_call(
        scores_kernel,
        grid=(ROUNDS,),
        in_specs=[fixed((rows, HEAD_DIM))] * 4
        + [per_round((32, TOK)), per_round((PAIRS, 256, 128))],
        out_specs=[per_round(shape) for shape in outs],
        out_shape=[
            jax.ShapeDtypeStruct((ROUNDS,) + shape, t) for shape, t in zip(outs, types)
        ],
        scratch_shapes=[pltpu.VMEM((4 * rows, HEAD_DIM), BF)],
        compiler_params=params(20),
        cost_estimate=cost(18),
        far_in=(5,),
        far_out=(0, 1, 2),
        name="attend_scores",
    )(*q_pieces, tgt, mask)


def values_kernel(
    v0, v1, v2, v3, tgt_ref, tgt_t_ref, probs_ref, log_ref, mixed_ref, ro_ref, lt_ref, values_ref, att
):
    this_round = pl.program_id(0)
    for m, piece in enumerate((v0, v1, v2, v3)):

        @pl.loop(0, 4, unroll=4)
        def _(pair, m=m, piece=piece):
            placed = [
                dot(
                    hot_slots(tgt_ref, m * 8 + pair * 2 + half),
                    piece[token_block(pair * 2 + half), :],
                )
                for half in range(2)
            ]
            both = spread(*placed)
            at = pl.ds(pl.multiple_of((m * 4 + pair) * 16, 16), 16)
            values_ref[0, :, at, :128] = both[:, 0]
            values_ref[0, :, at, 128:] = both[:, 1]

    ones = jnp.ones((128, 128), BF)

    @pl.loop(0, PAIRS, unroll=16)
    def _(p):
        out = t_dot(probs_ref[0, p], values_ref[0, p])
        log_total = log_ref[0, pl.ds(p, 1), :]
        logs = dot(jnp.where(eye(), log_total, 0.0).astype(BF), ones)
        att[p, 0, :, :128] = out[:64, :128]
        att[p, 1, :, :128] = out[64:, 128:]
        att[p, 0, :, 128:] = logs[:64]
        att[p, 1, :, 128:] = logs[64:]

    for s in range(8):
        slots = att[:, :, s * MOST : (s + 1) * MOST, :].reshape(256, 256)
        rows = dot(hot_tokens(tgt_t_ref, s), slots.astype(BF)).astype(BF)
        ro_ref[this_round, s * TOK : (s + 1) * TOK, :] = rows[:, :HEAD_DIM]
        lt_ref[this_round, s * TOK : (s + 1) * TOK, :] = rows[:, HEAD_DIM:]

    @pl.when(this_round == ROUNDS - 1)
    def _():
        @pl.loop(0, 8)
        def _(s):
            at = token_block(s)
            weights = round_weights(lt_ref, at)
            mixed = weights[0] * ro_ref[0, at, :].astype(F32)
            for r in range(1, ROUNDS):
                mixed = mixed + weights[r] * ro_ref[r, at, :].astype(F32)
            mixed_ref[at, :] = mixed.astype(BF)


def attend_values(v_pieces, tgt, tgt_t, probs, logs):
    rows = 8 * TOK
    return kernel_call(
        values_kernel,
        grid=(ROUNDS,),
        in_specs=[fixed((rows, HEAD_DIM))] * 4
        + [
            per_round((32, TOK)), per_round((TOK, 128)), per_round((PAIRS, 256, 128)),
            per_round((PAIRS, 128)),
        ],
        out_specs=[
            fixed((rows, HEAD_DIM)),
            fixed((ROUNDS, rows, HEAD_DIM)),
            fixed((ROUNDS, rows, HEAD_DIM)),
            per_round((PAIRS, 256, 256)),
        ],
        out_shape=[
            jax.ShapeDtypeStruct((rows, HEAD_DIM), BF),
            jax.ShapeDtypeStruct((ROUNDS, rows, HEAD_DIM), BF),
            jax.ShapeDtypeStruct((ROUNDS, rows, HEAD_DIM), BF),
            jax.ShapeDtypeStruct((ROUNDS, PAIRS, 256, 256), BF),
        ],
        scratch_shapes=[pltpu.VMEM((PAIRS, 2, 64, 256), F32)],
        compiler_params=params(22),
        cost_estimate=cost(14),
        far_in=(6,),
        far_out=(1, 2, 3),
        name="attend_values",
    )(*v_pieces, tgt, tgt_t, probs, logs)


def take_slots(tgt_t_ref, slots_ref, rows_ref, sources):
    for s in range(sources):
        slots = slots_ref[:, :, s * MOST : (s + 1) * MOST, :].reshape(256, HEAD_DIM)
        rows_ref[s * TOK : (s + 1) * TOK, :] += dot(hot_tokens(tgt_t_ref, s), slots.astype(BF))


def values_back_kernel(
    where, tgt_ref, tgt_t_ref, probs_ref, ro_ref, lt_ref, gm_ref, out_ref, gd_ref, gt_ref, gt_slots, slots, rows, token_rows,
):
    this_round = pl.program_id(0)

    @pl.when(this_round == 0)
    def _():
        rows[...] = jnp.zeros_like(rows)

        @pl.loop(0, 8, unroll=2)
        def _(s):
            at = token_block(s)
            weights = round_weights(lt_ref, at)
            grad = gm_ref[at, :].astype(F32)
            agree = [
                jnp.sum(grad * ro_ref[r, at, :].astype(F32), axis=-1, keepdims=True)
                for r in range(ROUNDS)
            ]
            mean = total_of([weights[r] * agree[r] for r in range(ROUNDS)])
            for r in range(ROUNDS):
                token_rows[r, at, :HEAD_DIM] = (weights[r] * grad).astype(BF)
                token_rows[r, at, HEAD_DIM:] = (weights[r] * (agree[r] - mean)).astype(BF)

    @pl.loop(0, 4, unroll=4)
    def _(pair):
        placed = [
            dot(
                hot_slots(tgt_ref, pair * 2 + half),
                token_rows[this_round, token_block(pair * 2 + half), :],
            )
            for half in range(2)
        ]
        both = spread(*placed)
        place(both[..., :HEAD_DIM], gd_ref.at[0], pair)
        place(both[..., HEAD_DIM:], gt_slots, pair)

    @pl.loop(0, PAIRS, unroll=16)
    def _(p):
        grad_values = dot(probs_ref[0, p], diagonal(gd_ref[0, p]))
        slots[p, 0] = grad_values[:, :128]
        slots[p, 1] = grad_values[:, 128:]
        gt_ref[0, pl.ds(p, 1), :] = jnp.sum(
            jnp.where(eye(), gt_slots[p].astype(F32), 0.0), axis=0, keepdims=True
        )

    take_slots(tgt_t_ref, slots, rows, 32)

    @pl.when(this_round == ROUNDS - 1)
    def _():
        for m in range(4):
            out_ref[(where[2] + m) & 3] = rows[m * 8 * TOK : (m + 1) * 8 * TOK, :].astype(BF)


def attend_values_back(where, tgt, tgt_t, probs, ro, lt, gm):
    rows = 8 * TOK
    return kernel_call(
        values_back_kernel,
        grid=(ROUNDS,),
        in_specs=[
            SMEM,
            per_round((32, TOK)),
            per_round((TOK, 128)),
            per_round((PAIRS, 256, 128)),
            fixed((ROUNDS, rows, HEAD_DIM)),
            fixed((ROUNDS, rows, HEAD_DIM)),
            fixed((rows, HEAD_DIM)),
        ],
        out_specs=[
            fixed((4, rows, HEAD_DIM)), per_round((PAIRS, 128, 128)), per_round((PAIRS, 128)),
        ],
        out_shape=[
            jax.ShapeDtypeStruct((4, rows, HEAD_DIM), BF),
            jax.ShapeDtypeStruct((ROUNDS, PAIRS, 128, 128), BF),
            jax.ShapeDtypeStruct((ROUNDS, PAIRS, 128), F32),
        ],
        scratch_shapes=[
            pltpu.VMEM((PAIRS, 128, 128), BF),
            pltpu.VMEM((PAIRS, 2, 256, HEAD_DIM), F32),
            pltpu.VMEM((4 * rows, HEAD_DIM), F32),
            pltpu.VMEM((ROUNDS, rows, 256), BF),
        ],
        compiler_params=params(26),
        cost_estimate=cost(12),
        far_in=(1, 2, 3, 4, 5),
        far_out=(0, 1, 2),
        name="attend_values_back",
    )(where, tgt, tgt_t, probs, ro, lt, gm)


def scores_back_kernel(
    half, where, tgt_t_ref, mask_ref, probs_ref, values_ref, qm_ref, gd_ref, gt_ref, *refs
):
    if half == 0:
        gs_ref, rows_out, slots, rows = refs
    else:
        rows_in, gs_ref, out_ref, slots, rows = refs
    step = pl.program_id(0)

    @pl.when(step == 0)
    def _():
        if half == 0:
            rows[...] = jnp.zeros_like(rows)
        else:
            rows[...] = rows_in[...]

    @pl.loop(0, PAIRS, unroll=16)
    def _(p):
        probs = probs_ref[0, p].astype(F32)
        grad_probs = dot(values_ref[0, p], diagonal_t(gd_ref[0, p]))
        agreement = jnp.sum(probs * grad_probs, axis=0, keepdims=True)
        grad_scores = probs * (grad_probs + (gt_ref[0, pl.ds(p, 1), :] - agreement))
        seen = mask_ref[0, p].astype(F32) == 0.0
        grad_scores = jnp.where(seen, grad_scores, 0.0).astype(BF)
        gs_ref[0, p] = grad_scores
        grad_keys = dot(grad_scores, diagonal(qm_ref[0, p]))
        slots[p, 0] = grad_keys[:, :128]
        slots[p, 1] = grad_keys[:, 128:]

    take_slots(tgt_t_ref, slots, rows, 32)

    @pl.when(step == 1)
    def _():
        if half == 0:
            rows_out[...] = rows[...]
        else:
            for m in range(4):
                out_ref[(where[2] + m) & 3] = rows[m * 8 * TOK : (m + 1) * 8 * TOK, :].astype(BF)


def attend_scores_back(half, where, arrays, begun):
    rows = 8 * TOK
    shapes = [
        (TOK, 128), (PAIRS, 256, 128), (PAIRS, 256, 128), (PAIRS, 256, 256),
        (PAIRS, 128, 128), (PAIRS, 128, 128), (PAIRS, 128),
    ]
    this_half = lambda shape: pl.BlockSpec(
        (1,) + shape, lambda r: (2 * half + r,) + (0,) * len(shape)
    )
    slots = (PAIRS, 256, 128)
    if half == 0:
        outs = [((4 * rows, HEAD_DIM), F32)]
    else:
        outs = [((4, rows, HEAD_DIM), BF)]
    return kernel_call(
        functools.partial(scores_back_kernel, half),
        grid=(2,),
        in_specs=[SMEM] + [this_half(shape) for shape in shapes] + [fixed(a.shape) for a in begun],
        out_specs=[per_round(slots)] + [fixed(shape) for shape, _ in outs],
        out_shape=[jax.ShapeDtypeStruct((2,) + slots, BF)]
        + [jax.ShapeDtypeStruct(shape, t) for shape, t in outs],
        scratch_shapes=[
            pltpu.VMEM((PAIRS, 2, 256, HEAD_DIM), F32),
            pltpu.VMEM((4 * rows, HEAD_DIM), F32),
        ],
        compiler_params=params(30),
        cost_estimate=cost(10),
        far_in=tuple(range(1, 8)),
        far_out=(0,) if half == 0 else (0, 1),
        name=f"attend_scores_back_{half}",
    )(where, *arrays, *begun)


def queries_back_kernel(tgt_t_ref, first_ref, second_ref, keys_ref, gq_ref, slots):
    step = pl.program_id(0)

    @pl.when(step == 0)
    def _():
        gq_ref[...] = jnp.zeros_like(gq_ref)

    def one_round(gs_ref):
        @pl.loop(0, PAIRS, unroll=16)
        def _(p):
            grad_queries = t_dot(gs_ref[0, p], keys_ref[0, p])
            slots[p, 0] = grad_queries[:64, :128]
            slots[p, 1] = grad_queries[64:, 128:]

    @pl.when(step < 2)
    def _():
        one_round(first_ref)

    @pl.when(step >= 2)
    def _():
        one_round(second_ref)

    take_slots(tgt_t_ref, slots, gq_ref, 8)


def attend_queries_back(tgt_t, first, second, keys):
    rows, slots = 8 * TOK, (1, PAIRS, 256, 128)
    return kernel_call(
        queries_back_kernel,
        grid=(ROUNDS,),
        in_specs=[
            per_round((TOK, 128)),
            pl.BlockSpec(slots, lambda r: (jnp.minimum(r, 1), 0, 0, 0)),
            pl.BlockSpec(slots, lambda r: (jnp.maximum(r, 2) - 2, 0, 0, 0)),
            per_round((PAIRS, 256, 256)),
        ],
        out_specs=[fixed((rows, HEAD_DIM))],
        out_shape=[jax.ShapeDtypeStruct((rows, HEAD_DIM), F32)],
        scratch_shapes=[pltpu.VMEM((PAIRS, 2, 64, HEAD_DIM), F32)],
        compiler_params=params(20),
        cost_estimate=cost(8),
        far_in=(0, 1, 2, 3),
        far_out=(0,),
        name="attend_queries_back",
    )(tgt_t, first, second, keys)[0]


def local(
    first_in, second_in, attn_gain, attn_shift, w_joint, w_value, w_output, ffn_gain, ffn_shift,
    w_inner, b_inner, w_outer, b_outer, buckets, cot_first, cot_second,
):
    y, z, x, c = (lax.axis_index(a) for a in AXES)
    where = jnp.stack([y, z, x, c]).astype(jnp.int32)
    low_core = c == 0

    def by_core(first, second):
        return jnp.where(low_core, first, second)

    vec = jnp.concatenate(
        [attn_gain, attn_shift, ffn_gain, ffn_shift, b_outer, b_inner, jnp.zeros((56,), BF)]
    ).astype(F32)
    keep, give = pack(
        where, w_joint, w_value, w_output, w_inner, vec.reshape(1, 128), buckets[:, :, 0]
    )
    tok_near = [send(second_in, "z", 3), send(second_in, "z", 1)]
    got = swap(give)
    gathered = lax.all_gather(
        payload(where, keep, got, w_outer)[0], CHIPS, axis=0, tiled=False
    ).reshape(64, 80, D)
    y_got = gather(chip_message(where, keep, got)[0], "y")
    heads_out, second_late, tok_near = sync(
        head_messages(where, *y_got), second_in, tok_near
    )
    z_got = scatter(heads_out, "z")
    tok_last = send(second_late, "z", 2)
    z_got, tok_last = sync(z_got, tok_last)
    tok_far = jnp.stack([tok_near[0], tok_last, tok_near[1]])
    sib_tok = swap(jnp.concatenate([second_in[None], tok_far]))
    tokens = (second_in, tok_far, sib_tok)
    x_got = gather(jnp.concatenate(z_got), "x")
    wq, par, tgt, tgt_t, counts, vec = assemble(where, *x_got)

    normed, queries = project(where, tokens, par, wq)
    queries, counts, vec = sync(queries, counts, vec)
    q_pieces = gather(queries, "x")
    mask, par_ffn, bias_inner = make_mask(where, counts, vec)
    values, wv = project_values(where, x_got, normed)
    values, q_pieces[1], q_pieces[3], sib_rows = sync(
        values, q_pieces[1], q_pieces[3], jnp.stack([first_in, cot_first, cot_second])
    )
    v_pieces = gather(values, "x")
    sib_rows = swap(sib_rows)
    probs, key_slots, query_slots, logs = attend_scores(q_pieces, tgt, mask)
    mixed_head, round_out, round_total, value_slots = attend_values(
        v_pieces, tgt, tgt_t, probs, logs
    )

    mix_own = jnp.concatenate(
        scatter([mixed_head[k * 256 : (k + 1) * 256] for k in range(4)], "z"), axis=1
    )
    mix_sib = swap(mix_own)
    first_sum, first_out, input_t, active, grad_hidden, back, hid_sum, cot_sum = feed(
        where, mix_own, mix_sib, first_in, cot_second, sib_rows, par_ffn, bias_inner, gathered
    )
    a_parts = inner_grads(where, active, grad_hidden, input_t, cot_second, sib_rows)
    back_sib, a_parts = sync(swap(back), a_parts)
    grad_first, branch, g0, g1, g2, g3, norm_sums = first_back(
        where, back, back_sib, first_sum, cot_first, sib_rows, par_ffn, gathered
    )
    grad_mixed = scatter([g0, g1, g2, g3], "z")
    a_got = [send(a_parts[1], "y", 1), send(a_parts[3], "y", 3)]
    sums = jnp.stack([norm_sums[0], norm_sums[1], cot_sum[0]]).reshape(3, 64, 16)
    sums = jnp.pad(jnp.transpose(sums, (1, 0, 2)), ((0, 0), (0, 0), (0, 16)))
    sums = jnp.concatenate([sums, hid_sum[0].reshape(64, 1, 32)], axis=1).astype(BF)
    sums = jnp.pad(sums, ((0, 0), (0, 12), (0, 96)))
    b_parts = outer_grads(
        where, active, cot_second, sib_rows, mix_own, mix_sib, branch, sums
    )
    grad_mixed, b_parts = sync(grad_mixed, b_parts)

    b_got = [send(b_parts[1], "z", 1), send(b_parts[3], "z", 3)]
    gv, grad_slots, log_slots = attend_values_back(
        where, tgt, tgt_t, probs, round_out, round_total, jnp.concatenate(grad_mixed)
    )

    gv, grad_slots = sync(gv, grad_slots)
    gv_got = exchange(gv, "x")
    back_in = (tgt_t, mask, probs, value_slots, query_slots, grad_slots, log_slots)
    gs_first, half = attend_scores_back(0, where, back_in, ())
    a_got, b_got, a_far, b_far, half = sync(a_got, b_got, a_parts[2], b_parts[2], half)
    a_far, b_far = send(a_far, "y", 2), send(b_far, "z", 2)
    gs_second, gk = attend_scores_back(1, where, back_in, (half,))
    gv_got, gk, gs_second = sync(gv_got, gk, gs_second)

    gk_got = exchange(gk, "x")
    gq = attend_queries_back(tgt_t, gs_first, gs_second, key_slots)
    b_far, gq = sync(b_far, gq)
    b_parts = recut_b(
        where, *[part.reshape(4, 4, 32, 1152) for part in [b_parts[0], b_far] + b_got]
    )
    b_parts, a_far = sync(b_parts, a_far)
    b_got = scatter(b_parts, "y")
    a_parts = recut_a(
        where, *[part.reshape(4, 4, 16, 2560) for part in [a_parts[0], a_far] + a_got]
    )
    gk_got, a_parts = sync(gk_got, a_parts)

    a_got = scatter(a_parts, "z")
    back_own, back_give, *w_parts = project_back(
        where, tokens, wq, wv, normed, queries, gq, gk_got, gv_got
    )

    back_give, w_parts, b_got[1], b_got[3], a_got[1], a_got[3] = sync(
        back_give, w_parts, b_got[1], b_got[3], a_got[1], a_got[3]
    )
    w_got = scatter(w_parts, "y")
    back_got, active = sync(swap(back_give), active)
    back_chip = (back_own.astype(F32) + back_got.astype(F32)).astype(BF)
    second_own, second_give = second_parts(where, active, gathered)
    back_parts = [back_chip[k] for k in range(4)]
    back_far = send(back_parts[2], "z", 2)
    back_parts, w_got, a_got, b_got, second_give = sync(
        back_parts, w_got, a_got, b_got, second_give
    )
    second_got = swap(second_give)


    x_parts = scatter(join(where, *w_got, *a_got, *b_got), "x")
    x_parts[1], back_parts, back_far = sync(x_parts[1], back_parts, back_far)
    back_sum = [
        back_parts[0], send(back_parts[1], "z", 1), send(back_parts[3], "z", 3), back_far
    ]

    second_out = (second_in.astype(F32) + second_own + second_got + par_ffn[2]).astype(BF)
    *z_parts, chip_keep, chip_give, grad_outer, small = divide(where, *x_parts)
    w_got = scatter(z_parts, "z")
    w_keep, last_give = last(where, *w_got, chip_give)
    grad_joint, grad_value, norm, grad_inner, grad_output = finish(
        where, w_keep, chip_keep, swap(last_give)
    )
    grad_attn_gain, grad_attn_shift = norm[:, 0], norm[:, 64]
    mine16 = by_core(small[:3, :8], small[:3, 8:16])
    grad_ffn_gain, grad_ffn_shift, grad_b_outer = mine16[0], mine16[1], mine16[2]
    grad_b_inner = small[3, :32]

    attn_xhat, attn_scale = normalized(second_in.astype(F32))
    attn_back = norm_back(total_of(back_sum) * par[0], attn_xhat, attn_scale)
    grad_second = (cot_second.astype(F32) + attn_back).astype(BF)

    return (
        first_out, second_out, grad_first, grad_second, grad_attn_gain, grad_attn_shift,
        grad_joint, grad_value, grad_output, grad_ffn_gain, grad_ffn_shift, grad_inner,
        grad_b_inner, grad_outer, grad_b_outer,
    )


def solution(mesh):
    chips = Mesh(mesh.devices.reshape(4, 4, 4, 2), AXES)
    rows, flat = P(AXES, None), P(AXES)
    return jax.shard_map(
        local,
        mesh=chips,
        in_specs=(
            rows, rows, flat, flat, rows, rows, rows, flat, flat, rows, flat, rows, flat,
            P(None, AXES, None), rows, rows,
        ),
        out_specs=(
            rows, rows, rows, rows, flat, flat, rows, rows, rows, flat, flat, rows, flat, rows,
            flat,
        ),
        check_vma=False,
    )
```

```python
import functools

import jax
import jax.numpy as jnp
from jax import lax
from jax.experimental import pallas as pl
from jax.experimental.pallas import tpu as pltpu
from jax.sharding import Mesh, PartitionSpec as P

HEADS = 8
HEAD_DIM = 128
ROUNDS = 4
BUCKETS = 32
MOST = 8
TOK = 128
D = 1024
FF = 4096

EPS_NORM = 1e-05
EPS_KEY = 1e-06
SELF_SCORE = -10000.0
MASKED_SCORE = -1000000000.0

BF = jnp.bfloat16
F32 = jnp.float32

AXES = ("y", "z", "x", "c")
CHIPS = ("y", "z", "x")


def send(piece, axis, k):
    return lax.ppermute(piece, axis, [(i, (i + k) % 4) for i in range(4)])


def swap(piece):
    return lax.ppermute(piece, "c", [(0, 1), (1, 0)])


def gather(piece, axis):
    back, front, far = send(piece, axis, 3), send(piece, axis, 1), send(piece, axis, 2)
    return [piece, back, far, front]


def scatter(pieces, axis):
    front, back, far = (
        send(pieces[1], axis, 1),
        send(pieces[3], axis, 3),
        send(pieces[2], axis, 2),
    )
    return [pieces[0], back, far, front]


def sync(*groups):
    return lax.optimization_barrier(groups)


def dot(a, b):
    return jnp.dot(a, b, preferred_element_type=F32)


def dot_t(a, b):
    return lax.dot_general(a, b, (((1,), (1,)), ((), ())), preferred_element_type=F32)


def t_dot(a, b):
    return lax.dot_general(a, b, (((0,), (0,)), ((), ())), preferred_element_type=F32)


def cost(us):
    return pl.CostEstimate(flops=int(us * 0.35e9), bytes_accessed=0, transcendentals=0)


def params(mib):
    return pltpu.CompilerParams(vmem_limit_bytes=mib * 1024 * 1024)


SMEM = pl.BlockSpec(memory_space=pltpu.SMEM)


def kernel_call(kernel, *, out_shape, far_in=(), far_out=(), **rest):
    inner = pl.pallas_call(
        kernel,
        out_shape=[
            pltpu.HBM(o.shape, o.dtype) if at in far_out else o for at, o in enumerate(out_shape)
        ],
        **rest,
    )

    def run(*arrays):
        return inner(
            *[
                pltpu.with_memory_space_constraint(a, pltpu.HBM) if at in far_in else a
                for at, a in enumerate(arrays)
            ]
        )

    return run


def iota(shape, dim):
    return lax.broadcasted_iota(jnp.int32, shape, dim)


def whole_call(kernel, name, outs, us, mib=16, scratch=(), far_in=(), far_out=()):
    def call(where, *arrays):
        return kernel_call(
            kernel,
            grid=(1,),
            in_specs=[SMEM] + [fixed(a.shape) for a in arrays],
            out_specs=[fixed(s) for s, _ in outs],
            out_shape=[jax.ShapeDtypeStruct(s, t) for s, t in outs],
            scratch_shapes=list(scratch),
            compiler_params=params(mib),
            cost_estimate=cost(us),
            far_in=far_in,
            far_out=far_out,
            name=name,
        )(where, *arrays)

    return call


def fixed(shape):
    return pl.BlockSpec(shape, lambda r: (0,) * len(shape))


def per_round(shape):
    return pl.BlockSpec((1,) + shape, lambda r: (r,) + (0,) * len(shape))


PAIRS = BUCKETS // 2


def exchange(stacked, axis):
    return lax.all_to_all(stacked, axis, split_axis=0, concat_axis=0, tiled=True)


def total_of(parts):
    total = parts[0].astype(F32)
    for extra in parts[1:]:
        total = total + extra.astype(F32)
    return total


def pack_kernel(
    where, joint_ref, value_ref, output_ref, inner_ref, vec_ref, bucket_ref,
    keep_ref, give_ref,
):
    low_core = where[3] == 0
    joint, value = joint_ref[...].astype(F32), value_ref[...].astype(F32)
    inner_rows = inner_ref[...].astype(F32)
    heads = []
    for core in range(2):
        rows = []
        for h in range(4):
            cols = slice((core * 4 + h) * 128, (core * 4 + h + 1) * 128)
            rows += [joint[:, cols], value[:, cols]]
        heads.append(jnp.concatenate(rows, axis=0))

    sub, along = iota((128, 128), 0), iota((128, 128), 1)
    targets, counts = [], []
    for r in range(ROUNDS):
        chosen = jnp.broadcast_to(bucket_ref[r : r + 1, :].astype(F32), (128, 128))
        column = jnp.sum(jnp.where(sub == along, chosen, 0.0), axis=1, keepdims=True)
        earlier = (column == chosen) & (sub < along)
        rank = jnp.sum(earlier.astype(F32), axis=0, keepdims=True)
        targets.append(chosen[0:1] * MOST + rank)
        counts.append(jnp.sum((column == along.astype(F32)).astype(F32), axis=0, keepdims=True))
    vec = jnp.concatenate([vec_ref[...], jnp.zeros((7, 128), F32)], axis=0)
    aux = jnp.concatenate([vec] + targets + counts, axis=0)
    keep_ref[:80, :] = jnp.concatenate([jnp.where(low_core, *heads), aux], axis=0).astype(BF)
    give_ref[:80, :] = jnp.concatenate([jnp.where(low_core, *heads[::-1]), aux], axis=0).astype(BF)

    chunks = [inner_rows[:, t * 256 : (t + 1) * 256] for t in range(16)]
    src, dst = iota((256, 256), 0), iota((256, 256), 1)
    wanted = 64 * ((dst % 128) // 32) + 32 * (dst // 128) + dst % 32
    picked = dot(jnp.concatenate(chunks, axis=0).astype(BF), (src == wanted).astype(F32).astype(BF))
    inner = []
    for core in range(2):
        halves = [
            jnp.concatenate(
                [
                    picked[t * 8 : (t + 1) * 8, core * 128 : (core + 1) * 128]
                    for t in range(half * 8, half * 8 + 8)
                ],
                axis=1,
            )
            for half in range(2)
        ]
        inner.append(jnp.concatenate(halves, axis=0))
    rest = jnp.concatenate([output_ref[...].astype(F32), jnp.zeros((8, D), F32)], axis=0)
    keep = jnp.concatenate([jnp.where(low_core, *inner), rest], axis=0).astype(BF)
    give = jnp.concatenate([jnp.where(low_core, *inner[::-1]), rest], axis=0).astype(BF)
    for j in range(8):
        lanes = slice(j * 128, j * 128 + 128)
        keep_ref[80 + j * 32 : 112 + j * 32, :] = keep[:, lanes]
        give_ref[80 + j * 32 : 112 + j * 32, :] = give[:, lanes]


pack = whole_call(
    pack_kernel, "pack", [((336, 128), BF)] * 2, 3, far_in=(1, 2, 3, 4, 6)
)


def chip_message_kernel(where, keep_ref, got_ref, out_ref):
    low_core = where[3] == 0
    keep, got = keep_ref[:80, :].astype(F32), got_ref[:80, :].astype(F32)
    first, second = jnp.where(low_core, keep, got), jnp.where(low_core, got, keep)
    rows = []
    for at in (0, 16, 32, 48, 8, 24, 40, 56, 64, 72):
        rows += [first[at : at + 8], second[at : at + 8]]
    out_ref[...] = jnp.concatenate(rows, axis=0).astype(BF)


chip_message = whole_call(chip_message_kernel, "chip_message", [((160, 128), BF)], 1)


def head_messages_kernel(where, y0, y1, y2, y3, *outs):
    pieces = (y0, y1, y2, y3)
    vec = []
    for piece in pieces:
        rows = piece[128:144, :].astype(F32)
        vec += [rows[0:1], rows[8:9]]
    vec = jnp.concatenate(vec + [jnp.zeros((8, 128), F32)], axis=0).astype(BF)
    for k in range(4):
        head = (where[1] + k) & 3
        q_rows = pl.ds(pl.multiple_of(head * 16, 16), 16)
        v_rows = pl.ds(pl.multiple_of(64 + head * 16, 16), 16)
        for n, piece in enumerate(pieces):
            outs[k][n * 16 : n * 16 + 16, :] = piece[q_rows, :]
            outs[k][96 + n * 16 : 112 + n * 16, :] = piece[v_rows, :]
        outs[k][64:80, :] = vec
        outs[k][80:96, :] = y0[144:160, :]


head_messages = whole_call(
    head_messages_kernel, "head_messages", [((160, 128), BF)] * 4, 1
)


def payload_kernel(where, keep_ref, got_ref, outer_ref, out_ref):
    low_core = where[3] == 0
    for j in range(8):
        lanes = slice(j * 128, j * 128 + 128)
        block = slice(80 + j * 32, 112 + j * 32)
        keep, got = keep_ref[block, :].astype(F32), got_ref[block, :].astype(F32)
        first, second = jnp.where(low_core, keep, got), jnp.where(low_core, got, keep)
        for at, to in ((0, 0), (8, 16), (16, 64)):
            out_ref[to : to + 16, lanes] = jnp.concatenate(
                [first[at : at + 8], second[at : at + 8]], axis=0
            ).astype(BF)
    out_ref[32:64, :] = outer_ref[...]


payload = whole_call(payload_kernel, "payload", [((80, D), BF)], 1)


def by_rows(where, pieces, ref):
    for m, rows in enumerate(pieces):
        for n in range(4):
            for k in range(4):
                chip = ((where[0] + n) % 4 * 4 + (where[1] + k) % 4) * 4 + (where[2] + m) % 4
                ref[pl.ds(pl.multiple_of(chip * 16, 16), 16), :] = rows(k, n)


def device_of(where, shape):
    row = iota(shape, 0)
    x, z, y = (where[2] + (row >> 5)) & 3, (where[1] + (row >> 3)) & 3, (where[0] + (row >> 1)) & 3
    return ((y * 4 + z) * 4 + x) * 2 + (row & 1)


def parameter(where, vec, v):
    shape = (128, D)
    lane = iota(shape, 1)
    picked = dot(vec, (iota(shape, 0) == 8 * v + (lane & 7)).astype(F32).astype(BF))
    mine = device_of(where, shape) == (lane >> 3)
    return jnp.sum(jnp.where(mine, picked, 0.0), axis=0, keepdims=True)


def assemble_kernel(where, x0, x1, x2, x3, w_ref, par_ref, tgt_ref, tgt_t_ref, count_ref, vec_ref):
    pieces = (x0, x1, x2, x3)
    by_rows(
        where,
        [
            lambda k, n, piece=piece: piece[k * 160 + n * 16 : k * 160 + n * 16 + 16, :]
            for piece in pieces
        ],
        w_ref,
    )
    vec = jnp.concatenate(
        [
            piece[k * 160 + 64 : k * 160 + 80, :].astype(F32)[:8]
            for piece in pieces
            for k in range(4)
        ],
        axis=0,
    ).astype(BF)
    vec_ref[...] = vec
    par_ref[...] = jnp.concatenate(
        [parameter(where, vec, 0), parameter(where, vec, 1), jnp.zeros((6, D), F32)], axis=0
    )
    empty = jnp.zeros((96, 128), F32)
    slots = [
        jnp.concatenate(
            [piece[k * 160 + 80 : k * 160 + 96, :] for k in range(4)], axis=0
        ).astype(F32)
        for piece in pieces
    ]
    for r in range(ROUNDS):
        rows = jnp.concatenate(
            [slots[m][s * 8 + r : s * 8 + r + 1] for m in range(4) for s in range(8)], axis=0
        )
        tgt_ref[r] = rows.astype(jnp.int32)
        tgt_t_ref[r] = jnp.transpose(jnp.concatenate([rows, empty], axis=0)).astype(jnp.int32)
        count_ref[r] = jnp.concatenate(
            [slots[m][s * 8 + 4 + r : s * 8 + 5 + r] for m in range(4) for s in range(8)], axis=0
        )


assemble = whole_call(
    assemble_kernel, "assemble",
    [
        ((D, 128), BF), ((8, D), F32), ((ROUNDS, 32, 128), jnp.int32),
        ((ROUNDS, 128, 128), jnp.int32), ((ROUNDS, 32, 128), F32), ((128, 128), BF),
    ],
    2, far_out=(2, 3),
)


def mask_kernel(where, count_ref, vec_ref, mask_ref, par_ref, bias_ref):
    z, x, c = where[1], where[2], where[3]

    @pl.when(pl.program_id(0) == 0)
    def _():
        vec = vec_ref[...]
        par_ref[...] = jnp.concatenate(
            [parameter(where, vec, v) for v in (2, 3, 4)] + [jnp.zeros((5, D), F32)], axis=0
        )
        wide = (128, 2048)
        lane = iota(wide, 1)
        picked = dot(vec, (iota(wide, 0) == 40 + (lane & 31)).astype(F32).astype(BF))
        mine = device_of(where, wide) == 2 * (lane >> 5) + c
        bias = jnp.sum(jnp.where(mine, picked, 0.0), axis=0, keepdims=True)
        bias_ref[...] = jnp.broadcast_to(bias, (8, 2048))

    shape = (256, 128)
    row, lane = iota(shape, 0), iota(shape, 1)
    source, rank = row >> 3, row & 7
    of_chip = lambda z_of, x_of, core: ((z_of & 3) * 8 + (x_of & 3) * 2 + core) * 8
    kpos = of_chip(z + ((source >> 1) & 3), x + (source >> 3), source & 1) + rank
    asker = (lane >> 3) & 7
    qpos = of_chip(z + (asker >> 1), x, asker & 1) + (lane & 7)
    code = jnp.where(kpos == qpos, -1.0, jnp.where(kpos < qpos, 0.0, -1e5))
    rank_f = rank.astype(F32)
    expand = (iota((256, 32), 0) >> 3) == iota((256, 32), 1)
    by_slot = dot(expand.astype(F32).astype(BF), count_ref[0].astype(BF)).astype(BF)
    bucket, side = iota((128, 128), 0), iota((128, 128), 1) >> 6

    @pl.loop(0, PAIRS, unroll=8)
    def _(p):
        select = (bucket == 2 * p + side).astype(F32).astype(BF)
        live = rank_f < dot(by_slot, select)
        mask_ref[0, p] = jnp.where(live, code, -1e5).astype(BF)


def make_mask(where, counts, vec):
    return kernel_call(
        mask_kernel,
        grid=(ROUNDS,),
        in_specs=[SMEM, per_round((32, 128)), fixed((128, 128))],
        out_specs=[per_round((PAIRS, 256, 128)), fixed((8, D)), fixed((8, 2048))],
        out_shape=[
            jax.ShapeDtypeStruct((ROUNDS, PAIRS, 256, 128), BF),
            jax.ShapeDtypeStruct((8, D), F32),
            jax.ShapeDtypeStruct((8, 2048), F32),
        ],
        far_out=(0,),
        compiler_params=params(16),
        cost_estimate=cost(7),
        name="make_mask",
    )(where, counts, vec)


def chip_rows(where, own, sib):
    low_core = where[3] == 0
    return jnp.concatenate([jnp.where(low_core, own, sib), jnp.where(low_core, sib, own)], axis=0)


def token_rows(where, own0, own3, sib):
    near = pl.program_id(0) == 0
    own = jnp.where(near, own0[...].astype(F32), own3[0].astype(F32))
    return chip_rows(where, own, sib[0].astype(F32))


def token_specs():
    return [
        pl.BlockSpec((TOK, D), lambda i: (0, 0)),
        pl.BlockSpec((1, TOK, D), lambda i: (jnp.maximum(i - 1, 0), 0, 0)),
        pl.BlockSpec((1, TOK, D), lambda i: (i, 0, 0)),
    ]


def project_kernel(where, own0, own3, sib, par_ref, w_ref, normed_ref, q_ref):
    rows = token_rows(where, own0, own3, sib)
    centered = rows - jnp.mean(rows, axis=-1, keepdims=True)
    spread = jnp.mean(centered * centered, axis=-1, keepdims=True)
    normed = centered * lax.rsqrt(spread + EPS_NORM) * par_ref[0:1, :] + par_ref[1:2, :]
    normed = normed.astype(BF)
    normed_ref[...] = normed
    q_ref[...] = dot(normed, w_ref[...]).astype(BF)


def project(where, tokens, par, w):
    whole = lambda i: (0, 0)
    return kernel_call(
        project_kernel,
        grid=(4,),
        in_specs=[SMEM] + token_specs()
        + [pl.BlockSpec((8, D), whole), pl.BlockSpec((D, HEAD_DIM), whole)],
        out_specs=[
            pl.BlockSpec((2 * TOK, D), lambda i: (i, 0)),
            pl.BlockSpec((2 * TOK, HEAD_DIM), lambda i: (i, 0)),
        ],
        out_shape=[
            jax.ShapeDtypeStruct((8 * TOK, D), BF),
            jax.ShapeDtypeStruct((8 * TOK, HEAD_DIM), BF),
        ],
        compiler_params=params(20),
        cost_estimate=cost(4),
        far_out=(0,),
        name="project",
    )(where, *tokens, par, w)


def project_values_kernel(where, x0, x1, x2, x3, normed_ref, v_ref, w_ref):
    @pl.when(pl.program_id(0) == 0)
    def _():
        by_rows(
            where,
            [
                lambda k, n, piece=piece: piece[k * 160 + n * 16 + 96 : k * 160 + n * 16 + 112, :]
                for piece in (x0, x1, x2, x3)
            ],
            w_ref,
        )

    v_ref[...] = dot(normed_ref[...], w_ref[...]).astype(BF)


def project_values(where, pieces, normed):
    return kernel_call(
        project_values_kernel,
        grid=(4,),
        in_specs=[SMEM] + [fixed(p.shape) for p in pieces]
        + [pl.BlockSpec((2 * TOK, D), lambda i: (i, 0))],
        out_specs=[
            pl.BlockSpec((2 * TOK, HEAD_DIM), lambda i: (i, 0)), fixed((D, HEAD_DIM)),
        ],
        out_shape=[
            jax.ShapeDtypeStruct((8 * TOK, HEAD_DIM), BF),
            jax.ShapeDtypeStruct((D, HEAD_DIM), BF),
        ],
        compiler_params=params(16),
        cost_estimate=cost(3),
        far_in=(5,),
        name="project_values",
    )(where, *pieces, normed)


def project_back_kernel(
    where, own0, own3, sib, wq_ref, wv_ref, normed_ref, q_ref, gq_ref,
    gk_ref, gv_ref, own_out, sib_out, wg0, wg1, wg2, wg3, total, sums,
):
    step = pl.program_id(0)
    x = token_rows(where, own0, own3, sib)
    q = q_ref[...].astype(F32)
    inv = lax.rsqrt(jnp.sum(q * q, axis=-1, keepdims=True) + EPS_KEY)
    gk = total_of([gk_ref[m] for m in range(4)])
    gv = total_of([gv_ref[m] for m in range(4)])
    along = jnp.sum(q * gk, axis=-1, keepdims=True)
    gq = gq_ref[...] + gk * inv - q * (inv * inv * inv * along)
    rows = jnp.concatenate([gq.astype(BF), gv.astype(BF)], axis=1)
    back = dot_t(rows[:, :HEAD_DIM], wq_ref[...]) + dot_t(rows[:, HEAD_DIM:], wv_ref[...])

    low_core = where[3] == 0
    own_out[0] = jnp.where(low_core, back[:TOK], back[TOK:]).astype(BF)
    sib_out[0] = jnp.where(low_core, back[TOK:], back[:TOK]).astype(BF)
    centered = x - jnp.mean(x, axis=-1, keepdims=True)
    spread = jnp.mean(centered * centered, axis=-1, keepdims=True)
    xhat = centered * lax.rsqrt(spread + EPS_NORM)
    gain_part = jnp.sum((back * xhat).reshape(TOK // 4, 8, D), axis=0)
    shift_part = jnp.sum(back.reshape(TOK // 4, 8, D), axis=0)
    weight_part = t_dot(normed_ref[...], rows)

    @pl.when(step == 0)
    def _():
        total[:, :256] = weight_part
        sums[0:8, :] = gain_part
        sums[8:16, :] = shift_part

    @pl.when(step > 0)
    def _():
        total[:, :256] += weight_part
        sums[0:8, :] += gain_part
        sums[8:16, :] += shift_part

    @pl.when(step == 3)
    def _():
        gain_sum = jnp.sum(sums[0:8, :], axis=0, keepdims=True)
        shift_sum = jnp.sum(sums[8:16, :], axis=0, keepdims=True)
        both = jnp.where(iota((HEAD_DIM, D), 0) < 64, gain_sum, shift_sum)
        total[:, 256:] = jnp.transpose(both)
        for k, out in enumerate((wg0, wg1, wg2, wg3)):
            rows = pl.ds(pl.multiple_of(((where[0] + k) & 3) * 256, 256), 256)
            out[...] = total[rows, :].astype(BF)


def project_back(where, tokens, wq, wv, normed, q, gq, gk, gv):
    token_block = pl.BlockSpec((1, TOK, D), lambda i: (i, 0, 0))
    whole = lambda i: (0, 0)
    row_block = lambda width: pl.BlockSpec((2 * TOK, width), lambda i: (i, 0))
    return kernel_call(
        project_back_kernel,
        grid=(4,),
        in_specs=[SMEM] + token_specs()
        + [
            pl.BlockSpec((D, HEAD_DIM), whole),
            pl.BlockSpec((D, HEAD_DIM), whole),
            row_block(D),
            row_block(HEAD_DIM),
            row_block(HEAD_DIM),
        ]
        + [pl.BlockSpec((4, 2 * TOK, HEAD_DIM), lambda i: (0, i, 0))] * 2,
        out_specs=[token_block, token_block] + [pl.BlockSpec((256, 384), whole)] * 4,
        out_shape=[
            jax.ShapeDtypeStruct((4, TOK, D), BF),
            jax.ShapeDtypeStruct((4, TOK, D), BF),
        ]
        + [jax.ShapeDtypeStruct((256, 384), BF)] * 4,
        scratch_shapes=[pltpu.VMEM((D, 384), F32), pltpu.VMEM((16, D), F32)],
        compiler_params=params(30),
        cost_estimate=cost(8),
        far_in=(2, 3, 4, 5, 6, 7, 8),
        far_out=(0, 1, 2, 3, 4, 5),
        name="project_back",
    )(where, *tokens, wq, wv, normed, q, gq, gk, gv)


def normalized(values):
    centered = values - jnp.mean(values, axis=-1, keepdims=True)
    spread = jnp.mean(centered * centered, axis=-1, keepdims=True)
    scale = lax.rsqrt(spread + EPS_NORM)
    return centered * scale, scale


def norm_back(u, xhat, scale):
    mean_u = jnp.mean(u, axis=-1, keepdims=True)
    mean_ux = jnp.mean(u * xhat, axis=-1, keepdims=True)
    return (u - mean_u - xhat * mean_ux) * scale


def head_rows(w_ref, head):
    return w_ref[pl.ds(head * 8, 8)].reshape(HEAD_DIM, D)


def heads_of(where):
    for side in range(2):
        core = where[3] if side == 0 else 1 - where[3]
        for m in range(4):
            yield side, m, core * 4 + (where[1] + m) % 4


GELU_IN = 0.7978845608028654
GELU_CUBE = 0.044715


def feed_kernel(
    where, mix_own, mix_sib, first_own, first_sib, cot_own, cot_sib, par_ref, bias_ref,
    out_w, inner_ref, outer_ref,
    sum_ref, first_out, input_t_ref, active_ref, grad_ref, back_ref, hid_sum_ref, cot_sum_ref,
    ffn_in, cot_t, back_t,
):
    step = pl.program_id(0)

    @pl.when(step == 0)
    def _():
        total = chip_rows(where, first_own[...].astype(F32), first_sib[0].astype(F32))
        mixes = (mix_own, mix_sib)
        for side, m, head in heads_of(where):
            total = total + dot(mixes[side][:, m * 128 : m * 128 + 128], head_rows(out_w, head))
        sum_ref[...] = total
        own = jnp.where(where[3] == 0, total[:TOK], total[TOK:])
        first_out[...] = own.astype(BF)
        xhat, _ = normalized(total)
        rows = xhat * par_ref[0:1, :] + par_ref[1:2, :]
        ffn_in[...] = rows.astype(BF)
        input_t_ref[...] = jnp.transpose(rows).astype(BF)
        cot = chip_rows(where, cot_own[...].astype(F32), cot_sib[0].astype(F32))
        cot_t[...] = jnp.transpose(cot).astype(BF)
        cot_sum_ref[...] = jnp.broadcast_to(jnp.sum(cot, axis=0, keepdims=True), (8, D))

    inner = inner_ref[...].reshape(D, 512)
    outer = outer_ref[...].reshape(512, D)
    hidden = dot(ffn_in[...], inner) + bias_ref[0:1, :]
    square = hidden * hidden
    bent = jnp.tanh(GELU_IN * hidden * (1.0 + GELU_CUBE * square))
    half = 0.5 * (1.0 + bent)
    active_ref[...] = (hidden * half).astype(BF)
    slope = half + 0.5 * hidden * (1.0 - bent * bent) * GELU_IN * (
        1.0 + 3.0 * GELU_CUBE * square
    )
    grad_active = jnp.transpose(dot(outer, cot_t[...]))
    grad = (grad_active * slope).astype(BF)
    grad_ref[...] = grad
    hid_sum_ref[...] = jnp.broadcast_to(
        jnp.sum(grad.astype(F32), axis=0, keepdims=True), (8, 512)
    )
    part = dot(inner, jnp.transpose(grad))

    @pl.when(step == 0)
    def _():
        back_t[...] = part

    @pl.when(step > 0)
    def _():
        back_t[...] += part

    @pl.when(step == 3)
    def _():
        back_ref[...] = jnp.transpose(back_t[...])


def feed(where, mix_own, mix_sib, first_in, cot_second, sib_rows, par, bias, gathered):
    whole = lambda i: (0, 0)
    two = 2 * TOK
    return kernel_call(
        feed_kernel,
        grid=(4,),
        in_specs=[
            SMEM,
            pl.BlockSpec((two, 512), whole),
            pl.BlockSpec((two, 512), whole),
            pl.BlockSpec((TOK, D), whole),
            pl.BlockSpec((1, TOK, D), lambda i: (0, 0, 0)),
            pl.BlockSpec((TOK, D), whole),
            pl.BlockSpec((1, TOK, D), lambda i: (2, 0, 0)),
            pl.BlockSpec((8, D), whole),
            pl.BlockSpec((8, 512), lambda i: (0, i)),
            pl.BlockSpec((64, 16, D), lambda i: (0, 4, 0)),
            pl.BlockSpec((64, 16, 512), lambda i: (0, i // 2, i % 2)),
            pl.BlockSpec((16, 32, D), lambda i: (i, 1, 0)),
        ],
        out_specs=[
            pl.BlockSpec((two, D), whole),
            pl.BlockSpec((TOK, D), whole),
            pl.BlockSpec((D, two), whole),
            pl.BlockSpec((two, 512), lambda i: (0, i)),
            pl.BlockSpec((two, 512), lambda i: (0, i)),
            pl.BlockSpec((two, D), whole),
            pl.BlockSpec((8, 512), lambda i: (0, i)),
            pl.BlockSpec((8, D), whole),
        ],
        out_shape=[
            jax.ShapeDtypeStruct((two, D), F32),
            jax.ShapeDtypeStruct((TOK, D), BF),
            jax.ShapeDtypeStruct((D, two), BF),
            jax.ShapeDtypeStruct((two, 2048), BF),
            jax.ShapeDtypeStruct((two, 2048), BF),
            jax.ShapeDtypeStruct((two, D), F32),
            jax.ShapeDtypeStruct((8, 2048), F32),
            jax.ShapeDtypeStruct((8, D), F32),
        ],
        scratch_shapes=[
            pltpu.VMEM((two, D), BF),
            pltpu.VMEM((D, two), BF),
            pltpu.VMEM((D, two), F32),
        ],
        compiler_params=params(32),
        cost_estimate=cost(16),
        far_in=(4, 6, 9, 10, 11),
        far_out=(0, 2, 3, 4, 5),
        name="feed",
    )(
        where, mix_own, mix_sib, first_in, sib_rows, cot_second, sib_rows, par, bias,
        gathered, gathered, gathered,
    )


def first_back_kernel(
    where, back_own, back_sib, sum_ref, cot_own, cot_sib, par_ref, out_w,
    grad_first, branch_ref, m0, m1, m2, m3, sums_ref,
):
    back = back_own[...] + back_sib[...]
    xhat, scale = normalized(sum_ref[...])
    total = chip_rows(where, cot_own[...].astype(F32), cot_sib[0].astype(F32))
    total = total + norm_back(back * par_ref[0:1, :], xhat, scale)
    branch = total.astype(BF)
    branch_ref[...] = branch
    grad_first[...] = jnp.where(where[3] == 0, total[:TOK], total[TOK:]).astype(BF)
    outs = (m0, m1, m2, m3)
    for side, m, head in heads_of(where):
        if side == 0:
            outs[m][...] = dot_t(branch, head_rows(out_w, head)).astype(BF)
    gain = jnp.sum(back * xhat, axis=0, keepdims=True)
    shift = jnp.sum(back, axis=0, keepdims=True)
    sums_ref[...] = jnp.concatenate([gain, shift, jnp.zeros((6, D), F32)], axis=0)


def first_back(where, back_own, back_sib, first_sum, cot_first, sib_rows, par, gathered):
    two = 2 * TOK
    one = lambda shape: pl.BlockSpec(shape, lambda i: (0,) * len(shape))
    return kernel_call(
        first_back_kernel,
        grid=(1,),
        in_specs=[
            SMEM, one((two, D)), one((two, D)), one((two, D)), one((TOK, D)),
            pl.BlockSpec((1, TOK, D), lambda i: (1, 0, 0)),
            one((8, D)),
            pl.BlockSpec((64, 16, D), lambda i: (0, 4, 0)),
        ],
        out_specs=[one((TOK, D)), one((two, D))] + [one((two, 128))] * 4 + [one((8, D))],
        out_shape=[jax.ShapeDtypeStruct((TOK, D), BF), jax.ShapeDtypeStruct((two, D), BF)]
        + [jax.ShapeDtypeStruct((two, 128), BF)] * 4
        + [jax.ShapeDtypeStruct((8, D), F32)],
        compiler_params=params(24),
        cost_estimate=cost(6),
        far_in=(1, 3, 5, 7),
        far_out=(1,),
        name="first_back",
    )(where, back_own, back_sib, first_sum, cot_first, sib_rows, par, gathered)


def inner_grads_kernel(where, active_ref, grad_ref, input_t, cot_own, cot_sib, a0, a1, a2, a3, cot):
    step = pl.program_id(0)

    @pl.when(step == 0)
    def _():
        cot[...] = chip_rows(
            where, cot_own[:, :256].astype(F32), cot_sib[0, :, :256].astype(F32)
        ).astype(BF)

    lanes = pl.ds(pl.multiple_of(step * 512, 512), 512)
    outs = (a0, a1, a2, a3)
    inner = dot(input_t[...], grad_ref[...]).astype(BF).reshape(4, 16, 16, 512)
    outer = t_dot(active_ref[...], cot[...]).astype(BF).reshape(16, 32, 256)
    for k, out in enumerate(outs):
        for y in range(4):

            @pl.when(((y - where[0]) & 3) == k)
            def _(out=out, y=y):
                out[:, :, lanes] = inner[y]

        @pl.when(((step - where[0]) & 3) == k)
        def _(out=out):
            out[:, :, 2048:2304] = outer[:, :16]
            out[:, :, 2304:] = outer[:, 16:]


def inner_grads(where, active, grad, input_t, cot_second, sib_rows):
    two = 2 * TOK
    whole = lambda i: (0, 0)
    return kernel_call(
        inner_grads_kernel,
        grid=(4,),
        in_specs=[
            SMEM,
            pl.BlockSpec((two, 512), lambda i: (0, i)),
            pl.BlockSpec((two, 512), lambda i: (0, i)),
            pl.BlockSpec((D, two), whole),
            pl.BlockSpec((TOK, D), whole),
            pl.BlockSpec((1, TOK, D), lambda i: (2, 0, 0)),
        ],
        out_specs=[pl.BlockSpec((16, 16, 2560), lambda i: (0, 0, 0))] * 4,
        out_shape=[jax.ShapeDtypeStruct((16, 16, 2560), BF)] * 4,
        scratch_shapes=[pltpu.VMEM((two, 256), BF)],
        compiler_params=params(32),
        cost_estimate=cost(9),
        far_in=(1, 2, 3, 5),
        far_out=(0, 1, 2, 3),
        name="inner_grads",
    )(where, active, grad, input_t, cot_second, sib_rows)


def outer_grads_kernel(
    where, active_ref, cot_own, cot_sib, mix_own, mix_sib, branch_ref, sums_ref,
    b0, b1, b2, b3, cot,
):
    step = pl.program_id(0)
    outs = (b0, b1, b2, b3)

    @pl.when(step == 0)
    def _():
        cot[...] = chip_rows(
            where, cot_own[:, 256:].astype(F32), cot_sib[0, :, 256:].astype(F32)
        ).astype(BF)
        cols = jnp.where(
            where[3] == 0, branch_ref[:, :512].astype(F32), branch_ref[:, 512:].astype(F32)
        ).astype(BF)
        mixes = (mix_own, mix_sib)
        for side, m, head in heads_of(where):
            rows = t_dot(mixes[side][:, m * 128 : m * 128 + 128], cols).astype(BF)
            rows = rows.reshape(2, 4, 16, 512)
            at = pl.ds((head >> 1) * 4, 4)
            for part in range(2):
                near = (2 * (head & 1) + part - where[1]) & 3
                for k, out in enumerate(outs):

                    @pl.when(near == k)
                    def _(part=part, out=out, rows=rows, at=at):
                        out[at, 0:16, :256] = rows[part, :, :, :256]
                        out[at, 16:32, :256] = rows[part, :, :, 256:]

        for k, out in enumerate(outs):
            near = (where[1] + k) & 3
            for y in range(4):
                out[y * 4 : y * 4 + 4, 0:16, 256:384] = sums_ref[pl.ds(y * 16 + near * 4, 4)]
                out[y * 4 : y * 4 + 4, 16:32, 256:384] = jnp.zeros((4, 16, 128), BF)

    outer = t_dot(active_ref[...], cot[...]).astype(BF).reshape(4, 4, 32, 768)
    for z in range(4):
        for k, out in enumerate(outs):

            @pl.when(((z - where[1]) & 3) == k)
            def _(z=z, out=out):
                out[pl.ds(step * 4, 4), :, 384:] = outer[z]


def outer_grads(where, active, cot_second, sib_rows, mix_own, mix_sib, branch, sums):
    two = 2 * TOK
    whole = lambda i: (0, 0)
    whole3 = lambda i: (0, 0, 0)
    return kernel_call(
        outer_grads_kernel,
        grid=(4,),
        in_specs=[
            SMEM,
            pl.BlockSpec((two, 512), lambda i: (0, i)),
            pl.BlockSpec((TOK, D), whole),
            pl.BlockSpec((1, TOK, D), lambda i: (2, 0, 0)),
            pl.BlockSpec((two, 512), whole),
            pl.BlockSpec((two, 512), whole),
            pl.BlockSpec((two, D), whole),
            pl.BlockSpec((64, 16, 128), whole3),
        ],
        out_specs=[pl.BlockSpec((16, 32, 1152), whole3)] * 4,
        out_shape=[jax.ShapeDtypeStruct((16, 32, 1152), BF)] * 4,
        scratch_shapes=[pltpu.VMEM((two, 768), BF)],
        compiler_params=params(32),
        cost_estimate=cost(10),
        far_in=(1, 3, 5, 6),
        far_out=tuple(range(4)),
        name="outer_grads",
    )(where, active, cot_second, sib_rows, mix_own, mix_sib, branch, sums)


def second_kernel(where, active_ref, outer_ref, own_ref, give_ref, total):
    step = pl.program_id(0)
    part = dot(active_ref[...], outer_ref[...].reshape(512, D))

    @pl.when(step == 0)
    def _():
        total[...] = part

    @pl.when(step > 0)
    def _():
        total[...] += part

    @pl.when(step == 3)
    def _():
        low_core = where[3] == 0
        own_ref[...] = jnp.where(low_core, total[:TOK], total[TOK:])
        give_ref[...] = jnp.where(low_core, total[TOK:], total[:TOK])


def second_parts(where, active, gathered):
    two = 2 * TOK
    whole = lambda i: (0, 0)
    return kernel_call(
        second_kernel,
        grid=(4,),
        in_specs=[
            SMEM,
            pl.BlockSpec((two, 512), lambda i: (0, i)),
            pl.BlockSpec((16, 32, D), lambda i: (i, 1, 0)),
        ],
        out_specs=[pl.BlockSpec((TOK, D), whole)] * 2,
        out_shape=[jax.ShapeDtypeStruct((TOK, D), F32)] * 2,
        scratch_shapes=[pltpu.VMEM((two, D), F32)],
        compiler_params=params(20),
        cost_estimate=cost(4),
        far_in=(1, 2),
        name="second_parts",
    )(where, active, gathered)


def recut_kernel(axis, where, *refs):
    parts, outs = refs[:4], refs[4:]
    for k, out in enumerate(outs):
        mine = (where[axis] + k) & 3
        out[...] = total_of([part[mine] for part in parts]).astype(BF)


recut_a = whole_call(
    functools.partial(recut_kernel, 1), "recut_a", [((4, 16, 2560), BF)] * 4, 4, mib=32,
    far_in=(1,), far_out=(0, 1, 2, 3),
)
recut_b = whole_call(
    functools.partial(recut_kernel, 0), "recut_b", [((4, 32, 1152), BF)] * 4, 3, mib=24,
    far_in=(1,), far_out=(0, 1, 2, 3),
)


def join_kernel(where, *refs):
    w, a, b, outs = refs[:4], refs[4:8], refs[8:12], refs[12:]
    for k, out in enumerate(outs):
        x = (where[2] + k) & 3
        for z in range(4):
            rows = pl.ds(pl.multiple_of(z * 64 + x * 16, 16), 16)
            total = total_of([part[rows, :] for part in w]).astype(BF)
            for j in range(3):
                at = (z * 3 + j) * 16
                out[at : at + 16, :] = total[:, j * 128 : j * 128 + 128]
        total = total_of([part[x] for part in a]).astype(BF)
        for j in range(20):
            out[192 + j * 16 : 208 + j * 16, :] = total[:, j * 128 : j * 128 + 128]
        total = total_of([part[x] for part in b]).astype(BF)
        for j in range(9):
            out[512 + j * 32 : 544 + j * 32, :] = total[:, j * 128 : j * 128 + 128]


join = whole_call(join_kernel, "join", [((800, 128), BF)] * 4, 3)


def divide_kernel(where, x0, x1, x2, x3, w0, w1, w2, w3, keep_ref, give_ref, outer_ref, small_ref, total):
    low_core = where[3] == 0
    total[...] = total_of([part[...] for part in (x0, x1, x2, x3)])
    for k, out in enumerate((w0, w1, w2, w3)):
        z = (where[1] + k) & 3
        for j in range(3):
            rows = pl.ds(pl.multiple_of((z * 3 + j) * 16, 16), 16)
            out[:, j * 128 : j * 128 + 128] = total[rows, :].astype(BF)
    blocks = [total[192 + j * 16 : 208 + j * 16, :] for j in range(16)]
    for at in (512, 528):
        blocks += [total[at : at + 16, :], total[at + 32 : at + 48, :]]
    low = jnp.concatenate([block[:8] for block in blocks], axis=0)
    high = jnp.concatenate([block[8:] for block in blocks], axis=0)
    keep_ref[...] = jnp.where(low_core, low, high)
    give_ref[...] = jnp.where(low_core, high, low).astype(BF)
    for j in range(2):
        lanes = slice(j * 128, j * 128 + 128)
        outer_ref[:16, lanes] = total[448 + j * 16 : 464 + j * 16, :]
        outer_ref[16:, lanes] = total[480 + j * 16 : 496 + j * 16, :]
    for j in range(6):
        lanes = slice(256 + j * 128, 384 + j * 128)
        outer_ref[:, lanes] = total[608 + j * 32 : 640 + j * 32, :]
    small_ref[...] = total[576:584, :]


divide = whole_call(
    divide_kernel, "divide",
    [((16, 384), BF)] * 4 + [((160, 128), F32), ((160, 128), BF), ((32, D), F32), ((8, 128), F32)],
    2, scratch=[pltpu.VMEM((800, 128), F32)],
)


def last_kernel(where, w0, w1, w2, w3, give_ref, keep_w, out_ref, kept, given):
    low_core = where[3] == 0
    for m, piece in enumerate((w0, w1, w2, w3)):
        z = (where[1] + m) & 3
        rows = piece[...].astype(F32)
        mine = jnp.where(low_core, rows[:8], rows[8:])
        other = jnp.where(low_core, rows[8:], rows[:8])
        for j in range(3):
            at = pl.ds(pl.multiple_of((z * 3 + j) * 8, 8), 8)
            kept[at, :] = mine[:, j * 128 : j * 128 + 128]
            given[at, :] = other[:, j * 128 : j * 128 + 128]
    keep_w[...] = kept[...]
    out_ref[:96, :] = given[...].astype(BF)
    out_ref[96:, :] = give_ref[...]


last = whole_call(
    last_kernel, "last", [((96, 128), F32), ((256, 128), BF)], 1,
    scratch=[pltpu.VMEM((96, 128), F32)] * 2,
)


def finish_kernel(
    where, keep_w, keep_ref, got_ref, joint_ref, value_ref, norm_ref, inner_ref, output_ref
):
    low_core = where[3] == 0
    got = got_ref[...].astype(F32)
    mine, other = keep_w[...], got[:96]
    norm = jnp.zeros((8, 128), F32)
    for core in range(2):
        rows = jnp.where(low_core, *((mine, other) if core == 0 else (other, mine)))
        for z in range(4):
            lanes = slice((core * 4 + z) * 128, (core * 4 + z + 1) * 128)
            joint_ref[:, lanes] = rows[z * 24 : z * 24 + 8]
            value_ref[:, lanes] = rows[z * 24 + 8 : z * 24 + 16]
            norm = norm + rows[z * 24 + 16 : z * 24 + 24]
    norm_ref[...] = norm
    mine, other = keep_ref[...], got[96:]
    low, high = jnp.where(low_core, mine, other), jnp.where(low_core, other, mine)
    both = jnp.concatenate([low[:128], high[:128]], axis=1).astype(BF)
    dst, src = iota((256, 256), 1), iota((256, 256), 0)
    wanted = 128 * ((dst >> 5) & 1) + 32 * (dst >> 6) + (dst & 31)
    mixed = dot(both, (src == wanted).astype(F32).astype(BF))
    for t in range(16):
        inner_ref[:, t * 256 : (t + 1) * 256] = mixed[t * 8 : t * 8 + 8, :]
    for core, rows in enumerate((low, high)):
        for at, lane in enumerate((0, 128, 256, 384)):
            lanes = slice(core * 512 + lane, core * 512 + lane + 128)
            output_ref[:, lanes] = rows[128 + at * 8 : 136 + at * 8]


finish = whole_call(
    finish_kernel, "finish",
    [((8, D), F32), ((8, D), F32), ((8, 128), F32), ((8, FF), F32), ((8, D), F32)], 1,
)


def make_keys(pieces, rows_ref):
    for m, piece in enumerate(pieces):

        @pl.loop(0, 8, unroll=4)
        def _(s, m=m, piece=piece):
            rows = pl.ds(pl.multiple_of(s * TOK, TOK), TOK)
            to = pl.ds(pl.multiple_of(m * 8 * TOK + s * TOK, TOK), TOK)
            q = piece[rows, :].astype(F32)
            inv = lax.rsqrt(jnp.sum(q * q, axis=-1, keepdims=True) + EPS_KEY)
            rows_ref[to, :] = (q * inv).astype(BF)


def round_weights(lt_ref, at):
    totals = [lt_ref[r, at, :].astype(F32) for r in range(ROUNDS)]
    peak = jnp.maximum(jnp.maximum(totals[0], totals[1]), jnp.maximum(totals[2], totals[3]))
    exps = [jnp.exp(t - peak) for t in totals]
    scale = 1.0 / (exps[0] + exps[1] + exps[2] + exps[3])
    return [e * scale for e in exps]


def hot_slots(tgt_ref, source):
    slots = iota((BUCKETS * MOST, TOK), 0)
    return (slots == tgt_ref[0, pl.ds(source, 1), :]).astype(F32).astype(BF)


def hot_tokens(tgt_t_ref, source):
    slots = iota((TOK, BUCKETS * MOST), 1)
    return (slots == tgt_t_ref[0, :, source : source + 1]).astype(F32).astype(BF)


def spread(first, second):
    width = first.shape[-1]
    both = [a.reshape(PAIRS, 2, MOST, width) for a in (first, second)]
    return jnp.concatenate(both, axis=2).astype(BF)


def fill(tgt_ref, read_rows, ref):
    @pl.loop(0, 16, unroll=4)
    def _(pair):
        placed = [
            dot(hot_slots(tgt_ref, pair * 2 + half), read_rows(pair * 2 + half))
            for half in range(2)
        ]
        both = spread(*placed)
        at = pl.ds(pl.multiple_of(pair * 16, 16), 16)
        ref[0, :, at, :128] = both[:, 0]
        ref[0, :, at, 128:] = both[:, 1]


def place(both, ref, pair):
    at = pl.multiple_of(pair * 16, 16)
    ref[:, pl.ds(at, 16), :] = both[:, 0]
    ref[:, pl.ds(64 + at, 16), :] = both[:, 1]


def diagonal(rows):
    first = iota((128, 128), 0) < 64
    none = jnp.zeros((128, 128), BF)
    return jnp.concatenate([jnp.where(first, rows, none), jnp.where(first, none, rows)], axis=1)


def diagonal_t(rows):
    turned = jnp.transpose(rows)
    first = iota((128, 128), 1) < 64
    none = jnp.zeros((128, 128), BF)
    return jnp.concatenate([jnp.where(first, turned, none), jnp.where(first, none, turned)], axis=0)


def eye():
    return iota((128, 128), 0) == iota((128, 128), 1)


def token_block(s):
    return pl.ds(pl.multiple_of(s * TOK, TOK), TOK)


def scores_kernel(q0, q1, q2, q3, tgt_ref, mask_ref, probs_ref, keys_ref, qm_ref, log_ref, k_rows):
    @pl.when(pl.program_id(0) == 0)
    def _():
        make_keys((q0, q1, q2, q3), k_rows)

    fill(tgt_ref, lambda source: k_rows[token_block(source), :], keys_ref)

    @pl.loop(0, 4, unroll=4)
    def _(pair):
        placed = [
            dot(hot_slots(tgt_ref, pair * 2 + half), q0[token_block(pair * 2 + half), :])
            for half in range(2)
        ]
        place(spread(*placed), qm_ref.at[0], pair)

    @pl.loop(0, PAIRS, unroll=16)
    def _(p):
        code = mask_ref[0, p].astype(F32)
        scores = dot(keys_ref[0, p], diagonal_t(qm_ref[0, p]))
        scores = jnp.where(code == 0.0, scores, code * 1e4)
        peak = jnp.max(scores, axis=0, keepdims=True)
        exponent = jnp.exp(scores - peak)
        total = jnp.sum(exponent, axis=0, keepdims=True)
        probs_ref[0, p] = (exponent * (1.0 / total)).astype(BF)
        log_ref[0, pl.ds(p, 1), :] = peak + jnp.log(total)


def attend_scores(q_pieces, tgt, mask):
    rows = 8 * TOK
    outs = [(PAIRS, 256, 128), (PAIRS, 256, 256), (PAIRS, 128, 128), (PAIRS, 128)]
    types = [BF, BF, BF, F32]
    return kernel_call(
        scores_kernel,
        grid=(ROUNDS,),
        in_specs=[fixed((rows, HEAD_DIM))] * 4
        + [per_round((32, TOK)), per_round((PAIRS, 256, 128))],
        out_specs=[per_round(shape) for shape in outs],
        out_shape=[
            jax.ShapeDtypeStruct((ROUNDS,) + shape, t) for shape, t in zip(outs, types)
        ],
        scratch_shapes=[pltpu.VMEM((4 * rows, HEAD_DIM), BF)],
        compiler_params=params(20),
        cost_estimate=cost(18),
        far_in=(5,),
        far_out=(0, 1, 2),
        name="attend_scores",
    )(*q_pieces, tgt, mask)


def values_kernel(
    v0, v1, v2, v3, tgt_ref, tgt_t_ref, probs_ref, log_ref, mixed_ref, ro_ref, lt_ref, values_ref, att
):
    this_round = pl.program_id(0)
    for m, piece in enumerate((v0, v1, v2, v3)):

        @pl.loop(0, 4, unroll=4)
        def _(pair, m=m, piece=piece):
            placed = [
                dot(
                    hot_slots(tgt_ref, m * 8 + pair * 2 + half),
                    piece[token_block(pair * 2 + half), :],
                )
                for half in range(2)
            ]
            both = spread(*placed)
            at = pl.ds(pl.multiple_of((m * 4 + pair) * 16, 16), 16)
            values_ref[0, :, at, :128] = both[:, 0]
            values_ref[0, :, at, 128:] = both[:, 1]

    ones = jnp.ones((128, 128), BF)

    @pl.loop(0, PAIRS, unroll=16)
    def _(p):
        out = t_dot(probs_ref[0, p], values_ref[0, p])
        log_total = log_ref[0, pl.ds(p, 1), :]
        logs = dot(jnp.where(eye(), log_total, 0.0).astype(BF), ones)
        att[p, 0, :, :128] = out[:64, :128]
        att[p, 1, :, :128] = out[64:, 128:]
        att[p, 0, :, 128:] = logs[:64]
        att[p, 1, :, 128:] = logs[64:]

    for s in range(8):
        slots = att[:, :, s * MOST : (s + 1) * MOST, :].reshape(256, 256)
        rows = dot(hot_tokens(tgt_t_ref, s), slots.astype(BF)).astype(BF)
        ro_ref[this_round, s * TOK : (s + 1) * TOK, :] = rows[:, :HEAD_DIM]
        lt_ref[this_round, s * TOK : (s + 1) * TOK, :] = rows[:, HEAD_DIM:]

    @pl.when(this_round == ROUNDS - 1)
    def _():
        @pl.loop(0, 8, unroll=4)
        def _(s):
            at = token_block(s)
            weights = round_weights(lt_ref, at)
            mixed = weights[0] * ro_ref[0, at, :].astype(F32)
            for r in range(1, ROUNDS):
                mixed = mixed + weights[r] * ro_ref[r, at, :].astype(F32)
            mixed_ref[at, :] = mixed.astype(BF)


def attend_values(v_pieces, tgt, tgt_t, probs, logs):
    rows = 8 * TOK
    return kernel_call(
        values_kernel,
        grid=(ROUNDS,),
        in_specs=[fixed((rows, HEAD_DIM))] * 4
        + [
            per_round((32, TOK)), per_round((TOK, 128)), per_round((PAIRS, 256, 128)),
            per_round((PAIRS, 128)),
        ],
        out_specs=[
            fixed((rows, HEAD_DIM)),
            fixed((ROUNDS, rows, HEAD_DIM)),
            fixed((ROUNDS, rows, HEAD_DIM)),
            per_round((PAIRS, 256, 256)),
        ],
        out_shape=[
            jax.ShapeDtypeStruct((rows, HEAD_DIM), BF),
            jax.ShapeDtypeStruct((ROUNDS, rows, HEAD_DIM), BF),
            jax.ShapeDtypeStruct((ROUNDS, rows, HEAD_DIM), BF),
            jax.ShapeDtypeStruct((ROUNDS, PAIRS, 256, 256), BF),
        ],
        scratch_shapes=[pltpu.VMEM((PAIRS, 2, 64, 256), F32)],
        compiler_params=params(22),
        cost_estimate=cost(14),
        far_in=(6,),
        far_out=(1, 2, 3),
        name="attend_values",
    )(*v_pieces, tgt, tgt_t, probs, logs)


def take_slots(tgt_t_ref, slots_ref, rows_ref, sources):
    for s in range(sources):
        slots = slots_ref[:, :, s * MOST : (s + 1) * MOST, :].reshape(256, HEAD_DIM)
        rows_ref[s * TOK : (s + 1) * TOK, :] += dot(hot_tokens(tgt_t_ref, s), slots.astype(BF))


def values_back_kernel(
    where, tgt_ref, tgt_t_ref, probs_ref, ro_ref, lt_ref, gm_ref, out_ref, gd_ref, gt_ref, gt_slots, slots, rows, token_rows,
):
    this_round = pl.program_id(0)

    @pl.when(this_round == 0)
    def _():
        rows[...] = jnp.zeros_like(rows)

        @pl.loop(0, 8, unroll=4)
        def _(s):
            at = token_block(s)
            weights = round_weights(lt_ref, at)
            grad = gm_ref[at, :].astype(F32)
            agree = [
                jnp.sum(grad * ro_ref[r, at, :].astype(F32), axis=-1, keepdims=True)
                for r in range(ROUNDS)
            ]
            mean = total_of([weights[r] * agree[r] for r in range(ROUNDS)])
            for r in range(ROUNDS):
                token_rows[r, at, :HEAD_DIM] = (weights[r] * grad).astype(BF)
                token_rows[r, at, HEAD_DIM:] = (weights[r] * (agree[r] - mean)).astype(BF)

    @pl.loop(0, 4, unroll=4)
    def _(pair):
        placed = [
            dot(
                hot_slots(tgt_ref, pair * 2 + half),
                token_rows[this_round, token_block(pair * 2 + half), :],
            )
            for half in range(2)
        ]
        both = spread(*placed)
        place(both[..., :HEAD_DIM], gd_ref.at[0], pair)
        place(both[..., HEAD_DIM:], gt_slots, pair)

    @pl.loop(0, PAIRS, unroll=16)
    def _(p):
        grad_values = dot(probs_ref[0, p], diagonal(gd_ref[0, p]))
        slots[p, 0] = grad_values[:, :128]
        slots[p, 1] = grad_values[:, 128:]
        gt_ref[0, pl.ds(p, 1), :] = jnp.sum(
            jnp.where(eye(), gt_slots[p].astype(F32), 0.0), axis=0, keepdims=True
        )

    take_slots(tgt_t_ref, slots, rows, 32)

    @pl.when(this_round == ROUNDS - 1)
    def _():
        for m in range(4):
            out_ref[(where[2] + m) & 3] = rows[m * 8 * TOK : (m + 1) * 8 * TOK, :].astype(BF)


def attend_values_back(where, tgt, tgt_t, probs, ro, lt, gm):
    rows = 8 * TOK
    return kernel_call(
        values_back_kernel,
        grid=(ROUNDS,),
        in_specs=[
            SMEM,
            per_round((32, TOK)),
            per_round((TOK, 128)),
            per_round((PAIRS, 256, 128)),
            fixed((ROUNDS, rows, HEAD_DIM)),
            fixed((ROUNDS, rows, HEAD_DIM)),
            fixed((rows, HEAD_DIM)),
        ],
        out_specs=[
            fixed((4, rows, HEAD_DIM)), per_round((PAIRS, 128, 128)), per_round((PAIRS, 128)),
        ],
        out_shape=[
            jax.ShapeDtypeStruct((4, rows, HEAD_DIM), BF),
            jax.ShapeDtypeStruct((ROUNDS, PAIRS, 128, 128), BF),
            jax.ShapeDtypeStruct((ROUNDS, PAIRS, 128), F32),
        ],
        scratch_shapes=[
            pltpu.VMEM((PAIRS, 128, 128), BF),
            pltpu.VMEM((PAIRS, 2, 256, HEAD_DIM), F32),
            pltpu.VMEM((4 * rows, HEAD_DIM), F32),
            pltpu.VMEM((ROUNDS, rows, 256), BF),
        ],
        compiler_params=params(26),
        cost_estimate=cost(12),
        far_in=(1, 2, 3, 4, 5),
        far_out=(0, 1, 2),
        name="attend_values_back",
    )(where, tgt, tgt_t, probs, ro, lt, gm)


def scores_back_kernel(
    half, where, tgt_t_ref, mask_ref, probs_ref, values_ref, qm_ref, gd_ref, gt_ref, *refs
):
    if half == 0:
        gs_ref, rows_out, slots, rows = refs
    else:
        rows_in, gs_ref, out_ref, slots, rows = refs
    step = pl.program_id(0)

    @pl.when(step == 0)
    def _():
        if half == 0:
            rows[...] = jnp.zeros_like(rows)
        else:
            rows[...] = rows_in[...]

    @pl.loop(0, PAIRS, unroll=16)
    def _(p):
        probs = probs_ref[0, p].astype(F32)
        grad_probs = dot(values_ref[0, p], diagonal_t(gd_ref[0, p]))
        agreement = jnp.sum(probs * grad_probs, axis=0, keepdims=True)
        grad_scores = probs * (grad_probs + (gt_ref[0, pl.ds(p, 1), :] - agreement))
        seen = mask_ref[0, p].astype(F32) == 0.0
        grad_scores = jnp.where(seen, grad_scores, 0.0).astype(BF)
        gs_ref[0, p] = grad_scores
        grad_keys = dot(grad_scores, diagonal(qm_ref[0, p]))
        slots[p, 0] = grad_keys[:, :128]
        slots[p, 1] = grad_keys[:, 128:]

    take_slots(tgt_t_ref, slots, rows, 32)

    @pl.when(step == 1)
    def _():
        if half == 0:
            rows_out[...] = rows[...]
        else:
            for m in range(4):
                out_ref[(where[2] + m) & 3] = rows[m * 8 * TOK : (m + 1) * 8 * TOK, :].astype(BF)


def attend_scores_back(half, where, arrays, begun):
    rows = 8 * TOK
    shapes = [
        (TOK, 128), (PAIRS, 256, 128), (PAIRS, 256, 128), (PAIRS, 256, 256),
        (PAIRS, 128, 128), (PAIRS, 128, 128), (PAIRS, 128),
    ]
    this_half = lambda shape: pl.BlockSpec(
        (1,) + shape, lambda r: (2 * half + r,) + (0,) * len(shape)
    )
    slots = (PAIRS, 256, 128)
    if half == 0:
        outs = [((4 * rows, HEAD_DIM), F32)]
    else:
        outs = [((4, rows, HEAD_DIM), BF)]
    return kernel_call(
        functools.partial(scores_back_kernel, half),
        grid=(2,),
        in_specs=[SMEM] + [this_half(shape) for shape in shapes] + [fixed(a.shape) for a in begun],
        out_specs=[per_round(slots)] + [fixed(shape) for shape, _ in outs],
        out_shape=[jax.ShapeDtypeStruct((2,) + slots, BF)]
        + [jax.ShapeDtypeStruct(shape, t) for shape, t in outs],
        scratch_shapes=[
            pltpu.VMEM((PAIRS, 2, 256, HEAD_DIM), F32),
            pltpu.VMEM((4 * rows, HEAD_DIM), F32),
        ],
        compiler_params=params(30),
        cost_estimate=cost(10),
        far_in=tuple(range(1, 8)),
        far_out=(0,) if half == 0 else (0, 1),
        name=f"attend_scores_back_{half}",
    )(where, *arrays, *begun)


def queries_back_kernel(tgt_t_ref, first_ref, second_ref, keys_ref, gq_ref, slots):
    step = pl.program_id(0)

    @pl.when(step == 0)
    def _():
        gq_ref[...] = jnp.zeros_like(gq_ref)

    def one_round(gs_ref):
        @pl.loop(0, PAIRS, unroll=16)
        def _(p):
            grad_queries = t_dot(gs_ref[0, p], keys_ref[0, p])
            slots[p, 0] = grad_queries[:64, :128]
            slots[p, 1] = grad_queries[64:, 128:]

    @pl.when(step < 2)
    def _():
        one_round(first_ref)

    @pl.when(step >= 2)
    def _():
        one_round(second_ref)

    take_slots(tgt_t_ref, slots, gq_ref, 8)


def attend_queries_back(tgt_t, first, second, keys):
    rows, slots = 8 * TOK, (1, PAIRS, 256, 128)
    return kernel_call(
        queries_back_kernel,
        grid=(ROUNDS,),
        in_specs=[
            per_round((TOK, 128)),
            pl.BlockSpec(slots, lambda r: (jnp.minimum(r, 1), 0, 0, 0)),
            pl.BlockSpec(slots, lambda r: (jnp.maximum(r, 2) - 2, 0, 0, 0)),
            per_round((PAIRS, 256, 256)),
        ],
        out_specs=[fixed((rows, HEAD_DIM))],
        out_shape=[jax.ShapeDtypeStruct((rows, HEAD_DIM), F32)],
        scratch_shapes=[pltpu.VMEM((PAIRS, 2, 64, HEAD_DIM), F32)],
        compiler_params=params(20),
        cost_estimate=cost(8),
        far_in=(0, 1, 2, 3),
        far_out=(0,),
        name="attend_queries_back",
    )(tgt_t, first, second, keys)[0]


def local(
    first_in, second_in, attn_gain, attn_shift, w_joint, w_value, w_output, ffn_gain, ffn_shift,
    w_inner, b_inner, w_outer, b_outer, buckets, cot_first, cot_second,
):
    y, z, x, c = (lax.axis_index(a) for a in AXES)
    where = jnp.stack([y, z, x, c]).astype(jnp.int32)
    low_core = c == 0

    def by_core(first, second):
        return jnp.where(low_core, first, second)

    vec = jnp.concatenate(
        [attn_gain, attn_shift, ffn_gain, ffn_shift, b_outer, b_inner, jnp.zeros((56,), BF)]
    ).astype(F32)
    keep, give = pack(
        where, w_joint, w_value, w_output, w_inner, vec.reshape(1, 128), buckets[:, :, 0]
    )
    tok_near = [send(second_in, "z", 3), send(second_in, "z", 1)]
    got = swap(give)
    gathered = lax.all_gather(
        payload(where, keep, got, w_outer)[0], CHIPS, axis=0, tiled=False
    ).reshape(64, 80, D)
    y_got = gather(chip_message(where, keep, got)[0], "y")
    heads_out, second_late, tok_near = sync(
        head_messages(where, *y_got), second_in, tok_near
    )
    z_got = scatter(heads_out, "z")
    tok_last = send(second_late, "z", 2)
    z_got, tok_last = sync(z_got, tok_last)
    tok_far = jnp.stack([tok_near[0], tok_last, tok_near[1]])
    sib_tok = swap(jnp.concatenate([second_in[None], tok_far]))
    tokens = (second_in, tok_far, sib_tok)
    x_got = gather(jnp.concatenate(z_got), "x")
    wq, par, tgt, tgt_t, counts, vec = assemble(where, *x_got)

    normed, queries = project(where, tokens, par, wq)
    queries, counts, vec = sync(queries, counts, vec)
    q_pieces = gather(queries, "x")
    mask, par_ffn, bias_inner = make_mask(where, counts, vec)
    values, wv = project_values(where, x_got, normed)
    values, q_pieces[1], q_pieces[3], sib_rows = sync(
        values, q_pieces[1], q_pieces[3], jnp.stack([first_in, cot_first, cot_second])
    )
    v_pieces = gather(values, "x")
    sib_rows = swap(sib_rows)
    probs, key_slots, query_slots, logs = attend_scores(q_pieces, tgt, mask)
    mixed_head, round_out, round_total, value_slots = attend_values(
        v_pieces, tgt, tgt_t, probs, logs
    )

    mix_own = jnp.concatenate(
        scatter([mixed_head[k * 256 : (k + 1) * 256] for k in range(4)], "z"), axis=1
    )
    mix_sib = swap(mix_own)
    first_sum, first_out, input_t, active, grad_hidden, back, hid_sum, cot_sum = feed(
        where, mix_own, mix_sib, first_in, cot_second, sib_rows, par_ffn, bias_inner, gathered
    )
    a_parts = inner_grads(where, active, grad_hidden, input_t, cot_second, sib_rows)
    back_sib, a_parts = sync(swap(back), a_parts)
    grad_first, branch, g0, g1, g2, g3, norm_sums = first_back(
        where, back, back_sib, first_sum, cot_first, sib_rows, par_ffn, gathered
    )
    grad_mixed = scatter([g0, g1, g2, g3], "z")
    a_got = [send(a_parts[1], "y", 1), send(a_parts[3], "y", 3)]
    sums = jnp.stack([norm_sums[0], norm_sums[1], cot_sum[0]]).reshape(3, 64, 16)
    sums = jnp.pad(jnp.transpose(sums, (1, 0, 2)), ((0, 0), (0, 0), (0, 16)))
    sums = jnp.concatenate([sums, hid_sum[0].reshape(64, 1, 32)], axis=1).astype(BF)
    sums = jnp.pad(sums, ((0, 0), (0, 12), (0, 96)))
    b_parts = outer_grads(
        where, active, cot_second, sib_rows, mix_own, mix_sib, branch, sums
    )
    grad_mixed, b_parts = sync(grad_mixed, b_parts)

    b_got = [send(b_parts[1], "z", 1), send(b_parts[3], "z", 3)]
    gv, grad_slots, log_slots = attend_values_back(
        where, tgt, tgt_t, probs, round_out, round_total, jnp.concatenate(grad_mixed)
    )

    gv, grad_slots = sync(gv, grad_slots)
    gv_got = exchange(gv, "x")
    back_in = (tgt_t, mask, probs, value_slots, query_slots, grad_slots, log_slots)
    gs_first, half = attend_scores_back(0, where, back_in, ())
    a_got, b_got, a_far, b_far, half = sync(a_got, b_got, a_parts[2], b_parts[2], half)
    a_far, b_far = send(a_far, "y", 2), send(b_far, "z", 2)
    gs_second, gk = attend_scores_back(1, where, back_in, (half,))
    gv_got, gk, gs_second = sync(gv_got, gk, gs_second)

    gk_got = exchange(gk, "x")
    gq = attend_queries_back(tgt_t, gs_first, gs_second, key_slots)
    b_far, gq = sync(b_far, gq)
    b_parts = recut_b(
        where, *[part.reshape(4, 4, 32, 1152) for part in [b_parts[0], b_far] + b_got]
    )
    b_parts, a_far = sync(b_parts, a_far)
    b_got = scatter(b_parts, "y")
    a_parts = recut_a(
        where, *[part.reshape(4, 4, 16, 2560) for part in [a_parts[0], a_far] + a_got]
    )
    gk_got, a_parts = sync(gk_got, a_parts)

    a_got = scatter(a_parts, "z")
    back_own, back_give, *w_parts = project_back(
        where, tokens, wq, wv, normed, queries, gq, gk_got, gv_got
    )

    back_give, w_parts, b_got[1], b_got[3], a_got[1], a_got[3] = sync(
        back_give, w_parts, b_got[1], b_got[3], a_got[1], a_got[3]
    )
    w_got = scatter(w_parts, "y")
    back_got, active = sync(swap(back_give), active)
    back_chip = (back_own.astype(F32) + back_got.astype(F32)).astype(BF)
    second_own, second_give = second_parts(where, active, gathered)
    back_parts = [back_chip[k] for k in range(4)]
    back_far = send(back_parts[2], "z", 2)
    back_parts, w_got, a_got, b_got, second_give = sync(
        back_parts, w_got, a_got, b_got, second_give
    )
    second_got = swap(second_give)


    x_parts = scatter(join(where, *w_got, *a_got, *b_got), "x")
    x_parts[1], back_parts, back_far = sync(x_parts[1], back_parts, back_far)
    back_sum = [
        back_parts[0], send(back_parts[1], "z", 1), send(back_parts[3], "z", 3), back_far
    ]

    second_out = (second_in.astype(F32) + second_own + second_got + par_ffn[2]).astype(BF)
    *z_parts, chip_keep, chip_give, grad_outer, small = divide(where, *x_parts)
    w_got = scatter(z_parts, "z")
    w_keep, last_give = last(where, *w_got, chip_give)
    grad_joint, grad_value, norm, grad_inner, grad_output = finish(
        where, w_keep, chip_keep, swap(last_give)
    )
    grad_attn_gain, grad_attn_shift = norm[:, 0], norm[:, 64]
    mine16 = by_core(small[:3, :8], small[:3, 8:16])
    grad_ffn_gain, grad_ffn_shift, grad_b_outer = mine16[0], mine16[1], mine16[2]
    grad_b_inner = small[3, :32]

    attn_xhat, attn_scale = normalized(second_in.astype(F32))
    attn_back = norm_back(total_of(back_sum) * par[0], attn_xhat, attn_scale)
    grad_second = (cot_second.astype(F32) + attn_back).astype(BF)

    return (
        first_out, second_out, grad_first, grad_second, grad_attn_gain, grad_attn_shift,
        grad_joint, grad_value, grad_output, grad_ffn_gain, grad_ffn_shift, grad_inner,
        grad_b_inner, grad_outer, grad_b_outer,
    )


def solution(mesh):
    chips = Mesh(mesh.devices.reshape(4, 4, 4, 2), AXES)
    rows, flat = P(AXES, None), P(AXES)
    return jax.shard_map(
        local,
        mesh=chips,
        in_specs=(
            rows, rows, flat, flat, rows, rows, rows, flat, flat, rows, flat, rows, flat,
            P(None, AXES, None), rows, rows,
        ),
        out_specs=(
            rows, rows, rows, rows, flat, flat, rows, rows, rows, flat, flat, rows, flat, rows,
            flat,
        ),
        check_vma=False,
    )
```
